32 devices in a mesh: ep: 8 (over z, y), tp: 4 (over x, core).
Axes of the slice: x: 2, y: 2, z: 4, core: 2. Of those that a mesh axis runs over, the one named last changes fastest.
Arguments:
- hidden_in: bfloat16 [4096, 1280], P(('ep', 'tp')), may hold values from -6 to 6
- seq_lengths: int32 [8, 3], P('ep'), may hold values from 16 to 480, as said below
- expert_ids: int32 [4096, 7], P(('ep', 'tp')), may hold values from 0 to 15, all different within a row; in each aligned block of 128 rows (0 to 127, 128 to 255, ...) at most 96 rows name the same one
- attn_gain: bfloat16 [1280], P(('ep', 'tp')), may hold values from 0.5 to 1.5
- w_query: bfloat16 [1280, 1280], P(('ep', 'tp')), may hold values from -0.15625 to 0.15625
- w_key: bfloat16 [1280, 1280], P(('ep', 'tp')), may hold values from -0.15625 to 0.15625
- w_value: bfloat16 [1280, 1280], P(('ep', 'tp')), may hold values from -0.15625 to 0.15625
- w_out: bfloat16 [1280, 1280], P(('ep', 'tp')), may hold values from -2 to 2
- ffn_gain: bfloat16 [1280], P(('ep', 'tp')), may hold values from 0.5 to 1.5
- shared_gate: bfloat16 [1280, 1792], P(('ep', 'tp')), may hold values from -0.15625 to 0.15625
- shared_up: bfloat16 [1280, 1792], P(('ep', 'tp')), may hold values from -0.15625 to 0.15625
- shared_down: bfloat16 [1792, 1280], P(('ep', 'tp')), may hold values from -0.125 to 0.125
- router: bfloat16 [1280, 16], P(('ep', 'tp')), may hold values from -0.078125 to 0.078125
- expert_gate: bfloat16 [16, 896, 1280], P('ep', 'tp'), may hold values from -0.15625 to 0.15625
- expert_up: bfloat16 [16, 896, 1280], P('ep', 'tp'), may hold values from -0.15625 to 0.15625
- expert_down: bfloat16 [16, 896, 1280], P('ep', 'tp'), may hold values from -6 to 6
- cotangent: bfloat16 [4096, 1280], P(('ep', 'tp')), may hold values from -6 to 6
Outputs:
- layer_output: bfloat16 [4096, 1280], P(('ep', 'tp'))
- input_grad: float32 [4096, 1280], P(('ep', 'tp'))
- attn_gain_grad: float32 [1280], P(('ep', 'tp'))
- query_grad: float32 [1280, 1280], P(('ep', 'tp'))
- key_grad: float32 [1280, 1280], P(('ep', 'tp'))
- value_grad: float32 [1280, 1280], P(('ep', 'tp'))
- out_proj_grad: float32 [1280, 1280], P(('ep', 'tp'))
- ffn_gain_grad: float32 [1280], P(('ep', 'tp'))
- shared_gate_grad: float32 [1280, 1792], P(('ep', 'tp'))
- shared_up_grad: float32 [1280, 1792], P(('ep', 'tp'))
- shared_down_grad: float32 [1792, 1280], P(('ep', 'tp'))
- router_grad: float32 [1280, 16], P(('ep', 'tp'))
- expert_gate_grad: float32 [16, 896, 1280], P('ep', 'tp')
- expert_up_grad: float32 [16, 896, 1280], P('ep', 'tp')
- expert_down_grad: float32 [16, 896, 1280], P('ep', 'tp')
The draws below stay inside these ranges and needn't reach their ends.
Inputs may be any that keep to these rules, and one draw needn't show every extreme that they name: `seq_lengths`: each row holds, in order, the lengths of the three sequences of one group; they sum to 512. `expert_ids`: each token names 7 different experts; among the 128 tokens of one device no expert is named by more than 96 tokens.
All inputs are finite; a program needn't handle non-finite values.
Results may differ from the reference program's by a relative error of at most 0.019.
Values may be sent and summed in bfloat16 or wider, within the bound.
A program may use at most 384 MiB of HBM per device.

```python
import math
import jax
import jax.numpy as jnp
import numpy as np
from jax import lax

D = 1280
HEADS = 10
HEAD_DIM = 128
FS = 1792
FE = 896
TOP = 7
TOK_DEV = 128
QD = 1280
EXPERTS = 16
GLEN = 512
GROUPS = 8
TOKENS = 4096
CAP = 96
N_TP = 4


def draw_seq_lengths(key, part):
    key = jax.random.fold_in(key, 11)
    first_key, last_key = jax.random.split(key)
    first_len = jax.random.randint(first_key, (GROUPS, 1), TOK_DEV // 8, TOK_DEV // 2 + 1)
    last_len = jax.random.randint(last_key, (GROUPS, 1), TOK_DEV // 8, TOK_DEV // 2 + 1)
    middle_len = N_TP * TOK_DEV - first_len - last_len
    return jnp.concatenate([first_len, middle_len, last_len], axis=1).astype(jnp.int32)


def shard_levels(rng, shape, cuts, low, high):
    def one(position, shards_of):
        draws = jax.random.uniform(jax.random.fold_in(jax.random.fold_in(rng, 6), position), (shards_of,), jnp.float32, low / len(cuts), high / len(cuts))
        return jnp.repeat(jnp.exp(draws), shape[position] // shards_of).reshape((-1,) + (1,) * (len(shape) - position - 1))

    level = one(*cuts[0])
    for cut in cuts[1:]:
        level = level * one(*cut)
    return level


def assign_block(rng, own, number, rows, amount, top, most, skew):
    sequence = jax.random.permutation(rng, amount)
    packed, usual = load_shares(amount, rows * top, most, skew, True), load_shares(amount, rows * top, most, skew, False)
    places = jnp.arange(amount)

    def named(tallies, rotation):
        used = int((tallies > 0).sum())
        fixed = max(1, used // 4)
        passed = fixed + (places - fixed + rotation * (used - fixed)) % max(1, amount - fixed)
        return jnp.zeros((amount,), jnp.int32).at[sequence[jnp.where(places < fixed, places, passed)]].set(jnp.asarray(tallies, jnp.int32))

    tallies = jnp.where(number % 4 == 0, named(packed, number // 4), named(usual, number - number // 4 - 1))
    mixed = jax.random.permutation(jax.random.fold_in(own, 3), amount)
    giver, receiver = mixed[0:amount // 2 * 2:2], mixed[1:amount // 2 * 2:2]
    slack = jnp.minimum(tallies[giver] - 1, most - tallies[receiver]) // 2
    slack = jnp.where((giver == sequence[0]) | (receiver == sequence[0]) | (tallies[receiver] == 0), 0, jnp.maximum(slack, 0))
    passed = jax.random.randint(jax.random.fold_in(own, 4), (amount // 2,), 0, 1 << 20) % (slack + 1)
    tallies = tallies.at[giver].add(-passed).at[receiver].add(passed)
    labels = jnp.searchsorted(jnp.cumsum(tallies), jnp.arange(rows * top), side="right").astype(jnp.int32)
    listing = labels.reshape(top, rows).T
    listing = listing[jax.random.permutation(jax.random.fold_in(own, 1), rows)]
    rotation = jax.random.randint(jax.random.fold_in(own, 2), (rows, 1), 0, top)
    return jnp.take_along_axis(listing, (jnp.arange(top)[None, :] + rotation) % top, axis=1)


def load_shares(count, total, bound, slope, full):
    loads = [(1 << 20) // math.isqrt(standing ** slope) + 1 for standing in range(1, count + 1)]
    largest = bound if full else min(bound, max(-(-total // count), total * loads[0] // sum(loads)))
    least = 1 if total - largest >= count - 1 else 0
    holding, rest = [largest] + [least] * (count - 1), total - largest - least * (count - 1)
    while rest > 0:
        free = [i for i in range(1, count) if holding[i] < largest] or [i for i in range(1, count) if holding[i] < bound]
        pool, remaining = sum([loads[i] for i in free]), rest
        for i in free:
            more = min(bound - holding[i], max(1, remaining * loads[i] // pool), rest)
            holding[i] = holding[i] + more
            rest = rest - more
    return np.array(holding)


def noise(own_key, shape, spread, limit, cuts=(), kind=jnp.bfloat16):
    array = jax.random.normal(own_key, shape, jnp.float32) * spread
    if len(cuts) > 0:
        array = shard_levels(own_key, shape, cuts, -0.22, 0.18) * array
    return jnp.clip(array, min=-limit, max=limit).astype(kind)


def setup_inputs(seed: int = 0) -> dict:
    seeds = jax.random.split(jax.random.key(seed), 18)
    hidden_in = noise(seeds[0], (TOKENS, D), 1.0, 6.0, ((0, 32),))
    seq_lengths = draw_seq_lengths(jax.random.fold_in(seeds[17], 71), 0)
    expert_ids_keys = jax.random.split(jax.random.fold_in(seeds[2], 1), TOKENS // TOK_DEV)
    expert_ids_turns = jax.random.permutation(jax.random.fold_in(seeds[2], 3), TOKENS // TOK_DEV)
    expert_ids = jax.vmap(lambda own, number: assign_block(jax.random.fold_in(seeds[2], 2), own, number, TOK_DEV, EXPERTS, TOP, CAP, 1))(expert_ids_keys, expert_ids_turns).reshape((TOKENS, TOP))
    attn_gain = jnp.clip(1.0 + 0.1 * jax.random.normal(seeds[3], (D,), jnp.float32), 0.5, 1.5).astype(jnp.bfloat16)
    w_query = noise(seeds[4], (D, QD), D ** -0.5, 0.15625, ((0, 32),))
    w_key = noise(seeds[5], (D, QD), D ** -0.5, 0.15625, ((0, 32),))
    w_value = noise(seeds[6], (D, QD), D ** -0.5, 0.15625, ((0, 32),))
    w_out = noise(seeds[7], (QD, D), (max(QD // 128, 1)) ** -0.5, 2.0, ((0, 32),))
    ffn_gain = jnp.clip(1.0 + 0.1 * jax.random.normal(seeds[8], (D,), jnp.float32), 0.5, 1.5).astype(jnp.bfloat16)
    shared_gate = noise(seeds[9], (D, FS), D ** -0.5, 0.15625, ((0, 32),))
    shared_up = noise(seeds[10], (D, FS), D ** -0.5, 0.15625, ((0, 32),))
    shared_down = noise(seeds[11], (FS, D), FS ** -0.5, 0.125, ((0, 32),))
    router = noise(seeds[12], (D, EXPERTS), (4 * D) ** -0.5, 0.078125, ((0, 32),))
    expert_gate = noise(seeds[13], (EXPERTS, FE, D), D ** -0.5, 0.15625, ((0, 8), (1, 4)))
    expert_up = noise(seeds[14], (EXPERTS, FE, D), D ** -0.5, 0.15625, ((0, 8), (1, 4)))
    expert_down = noise(seeds[15], (EXPERTS, FE, D), 1 ** -0.5, 6.0, ((0, 8), (1, 4)))
    cotangent = noise(seeds[16], (TOKENS, D), 1.0, 6.0, ((0, 32),))
    return dict(hidden_in=hidden_in, seq_lengths=seq_lengths, expert_ids=expert_ids, attn_gain=attn_gain, w_query=w_query, w_key=w_key, w_value=w_value, w_out=w_out, ffn_gain=ffn_gain, shared_gate=shared_gate, shared_up=shared_up, shared_down=shared_down, router=router, expert_gate=expert_gate, expert_up=expert_up, expert_down=expert_down, cotangent=cotangent)


@jax.custom_vjp
def low(v):
    return lax.optimization_barrier(v.astype(jnp.bfloat16)).astype(jnp.float32)

@jax.custom_vjp
def low_back(v):
    return v

def low_keep(v):
    return (low(v), None)

def low_pass(kept, grad):
    return (grad,)

def back_keep(v):
    return (v, None)

def back_low(kept, grad):
    return (low(grad),)
low.defvjp(low_keep, low_pass)
low_back.defvjp(back_keep, back_low)
epsilon = 1e-06

def matmul(left_side, right_side):
    return jnp.dot(left_side, right_side, precision=lax.Precision.HIGHEST)

def rms_norm(values, gain):
    inverse = lax.rsqrt(lax.optimization_barrier(jnp.mean(values * values, axis=-1, keepdims=True)) + epsilon)
    return values * inverse * gain

def documents(positions, lengths):
    seq_ends = jnp.cumsum(lengths).astype(jnp.int32)
    doc_index = (positions >= seq_ends[0]).astype(jnp.int32) + (positions >= seq_ends[1]).astype(jnp.int32)
    seq_starts = jnp.where(doc_index == 0, 0, jnp.where(doc_index == 1, seq_ends[0], seq_ends[1]))
    return (doc_index, positions - seq_starts)

def rotary_tables(offsets):
    half_dim = HEAD_DIM // 2
    frequency = 10000.0 ** (-2.0 * jnp.arange(half_dim, dtype=jnp.float32) / HEAD_DIM)
    angles = offsets.astype(jnp.float32)[:, None] * frequency[None, :]
    return (jnp.cos(angles)[:, None, :], jnp.sin(angles)[:, None, :])

def rotate(values, cosine, sine_table):
    half_dim = values.shape[-1] // 2
    first_half = values[..., :half_dim]
    second_half = values[..., half_dim:]
    return jnp.concatenate([first_half * cosine - second_half * sine_table, first_half * sine_table + second_half * cosine], axis=-1)

def group_layer(params, inputs, lengths, route_ids):
    attn_gain, w_query, w_key, w_value, w_out, ffn_gain, shared_gate, shared_up, shared_down, router, expert_gate, expert_up, expert_down = params
    highest = lax.Precision.HIGHEST
    positions = jnp.arange(GLEN, dtype=jnp.int32)
    doc_index, offsets = documents(positions, lengths)
    allowed = (doc_index[:, None] == doc_index[None, :]) & (positions[:, None] >= positions[None, :])
    cosine, sine_table = rotary_tables(offsets)
    normed = low(rms_norm(inputs, attn_gain))
    queries = low(rotate(low_back(matmul(normed, w_query)).reshape(GLEN, HEADS, HEAD_DIM), cosine, sine_table))
    key_rows = low(rotate(low_back(matmul(normed, w_key)).reshape(GLEN, HEADS, HEAD_DIM), cosine, sine_table))
    value_rows = low(low_back(matmul(normed, w_value))).reshape(GLEN, HEADS, HEAD_DIM)
    scores = low_back(jnp.einsum('qhd,khd->hqk', queries, key_rows, precision=highest) * HEAD_DIM ** (-0.5))
    softmaxed = jax.nn.softmax(jnp.where(allowed[None], scores, -1e+30), axis=-1)
    attended = jnp.einsum('hqk,khd->qhd', low(softmaxed), value_rows, precision=highest).reshape(GLEN, QD)
    attn_out = low_back(matmul(low(low_back(attended)), w_out))
    residual = inputs + attn_out
    normed_two = low(rms_norm(residual, ffn_gain))
    shared_gate_pre = low_back(matmul(normed_two, shared_gate))
    shared_up_pre = low_back(matmul(normed_two, shared_up))
    shared_act = low(jax.nn.silu(shared_gate_pre) * shared_up_pre)
    shared_out = low_back(matmul(shared_act, shared_down))
    logits = matmul(normed_two, router)
    affinity = jax.nn.softmax(logits, axis=-1)
    expert_range = jnp.arange(EXPERTS, dtype=jnp.int32)
    choose = (route_ids[:, :, None] == expert_range[None, None, :]).astype(jnp.float32)
    gate_values = jnp.einsum('tje,te->tj', choose, affinity, precision=highest)
    flat_ids = route_ids.reshape(-1).astype(jnp.int32)
    route_hits = (flat_ids[:, None] == expert_range[None, :]).astype(jnp.int32)
    route_rank = lax.optimization_barrier(jnp.sum(jnp.cumsum(route_hits, axis=0) * route_hits, axis=1)) - 1
    group_cap = N_TP * CAP
    slot_index = flat_ids * group_cap + route_rank
    routed_in = low_back(jnp.broadcast_to(normed_two[:, None, :], (GLEN, TOP, D)).reshape(GLEN * TOP, D))
    buffer = jnp.zeros((EXPERTS * group_cap, D), jnp.float32).at[slot_index].set(routed_in).reshape(EXPERTS, group_cap, D)
    expert_gate_pre = low_back(jnp.einsum('ecd,efd->ecf', buffer, expert_gate, precision=highest))
    expert_up_pre = low_back(jnp.einsum('ecd,efd->ecf', buffer, expert_up, precision=highest))
    expert_act = low(jax.nn.silu(expert_gate_pre) * expert_up_pre)
    expert_out = jnp.einsum('ecf,efd->ecd', expert_act, expert_down, precision=highest).reshape(EXPERTS * group_cap, D)
    routed = low(low_back(expert_out[slot_index])).reshape(GLEN, TOP, D)
    routed_sum = jnp.einsum('tj,tjd->td', gate_values, routed, precision=highest)
    return residual + shared_out + routed_sum

def reference(hidden_in, seq_lengths, expert_ids, attn_gain, w_query, w_key, w_value, w_out, ffn_gain, shared_gate, shared_up, shared_down, router, expert_gate, expert_up, expert_down, cotangent):
    params = tuple((weight.astype(jnp.float32) for weight in (attn_gain, w_query, w_key, w_value, w_out, ffn_gain, shared_gate, shared_up, shared_down, router, expert_gate, expert_up, expert_down)))
    inputs = hidden_in.astype(jnp.float32).reshape(GROUPS, GLEN, D)
    route_ids = expert_ids.reshape(GROUPS, GLEN, TOP)
    layer_step = jax.checkpoint(group_layer)

    def forward(weights, values):

        def scan_step(scan_carry, group_item):
            return (scan_carry, layer_step(weights, group_item[0], group_item[1], group_item[2]))
        unused_carry, layer_outs = lax.scan(scan_step, jnp.zeros((), jnp.float32), (values, seq_lengths, route_ids))
        return layer_outs
    layer_outs, pullback = jax.vjp(forward, params, inputs)
    weight_grads, input_grad = pullback(cotangent.astype(jnp.float32).reshape(GROUPS, GLEN, D))
    return (layer_outs.reshape(TOKENS, D).astype(jnp.bfloat16), input_grad.reshape(TOKENS, D), weight_grads[0], weight_grads[1], weight_grads[2], weight_grads[3], weight_grads[4], weight_grads[5], weight_grads[6], weight_grads[7], weight_grads[8], weight_grads[9], weight_grads[10], weight_grads[11], weight_grads[12])
```

```python
import functools

import jax
import jax.numpy as jnp
from jax import lax
from jax.experimental import pallas as pl
from jax.experimental.pallas import tpu as pltpu
from jax.sharding import PartitionSpec as P

HEADS = 10
AXES = ("ep", "tp")
MESH = pl.DeviceIdType.MESH
VMEM_BUDGET = 56 * 2**20

epsilon = 1e-06

bf16 = jnp.bfloat16
f32 = jnp.float32


def place():
    ep, tp = lax.axis_index("ep"), lax.axis_index("tp")
    return ep // 2, ep % 2, tp // 2, tp % 2


def device(line, a, b, c):
    return (line * 2 + a, b * 2 + c)


def number(line, a, b, c):
    return ((line * 2 + a) * 2 + b) * 2 + c


def halves(shape):
    rows, cols = shape
    if cols % 256 == 0:
        return (
            (pl.ds(0, rows), pl.ds(0, cols // 2)),
            (pl.ds(0, rows), pl.ds(cols // 2, cols // 2)),
        )
    return ((pl.ds(0, rows // 2), pl.ds(0, cols)), (pl.ds(rows // 2, rows // 2), pl.ds(0, cols)))


def greet(partners):
    barrier = pltpu.get_barrier_semaphore()
    for partner in partners:
        pl.semaphore_signal(barrier, inc=1, device_id=partner, device_id_type=MESH)
    pl.semaphore_wait(barrier, len(partners))


def gather_kernel(lines, n_all, n_group, *refs):
    n = n_all + n_group
    ins, outs = refs[:n], refs[n : 2 * n]
    send_sem, recv_sem, group_send, group_recv, local_sem = refs[2 * n :]
    z, a, b, c = place()
    oa, ob, oc = 1 - a, 1 - b, 1 - c
    to_b, to_a, to_c = device(z, a, ob, c), device(z, oa, b, c), device(z, a, b, oc)
    to_line = [None] + [device(lax.rem(z + s, lines), a, b, c) for s in range(1, lines)]
    greet([to_b, to_a, to_c] + to_line[1:])

    back = [lax.rem(z + lines - s, lines) for s in range(lines)]
    started = []

    def slot(kind, step=0):
        return {"z": 0, "x": 1, "y": 2, "p": 3, "q": 4, "sz": 5, "sx": 6, "sy": 7, "sp": 8, "sq": 9}[
            kind
        ] * lines + step

    def send(i, kind, step, src, dst, to):
        copy = pltpu.make_async_remote_copy(
            src, dst, send_sem.at[i, slot(kind, step)], recv_sem.at[i, slot(kind, step)],
            device_id=to, device_id_type=MESH,
        )
        copy.start()
        started.append(copy)

    def arrived(i, kind, step, dst):
        pltpu.make_async_remote_copy(
            dst, dst, send_sem.at[i, slot(kind, step)], recv_sem.at[i, slot(kind, step)],
            device_id=to_c, device_id_type=MESH,
        ).wait_recv()

    locals_ = []
    group_copies = []
    for g in range(n_group):
        src, out = ins[n_all + g], outs[n_all + g]
        dst = out.at[b * 2 + c]
        keep = pltpu.make_async_copy(src, dst, local_sem.at[n_all + g])
        keep.start()
        locals_.append(keep)
        for k, to in enumerate((to_c, to_b)):
            copy = pltpu.make_async_remote_copy(
                src, dst, group_send.at[g, k], group_recv.at[g, k], device_id=to, device_id_type=MESH
            )
            copy.start()
            group_copies.append(copy)
    for i in range(n_all):
        src, own = ins[i], outs[i].at[number(z, a, b, c)]
        keep = pltpu.make_async_copy(src, own, local_sem.at[i])
        keep.start()
        locals_.append(keep)
        send(i, "x", 0, src, own, to_b)
        send(i, "y", 0, src, own, to_a)
        for s in range(1, lines):
            send(i, "z", s, src, own, to_line[s])
        send(i, "sz", 0, src, own, to_c)
    for g in range(n_group):
        out = outs[n_all + g]
        got = out.at[ob * 2 + c]
        pltpu.make_async_remote_copy(
            got, got, group_send.at[g, 1], group_recv.at[g, 1], device_id=to_b, device_id_type=MESH
        ).wait_recv()
        copy = pltpu.make_async_remote_copy(
            got, got, group_send.at[g, 2], group_recv.at[g, 2], device_id=to_c, device_id_type=MESH
        )
        copy.start()
        group_copies.append(copy)
    for s in range(lines):
        for i in range(n_all):
            out = outs[i]
            first, second = halves(out.shape[1:])
            at = back[s]
            if s > 0:
                got = out.at[number(at, a, b, c)]
                arrived(i, "z", s, got)
                send(i, "x", s, got, got, to_b)
                send(i, "y", s, got, got, to_a)
                send(i, "sz", s, got, got, to_c)
        for i in range(n_all):
            out = outs[i]
            first, second = halves(out.shape[1:])
            at = back[s]
            got = out.at[number(at, a, ob, c)]
            arrived(i, "x", s, got)
            half = out.at[(number(at, a, ob, c),) + first]
            send(i, "p", s, half, half, to_a)
            send(i, "sx", s, got, got, to_c)
            got = out.at[number(at, oa, b, c)]
            arrived(i, "y", s, got)
            half = out.at[(number(at, oa, b, c),) + second]
            send(i, "q", s, half, half, to_b)
            send(i, "sy", s, got, got, to_c)
    for s in range(lines):
        for i in range(n_all):
            out = outs[i]
            first, second = halves(out.shape[1:])
            at = back[s]
            for kind, part in (("p", first), ("q", second)):
                half = out.at[(number(at, oa, ob, c),) + part]
                arrived(i, kind, s, half)
                send(i, "s" + kind, s, half, half, to_c)
    for s in range(lines):
        for i in range(n_all):
            out = outs[i]
            first, second = halves(out.shape[1:])
            at = back[s]
            arrived(i, "sz", s, out.at[number(at, a, b, oc)])
            arrived(i, "sx", s, out.at[number(at, a, ob, oc)])
            arrived(i, "sy", s, out.at[number(at, oa, b, oc)])
            arrived(i, "sp", s, out.at[(number(at, oa, ob, oc),) + first])
            arrived(i, "sq", s, out.at[(number(at, oa, ob, oc),) + second])
    for g in range(n_group):
        out = outs[n_all + g]
        for k, t in ((0, b * 2 + oc), (2, ob * 2 + oc)):
            pltpu.make_async_remote_copy(
                out.at[t], out.at[t], group_send.at[g, k], group_recv.at[g, k],
                device_id=to_c, device_id_type=MESH,
            ).wait_recv()
    for copy in started + group_copies:
        copy.wait_send()
    for keep in locals_:
        keep.wait()


def gather(everyone, group, collective_id, name):
    eps, tps = lax.axis_size("ep"), lax.axis_size("tp")
    if eps % 2 or tps != 4 or eps * tps > 64:
        return [lax.all_gather(v, AXES, axis=0) for v in everyone], [
            lax.all_gather(v, "tp", axis=0) for v in group
        ]
    lines = eps // 2
    n_all, n_group = len(everyone), len(group)
    shapes = [jax.ShapeDtypeStruct((eps * tps,) + v.shape, v.dtype) for v in everyone] + [
        jax.ShapeDtypeStruct((tps,) + v.shape, v.dtype) for v in group
    ]
    anywhere = pl.BlockSpec(memory_space=pl.ANY)
    outs = pl.pallas_call(
        functools.partial(gather_kernel, lines, n_all, n_group),
        out_shape=shapes,
        in_specs=[anywhere] * (n_all + n_group),
        out_specs=[anywhere] * (n_all + n_group),
        scratch_shapes=[
            pltpu.SemaphoreType.DMA((n_all, 10 * lines)),
            pltpu.SemaphoreType.DMA((n_all, 10 * lines)),
            pltpu.SemaphoreType.DMA((max(n_group, 1), 3)),
            pltpu.SemaphoreType.DMA((max(n_group, 1), 3)),
            pltpu.SemaphoreType.DMA((n_all + n_group,)),
        ],
        compiler_params=pltpu.CompilerParams(collective_id=collective_id, has_side_effects=True),
        name=name,
    )(*everyone, *group)
    return outs[:n_all], outs[n_all:]


def add_into(dst, src, rows, first, cols, dst_at=(), src_at=()):
    step = 256 if cols % 256 == 0 else 128

    def body(k, carry):
        there = pl.ds(pl.multiple_of(first + k * step, 128), step)
        here = pl.ds(pl.multiple_of(k * step, 128), step)
        total = dst[dst_at + (slice(None), there)].astype(f32) + src[
            src_at + (slice(None), here)
        ].astype(f32)
        dst[dst_at + (slice(None), there)] = total.astype(bf16)
        return carry

    lax.fori_loop(0, cols // step, body, 0)


def reduce_kernel(lines, n_all, n_group, *refs):
    n = n_all + n_group
    ins, outs = refs[:n], refs[n : 2 * n]
    rest = list(refs[2 * n :])
    per_all = [[rest.pop(0) for _ in range(7)] for _ in range(n_all)]
    per_group = [[rest.pop(0) for _ in range(3)] for _ in range(n_group)]
    send_sem, recv_sem, group_send, group_recv, local_sem = rest
    z, a, b, c = place()
    oa, ob, oc = 1 - a, 1 - b, 1 - c
    to_b, to_a, to_c = device(z, a, ob, c), device(z, oa, b, c), device(z, a, b, oc)
    to_line = [None] + [device(lax.rem(z + s, lines), a, b, c) for s in range(1, lines)]
    greet([to_b, to_a, to_c] + to_line[1:])
    order = list(range(1, lines)) + [0]
    goal = [lax.rem(z + s, lines) for s in range(lines)]
    started = []
    kinds = {"s": 0, "p": 1, "q": 2, "x": 3, "y": 4, "z": 5}

    def sems(i, kind, step):
        k = kinds[kind] * lines + step
        return send_sem.at[i, k], recv_sem.at[i, k]

    def send(i, kind, step, src, dst, to):
        copy = pltpu.make_async_remote_copy(
            src, dst, *sems(i, kind, step), device_id=to, device_id_type=MESH
        )
        copy.start()
        started.append(copy)

    def arrived(i, kind, step, dst):
        pltpu.make_async_remote_copy(
            dst, dst, *sems(i, kind, step), device_id=to_c, device_id_type=MESH
        ).wait_recv()

    loads = {}
    for s in order:
        for i in range(n_all):
            acc, sib = per_all[i][:2]
            send(i, "s", s, ins[i].at[goal[s], :, :, oc], sib.at[s], to_c)
            load = pltpu.make_async_copy(
                ins[i].at[goal[s], :, :, c], acc.at[s], local_sem.at[i, s]
            )
            load.start()
            loads[i, s] = load
    group_copies, group_loads = [], []
    for g in range(n_group):
        acc, sib, far = per_group[g]
        src = ins[n_all + g]
        copy = pltpu.make_async_remote_copy(
            src.at[:, oc], sib, group_send.at[g, 0], group_recv.at[g, 0],
            device_id=to_c, device_id_type=MESH,
        )
        copy.start()
        group_copies.append(copy)
        load = pltpu.make_async_copy(src.at[:, c], acc, local_sem.at[n_all + g, 0])
        load.start()
        group_loads.append(load)
    for s in order:
        for i in range(n_all):
            acc, sib, p, q, x, y, line = per_all[i]
            rows, cols = acc.shape[-2:]
            first, second = halves((rows, cols))
            loads[i, s].wait()
            arrived(i, "s", s, sib.at[s])
            for u, v in ((oa, ob), (a, ob), (oa, b), (a, b)):
                add_into(acc, sib, rows, 0, cols, (s, u, v), (s, u, v))
                if (u is oa) and (v is ob):
                    send(i, "p", s, acc.at[(s, oa, ob) + first], p.at[s], to_a)
                    send(i, "q", s, acc.at[(s, oa, ob) + second], q.at[s], to_b)
    for g in range(n_group):
        acc, sib, far = per_group[g]
        rows, cols = acc.shape[-2:]
        group_loads[g].wait()
        pltpu.make_async_remote_copy(
            sib, sib, group_send.at[g, 0], group_recv.at[g, 0], device_id=to_c, device_id_type=MESH
        ).wait_recv()
        for u in (ob, b):
            add_into(acc, sib, rows, 0, cols, (u,), (u,))
            if u is ob:
                copy = pltpu.make_async_remote_copy(
                    acc.at[ob], far, group_send.at[g, 1], group_recv.at[g, 1],
                    device_id=to_b, device_id_type=MESH,
                )
                copy.start()
                group_copies.append(copy)
    for s in order:
        for i in range(n_all):
            acc, sib, p, q, x, y, line = per_all[i]
            rows, cols = acc.shape[-2:]
            arrived(i, "p", s, p.at[s])
            add_into(acc, p, rows, 0, cols // 2, (s, a, ob), (s,))
            send(i, "x", s, acc.at[s, a, ob], x.at[s], to_b)
            arrived(i, "q", s, q.at[s])
            add_into(acc, q, rows, cols // 2, cols // 2, (s, oa, b), (s,))
            send(i, "y", s, acc.at[s, oa, b], y.at[s], to_a)
    for s in order:
        for i in range(n_all):
            acc, sib, p, q, x, y, line = per_all[i]
            rows, cols = acc.shape[-2:]
            arrived(i, "x", s, x.at[s])
            add_into(acc, x, rows, 0, cols, (s, a, b), (s,))
            arrived(i, "y", s, y.at[s])
            add_into(acc, y, rows, 0, cols, (s, a, b), (s,))
            if s > 0:
                send(i, "z", s, acc.at[s, a, b], line.at[s - 1], to_line[s])
    for g in range(n_group):
        acc, sib, far = per_group[g]
        pltpu.make_async_remote_copy(
            far, far, group_send.at[g, 1], group_recv.at[g, 1], device_id=to_b, device_id_type=MESH
        ).wait_recv()
        outs[n_all + g][...] = acc[b].astype(f32) + far[...].astype(f32)
    for i in range(n_all):
        acc, sib, p, q, x, y, line = per_all[i]
        for s in range(1, lines):
            arrived(i, "z", s, line.at[s - 1])
        total = acc[0, a, b].astype(f32)
        for s in range(1, lines):
            total = total + line[s - 1].astype(f32)
        outs[i][...] = total
    for copy in started + group_copies:
        copy.wait_send()


def reduce_scatter(everyone, group, collective_id, name):
    eps, tps = lax.axis_size("ep"), lax.axis_size("tp")
    need = sum(v.size * 2 * 3 // 2 + v.size // v.shape[0] * 8 for v in everyone) + sum(
        v.size * 4 for v in group
    )
    if eps % 2 or tps != 4 or need > VMEM_BUDGET:
        return [
            lax.psum_scatter(v, AXES, scatter_dimension=0).astype(f32) for v in everyone
        ], [lax.psum_scatter(v, "tp", scatter_dimension=0).astype(f32) for v in group]
    lines = eps // 2
    n_all, n_group = len(everyone), len(group)
    anywhere = pl.BlockSpec(memory_space=pl.ANY)
    vmem = pl.BlockSpec(memory_space=pltpu.VMEM)
    scratch = []
    for v in everyone:
        rows, cols = v.shape[1:]
        scratch += [
            pltpu.VMEM((lines, 2, 2, rows, cols), bf16),
            pltpu.VMEM((lines, 2, 2, rows, cols), bf16),
            pltpu.VMEM((lines, rows, cols // 2), bf16),
            pltpu.VMEM((lines, rows, cols // 2), bf16),
            pltpu.VMEM((lines, rows, cols), bf16),
            pltpu.VMEM((lines, rows, cols), bf16),
            pltpu.VMEM((lines - 1, rows, cols), bf16),
        ]
    for v in group:
        rows, cols = v.shape[1:]
        scratch += [
            pltpu.VMEM((2, rows, cols), bf16),
            pltpu.VMEM((2, rows, cols), bf16),
            pltpu.VMEM((rows, cols), bf16),
        ]
    scratch += [
        pltpu.SemaphoreType.DMA((n_all, 6 * lines)),
        pltpu.SemaphoreType.DMA((n_all, 6 * lines)),
        pltpu.SemaphoreType.DMA((max(n_group, 1), 2)),
        pltpu.SemaphoreType.DMA((max(n_group, 1), 2)),
        pltpu.SemaphoreType.DMA((n_all + n_group, lines)),
    ]
    outs = pl.pallas_call(
        functools.partial(reduce_kernel, lines, n_all, n_group),
        out_shape=[jax.ShapeDtypeStruct(v.shape[1:], f32) for v in list(everyone) + list(group)],
        in_specs=[anywhere] * (n_all + n_group),
        out_specs=[vmem] * (n_all + n_group),
        scratch_shapes=scratch,
        compiler_params=pltpu.CompilerParams(
            collective_id=collective_id, has_side_effects=True, vmem_limit_bytes=VMEM_BUDGET
        ),
        name=name,
    )(
        *[v.reshape((lines, 2, 2, 2) + v.shape[1:]) for v in everyone],
        *[v.reshape((2, 2) + v.shape[1:]) for v in group],
    )
    return outs[:n_all], outs[n_all:]


def documents(positions, lengths):
    seq_ends = jnp.cumsum(lengths)
    doc_index = (positions >= seq_ends[0]).astype(jnp.int32) + (positions >= seq_ends[1]).astype(
        jnp.int32
    )
    seq_starts = jnp.where(doc_index == 0, 0, jnp.where(doc_index == 1, seq_ends[0], seq_ends[1]))
    return (doc_index, positions - seq_starts)


def rotary_tables(offsets, head_dim):
    half_dim = head_dim // 2
    frequency = 10000.0 ** (-2.0 * jnp.arange(half_dim, dtype=f32) / head_dim)
    angles = offsets.astype(f32)[:, None] * frequency[None, :]
    return (jnp.cos(angles)[:, None, :], jnp.sin(angles)[:, None, :])


def rotate(values, cosine, sine_table):
    half_dim = values.shape[-1] // 2
    first_half = values[..., :half_dim]
    second_half = values[..., half_dim:]
    return jnp.concatenate(
        [
            first_half * cosine - second_half * sine_table,
            first_half * sine_table + second_half * cosine,
        ],
        axis=-1,
    )


def norm_back(grad_normed, unit_rows, inverse, gain):
    scaled = grad_normed * gain
    return inverse * (scaled - unit_rows * jnp.mean(scaled * unit_rows, axis=-1, keepdims=True))


def dot(left, right, contract):
    return lax.dot_general(left, right, ((contract[0], contract[1]), ((), ())), preferred_element_type=f32)


def dense_dot(left, right):
    return dot(left, right, ((1,), (0,)))


def dot_nt(left, right):
    return dot(left, right, ((1,), (1,)))


def dot_tn(left, right):
    return dot(left, right, ((0,), (0,)))


def on_device(
    hidden_in,
    seq_lengths,
    expert_ids,
    attn_gain,
    w_query,
    w_key,
    w_value,
    w_out,
    ffn_gain,
    shared_gate,
    shared_up,
    shared_down,
    router,
    expert_gate,
    expert_up,
    expert_down,
    cotangent,
):
    tok_count, model_width = hidden_in.shape
    eps, tps = lax.axis_size("ep"), lax.axis_size("tp")
    devices = eps * tps
    exp_local, exp_hidden = expert_gate.shape[:2]
    experts = exp_local * eps
    group_len = tps * tok_count
    tokens = devices * tok_count
    d_rows = w_query.shape[0]
    width = w_query.shape[1]
    sh_rows = shared_down.shape[0]
    head_dim = width // HEADS
    attn_scale = head_dim ** (-0.5)

    flat = jnp.concatenate([router.reshape(-1), attn_gain, ffn_gain])
    small_len = -(-flat.shape[0] // model_width) * model_width
    small = jnp.pad(flat, (0, small_len - flat.shape[0])).reshape(-1, model_width)
    small = jnp.pad(small, ((0, -small.shape[0] % 16), (0, 0)))
    weights = jnp.concatenate([w_query, w_key, w_value, w_out], axis=1)

    (all_weights, all_small, all_cot), (group_hidden,) = gather(
        [weights, small, cotangent], [hidden_in], 0, "gather_weights"
    )
    all_weights = all_weights.reshape(devices * d_rows, 4 * width)
    full_query = all_weights[:, :width]
    full_key = all_weights[:, width : 2 * width]
    full_value = all_weights[:, 2 * width : 3 * width]
    full_out = all_weights[:, 3 * width :]
    all_small = all_small.reshape(devices, -1)
    n_router = d_rows * experts
    full_router = all_small[:, :n_router].reshape(devices * d_rows, experts)
    gain_one = all_small[:, n_router : n_router + d_rows].reshape(-1).astype(f32)
    gain_two = all_small[:, n_router + d_rows : n_router + 2 * d_rows].reshape(-1).astype(f32)
    cot_all = all_cot.reshape(tokens, model_width)

    shared_cols = jnp.stack([shared_gate, shared_up], axis=1).reshape(d_rows, 2, devices, sh_rows)
    shared_cols = lax.all_to_all(
        shared_cols.transpose(2, 1, 3, 0), AXES, split_axis=0, concat_axis=0, tiled=True
    )
    shared_t = shared_cols.transpose(1, 2, 0, 3).reshape(2, sh_rows, model_width)

    lengths = seq_lengths[0]
    tp_index = lax.axis_index("tp")
    own_pos = tp_index * tok_count + jnp.arange(tok_count, dtype=jnp.int32)
    all_pos = jnp.arange(group_len, dtype=jnp.int32)
    own_doc, own_offset = documents(own_pos, lengths)
    all_doc, all_offset = documents(all_pos, lengths)
    allowed = (own_doc[:, None] == all_doc[None, :]) & (own_pos[:, None] >= all_pos[None, :])
    cosine, sine_table = rotary_tables(own_offset, head_dim)
    cosine_all, sine_all = rotary_tables(all_offset, head_dim)

    inputs = hidden_in.astype(f32)
    inverse_one = lax.rsqrt(jnp.mean(inputs * inputs, axis=-1, keepdims=True) + epsilon)
    unit_one = inputs * inverse_one
    normed = (unit_one * gain_one).astype(bf16)
    group_in = group_hidden.reshape(group_len, model_width).astype(f32)
    group_unit = group_in * lax.rsqrt(jnp.mean(group_in * group_in, axis=-1, keepdims=True) + epsilon)
    group_normed = (group_unit * gain_one).astype(bf16)

    queries = rotate(
        dense_dot(normed, full_query).reshape(tok_count, HEADS, head_dim), cosine, sine_table
    ).astype(bf16)
    key_rows = rotate(
        dense_dot(group_normed, full_key).reshape(group_len, HEADS, head_dim), cosine_all, sine_all
    ).astype(bf16)
    value_rows = dense_dot(group_normed, full_value).astype(bf16).reshape(group_len, HEADS, head_dim)

    def masked_scores():
        raw_scores = (
            jnp.einsum("qhd,khd->hqk", queries, key_rows, preferred_element_type=f32) * attn_scale
        )
        return jnp.where(allowed[None], raw_scores, -1e30)

    scores = masked_scores()
    row_peak = jnp.max(scores, axis=-1, keepdims=True)
    row_total = jnp.sum(jnp.exp(scores - row_peak), axis=-1, keepdims=True)
    softmaxed = jnp.exp(scores - row_peak) / row_total
    attended = (
        jnp.einsum("hqk,khd->qhd", softmaxed.astype(bf16), value_rows, preferred_element_type=f32)
        .reshape(tok_count, width)
        .astype(bf16)
    )
    residual = inputs + dense_dot(attended, full_out)
    inverse_two = lax.rsqrt(jnp.mean(residual * residual, axis=-1, keepdims=True) + epsilon)
    unit_two = residual * inverse_two
    normed_two = (unit_two * gain_two).astype(bf16)

    affinity = jax.nn.softmax(dense_dot(normed_two, full_router), axis=-1)
    expert_range = jnp.arange(experts, dtype=jnp.int32)
    named = jnp.any(expert_ids[:, :, None] == expert_range[None, None, :], axis=1)
    signed = jnp.where(named, affinity, -affinity)

    (all_normed, all_signed), _ = gather([normed_two, signed.T], [], 1, "gather_tokens")
    rows = all_normed.reshape(tokens, model_width)
    signed = all_signed.transpose(0, 2, 1).reshape(tokens, experts)

    first_expert = lax.axis_index("ep") * exp_local
    n_routed = exp_local * exp_hidden
    hidden = n_routed + sh_rows
    gate_w = jnp.concatenate([expert_gate.reshape(n_routed, model_width), shared_t[0]])
    up_w = jnp.concatenate([expert_up.reshape(n_routed, model_width), shared_t[1]])
    down_w = jnp.concatenate([expert_down.reshape(n_routed, model_width), shared_down])

    def mixture(rows, cot_rows, signed):
        count = rows.shape[0]
        mine = lax.dynamic_slice_in_dim(signed, first_expert, exp_local, axis=1)
        mine_named = mine > 0
        gates = jnp.where(mine_named, mine, 0.0)
        scale = jnp.concatenate(
            [jnp.repeat(gates, exp_hidden, axis=1), jnp.ones((count, sh_rows), f32)], axis=1
        )
        gate_pre = dot_nt(rows, gate_w)
        up_pre = dot_nt(rows, up_w)
        sigma = jax.nn.sigmoid(gate_pre)
        silu = gate_pre * sigma
        act = silu * up_pre
        act_scaled = (act * scale).astype(bf16)
        out_part = dense_dot(act_scaled, down_w).astype(bf16)
        grad_hidden = dot_nt(cot_rows, down_w)
        grad_gates = jnp.sum(
            (act * grad_hidden)[:, :n_routed].reshape(count, exp_local, exp_hidden), axis=-1
        )
        grad_gates = jnp.where(mine_named, grad_gates, 0.0)
        grad_hidden = grad_hidden * scale
        grad_gate_pre = (grad_hidden * up_pre * sigma * (1.0 + gate_pre * (1.0 - sigma))).astype(
            bf16
        )
        grad_up_pre = (grad_hidden * silu).astype(bf16)
        affinity_all = jnp.abs(signed)
        grad_aff = lax.dynamic_update_slice_in_dim(
            jnp.zeros((count, experts), f32), grad_gates, first_expert, axis=1
        )
        grad_logits = (
            affinity_all * (grad_aff - jnp.sum(affinity_all * grad_aff, axis=-1, keepdims=True))
        ).astype(bf16)
        dn2_part = (
            dense_dot(grad_gate_pre, gate_w)
            + dense_dot(grad_up_pre, up_w)
            + dot_nt(grad_logits, full_router)
        ).astype(bf16)
        sums = (
            dot_tn(act_scaled, cot_rows),
            dot_tn(grad_gate_pre, rows),
            dot_tn(grad_up_pre, rows),
            dot_tn(rows, grad_logits),
        )
        return out_part, dn2_part, sums

    blocks = max(1, tokens * hidden * 4 // 2**23)
    while tokens % blocks:
        blocks += 1
    if blocks == 1:
        out_part, dn2_part, sums = mixture(rows, cot_all, signed)
    else:

        def step(totals, block):
            out_block, dn2_block, sums = mixture(*block)
            return jax.tree.map(jnp.add, totals, sums), (out_block, dn2_block)

        zeros = (jnp.zeros((hidden, model_width), f32),) * 3 + (
            jnp.zeros((model_width, experts), f32),
        )
        sums, (out_part, dn2_part) = lax.scan(
            step,
            zeros,
            jax.tree.map(lambda v: v.reshape((blocks, -1) + v.shape[1:]), (rows, cot_all, signed)),
        )
    grad_down, grad_gate, grad_up, router_part = sums

    (routed_sum, grad_normed_two), _ = reduce_scatter(
        [
            out_part.reshape(devices, tok_count, model_width),
            dn2_part.reshape(devices, tok_count, model_width),
        ],
        [],
        2,
        "reduce_tokens",
    )
    layer_output = (residual + routed_sum).astype(bf16)

    gain_two_part = jnp.sum(grad_normed_two * unit_two, axis=0)
    grad_resid = cotangent.astype(f32) + norm_back(grad_normed_two, unit_two, inverse_two, gain_two)
    grad_resid_low = grad_resid.astype(bf16)
    wout_part = dot_tn(attended, grad_resid_low)
    grad_att = dot_nt(grad_resid_low, full_out).astype(bf16).reshape(tok_count, HEADS, head_dim)
    softmax_again = jnp.exp(masked_scores() - row_peak) / row_total
    grad_soft = jnp.einsum("qhd,khd->hqk", grad_att, value_rows, preferred_element_type=f32)
    grad_scores = (
        softmax_again * (grad_soft - jnp.sum(softmax_again * grad_soft, axis=-1, keepdims=True))
    ).astype(bf16)
    grad_queries = (
        jnp.einsum("hqk,khd->qhd", grad_scores, key_rows, preferred_element_type=f32) * attn_scale
    )
    grad_key_rows = (
        jnp.einsum("hqk,qhd->khd", grad_scores, queries, preferred_element_type=f32) * attn_scale
    )
    grad_value_rows = jnp.einsum(
        "hqk,qhd->khd", softmax_again.astype(bf16), grad_att, preferred_element_type=f32
    )
    grad_q_pre = rotate(grad_queries, cosine, -sine_table).reshape(tok_count, width).astype(bf16)
    grad_k_pre = rotate(grad_key_rows, cosine_all, -sine_all).reshape(group_len, width).astype(bf16)
    grad_v_pre = grad_value_rows.reshape(group_len, width).astype(bf16)
    wq_part = dot_tn(normed, grad_q_pre)
    wk_part = dot_tn(group_normed, grad_k_pre)
    wv_part = dot_tn(group_normed, grad_v_pre)
    own_normed_grad = dot_nt(grad_q_pre, full_query)
    group_normed_grad = dot_nt(grad_k_pre, full_key) + dot_nt(grad_v_pre, full_value)
    gain_one_part = jnp.sum(own_normed_grad * unit_one, axis=0) + jnp.sum(
        group_normed_grad * group_unit, axis=0
    )

    weight_part = jnp.concatenate([wq_part, wk_part, wv_part, wout_part], axis=1).astype(bf16)
    small_part = jnp.concatenate(
        [
            router_part.reshape(devices, n_router),
            gain_one_part.reshape(devices, d_rows),
            gain_two_part.reshape(devices, d_rows),
        ],
        axis=1,
    )
    small_part = jnp.pad(small_part, ((0, 0), (0, small_len - small_part.shape[1])))
    small_part = small_part.reshape(devices, -1, model_width)
    small_part = jnp.pad(small_part, ((0, 0), (0, -small_part.shape[1] % 16), (0, 0))).astype(bf16)
    (weight_sum, small_sum), (normed_grad_sum,) = reduce_scatter(
        [weight_part.reshape(devices, d_rows, 4 * width), small_part],
        [group_normed_grad.astype(bf16).reshape(tps, tok_count, model_width)],
        3,
        "reduce_weights",
    )
    grad_normed = own_normed_grad + normed_grad_sum
    input_grad = grad_resid + norm_back(grad_normed, unit_one, inverse_one, gain_one)
    small_sum = small_sum.reshape(-1)

    shared_back = jnp.stack([grad_gate[n_routed:], grad_up[n_routed:]])
    shared_back = shared_back.reshape(2, sh_rows, devices, d_rows).transpose(2, 0, 1, 3)
    shared_back = lax.all_to_all(shared_back, AXES, split_axis=0, concat_axis=0, tiled=True)
    shared_back = shared_back.transpose(1, 3, 0, 2).reshape(2, d_rows, devices * sh_rows)

    return (
        layer_output,
        input_grad,
        small_sum[n_router : n_router + d_rows],
        weight_sum[:, :width],
        weight_sum[:, width : 2 * width],
        weight_sum[:, 2 * width : 3 * width],
        weight_sum[:, 3 * width :],
        small_sum[n_router + d_rows : n_router + 2 * d_rows],
        shared_back[0],
        shared_back[1],
        grad_down[n_routed:],
        small_sum[:n_router].reshape(d_rows, experts),
        grad_gate[:n_routed].reshape(expert_gate.shape),
        grad_up[:n_routed].reshape(expert_up.shape),
        grad_down[:n_routed].reshape(expert_down.shape),
    )


def solution(mesh):
    rows = P(AXES, None)
    vector = P(AXES)
    experts = P("ep", "tp", None)
    return jax.shard_map(
        on_device,
        mesh=mesh,
        in_specs=(
            rows, P("ep", None), rows, vector, rows, rows, rows, rows, vector,
            rows, rows, rows, rows, experts, experts, experts, rows,
        ),
        out_specs=(
            rows, rows, vector, rows, rows, rows, rows, vector,
            rows, rows, rows, rows, experts, experts, experts,
        ),
        check_vma=False,
    )
```

```python
import functools

import jax
import jax.numpy as jnp
from jax import lax
from jax.experimental import pallas as pl
from jax.experimental.pallas import tpu as pltpu
from jax.sharding import PartitionSpec as P

HEADS = 10
AXES = ("ep", "tp")
MESH = pl.DeviceIdType.MESH
VMEM_BUDGET = 56 * 2**20

epsilon = 1e-06

bf16 = jnp.bfloat16
f32 = jnp.float32


def place():
    ep, tp = lax.axis_index("ep"), lax.axis_index("tp")
    return ep // 2, ep % 2, tp // 2, tp % 2


def device(line, a, b, c):
    return (line * 2 + a, b * 2 + c)


def number(line, a, b, c):
    return ((line * 2 + a) * 2 + b) * 2 + c


def halves(shape):
    rows, cols = shape
    if cols % 256 == 0:
        return (
            (pl.ds(0, rows), pl.ds(0, cols // 2)),
            (pl.ds(0, rows), pl.ds(cols // 2, cols // 2)),
        )
    return ((pl.ds(0, rows // 2), pl.ds(0, cols)), (pl.ds(rows // 2, rows // 2), pl.ds(0, cols)))


def greet(partners):
    barrier = pltpu.get_barrier_semaphore()
    for partner in partners:
        pl.semaphore_signal(barrier, inc=1, device_id=partner, device_id_type=MESH)
    pl.semaphore_wait(barrier, len(partners))


def visit_order(lines):
    return [sorted(range(lines), key=lambda other: (abs(other - z), other)) for z in range(lines)]


def lookup(table, index):
    out = jnp.int32(table[0])
    for k in range(1, len(table)):
        out = jnp.where(index == k, jnp.int32(table[k]), out)
    return out


def pick(values, index):
    out = values[0]
    for k in range(1, len(values)):
        out = jnp.where(index == k, values[k], out)
    return out


def gather_kernel(lines, core_only, n_group, *refs):
    n_all = len(core_only)
    n = n_all + n_group
    ins, outs = refs[:n], refs[n : 2 * n]
    send_sem, recv_sem, group_send, group_recv, local_sem = refs[2 * n :]
    z, a, b, c = place()
    oa, ob, oc = 1 - a, 1 - b, 1 - c
    to_b, to_a, to_c = device(z, a, ob, c), device(z, oa, b, c), device(z, a, b, oc)
    up_next = device(lax.rem(z + 1, lines), a, b, c)
    down_next = device(lax.rem(z + lines - 1, lines), a, b, c)
    greet(
        [to_b, to_a, to_c] + [device(lax.rem(z + s, lines), a, b, c) for s in range(1, lines)]
    )
    table = visit_order(lines)
    zs = [lookup([table[k][u] for k in range(lines)], z) for u in range(lines)]
    O, X, Y, D = 0, 1, 2, 3
    sent = []

    def chunk(i, line, kind, part=None, core=None):
        if core_only[i]:
            at = line * 4 + kind
        else:
            at = number(line, (a, a, oa, oa)[kind], (b, ob, b, ob)[kind], c if core is None else core)
        if part is None:
            return outs[i].at[at]
        return outs[i].at[(at,) + halves(outs[i].shape[1:])[part]]

    def remote(i, slot, step, src, dst, to):
        k = slot * lines + step
        return pltpu.make_async_remote_copy(
            src, dst, send_sem.at[i, k], recv_sem.at[i, k], device_id=to, device_id_type=MESH
        )

    def hop(i, slot, step, kind, to_kind, line, to, part=None, own=False):
        src = ins[i] if own else chunk(i, line, kind, part)
        there = chunk(i, line, to_kind if core_only[i] else kind, part)
        return remote(i, slot, step, src, there, to)

    def arrival(i, slot, step, kind, line, part=None):
        here = chunk(i, line, kind, part)
        remote(i, slot, step, here, here, to_c).wait_recv()

    def send(copy):
        copy.start()
        sent.append(copy)

    def across(i, slot, u, kind, part=None, own=False):
        if not core_only[i]:
            here = chunk(i, zs[u], kind, part)
            send(remote(i, slot, u, ins[i] if own else here, here, to_c))

    def send_own(u):
        own = u == 0
        for i in range(n_all):
            send(hop(i, 0, u, O, X, zs[u], to_b, own=own))
            send(hop(i, 1, u, O, Y, zs[u], to_a, own=own))
        for i in range(n_all):
            across(i, 6, u, O, own=own)

    def xy_event(u):
        for i in range(n_all):
            arrival(i, 0, u, X, zs[u])
            send(hop(i, 2, u, X, D, zs[u], to_a, 0))
            arrival(i, 1, u, Y, zs[u])
            send(hop(i, 3, u, Y, D, zs[u], to_b, 1))
            across(i, 7, u, X)
            across(i, 8, u, Y)

    def diag_event(u):
        for i in range(n_all):
            arrival(i, 2, u, D, zs[u], 0)
            across(i, 9, u, D, 0)
            arrival(i, 3, u, D, zs[u], 1)
            across(i, 10, u, D, 1)

    def chain_up(i, k):
        return hop(i, 4, k, O, O, z - (k - 1), up_next, own=k == 1)

    def chain_down(i, k):
        return hop(i, 5, k, O, O, z + (k - 1), down_next, own=k == 1)

    def chain_start(k):
        if k >= lines:
            return

        @pl.when((z >= k - 1) & (z + 1 < lines))
        def _():
            for i in range(n_all):
                chain_up(i, k).start()

        @pl.when((z + k - 1 < lines) & (z > 0))
        def _():
            for i in range(n_all):
                chain_down(i, k).start()

    def chain_event(k):
        @pl.when(z >= k)
        def _():
            for i in range(n_all):
                arrival(i, 4, k, O, z - k)

        @pl.when(z + k < lines)
        def _():
            for i in range(n_all):
                arrival(i, 5, k, O, z + k)

        chain_start(k + 1)

    def chain_drain(k):
        @pl.when((z >= k - 1) & (z + 1 < lines))
        def _():
            for i in range(n_all):
                chain_up(i, k).wait_send()

        @pl.when((z + k - 1 < lines) & (z > 0))
        def _():
            for i in range(n_all):
                chain_down(i, k).wait_send()

    group_copies = []

    def group_copy(g, k, src, dst, to):
        return pltpu.make_async_remote_copy(
            src, dst, group_send.at[g, k], group_recv.at[g, k], device_id=to, device_id_type=MESH
        )

    keeps = []
    send_own(0)
    chain_start(1)
    for g in range(n_group):
        src, dst = ins[n_all + g], outs[n_all + g].at[b * 2 + c]
        for k, to in enumerate((to_c, to_b)):
            group_copies.append(group_copy(g, k, src, dst, to))
            group_copies[-1].start()
        keeps.append(pltpu.make_async_copy(src, dst, local_sem.at[n_all + g]))
    for i in range(n_all):
        keeps.append(pltpu.make_async_copy(ins[i], chunk(i, z, O), local_sem.at[i]))
    for keep in keeps:
        keep.start()
    for g in range(n_group):
        got = outs[n_all + g].at[ob * 2 + c]
        group_copy(g, 1, got, got, to_b).wait_recv()
        group_copies.append(group_copy(g, 2, got, got, to_c))
        group_copies[-1].start()
    xy_event(0)
    chain_event(1)
    send_own(1)
    for u in range(2, lines):
        chain_event(u)
        xy_event(u - 1)
        diag_event(u - 2)
        send_own(u)
    xy_event(lines - 1)
    diag_event(lines - 2)
    diag_event(lines - 1)
    for u in range(lines):
        for i in range(n_all):
            if not core_only[i]:
                for slot, kind, part in ((6, O, None), (7, X, None), (8, Y, None), (9, D, 0), (10, D, 1)):
                    there = chunk(i, zs[u], kind, part, oc)
                    remote(i, slot, u, there, there, to_c).wait_recv()
    for g in range(n_group):
        for k, t in ((0, b * 2 + oc), (2, ob * 2 + oc)):
            got = outs[n_all + g].at[t]
            group_copy(g, k, got, got, to_c).wait_recv()
    for copy in sent + group_copies:
        copy.wait_send()
    for k in range(1, lines):
        chain_drain(k)
    for keep in keeps:
        keep.wait()


def gather(everyone, core_only, group, collective_id, name):
    eps, tps = lax.axis_size("ep"), lax.axis_size("tp")
    lines = eps // 2
    n_all, n_group = len(everyone), len(group)
    shapes = [
        jax.ShapeDtypeStruct((eps * tps // (2 if core else 1),) + v.shape, v.dtype)
        for v, core in zip(everyone, core_only)
    ] + [jax.ShapeDtypeStruct((tps,) + v.shape, v.dtype) for v in group]
    anywhere = pl.BlockSpec(memory_space=pl.ANY)
    outs = pl.pallas_call(
        functools.partial(gather_kernel, lines, tuple(core_only), n_group),
        out_shape=shapes,
        in_specs=[anywhere] * (n_all + n_group),
        out_specs=[anywhere] * (n_all + n_group),
        scratch_shapes=[
            pltpu.SemaphoreType.DMA((n_all, 11 * lines)),
            pltpu.SemaphoreType.DMA((n_all, 11 * lines)),
            pltpu.SemaphoreType.DMA((max(n_group, 1), 3)),
            pltpu.SemaphoreType.DMA((max(n_group, 1), 3)),
            pltpu.SemaphoreType.DMA((n_all + n_group,)),
        ],
        compiler_params=pltpu.CompilerParams(collective_id=collective_id, has_side_effects=True),
        name=name,
    )(*everyone, *group)
    return outs[:n_all], outs[n_all:]


def add_into(dst, src, rows, first, cols, dst_at=(), src_at=()):
    step = 256 if cols % 256 == 0 else 128

    def body(k, carry):
        there = pl.ds(pl.multiple_of(first + k * step, 128), step)
        here = pl.ds(pl.multiple_of(k * step, 128), step)
        total = dst[dst_at + (slice(None), there)].astype(f32) + src[
            src_at + (slice(None), here)
        ].astype(f32)
        dst[dst_at + (slice(None), there)] = total.astype(bf16)
        return carry

    lax.fori_loop(0, cols // step, body, 0)


def reduce_kernel(lines, n_all, n_group, *refs):
    n = n_all + n_group
    ins, outs = refs[:n], refs[n : 2 * n]
    rest = list(refs[2 * n :])
    per_all = [[rest.pop(0) for _ in range(7)] for _ in range(n_all)]
    per_group = [[rest.pop(0) for _ in range(3)] for _ in range(n_group)]
    send_sem, recv_sem, group_send, group_recv, local_sem = rest
    z, a, b, c = place()
    oa, ob, oc = 1 - a, 1 - b, 1 - c
    to_b, to_a, to_c = device(z, a, ob, c), device(z, oa, b, c), device(z, a, b, oc)
    to_line = [None] + [device(lax.rem(z + s, lines), a, b, c) for s in range(1, lines)]
    greet([to_b, to_a, to_c] + to_line[1:])
    order = list(range(1, lines)) + [0]
    goal = [lax.rem(z + s, lines) for s in range(lines)]
    started = []
    kinds = {"s": 0, "p": 1, "q": 2, "x": 3, "y": 4, "z": 5}

    def sems(i, kind, step):
        k = kinds[kind] * lines + step
        return send_sem.at[i, k], recv_sem.at[i, k]

    def send(i, kind, step, src, dst, to):
        copy = pltpu.make_async_remote_copy(
            src, dst, *sems(i, kind, step), device_id=to, device_id_type=MESH
        )
        copy.start()
        started.append(copy)

    def arrived(i, kind, step, dst):
        pltpu.make_async_remote_copy(
            dst, dst, *sems(i, kind, step), device_id=to_c, device_id_type=MESH
        ).wait_recv()

    loads = {}
    for s in order:
        for i in range(n_all):
            acc, sib = per_all[i][:2]
            send(i, "s", s, ins[i].at[goal[s], :, :, oc], sib.at[s], to_c)
            load = pltpu.make_async_copy(
                ins[i].at[goal[s], :, :, c], acc.at[s], local_sem.at[i, s]
            )
            load.start()
            loads[i, s] = load
    group_copies, group_loads = [], []
    for g in range(n_group):
        acc, sib, far = per_group[g]
        src = ins[n_all + g]
        copy = pltpu.make_async_remote_copy(
            src.at[:, oc], sib, group_send.at[g, 0], group_recv.at[g, 0],
            device_id=to_c, device_id_type=MESH,
        )
        copy.start()
        group_copies.append(copy)
        load = pltpu.make_async_copy(src.at[:, c], acc, local_sem.at[n_all + g, 0])
        load.start()
        group_loads.append(load)
    for s in order:
        for i in range(n_all):
            acc, sib, p, q, x, y, line = per_all[i]
            rows, cols = acc.shape[-2:]
            first, second = halves((rows, cols))
            loads[i, s].wait()
            arrived(i, "s", s, sib.at[s])
            for u, v in ((oa, ob), (a, ob), (oa, b), (a, b)):
                add_into(acc, sib, rows, 0, cols, (s, u, v), (s, u, v))
                if (u is oa) and (v is ob):
                    send(i, "p", s, acc.at[(s, oa, ob) + first], p.at[s], to_a)
                    send(i, "q", s, acc.at[(s, oa, ob) + second], q.at[s], to_b)
    for g in range(n_group):
        acc, sib, far = per_group[g]
        rows, cols = acc.shape[-2:]
        group_loads[g].wait()
        pltpu.make_async_remote_copy(
            sib, sib, group_send.at[g, 0], group_recv.at[g, 0], device_id=to_c, device_id_type=MESH
        ).wait_recv()
        for u in (ob, b):
            add_into(acc, sib, rows, 0, cols, (u,), (u,))
            if u is ob:
                copy = pltpu.make_async_remote_copy(
                    acc.at[ob], far, group_send.at[g, 1], group_recv.at[g, 1],
                    device_id=to_b, device_id_type=MESH,
                )
                copy.start()
                group_copies.append(copy)
    for s in order:
        for i in range(n_all):
            acc, sib, p, q, x, y, line = per_all[i]
            rows, cols = acc.shape[-2:]
            arrived(i, "p", s, p.at[s])
            add_into(acc, p, rows, 0, cols // 2, (s, a, ob), (s,))
            send(i, "x", s, acc.at[s, a, ob], x.at[s], to_b)
            arrived(i, "q", s, q.at[s])
            add_into(acc, q, rows, cols // 2, cols // 2, (s, oa, b), (s,))
            send(i, "y", s, acc.at[s, oa, b], y.at[s], to_a)
    for s in order:
        for i in range(n_all):
            acc, sib, p, q, x, y, line = per_all[i]
            rows, cols = acc.shape[-2:]
            arrived(i, "x", s, x.at[s])
            add_into(acc, x, rows, 0, cols, (s, a, b), (s,))
            arrived(i, "y", s, y.at[s])
            add_into(acc, y, rows, 0, cols, (s, a, b), (s,))
            if s > 0:
                send(i, "z", s, acc.at[s, a, b], line.at[s - 1], to_line[s])
    for g in range(n_group):
        acc, sib, far = per_group[g]
        pltpu.make_async_remote_copy(
            far, far, group_send.at[g, 1], group_recv.at[g, 1], device_id=to_b, device_id_type=MESH
        ).wait_recv()
        outs[n_all + g][...] = acc[b].astype(f32) + far[...].astype(f32)
    for i in range(n_all):
        acc, sib, p, q, x, y, line = per_all[i]
        for s in range(1, lines):
            arrived(i, "z", s, line.at[s - 1])
        total = acc[0, a, b].astype(f32)
        for s in range(1, lines):
            total = total + line[s - 1].astype(f32)
        outs[i][...] = total
    for copy in started + group_copies:
        copy.wait_send()


def reduce_scatter(everyone, group, collective_id, name):
    eps, tps = lax.axis_size("ep"), lax.axis_size("tp")
    lines = eps // 2
    n_all, n_group = len(everyone), len(group)
    anywhere = pl.BlockSpec(memory_space=pl.ANY)
    vmem = pl.BlockSpec(memory_space=pltpu.VMEM)
    scratch = []
    for v in everyone:
        rows, cols = v.shape[1:]
        scratch += [
            pltpu.VMEM((lines, 2, 2, rows, cols), bf16),
            pltpu.VMEM((lines, 2, 2, rows, cols), bf16),
            pltpu.VMEM((lines, rows, cols // 2), bf16),
            pltpu.VMEM((lines, rows, cols // 2), bf16),
            pltpu.VMEM((lines, rows, cols), bf16),
            pltpu.VMEM((lines, rows, cols), bf16),
            pltpu.VMEM((lines - 1, rows, cols), bf16),
        ]
    for v in group:
        rows, cols = v.shape[1:]
        scratch += [
            pltpu.VMEM((2, rows, cols), bf16),
            pltpu.VMEM((2, rows, cols), bf16),
            pltpu.VMEM((rows, cols), bf16),
        ]
    scratch += [
        pltpu.SemaphoreType.DMA((n_all, 6 * lines)),
        pltpu.SemaphoreType.DMA((n_all, 6 * lines)),
        pltpu.SemaphoreType.DMA((max(n_group, 1), 2)),
        pltpu.SemaphoreType.DMA((max(n_group, 1), 2)),
        pltpu.SemaphoreType.DMA((n_all + n_group, lines)),
    ]
    outs = pl.pallas_call(
        functools.partial(reduce_kernel, lines, n_all, n_group),
        out_shape=[jax.ShapeDtypeStruct(v.shape[1:], f32) for v in list(everyone) + list(group)],
        in_specs=[anywhere] * (n_all + n_group),
        out_specs=[vmem] * (n_all + n_group),
        scratch_shapes=scratch,
        compiler_params=pltpu.CompilerParams(
            collective_id=collective_id, has_side_effects=True, vmem_limit_bytes=VMEM_BUDGET
        ),
        name=name,
    )(
        *[v.reshape((lines, 2, 2, 2) + v.shape[1:]) for v in everyone],
        *[v.reshape((2, 2) + v.shape[1:]) for v in group],
    )
    return outs[:n_all], outs[n_all:]


def mixture_kernel(lines, tok, aux, cot, wg, wu, wd, sel, sel_t, router_t, ones, *refs):
    (
        sums, dw_own, dw_sib, dr,
        nc, aux_all, vg, vu, vd, dw, acts, dg, du, daff, dlg, pr, qr, xr, yr, zr,
        ag_send, ag_recv, rs_send, rs_recv, w_send, w_recv, local_sem,
    ) = refs
    z, a, b, c = place()
    oa, ob, oc = 1 - a, 1 - b, 1 - c
    to_b, to_a, to_c = device(z, a, ob, c), device(z, oa, b, c), device(z, a, b, oc)
    count, width = tok.shape
    half = count // 2
    hc = wg.shape[0]
    hidden = 2 * hc
    n_sel = sel.shape[1]
    block = 256
    unit_rows = 4 * count
    table = visit_order(lines)
    zs = [lookup([table[k][u] for k in range(lines)], z) for u in range(lines)]
    O, X, Y, D = 0, 1, 2, 3

    barrier = pltpu.get_barrier_semaphore()
    partners = [to_b, to_a, to_c] + [
        device(lax.rem(z + s, lines), a, b, c) for s in range(1, lines)
    ]
    for partner in partners:
        pl.semaphore_signal(barrier, inc=1, device_id=partner, device_id_type=MESH)
    pl.semaphore_wait(barrier, len(partners))

    def remote(src, dst, send_sem, recv_sem, to):
        return pltpu.make_async_remote_copy(
            src, dst, send_sem, recv_sem, device_id=to, device_id_type=MESH
        )

    local = []
    mine = pl.ds(c * hc, hc)
    theirs = pl.ds(oc * hc, hc)
    w_copies = []
    for k, (src, dst) in enumerate(((wg, vg), (wu, vu), (wd, vd))):
        copy = pltpu.make_async_copy(src, dst.at[mine], local_sem.at[k])
        copy.start()
        local.append(copy)
        copy = remote(src, dst.at[mine], w_send.at[k], w_recv.at[k], to_c)
        copy.start()
        w_copies.append(copy)

    def spot(line, kind):
        return line * 4 + kind

    def tok_at(line, kind, part=None):
        first = spot(line, kind) * count
        if part is None:
            return nc.at[pl.ds(first, count), pl.ds(0, width)]
        return nc.at[pl.ds(first + part * half, half), pl.ds(0, width)]

    def ag(slot, step, arr):
        k = slot * lines + step
        return ag_send.at[arr, k], ag_recv.at[arr, k]

    def ag_copies(slot, step, src_kind, dst_kind, line, to, part=None, own=False):
        src = tok if own else tok_at(line, src_kind, part)
        copies = [remote(src, tok_at(line, dst_kind, part), *ag(slot, step, 0), to)]
        if part != 1:
            src = aux if own else aux_all.at[spot(line, src_kind)]
            copies.append(remote(src, aux_all.at[spot(line, dst_kind)], *ag(slot, step, 1), to))
        return copies

    def send_own(u):
        own = u == 0
        return ag_copies(0, u, O, X, zs[u], to_b, own=own) + ag_copies(1, u, O, Y, zs[u], to_a, own=own)

    def send_halves(u):
        return ag_copies(2, u, X, D, zs[u], to_a, 0) + ag_copies(3, u, Y, D, zs[u], to_b, 1)

    def start(copies):
        for copy in copies:
            copy.start()

    def wait_recv(copies):
        for copy in copies:
            copy.wait_recv()

    def wait_send(copies):
        for copy in copies:
            copy.wait_send()

    up_next = device(lax.rem(z + 1, lines), a, b, c)
    down_next = device(lax.rem(z + lines - 1, lines), a, b, c)

    def chain_up(k, own=False):
        return ag_copies(4, k, O, O, z - (k - 1), up_next, own=own)

    def chain_down(k, own=False):
        return ag_copies(5, k, O, O, z + (k - 1), down_next, own=own)

    def chain_event(k):
        @pl.when(z >= k)
        def _():
            wait_recv(ag_copies(4, k, O, O, z - k, up_next))

            if k + 1 < lines:

                @pl.when(z + 1 < lines)
                def _():
                    start(chain_up(k + 1))

        @pl.when(z + k < lines)
        def _():
            wait_recv(ag_copies(5, k, O, O, z + k, down_next))

            if k + 1 < lines:

                @pl.when(z > 0)
                def _():
                    start(chain_down(k + 1))

    def chain_drain(k):
        @pl.when((z >= k - 1) & (z + 1 < lines))
        def _():
            wait_send(chain_up(k, own=k == 1))

        @pl.when((z + k - 1 < lines) & (z > 0))
        def _():
            wait_send(chain_down(k, own=k == 1))

    def xy_event(u):
        wait_recv(ag_copies(0, u, O, X, zs[u], to_b))
        wait_recv(ag_copies(1, u, O, Y, zs[u], to_a))
        start(send_halves(u))

    def diag_event(u):
        wait_recv(ag_copies(2, u, X, D, zs[u], to_a, 0))
        wait_recv(ag_copies(3, u, Y, D, zs[u], to_b, 1))

    def sent_event(u):
        wait_send(send_own(u))
        wait_send(send_halves(u))

    start(send_own(0))

    @pl.when(z + 1 < lines)
    def _():
        start(chain_up(1, own=True))

    @pl.when(z > 0)
    def _():
        start(chain_down(1, own=True))

    copy = pltpu.make_async_copy(tok, tok_at(z, O), local_sem.at[3])
    copy.start()
    local.append(copy)
    copy = pltpu.make_async_copy(aux, aux_all.at[spot(z, O)], local_sem.at[4])
    copy.start()
    local.append(copy)
    copy = pltpu.make_async_copy(cot, nc.at[:, pl.ds(width, width)], local_sem.at[5])
    copy.start()
    local.append(copy)

    def zero(i, carry):
        dw[:, pl.ds(i * 64, 64), :] = jnp.zeros((3, 64, width), f32)
        return carry

    lax.fori_loop(0, hidden // 64, zero, 0)
    dr[...] = jnp.zeros_like(dr)

    def res(line, kind, part=None):
        first = spot(line, kind) * count
        if part is None:
            return nc.at[pl.ds(first, count)]
        return nc.at[pl.ds(first + part * half, half)]

    def part_of(ref, u, part):
        return ref.at[u, pl.ds(part * half, half)]

    def rs(slot, u):
        k = slot * lines + u
        return rs_send.at[k], rs_recv.at[k]

    def p_copy(u):
        return remote(res(zs[u], D, 0), pr.at[u], *rs(0, u), to_a)

    def q_copy(u):
        return remote(res(zs[u], D, 1), qr.at[u], *rs(1, u), to_b)

    def x_copy(u, part):
        return remote(res(zs[u], X, part), part_of(xr, u, part), *rs(2 + part, u), to_b)

    def y_copy(u, part):
        return remote(res(zs[u], Y, part), part_of(yr, u, part), *rs(4 + part, u), to_a)

    def z_copy(u):
        slot = lax.rem(z - zs[u] + lines, lines) - 1
        k = 6 * lines
        return remote(
            res(zs[u], O), zr.at[slot], rs_send.at[k + u], rs_recv.at[k + slot],
            device(zs[u], a, b, c),
        )

    def add(first, rows, others):
        def body(k, carry):
            there = pl.ds(pl.multiple_of(k * 256, 256), 256)
            at = pl.ds(first, rows)
            total = nc[at, there].astype(f32)
            for ref, u in others:
                total = total + ref[u, :, there].astype(f32)
            nc[at, there] = total.astype(bf16)
            return carry

        lax.fori_loop(0, 2 * width // 256, body, 0)

    def rs_start(u):
        p_copy(u).start()
        q_copy(u).start()
        x_copy(u, 1).start()
        y_copy(u, 0).start()

    def rs_mid(u):
        p_copy(u).wait_recv()
        add(spot(zs[u], X) * count, half, [(pr, u)])
        x_copy(u, 0).start()
        q_copy(u).wait_recv()
        add(spot(zs[u], Y) * count + half, half, [(qr, u)])
        y_copy(u, 1).start()

    def rs_end(u):
        for part in (0, 1):
            x_copy(u, part).wait_recv()
            y_copy(u, part).wait_recv()
        add(spot(zs[u], O) * count, count, [(xr, u), (yr, u)])
        if u > 0:
            z_copy(u).start()

    def expand(line, columns):
        return jnp.concatenate(
            [dot_tn(aux_all[spot(line, kind)], sel[:, columns]) for kind in range(4)], axis=0
        )

    def unit(u, carry):
        line = pick(zs, u)
        rows = pl.ds(pl.multiple_of(line * unit_rows, unit_rows), unit_rows)

        for v in range(lines):

            @pl.when(u == v)
            def _(v=v):
                diag_event(v)

        daff[...] = jnp.zeros_like(daff)

        def hidden_step(i, carry):
            h = pl.ds(pl.multiple_of(i * block, block), block)
            x = nc[rows, 0:width]
            gate_pre = dot_nt(x, vg[h, :])
            up_pre = dot_nt(x, vu[h, :])
            grad = dot_nt(nc[rows, width : 2 * width], vd[h, :])
            scale = jnp.maximum(expand(line, h) + ones[:, h], 0.0)
            sigma = 1.0 / (1.0 + jnp.exp(-gate_pre))
            silu = gate_pre * sigma
            act = silu * up_pre
            acts[:, h] = (act * scale).astype(bf16)
            daff[...] += dense_dot((act * grad).astype(bf16), sel_t[h, :])
            grad = grad * scale
            dg[:, h] = (grad * up_pre * sigma * (1.0 + gate_pre * (1.0 - sigma))).astype(bf16)
            du[:, h] = (grad * silu).astype(bf16)
            return carry

        lax.fori_loop(0, hidden // block, hidden_step, 0)
        signed = expand(line, pl.ds(hidden, n_sel - hidden))
        affinity = jnp.abs(signed)
        grad_aff = jnp.where(signed > 0, daff[...], 0.0)
        total = jnp.sum(affinity * grad_aff, axis=1, keepdims=True)
        dlg[...] = (affinity * (grad_aff - total)).astype(bf16)

        @pl.when(u == 0)
        def _():
            if lines > 2:
                chain_event(2)

        for v in range(1, lines - 1):

            @pl.when(u == v)
            def _(v=v):
                xy_event(v + 1)
                if v + 2 < lines:
                    start(send_own(v + 2))

        def weight_step(i, carry):
            h = pl.ds(pl.multiple_of(i * block, block), block)
            x = nc[rows, 0:width]
            dw[0, h, :] += dot_tn(dg[:, h], x)
            dw[1, h, :] += dot_tn(du[:, h], x)
            dw[2, h, :] += dot_tn(acts[:, h], nc[rows, width : 2 * width])
            return carry

        lax.fori_loop(0, hidden // block, weight_step, 0)
        dr[...] += dot_tn(dlg[...], nc[rows, 0:width])

        for v in range(lines):

            @pl.when(u == v)
            def _(v=v):
                if v == 0:
                    xy_event(1)
                    if lines > 2:
                        start(send_own(2))
                    chain_drain(1)
                elif v == 1:
                    for k in range(2, lines):
                        chain_drain(k)
                elif v == 2:
                    rs_mid(1)
                sent_event(v)

        def back_step(i, carry):
            n = pl.ds(pl.multiple_of(i * block, block), block)
            n2 = pl.ds(pl.multiple_of(width + i * block, block), block)
            out = dense_dot(acts[...], vd[:, n])
            back = (
                dense_dot(dg[...], vg[:, n])
                + dense_dot(du[...], vu[:, n])
                + dense_dot(dlg[...], router_t[:, n])
            )
            nc[rows, n] = out.astype(bf16)
            nc[rows, n2] = back.astype(bf16)
            return carry

        lax.fori_loop(0, width // block, back_step, 0)

        @pl.when(u == 0)
        def _():
            for k in range(3, lines):
                chain_event(k)

        for v in range(1, lines):

            @pl.when(u == v)
            def _(v=v):
                rs_start(v)

        return carry

    xy_event(0)
    chain_event(1)
    start(send_own(1))
    for copy in w_copies:
        copy.wait_recv()
    for copy in local:
        copy.wait()
    lax.fori_loop(0, lines, unit, 0)

    own_out = pltpu.make_async_copy(dw.at[:, mine], dw_own, local_sem.at[6])
    own_out.start()
    sib_out = remote(dw.at[:, theirs], dw_sib, w_send.at[3], w_recv.at[3], to_c)
    sib_out.start()
    rs_mid(2)
    rs_end(1)
    rs_start(0)
    rs_mid(3)
    rs_end(2)
    rs_mid(0)
    rs_end(3)
    rs_end(0)
    for slot in range(lines - 1):
        k = 6 * lines + slot
        remote(
            zr.at[slot], zr.at[slot], rs_send.at[k], rs_recv.at[k], to_c
        ).wait_recv()

    def finish(k, carry):
        there = pl.ds(pl.multiple_of(k * 128, 128), 128)
        total = nc[pl.ds(spot(z, O) * count, count), there].astype(f32)
        for slot in range(lines - 1):
            total = total + zr[slot, :, there].astype(f32)
        sums[:, there] = total
        return carry

    lax.fori_loop(0, 2 * width // 128, finish, 0)
    for u in range(lines):
        p_copy(u).wait_send()
        q_copy(u).wait_send()
        for part in (0, 1):
            x_copy(u, part).wait_send()
            y_copy(u, part).wait_send()
        if u > 0:
            z_copy(u).wait_send()
    for copy in w_copies:
        copy.wait_send()
    sib_out.wait()
    own_out.wait()


def mixture_call(tok, aux, cot, weights, sel, sel_t, router_t, ones, collective_id):
    lines = lax.axis_size("ep") // 2
    count, width = tok.shape
    hc = weights[0].shape[0]
    anywhere = pl.BlockSpec(memory_space=pl.ANY)
    vmem = pl.BlockSpec(memory_space=pltpu.VMEM)
    n_rows = lines * 4 * count
    return pl.pallas_call(
        functools.partial(mixture_kernel, lines),
        out_shape=(
            jax.ShapeDtypeStruct((count, 2 * width), f32),
            jax.ShapeDtypeStruct((3, hc, width), f32),
            jax.ShapeDtypeStruct((3, hc, width), f32),
            jax.ShapeDtypeStruct((128, width), f32),
        ),
        in_specs=[anywhere] * 6 + [vmem] * 4,
        out_specs=(vmem, anywhere, anywhere, vmem),
        scratch_shapes=[
            pltpu.VMEM((n_rows, 2 * width), bf16),
            pltpu.VMEM((lines * 4,) + aux.shape, bf16),
            pltpu.VMEM((2 * hc, width), bf16),
            pltpu.VMEM((2 * hc, width), bf16),
            pltpu.VMEM((2 * hc, width), bf16),
            pltpu.VMEM((3, 2 * hc, width), f32),
            pltpu.VMEM((4 * count, 2 * hc), bf16),
            pltpu.VMEM((4 * count, 2 * hc), bf16),
            pltpu.VMEM((4 * count, 2 * hc), bf16),
            pltpu.VMEM((4 * count, 128), f32),
            pltpu.VMEM((4 * count, 128), bf16),
            pltpu.VMEM((lines, count // 2, 2 * width), bf16),
            pltpu.VMEM((lines, count // 2, 2 * width), bf16),
            pltpu.VMEM((lines, count, 2 * width), bf16),
            pltpu.VMEM((lines, count, 2 * width), bf16),
            pltpu.VMEM((lines - 1, count, 2 * width), bf16),
            pltpu.SemaphoreType.DMA((2, 6 * lines)),
            pltpu.SemaphoreType.DMA((2, 6 * lines)),
            pltpu.SemaphoreType.DMA((7 * lines,)),
            pltpu.SemaphoreType.DMA((7 * lines,)),
            pltpu.SemaphoreType.DMA((4,)),
            pltpu.SemaphoreType.DMA((4,)),
            pltpu.SemaphoreType.DMA((7,)),
        ],
        compiler_params=pltpu.CompilerParams(
            collective_id=collective_id, has_side_effects=True, vmem_limit_bytes=62 * 2**20
        ),
        name="mixture",
    )(tok, aux, cot, *weights, sel, sel_t, router_t, ones)


def documents(positions, lengths):
    seq_ends = jnp.cumsum(lengths)
    doc_index = (positions >= seq_ends[0]).astype(jnp.int32) + (positions >= seq_ends[1]).astype(
        jnp.int32
    )
    seq_starts = jnp.where(doc_index == 0, 0, jnp.where(doc_index == 1, seq_ends[0], seq_ends[1]))
    return (doc_index, positions - seq_starts)


def rotary_tables(offsets, head_dim):
    half_dim = head_dim // 2
    frequency = 10000.0 ** (-2.0 * jnp.arange(half_dim, dtype=f32) / head_dim)
    angles = offsets.astype(f32)[:, None] * frequency[None, :]
    return (jnp.cos(angles)[:, None, :], jnp.sin(angles)[:, None, :])


def rotate(values, cosine, sine_table):
    half_dim = values.shape[-1] // 2
    first_half = values[..., :half_dim]
    second_half = values[..., half_dim:]
    return jnp.concatenate(
        [
            first_half * cosine - second_half * sine_table,
            first_half * sine_table + second_half * cosine,
        ],
        axis=-1,
    )


def norm_back(grad_normed, unit_rows, inverse, gain):
    scaled = grad_normed * gain
    return inverse * (scaled - unit_rows * jnp.mean(scaled * unit_rows, axis=-1, keepdims=True))


def dot(left, right, contract):
    return lax.dot_general(left, right, ((contract[0], contract[1]), ((), ())), preferred_element_type=f32)


def dense_dot(left, right):
    return dot(left, right, ((1,), (0,)))


def dot_nt(left, right):
    return dot(left, right, ((1,), (1,)))


def dot_tn(left, right):
    return dot(left, right, ((0,), (0,)))


def on_device(
    hidden_in,
    seq_lengths,
    expert_ids,
    attn_gain,
    w_query,
    w_key,
    w_value,
    w_out,
    ffn_gain,
    shared_gate,
    shared_up,
    shared_down,
    router,
    expert_gate,
    expert_up,
    expert_down,
    cotangent,
):
    tok_count, model_width = hidden_in.shape
    eps, tps = lax.axis_size("ep"), lax.axis_size("tp")
    devices = eps * tps
    exp_local, exp_hidden = expert_gate.shape[:2]
    experts = exp_local * eps
    group_len = tps * tok_count
    tokens = devices * tok_count
    d_rows = w_query.shape[0]
    width = w_query.shape[1]
    sh_rows = shared_down.shape[0]
    head_dim = width // HEADS
    attn_scale = head_dim ** (-0.5)

    flat = jnp.concatenate([router.reshape(-1), attn_gain, ffn_gain])
    small_len = -(-flat.shape[0] // model_width) * model_width
    small = jnp.pad(flat, (0, small_len - flat.shape[0])).reshape(-1, model_width)
    small = jnp.pad(small, ((0, -small.shape[0] % 16), (0, 0)))
    weights = jnp.concatenate([w_query, w_key, w_value, w_out], axis=1)

    small_slice = eps == 8 and tps == 4
    if small_slice:
        (all_weights, all_small, all_cot), (group_hidden,) = gather(
            [weights, small, cotangent], [False, False, True], [hidden_in], 0, "gather_weights"
        )
    else:
        all_weights, all_small, all_cot = [
            lax.all_gather(v, AXES, axis=0) for v in (weights, small, cotangent)
        ]
        group_hidden = lax.all_gather(hidden_in, "tp", axis=0)
    all_weights = all_weights.reshape(devices * d_rows, 4 * width)
    full_query = all_weights[:, :width]
    full_key = all_weights[:, width : 2 * width]
    full_value = all_weights[:, 2 * width : 3 * width]
    full_out = all_weights[:, 3 * width :]
    all_small = all_small.reshape(devices, -1)
    n_router = d_rows * experts
    full_router = all_small[:, :n_router].reshape(devices * d_rows, experts)
    gain_one = all_small[:, n_router : n_router + d_rows].reshape(-1).astype(f32)
    gain_two = all_small[:, n_router + d_rows : n_router + 2 * d_rows].reshape(-1).astype(f32)
    cot_all = all_cot.reshape(-1, model_width)

    shared_cols = jnp.stack([shared_gate, shared_up], axis=1).reshape(d_rows, 2, devices, sh_rows)
    shared_cols = lax.all_to_all(
        shared_cols.transpose(2, 1, 3, 0), AXES, split_axis=0, concat_axis=0, tiled=True
    )
    shared_t = shared_cols.transpose(1, 2, 0, 3).reshape(2, sh_rows, model_width)

    lengths = seq_lengths[0]
    tp_index = lax.axis_index("tp")
    own_pos = tp_index * tok_count + jnp.arange(tok_count, dtype=jnp.int32)
    all_pos = jnp.arange(group_len, dtype=jnp.int32)
    own_doc, own_offset = documents(own_pos, lengths)
    all_doc, all_offset = documents(all_pos, lengths)
    allowed = (own_doc[:, None] == all_doc[None, :]) & (own_pos[:, None] >= all_pos[None, :])
    cosine, sine_table = rotary_tables(own_offset, head_dim)
    cosine_all, sine_all = rotary_tables(all_offset, head_dim)

    inputs = hidden_in.astype(f32)
    inverse_one = lax.rsqrt(jnp.mean(inputs * inputs, axis=-1, keepdims=True) + epsilon)
    unit_one = inputs * inverse_one
    normed = (unit_one * gain_one).astype(bf16)
    group_in = group_hidden.reshape(group_len, model_width).astype(f32)
    group_unit = group_in * lax.rsqrt(jnp.mean(group_in * group_in, axis=-1, keepdims=True) + epsilon)
    group_normed = (group_unit * gain_one).astype(bf16)

    queries = rotate(
        dense_dot(normed, full_query).reshape(tok_count, HEADS, head_dim), cosine, sine_table
    ).astype(bf16)
    key_rows = rotate(
        dense_dot(group_normed, full_key).reshape(group_len, HEADS, head_dim), cosine_all, sine_all
    ).astype(bf16)
    value_rows = dense_dot(group_normed, full_value).astype(bf16).reshape(group_len, HEADS, head_dim)

    def masked_scores():
        raw_scores = (
            jnp.einsum("qhd,khd->hqk", queries, key_rows, preferred_element_type=f32) * attn_scale
        )
        return jnp.where(allowed[None], raw_scores, -1e30)

    scores = masked_scores()
    row_peak = jnp.max(scores, axis=-1, keepdims=True)
    row_total = jnp.sum(jnp.exp(scores - row_peak), axis=-1, keepdims=True)
    softmaxed = jnp.exp(scores - row_peak) / row_total
    attended = (
        jnp.einsum("hqk,khd->qhd", softmaxed.astype(bf16), value_rows, preferred_element_type=f32)
        .reshape(tok_count, width)
        .astype(bf16)
    )
    residual = inputs + dense_dot(attended, full_out)
    inverse_two = lax.rsqrt(jnp.mean(residual * residual, axis=-1, keepdims=True) + epsilon)
    unit_two = residual * inverse_two
    normed_two = (unit_two * gain_two).astype(bf16)

    affinity = jax.nn.softmax(dense_dot(normed_two, full_router), axis=-1)
    expert_range = jnp.arange(experts, dtype=jnp.int32)
    named = jnp.any(expert_ids[:, :, None] == expert_range[None, None, :], axis=1)
    signed = jnp.where(named, affinity, -affinity)

    first_expert = lax.axis_index("ep") * exp_local
    n_routed = exp_local * exp_hidden
    hidden = n_routed + sh_rows
    gate_w = jnp.concatenate([expert_gate.reshape(n_routed, model_width), shared_t[0]])
    up_w = jnp.concatenate([expert_up.reshape(n_routed, model_width), shared_t[1]])
    down_w = jnp.concatenate([expert_down.reshape(n_routed, model_width), shared_down])

    def mixture(rows, cot_rows, signed):
        count = rows.shape[0]
        mine = lax.dynamic_slice_in_dim(signed, first_expert, exp_local, axis=1)
        mine_named = mine > 0
        gates = jnp.where(mine_named, mine, 0.0)
        scale = jnp.concatenate(
            [jnp.repeat(gates, exp_hidden, axis=1), jnp.ones((count, sh_rows), f32)], axis=1
        )
        gate_pre = dot_nt(rows, gate_w)
        up_pre = dot_nt(rows, up_w)
        sigma = jax.nn.sigmoid(gate_pre)
        silu = gate_pre * sigma
        act = silu * up_pre
        act_scaled = (act * scale).astype(bf16)
        out_part = dense_dot(act_scaled, down_w).astype(bf16)
        grad_hidden = dot_nt(cot_rows, down_w)
        grad_gates = jnp.sum(
            (act * grad_hidden)[:, :n_routed].reshape(count, exp_local, exp_hidden), axis=-1
        )
        grad_gates = jnp.where(mine_named, grad_gates, 0.0)
        grad_hidden = grad_hidden * scale
        grad_gate_pre = (grad_hidden * up_pre * sigma * (1.0 + gate_pre * (1.0 - sigma))).astype(
            bf16
        )
        grad_up_pre = (grad_hidden * silu).astype(bf16)
        affinity_all = jnp.abs(signed)
        grad_aff = lax.dynamic_update_slice_in_dim(
            jnp.zeros((count, experts), f32), grad_gates, first_expert, axis=1
        )
        grad_logits = (
            affinity_all * (grad_aff - jnp.sum(affinity_all * grad_aff, axis=-1, keepdims=True))
        ).astype(bf16)
        dn2_part = (
            dense_dot(grad_gate_pre, gate_w)
            + dense_dot(grad_up_pre, up_w)
            + dot_nt(grad_logits, full_router)
        ).astype(bf16)
        sums = (
            dot_tn(act_scaled, cot_rows),
            dot_tn(grad_gate_pre, rows),
            dot_tn(grad_up_pre, rows),
            dot_tn(rows, grad_logits),
        )
        return out_part, dn2_part, sums

    if small_slice:
        lanes = 128
        h_core = -(-hidden // lanes) * lanes
        pad = ((0, h_core - hidden), (0, 0))
        signed_high = lax.reduce_precision(signed, 8, 7)
        aux = jnp.concatenate([signed_high.T, (signed - signed_high).T]).astype(bf16)
        owner = jnp.arange(h_core, dtype=jnp.int32)
        owner = jnp.where(owner < n_routed, first_expert + owner // exp_hidden, experts)
        owner = jnp.concatenate([owner, owner])
        sel_t = (owner[:, None] == jnp.arange(lanes, dtype=jnp.int32)[None, :]).astype(bf16)
        sel = jnp.concatenate([sel_t[:, :experts].T, jnp.eye(experts, lanes, dtype=bf16)], axis=1)
        sel = jnp.concatenate([sel, sel])
        ones = (jnp.arange(2 * h_core, dtype=jnp.int32) % h_core)[None, :]
        ones = ((ones >= n_routed) & (ones < hidden)).astype(f32)
        router_t = jnp.pad(full_router.T, ((0, lanes - experts), (0, 0)))
        token_sums, grads_here, grads_there, router_sum = mixture_call(
            normed_two,
            aux,
            cot_all,
            [jnp.pad(w, pad) for w in (gate_w, up_w, down_w)],
            sel,
            sel_t,
            router_t,
            ones,
            2,
        )
        routed_sum, grad_normed_two = token_sums[:, :model_width], token_sums[:, model_width:]
        grads = grads_here + grads_there
        grad_gate, grad_up, grad_down = [grads[k, :hidden] for k in range(3)]
        router_part = router_sum[:experts].T
    else:
        rows, signed_all = [lax.all_gather(v, AXES, axis=0, tiled=True) for v in (normed_two, signed)]
        blocks = max(1, tokens * hidden * 4 // 2**23)
        while tokens % blocks:
            blocks += 1

        def step(totals, block):
            out_block, dn2_block, sums = mixture(*block)
            return jax.tree.map(jnp.add, totals, sums), (out_block, dn2_block)

        zeros = (jnp.zeros((hidden, model_width), f32),) * 3 + (
            jnp.zeros((model_width, experts), f32),
        )
        sums, (out_part, dn2_part) = lax.scan(
            step,
            zeros,
            jax.tree.map(
                lambda v: v.reshape((blocks, -1) + v.shape[1:]), (rows, cot_all, signed_all)
            ),
        )
        grad_down, grad_gate, grad_up, router_part = sums
        routed_sum, grad_normed_two = [
            lax.psum_scatter(v.reshape(tokens, model_width), AXES, tiled=True).astype(f32)
            for v in (out_part, dn2_part)
        ]
    layer_output = (residual + routed_sum).astype(bf16)

    gain_two_part = jnp.sum(grad_normed_two * unit_two, axis=0)
    grad_resid = cotangent.astype(f32) + norm_back(grad_normed_two, unit_two, inverse_two, gain_two)
    grad_resid_low = grad_resid.astype(bf16)
    wout_part = dot_tn(attended, grad_resid_low)
    grad_att = dot_nt(grad_resid_low, full_out).astype(bf16).reshape(tok_count, HEADS, head_dim)
    softmax_again = jnp.exp(masked_scores() - row_peak) / row_total
    grad_soft = jnp.einsum("qhd,khd->hqk", grad_att, value_rows, preferred_element_type=f32)
    grad_scores = (
        softmax_again * (grad_soft - jnp.sum(softmax_again * grad_soft, axis=-1, keepdims=True))
    ).astype(bf16)
    grad_queries = (
        jnp.einsum("hqk,khd->qhd", grad_scores, key_rows, preferred_element_type=f32) * attn_scale
    )
    grad_key_rows = (
        jnp.einsum("hqk,qhd->khd", grad_scores, queries, preferred_element_type=f32) * attn_scale
    )
    grad_value_rows = jnp.einsum(
        "hqk,qhd->khd", softmax_again.astype(bf16), grad_att, preferred_element_type=f32
    )
    grad_q_pre = rotate(grad_queries, cosine, -sine_table).reshape(tok_count, width).astype(bf16)
    grad_k_pre = rotate(grad_key_rows, cosine_all, -sine_all).reshape(group_len, width).astype(bf16)
    grad_v_pre = grad_value_rows.reshape(group_len, width).astype(bf16)
    wq_part = dot_tn(normed, grad_q_pre)
    wk_part = dot_tn(group_normed, grad_k_pre)
    wv_part = dot_tn(group_normed, grad_v_pre)
    own_normed_grad = dot_nt(grad_q_pre, full_query)
    group_normed_grad = dot_nt(grad_k_pre, full_key) + dot_nt(grad_v_pre, full_value)
    gain_one_part = jnp.sum(own_normed_grad * unit_one, axis=0) + jnp.sum(
        group_normed_grad * group_unit, axis=0
    )

    weight_part = jnp.concatenate([wq_part, wk_part, wv_part, wout_part], axis=1).astype(bf16)
    small_part = jnp.concatenate(
        [
            router_part.reshape(devices, n_router),
            gain_one_part.reshape(devices, d_rows),
            gain_two_part.reshape(devices, d_rows),
        ],
        axis=1,
    )
    small_part = jnp.pad(small_part, ((0, 0), (0, small_len - small_part.shape[1])))
    small_part = small_part.reshape(devices, -1, model_width)
    small_part = jnp.pad(small_part, ((0, 0), (0, -small_part.shape[1] % 16), (0, 0))).astype(bf16)
    weight_part = weight_part.reshape(devices, d_rows, 4 * width)
    group_part = group_normed_grad.astype(bf16).reshape(tps, tok_count, model_width)
    if small_slice:
        (weight_sum, small_sum), (normed_grad_sum,) = reduce_scatter(
            [weight_part, small_part], [group_part], 3, "reduce_weights"
        )
    else:
        weight_sum, small_sum = [
            lax.psum_scatter(v, AXES).astype(f32) for v in (weight_part, small_part)
        ]
        normed_grad_sum = lax.psum_scatter(group_part, "tp").astype(f32)
    grad_normed = own_normed_grad + normed_grad_sum
    input_grad = grad_resid + norm_back(grad_normed, unit_one, inverse_one, gain_one)
    small_sum = small_sum.reshape(-1)

    shared_back = jnp.stack([grad_gate[n_routed:], grad_up[n_routed:]])
    shared_back = shared_back.reshape(2, sh_rows, devices, d_rows).transpose(2, 0, 1, 3)
    shared_back = lax.all_to_all(shared_back, AXES, split_axis=0, concat_axis=0, tiled=True)
    shared_back = shared_back.transpose(1, 3, 0, 2).reshape(2, d_rows, devices * sh_rows)

    return (
        layer_output,
        input_grad,
        small_sum[n_router : n_router + d_rows],
        weight_sum[:, :width],
        weight_sum[:, width : 2 * width],
        weight_sum[:, 2 * width : 3 * width],
        weight_sum[:, 3 * width :],
        small_sum[n_router + d_rows : n_router + 2 * d_rows],
        shared_back[0],
        shared_back[1],
        grad_down[n_routed:],
        small_sum[:n_router].reshape(d_rows, experts),
        grad_gate[:n_routed].reshape(expert_gate.shape),
        grad_up[:n_routed].reshape(expert_up.shape),
        grad_down[:n_routed].reshape(expert_down.shape),
    )


def solution(mesh):
    rows = P(AXES, None)
    vector = P(AXES)
    experts = P("ep", "tp", None)
    return jax.shard_map(
        on_device,
        mesh=mesh,
        in_specs=(
            rows, P("ep", None), rows, vector, rows, rows, rows, rows, vector,
            rows, rows, rows, rows, experts, experts, experts, rows,
        ),
        out_specs=(
            rows, rows, vector, rows, rows, rows, rows, vector,
            rows, rows, rows, rows, experts, experts, experts,
        ),
        check_vma=False,
    )
```

```python
import functools

import jax
import jax.numpy as jnp
from jax import lax
from jax.experimental import pallas as pl
from jax.experimental.pallas import tpu as pltpu
from jax.sharding import PartitionSpec as P

HEADS = 10
AXES = ("ep", "tp")
MESH = pl.DeviceIdType.MESH
VMEM_BUDGET = 56 * 2**20

epsilon = 1e-06

bf16 = jnp.bfloat16
f32 = jnp.float32


def place():
    ep, tp = lax.axis_index("ep"), lax.axis_index("tp")
    return ep // 2, ep % 2, tp // 2, tp % 2


def device(line, a, b, c):
    return (line * 2 + a, b * 2 + c)


def number(line, a, b, c):
    return ((line * 2 + a) * 2 + b) * 2 + c


def greet(partners):
    barrier = pltpu.get_barrier_semaphore()
    for partner in partners:
        pl.semaphore_signal(barrier, inc=1, device_id=partner, device_id_type=MESH)
    pl.semaphore_wait(barrier, len(partners))


O, X, Y, D = 0, 1, 2, 3


def visit_order(lines):
    return [sorted(range(lines), key=lambda other: (abs(other - z), other)) for z in range(lines)]


def lookup(table, index):
    out = jnp.int32(table[0])
    for k in range(1, len(table)):
        out = jnp.where(index == k, jnp.int32(table[k]), out)
    return out


def pick(values, index):
    out = values[0]
    for k in range(1, len(values)):
        out = jnp.where(index == k, values[k], out)
    return out


class Ways:
    def __init__(self, lines):
        self.lines = lines
        z, a, b, c = self.spot = place()
        oa, ob, oc = 1 - a, 1 - b, 1 - c
        self.to_b, self.to_a = device(z, a, ob, c), device(z, oa, b, c)
        self.to_c = device(z, a, b, oc)
        self.up_next = device(lax.rem(z + 1, lines), a, b, c)
        self.down_next = device(lax.rem(z + lines - 1, lines), a, b, c)
        self.peers = [device(lax.rem(z + s, lines), a, b, c) for s in range(1, lines)]
        table = visit_order(lines)
        self.zs = [lookup([table[k][u] for k in range(lines)], z) for u in range(lines)]
        self.column = ((a, b), (a, ob), (oa, b), (oa, ob))

    def greet(self):
        greet([self.to_b, self.to_a, self.to_c] + self.peers)

    def chip(self, line, kind):
        a, b = self.column[kind]
        return (line * 2 + a) * 2 + b


def remote(src, dst, send_sem, recv_sem, to):
    return pltpu.make_async_remote_copy(
        src, dst, send_sem, recv_sem, device_id=to, device_id_type=MESH
    )


class Gather:
    def __init__(self, ways, chunk, sems, own=None, relative=False, across=False):
        self.ways, self.chunk, self.own = ways, chunk, own
        self.send_sem, self.recv_sem = sems
        self.relative, self.across_core = relative, across
        self.sent = []

    def copy(self, slot, step, src, dst, to):
        k = slot * self.ways.lines + step
        return remote(src, dst, self.send_sem(k), self.recv_sem(k), to)

    def hop(self, slot, step, kind, to_kind, line, to, part=None, own=False):
        src = self.own if own and self.own is not None else self.chunk(line, kind, part, False)
        dst = self.chunk(line, to_kind if self.relative else kind, part, False)
        return self.copy(slot, step, src, dst, to)

    def send(self, copy):
        copy.start()
        self.sent.append(copy)

    def arrival(self, slot, step, kind, line, part=None, other=False):
        here = self.chunk(line, kind, part, other)
        self.copy(slot, step, here, here, self.ways.to_c).wait_recv()

    def across(self, slot, u, kind, part=None, own=False):
        if self.across_core:
            here = self.chunk(self.ways.zs[u], kind, part, False)
            src = self.own if own and self.own is not None else here
            self.send(self.copy(slot, u, src, here, self.ways.to_c))

    def send_own(self, u):
        w, own = self.ways, u == 0
        self.send(self.hop(0, u, O, X, w.zs[u], w.to_b, own=own))
        self.send(self.hop(1, u, O, Y, w.zs[u], w.to_a, own=own))
        self.across(6, u, O, own=own)

    def xy_event(self, u):
        w = self.ways
        self.arrival(0, u, X, w.zs[u])
        self.send(self.hop(2, u, X, D, w.zs[u], w.to_a, 0))
        self.arrival(1, u, Y, w.zs[u])
        self.send(self.hop(3, u, Y, D, w.zs[u], w.to_b, 1))
        self.across(7, u, X)
        self.across(8, u, Y)

    def diag_event(self, u):
        line = self.ways.zs[u]
        self.arrival(2, u, D, line, 0)
        self.across(9, u, D, 0)
        self.arrival(3, u, D, line, 1)
        self.across(10, u, D, 1)

    def chain_up(self, k):
        w = self.ways
        return self.hop(4, k, O, O, w.spot[0] - (k - 1), w.up_next, own=k == 1)

    def chain_down(self, k):
        w = self.ways
        return self.hop(5, k, O, O, w.spot[0] + (k - 1), w.down_next, own=k == 1)

    def chain_start(self, k):
        z, lines = self.ways.spot[0], self.ways.lines
        if k >= lines:
            return

        @pl.when((z >= k - 1) & (z + 1 < lines))
        def _():
            self.chain_up(k).start()

        @pl.when((z + k - 1 < lines) & (z > 0))
        def _():
            self.chain_down(k).start()

    def chain_event(self, k):
        z, lines = self.ways.spot[0], self.ways.lines

        @pl.when(z >= k)
        def _():
            self.arrival(4, k, O, z - k)

        @pl.when(z + k < lines)
        def _():
            self.arrival(5, k, O, z + k)

        self.chain_start(k + 1)

    def begin(self):
        self.send_own(0)
        self.chain_start(1)

    def events(self):
        lines = self.ways.lines
        out = [
            lambda: (self.xy_event(0), self.chain_event(1), self.send_own(1)),
        ]
        for u in range(2, lines):
            out.append(lambda u=u: (self.chain_event(u), self.xy_event(u - 1), self.send_own(u)))
            out.append(lambda u=u: self.diag_event(u - 2))
        out.append(lambda: self.xy_event(lines - 1))
        out.append(lambda: self.diag_event(lines - 2))
        out.append(lambda: self.diag_event(lines - 1))
        return out

    def other_core(self):
        if self.across_core:
            for u in range(self.ways.lines):
                for slot, kind, part in (
                    (6, O, None), (7, X, None), (8, Y, None), (9, D, 0), (10, D, 1),
                ):
                    self.arrival(slot, u, kind, self.ways.zs[u], part, True)

    def drain(self):
        z, lines = self.ways.spot[0], self.ways.lines
        for copy in self.sent:
            copy.wait_send()
        for k in range(1, lines):

            @pl.when((z >= k - 1) & (z + 1 < lines))
            def _(k=k):
                self.chain_up(k).wait_send()

            @pl.when((z + k - 1 < lines) & (z > 0))
            def _(k=k):
                self.chain_down(k).wait_send()


def softmax_rows(scores):
    weights = jnp.exp(scores - jnp.max(scores, axis=-1, keepdims=True))
    return weights * (1.0 / jnp.sum(weights, axis=-1, keepdims=True))


def turn(values, cosine, signed_sine):
    return values * cosine + pltpu.roll(values, values.shape[-1] // 2, 1) * signed_sine


def document_of(positions, first_end, second_end):
    return (positions >= first_end).astype(jnp.int32) + (positions >= second_end).astype(jnp.int32)


def make_bias(bias, lengths, tp_index):
    rows, cols = bias.shape
    first_end = lengths[0, 0]
    second_end = first_end + lengths[0, 1]
    q_pos = lax.broadcasted_iota(jnp.int32, (rows, cols), 0) + tp_index * rows
    k_pos = lax.broadcasted_iota(jnp.int32, (rows, cols), 1)
    allowed = (
        document_of(q_pos, first_end, second_end) == document_of(k_pos, first_end, second_end)
    ) & (q_pos >= k_pos)
    bias[...] = jnp.where(allowed, 0.0, -1e30)


def front_kernel(lines, experts, scale, *refs):
    (
        lengths, ids, freq, hidden, small, wq, wk, wv, wo, cot,
        w_out, cot_out, tok, aux, small_t, residual, attended, q_out, k_out, v_out, n_out,
        cos_out, sin_out, group,
        wall, stage, small_stage, small_all, bias,
        g_send, g_recv, s_send, s_recv, x_send, x_recv, local_sem,
    ) = refs
    ways = Ways(lines)
    z, a, b, c = ways.spot
    ob, oc = 1 - b, 1 - c
    count, width = hidden.shape
    d_rows = wq.shape[0]
    chip_rows = 2 * d_rows
    half = width // 2
    heads = width // 128
    group_len = 4 * count
    ways.greet()

    shards = (wq, wk, wv, wo)
    swaps = [
        remote(
            shards[k].at[:, pl.ds(pl.multiple_of(oc * half, 128), half)], stage.at[k],
            s_send.at[k], s_recv.at[k], ways.to_c,
        )
        for k in range(4)
    ] + [remote(small, small_stage, s_send.at[4], s_recv.at[4], ways.to_c)]
    for copy in swaps:
        copy.start()

    def group_copy(k, src, dst, to):
        return remote(src, dst, x_send.at[k], x_recv.at[k], to)

    own_group = group.at[b * 2 + c]
    group_copies = [group_copy(0, hidden, own_group, ways.to_c), group_copy(1, hidden, own_group, ways.to_b)]
    for copy in group_copies:
        copy.start()
    own_group[...] = hidden[...]

    def chip_block(own, other):
        own, other = own.astype(f32), other.astype(f32)
        first = jnp.where(c == 0, own, other)
        second = jnp.where(c == 0, other, own)
        return jnp.concatenate([first, second], axis=0).astype(bf16)

    base = pl.multiple_of(ways.chip(z, O) * chip_rows, 16)
    for copy in swaps:
        copy.wait_recv()
    small_all[pl.ds(base, chip_rows), :] = chip_block(small[...], small_stage[...])
    for k in range(4):
        mine = shards[k][:, pl.ds(pl.multiple_of(c * half, 128), half)]
        wall[pl.ds(base, chip_rows), pl.ds(pl.multiple_of((c * 4 + k) * half, 128), half)] = chip_block(
            mine, stage[k]
        )

    def small_chunk(line, kind, part, other):
        rows = pl.multiple_of(ways.chip(line, kind) * chip_rows, 16)
        if part is None:
            return small_all.at[pl.ds(rows, chip_rows)]
        low = chip_rows // 32 * 16
        return small_all.at[pl.ds(rows, low) if part == 0 else pl.ds(rows + low, chip_rows - low)]

    def weight_chunk(first, cols, cut):
        def chunk(line, kind, part, other):
            rows = pl.multiple_of(ways.chip(line, kind) * chip_rows, 16)
            col = (oc if other else c) * 4 * half + first
            if part is None:
                start, size = col, cols
            elif part == 0:
                start, size = col, cut
            else:
                start, size = col + cut, cols - cut
            return wall.at[pl.ds(rows, chip_rows), pl.ds(pl.multiple_of(start, 128), size)]

        return chunk

    def cot_chunk(line, kind, part, other):
        first = (line * 4 + kind) * count
        if part is None:
            return cot_out.at[pl.ds(first, count)]
        return cot_out.at[pl.ds(first + part * (count // 2), count // 2)]

    def sems(i):
        return (lambda k: g_send.at[i, k], lambda k: g_recv.at[i, k])

    tiles = half // 128
    g_small = Gather(ways, small_chunk, sems(0))
    g_qkv = Gather(ways, weight_chunk(0, 3 * half, (3 * tiles + 1) // 2 * 128), sems(1), across=True)
    g_out = Gather(ways, weight_chunk(3 * half, half, tiles // 2 * 128), sems(2), across=True)
    g_cot = Gather(ways, cot_chunk, sems(3), own=cot, relative=True)
    keep = pltpu.make_async_copy(cot, cot_chunk(z, O, None, False), local_sem.at[0])
    keep.start()
    g_small.begin()
    g_qkv.begin()

    first_end = lengths[0, 0]
    second_end = first_end + lengths[0, 1]
    position = lax.broadcasted_iota(jnp.int32, (group_len, 128), 0)
    doc = document_of(position, first_end, second_end)
    start = jnp.where(doc == 0, 0, jnp.where(doc == 1, first_end, second_end))
    angles = (position - start).astype(f32) * freq[...]
    lane = lax.broadcasted_iota(jnp.int32, (group_len, 128), 1)
    cos_out[...] = jnp.cos(angles)
    sin_out[...] = jnp.where(lane < 64, -1.0, 1.0) * jnp.sin(angles)
    make_bias(bias, lengths, b * 2 + c)
    got = group.at[ob * 2 + c]
    group_copy(1, got, got, ways.to_b).wait_recv()
    group_copies.append(group_copy(2, got, got, ways.to_c))
    group_copies[-1].start()
    for k, t in ((0, b * 2 + oc), (2, ob * 2 + oc)):
        got = group.at[t]
        group_copy(k, got, got, ways.to_c).wait_recv()

    for k, events in enumerate(zip(g_small.events(), g_qkv.events())):
        for event in events:
            event()
        if k == 2 * lines - 3:
            g_out.begin()
    flat = jnp.transpose(small_all[...].astype(f32))
    small_t[...] = flat.astype(bf16)
    gain_one = flat[experts : experts + 1, :]
    gain_two = flat[experts + 1 : experts + 2, :]
    for t in range(4):
        x = group[t].astype(f32)
        r = lax.rsqrt(jnp.mean(x * x, axis=-1, keepdims=True) + epsilon)
        n_out[t * count : (t + 1) * count, :] = (x * r * gain_one).astype(bf16)
    g_qkv.other_core()

    out_events = g_out.events()
    later = out_events[:-2] + [g_cot.begin] + out_events[-2:] + [g_out.other_core] + g_cot.events()

    def service(n=1):
        for _ in range(n):
            if later:
                later.pop(0)()

    own_rows = pl.ds(pl.multiple_of((b * 2 + c) * count, count), count)
    for h in range(2):
        cols = pl.ds((h * 4 + 1) * half, half)
        keys = dense_dot(n_out[...], wall[:, cols])
        for j in range(half // 128):
            k_out[:, h * half + j * 128 : h * half + (j + 1) * 128] = turn(
                keys[:, j * 128 : (j + 1) * 128], cos_out[...], sin_out[...]
            ).astype(bf16)
        service()
        cols = pl.ds((h * 4 + 2) * half, half)
        v_out[:, h * half : (h + 1) * half] = dense_dot(n_out[...], wall[:, cols]).astype(bf16)
        service()
        queries = dense_dot(n_out[own_rows, :], wall[:, pl.ds(h * 4 * half, half)])
        for j in range(half // 128):
            q_out[:, h * half + j * 128 : h * half + (j + 1) * 128] = turn(
                queries[:, j * 128 : (j + 1) * 128], cos_out[own_rows, :], sin_out[own_rows, :]
            ).astype(bf16)
        service()
    for h in range(heads):
        cols = pl.ds(h * 128, 128)
        probs = softmax_rows(dot_nt(q_out[:, cols], k_out[:, cols]) * scale + bias[...])
        attended[:, cols] = dense_dot(probs.astype(bf16), v_out[:, cols]).astype(bf16)
        if h % 2:
            service()
    while len(later) > len(g_cot.events()):
        service()
    for h in range(2):
        projected = dense_dot(attended[...], wall[:, pl.ds((h * 4 + 3) * half, half)])
        residual[:, h * half : (h + 1) * half] = (
            hidden[:, h * half : (h + 1) * half].astype(f32) + projected
        )
    service()
    res = residual[...]
    r2 = lax.rsqrt(jnp.mean(res * res, axis=-1, keepdims=True) + epsilon)
    normed = (res * r2 * gain_two).astype(bf16)
    tok[...] = normed
    logits = dense_dot(normed, small_all[...])
    lane = lax.broadcasted_iota(jnp.int32, (count, 128), 1)
    affinity = softmax_rows(jnp.where(lane < experts, logits, -1e30))
    named = lane < 0
    for j in range(ids.shape[1]):
        named = named | (ids[:, j : j + 1] == lane)
    signed = jnp.transpose(jnp.where(named, affinity, -affinity))[:experts, :]
    high = signed.astype(bf16)
    aux[0:experts, :] = high
    aux[experts : 2 * experts, :] = (signed - high.astype(f32)).astype(bf16)
    save = pltpu.make_async_copy(wall, w_out, local_sem.at[1])
    save.start()
    service(len(later))
    for g in (g_small, g_qkv, g_out, g_cot):
        g.drain()
    for copy in swaps + group_copies:
        copy.wait_send()
    keep.wait()
    save.wait()


def front_call(lengths, ids, hidden, small, wq, wk, wv, wo, cot, experts, scale, collective_id):
    lines = lax.axis_size("ep") // 2
    count, width = hidden.shape
    d_rows = wq.shape[0]
    group_len = 4 * count
    anywhere = pl.BlockSpec(memory_space=pl.ANY)
    vmem = pl.BlockSpec(memory_space=pltpu.VMEM)
    smem = pl.BlockSpec(memory_space=pltpu.SMEM)
    lane = jnp.arange(128) % 64
    freq = (10000.0 ** (-2.0 * lane.astype(f32) / 128))[None, :]
    shape = jax.ShapeDtypeStruct
    return pl.pallas_call(
        functools.partial(front_kernel, lines, experts, scale),
        out_shape=(
            shape((width, 4 * width), bf16),
            shape((lines * 4 * count, width), bf16),
            shape((count, width), bf16),
            shape((2 * experts, count), bf16),
            shape((128, width), bf16),
            shape((count, width), f32),
            shape((count, width), bf16),
            shape((count, width), bf16),
            shape((group_len, width), bf16),
            shape((group_len, width), bf16),
            shape((group_len, width), bf16),
            shape((group_len, 128), f32),
            shape((group_len, 128), f32),
            shape((4, count, width), bf16),
        ),
        in_specs=[smem] + [vmem] * 8 + [anywhere],
        out_specs=(anywhere, anywhere) + (vmem,) * 12,
        scratch_shapes=[
            pltpu.VMEM((width, 4 * width), bf16),
            pltpu.VMEM((4, d_rows, width // 2), bf16),
            pltpu.VMEM((d_rows, 128), bf16),
            pltpu.VMEM((width, 128), bf16),
            pltpu.VMEM((count, group_len), f32),
            pltpu.SemaphoreType.DMA((4, 11 * lines)),
            pltpu.SemaphoreType.DMA((4, 11 * lines)),
            pltpu.SemaphoreType.DMA((5,)),
            pltpu.SemaphoreType.DMA((5,)),
            pltpu.SemaphoreType.DMA((3,)),
            pltpu.SemaphoreType.DMA((3,)),
            pltpu.SemaphoreType.DMA((2,)),
        ],
        compiler_params=pltpu.CompilerParams(
            collective_id=collective_id, has_side_effects=True, vmem_limit_bytes=60 * 2**20
        ),
        name="front",
    )(lengths, ids, freq, hidden, small, wq, wk, wv, wo, cot)


def mixture_kernel(lines, tok, aux, cot, wg, wu, wd, sel, sel_t, router_t, ones, *refs):
    (
        sums, dw_own, dw_sib, dr,
        nc, aux_all, vg, vu, vd, dw, acts, dg, du, daff, dlg, pr, qr, xr, yr, zr,
        ag_send, ag_recv, rs_send, rs_recv, w_send, w_recv, local_sem,
    ) = refs
    z, a, b, c = place()
    oa, ob, oc = 1 - a, 1 - b, 1 - c
    to_b, to_a, to_c = device(z, a, ob, c), device(z, oa, b, c), device(z, a, b, oc)
    count, width = tok.shape
    half = count // 2
    hc = wg.shape[0]
    hidden = 2 * hc
    n_sel = sel.shape[1]
    block = 256
    unit_rows = 4 * count
    table = visit_order(lines)
    zs = [lookup([table[k][u] for k in range(lines)], z) for u in range(lines)]
    O, X, Y, D = 0, 1, 2, 3

    barrier = pltpu.get_barrier_semaphore()
    partners = [to_b, to_a, to_c] + [
        device(lax.rem(z + s, lines), a, b, c) for s in range(1, lines)
    ]
    for partner in partners:
        pl.semaphore_signal(barrier, inc=1, device_id=partner, device_id_type=MESH)
    pl.semaphore_wait(barrier, len(partners))

    def remote(src, dst, send_sem, recv_sem, to):
        return pltpu.make_async_remote_copy(
            src, dst, send_sem, recv_sem, device_id=to, device_id_type=MESH
        )

    local = []
    mine = pl.ds(c * hc, hc)
    theirs = pl.ds(oc * hc, hc)
    w_copies = []
    for k, (src, dst) in enumerate(((wg, vg), (wu, vu), (wd, vd))):
        copy = pltpu.make_async_copy(src, dst.at[mine], local_sem.at[k])
        copy.start()
        local.append(copy)
        copy = remote(src, dst.at[mine], w_send.at[k], w_recv.at[k], to_c)
        copy.start()
        w_copies.append(copy)

    def spot(line, kind):
        return line * 4 + kind

    def tok_at(line, kind, part=None):
        first = spot(line, kind) * count
        if part is None:
            return nc.at[pl.ds(first, count), pl.ds(0, width)]
        return nc.at[pl.ds(first + part * half, half), pl.ds(0, width)]

    def ag(slot, step, arr):
        k = slot * lines + step
        return ag_send.at[arr, k], ag_recv.at[arr, k]

    def ag_copies(slot, step, src_kind, dst_kind, line, to, part=None, own=False):
        src = tok if own else tok_at(line, src_kind, part)
        copies = [remote(src, tok_at(line, dst_kind, part), *ag(slot, step, 0), to)]
        if part != 1:
            src = aux if own else aux_all.at[spot(line, src_kind)]
            copies.append(remote(src, aux_all.at[spot(line, dst_kind)], *ag(slot, step, 1), to))
        return copies

    def send_own(u):
        own = u == 0
        return ag_copies(0, u, O, X, zs[u], to_b, own=own) + ag_copies(1, u, O, Y, zs[u], to_a, own=own)

    def send_halves(u):
        return ag_copies(2, u, X, D, zs[u], to_a, 0) + ag_copies(3, u, Y, D, zs[u], to_b, 1)

    def start(copies):
        for copy in copies:
            copy.start()

    def wait_recv(copies):
        for copy in copies:
            copy.wait_recv()

    def wait_send(copies):
        for copy in copies:
            copy.wait_send()

    up_next = device(lax.rem(z + 1, lines), a, b, c)
    down_next = device(lax.rem(z + lines - 1, lines), a, b, c)

    def chain_up(k, own=False):
        return ag_copies(4, k, O, O, z - (k - 1), up_next, own=own)

    def chain_down(k, own=False):
        return ag_copies(5, k, O, O, z + (k - 1), down_next, own=own)

    def chain_event(k):
        @pl.when(z >= k)
        def _():
            wait_recv(ag_copies(4, k, O, O, z - k, up_next))

            if k + 1 < lines:

                @pl.when(z + 1 < lines)
                def _():
                    start(chain_up(k + 1))

        @pl.when(z + k < lines)
        def _():
            wait_recv(ag_copies(5, k, O, O, z + k, down_next))

            if k + 1 < lines:

                @pl.when(z > 0)
                def _():
                    start(chain_down(k + 1))

    def chain_drain(k):
        @pl.when((z >= k - 1) & (z + 1 < lines))
        def _():
            wait_send(chain_up(k, own=k == 1))

        @pl.when((z + k - 1 < lines) & (z > 0))
        def _():
            wait_send(chain_down(k, own=k == 1))

    def xy_event(u):
        wait_recv(ag_copies(0, u, O, X, zs[u], to_b))
        wait_recv(ag_copies(1, u, O, Y, zs[u], to_a))
        start(send_halves(u))

    def diag_event(u):
        wait_recv(ag_copies(2, u, X, D, zs[u], to_a, 0))
        wait_recv(ag_copies(3, u, Y, D, zs[u], to_b, 1))

    def sent_event(u):
        wait_send(send_own(u))
        wait_send(send_halves(u))

    start(send_own(0))

    @pl.when(z + 1 < lines)
    def _():
        start(chain_up(1, own=True))

    @pl.when(z > 0)
    def _():
        start(chain_down(1, own=True))

    copy = pltpu.make_async_copy(tok, tok_at(z, O), local_sem.at[3])
    copy.start()
    local.append(copy)
    copy = pltpu.make_async_copy(aux, aux_all.at[spot(z, O)], local_sem.at[4])
    copy.start()
    local.append(copy)
    copy = pltpu.make_async_copy(cot, nc.at[:, pl.ds(width, width)], local_sem.at[5])
    copy.start()
    local.append(copy)

    def zero(i, carry):
        dw[:, pl.ds(i * 64, 64), :] = jnp.zeros((3, 64, width), f32)
        return carry

    lax.fori_loop(0, hidden // 64, zero, 0)
    dr[...] = jnp.zeros_like(dr)

    def res(line, kind, part=None):
        first = spot(line, kind) * count
        if part is None:
            return nc.at[pl.ds(first, count)]
        return nc.at[pl.ds(first + part * half, half)]

    def part_of(ref, u, part):
        return ref.at[u, pl.ds(part * half, half)]

    def rs(slot, u):
        k = slot * lines + u
        return rs_send.at[k], rs_recv.at[k]

    def p_copy(u):
        return remote(res(zs[u], D, 0), pr.at[u], *rs(0, u), to_a)

    def q_copy(u):
        return remote(res(zs[u], D, 1), qr.at[u], *rs(1, u), to_b)

    def x_copy(u, part):
        return remote(res(zs[u], X, part), part_of(xr, u, part), *rs(2 + part, u), to_b)

    def y_copy(u, part):
        return remote(res(zs[u], Y, part), part_of(yr, u, part), *rs(4 + part, u), to_a)

    def z_copy(u):
        slot = lax.rem(z - zs[u] + lines, lines) - 1
        k = 6 * lines
        return remote(
            res(zs[u], O), zr.at[slot], rs_send.at[k + u], rs_recv.at[k + slot],
            device(zs[u], a, b, c),
        )

    def add(first, rows, others):
        def body(k, carry):
            there = pl.ds(pl.multiple_of(k * 256, 256), 256)
            at = pl.ds(first, rows)
            total = nc[at, there].astype(f32)
            for ref, u in others:
                total = total + ref[u, :, there].astype(f32)
            nc[at, there] = total.astype(bf16)
            return carry

        lax.fori_loop(0, 2 * width // 256, body, 0)

    def rs_start(u):
        p_copy(u).start()
        q_copy(u).start()
        x_copy(u, 1).start()
        y_copy(u, 0).start()

    def rs_mid(u):
        p_copy(u).wait_recv()
        add(spot(zs[u], X) * count, half, [(pr, u)])
        x_copy(u, 0).start()
        q_copy(u).wait_recv()
        add(spot(zs[u], Y) * count + half, half, [(qr, u)])
        y_copy(u, 1).start()

    def rs_end(u):
        for part in (0, 1):
            x_copy(u, part).wait_recv()
            y_copy(u, part).wait_recv()
        add(spot(zs[u], O) * count, count, [(xr, u), (yr, u)])
        if u > 0:
            z_copy(u).start()

    def expand(line, columns):
        return jnp.concatenate(
            [dot_tn(aux_all[spot(line, kind)], sel[:, columns]) for kind in range(4)], axis=0
        )

    def unit(u, carry):
        line = pick(zs, u)
        rows = pl.ds(pl.multiple_of(line * unit_rows, unit_rows), unit_rows)

        for v in range(lines):

            @pl.when(u == v)
            def _(v=v):
                diag_event(v)

        daff[...] = jnp.zeros_like(daff)

        def hidden_step(i, carry):
            h = pl.ds(pl.multiple_of(i * block, block), block)
            x = nc[rows, 0:width]
            gate_pre = dot_nt(x, vg[h, :])
            up_pre = dot_nt(x, vu[h, :])
            grad = dot_nt(nc[rows, width : 2 * width], vd[h, :])
            scale = jnp.maximum(expand(line, h) + ones[:, h], 0.0)
            sigma = 1.0 / (1.0 + jnp.exp(-gate_pre))
            silu = gate_pre * sigma
            act = silu * up_pre
            acts[:, h] = (act * scale).astype(bf16)
            daff[...] += dense_dot((act * grad).astype(bf16), sel_t[h, :])
            grad = grad * scale
            dg[:, h] = (grad * up_pre * sigma * (1.0 + gate_pre * (1.0 - sigma))).astype(bf16)
            du[:, h] = (grad * silu).astype(bf16)
            return carry

        lax.fori_loop(0, hidden // block, hidden_step, 0)
        signed = expand(line, pl.ds(hidden, n_sel - hidden))
        affinity = jnp.abs(signed)
        grad_aff = jnp.where(signed > 0, daff[...], 0.0)
        total = jnp.sum(affinity * grad_aff, axis=1, keepdims=True)
        dlg[...] = (affinity * (grad_aff - total)).astype(bf16)

        @pl.when(u == 0)
        def _():
            if lines > 2:
                chain_event(2)

        for v in range(1, lines - 1):

            @pl.when(u == v)
            def _(v=v):
                xy_event(v + 1)
                if v + 2 < lines:
                    start(send_own(v + 2))

        def weight_step(i, carry):
            h = pl.ds(pl.multiple_of(i * block, block), block)
            x = nc[rows, 0:width]
            dw[0, h, :] += dot_tn(dg[:, h], x)
            dw[1, h, :] += dot_tn(du[:, h], x)
            dw[2, h, :] += dot_tn(acts[:, h], nc[rows, width : 2 * width])
            return carry

        lax.fori_loop(0, hidden // block, weight_step, 0)
        dr[...] += dot_tn(dlg[...], nc[rows, 0:width])

        for v in range(lines):

            @pl.when(u == v)
            def _(v=v):
                if v == 0:
                    xy_event(1)
                    if lines > 2:
                        start(send_own(2))
                    chain_drain(1)
                elif v == 1:
                    for k in range(2, lines):
                        chain_drain(k)
                elif v == 2:
                    rs_mid(1)
                sent_event(v)

        def back_step(i, carry):
            n = pl.ds(pl.multiple_of(i * block, block), block)
            n2 = pl.ds(pl.multiple_of(width + i * block, block), block)
            out = dense_dot(acts[...], vd[:, n])
            back = (
                dense_dot(dg[...], vg[:, n])
                + dense_dot(du[...], vu[:, n])
                + dense_dot(dlg[...], router_t[:, n])
            )
            nc[rows, n] = out.astype(bf16)
            nc[rows, n2] = back.astype(bf16)
            return carry

        lax.fori_loop(0, width // block, back_step, 0)

        @pl.when(u == 0)
        def _():
            for k in range(3, lines):
                chain_event(k)

        for v in range(1, lines):

            @pl.when(u == v)
            def _(v=v):
                rs_start(v)

        return carry

    xy_event(0)
    chain_event(1)
    start(send_own(1))
    for copy in w_copies:
        copy.wait_recv()
    for copy in local:
        copy.wait()
    lax.fori_loop(0, lines, unit, 0)

    own_out = pltpu.make_async_copy(dw.at[:, mine], dw_own, local_sem.at[6])
    own_out.start()
    sib_out = remote(dw.at[:, theirs], dw_sib, w_send.at[3], w_recv.at[3], to_c)
    sib_out.start()
    rs_mid(2)
    rs_end(1)
    rs_start(0)
    rs_mid(3)
    rs_end(2)
    rs_mid(0)
    rs_end(3)
    rs_end(0)
    for slot in range(lines - 1):
        k = 6 * lines + slot
        remote(
            zr.at[slot], zr.at[slot], rs_send.at[k], rs_recv.at[k], to_c
        ).wait_recv()

    def finish(k, carry):
        there = pl.ds(pl.multiple_of(k * 128, 128), 128)
        total = nc[pl.ds(spot(z, O) * count, count), there].astype(f32)
        for slot in range(lines - 1):
            total = total + zr[slot, :, there].astype(f32)
        sums[:, there] = total
        return carry

    lax.fori_loop(0, 2 * width // 128, finish, 0)
    for u in range(lines):
        p_copy(u).wait_send()
        q_copy(u).wait_send()
        for part in (0, 1):
            x_copy(u, part).wait_send()
            y_copy(u, part).wait_send()
        if u > 0:
            z_copy(u).wait_send()
    for copy in w_copies:
        copy.wait_send()
    sib_out.wait()
    own_out.wait()


def mixture_call(tok, aux, cot, weights, sel, sel_t, router_t, ones, collective_id):
    lines = lax.axis_size("ep") // 2
    count, width = tok.shape
    hc = weights[0].shape[0]
    anywhere = pl.BlockSpec(memory_space=pl.ANY)
    vmem = pl.BlockSpec(memory_space=pltpu.VMEM)
    n_rows = lines * 4 * count
    return pl.pallas_call(
        functools.partial(mixture_kernel, lines),
        out_shape=(
            jax.ShapeDtypeStruct((count, 2 * width), f32),
            jax.ShapeDtypeStruct((3, hc, width), f32),
            jax.ShapeDtypeStruct((3, hc, width), f32),
            jax.ShapeDtypeStruct((128, width), f32),
        ),
        in_specs=[anywhere] * 6 + [vmem] * 4,
        out_specs=(vmem, anywhere, anywhere, vmem),
        scratch_shapes=[
            pltpu.VMEM((n_rows, 2 * width), bf16),
            pltpu.VMEM((lines * 4,) + aux.shape, bf16),
            pltpu.VMEM((2 * hc, width), bf16),
            pltpu.VMEM((2 * hc, width), bf16),
            pltpu.VMEM((2 * hc, width), bf16),
            pltpu.VMEM((3, 2 * hc, width), f32),
            pltpu.VMEM((4 * count, 2 * hc), bf16),
            pltpu.VMEM((4 * count, 2 * hc), bf16),
            pltpu.VMEM((4 * count, 2 * hc), bf16),
            pltpu.VMEM((4 * count, 128), f32),
            pltpu.VMEM((4 * count, 128), bf16),
            pltpu.VMEM((lines, count // 2, 2 * width), bf16),
            pltpu.VMEM((lines, count // 2, 2 * width), bf16),
            pltpu.VMEM((lines, count, 2 * width), bf16),
            pltpu.VMEM((lines, count, 2 * width), bf16),
            pltpu.VMEM((lines - 1, count, 2 * width), bf16),
            pltpu.SemaphoreType.DMA((2, 6 * lines)),
            pltpu.SemaphoreType.DMA((2, 6 * lines)),
            pltpu.SemaphoreType.DMA((7 * lines,)),
            pltpu.SemaphoreType.DMA((7 * lines,)),
            pltpu.SemaphoreType.DMA((4,)),
            pltpu.SemaphoreType.DMA((4,)),
            pltpu.SemaphoreType.DMA((7,)),
        ],
        compiler_params=pltpu.CompilerParams(
            collective_id=collective_id, has_side_effects=True, vmem_limit_bytes=62 * 2**20
        ),
        name="mixture",
    )(tok, aux, cot, *weights, sel, sel_t, router_t, ones)


class Reduce:
    def __init__(self, ways, chunk, cut, pq, xr, yr, zr, sems):
        self.ways, self.chunk, self.cut = ways, chunk, cut
        self.pq, self.xr, self.yr, self.zr = pq, xr, yr, zr
        self.send_sem, self.recv_sem = sems

    def copy(self, slot, u, src, dst, to):
        k = slot * self.ways.lines + u
        return remote(src, dst, self.send_sem(k), self.recv_sem(k), to)

    def diag(self, part, u):
        w = self.ways
        return self.copy(
            part, u, self.chunk(w.zs[u], D, part), self.cut(self.pq, u, part),
            w.to_b if part else w.to_a,
        )

    def side_b(self, part, u):
        w = self.ways
        return self.copy(2 + part, u, self.chunk(w.zs[u], X, part), self.cut(self.xr, u, part), w.to_b)

    def side_a(self, part, u):
        w = self.ways
        return self.copy(4 + part, u, self.chunk(w.zs[u], Y, part), self.cut(self.yr, u, part), w.to_a)

    def along(self, u):
        w = self.ways
        z, a, b, c = w.spot
        slot = lax.rem(z - w.zs[u] + w.lines, w.lines) - 1
        k = 6 * w.lines
        return remote(
            self.chunk(w.zs[u], O, None), self.zr(slot), self.send_sem(k + u),
            self.recv_sem(k + slot), device(w.zs[u], a, b, c),
        )

    def start(self, u):
        self.diag(0, u).start()
        self.diag(1, u).start()
        self.side_b(1, u).start()
        self.side_a(0, u).start()

    def mid(self, u):
        w = self.ways
        self.diag(0, u).wait_recv()
        accumulate(self.chunk(w.zs[u], X, 0), [self.cut(self.pq, u, 0)])
        self.side_b(0, u).start()
        self.diag(1, u).wait_recv()
        accumulate(self.chunk(w.zs[u], Y, 1), [self.cut(self.pq, u, 1)])
        self.side_a(1, u).start()

    def end(self, u):
        w = self.ways
        for part in (0, 1):
            self.side_b(part, u).wait_recv()
            self.side_a(part, u).wait_recv()
            accumulate(
                self.chunk(w.zs[u], O, part), [self.cut(self.xr, u, part), self.cut(self.yr, u, part)]
            )
        if u > 0:
            self.along(u).start()

    def events(self):
        lines = self.ways.lines
        order = list(range(1, lines)) + [0]
        out = []
        for k in range(lines + 2):
            if k < lines:
                out.append(lambda k=k: self.start(order[k]))
            if 1 <= k <= lines:
                out.append(lambda k=k: self.mid(order[k - 1]))
            if k >= 2:
                out.append(lambda k=k: self.end(order[k - 2]))
        return out

    def total(self):
        w = self.ways
        sums = self.chunk(w.spot[0], O, None)[...].astype(f32)
        for slot in range(w.lines - 1):
            k = 6 * w.lines + slot
            here = self.zr(slot)
            remote(here, here, self.send_sem(k), self.recv_sem(k), w.to_c).wait_recv()
            sums = sums + here[...].astype(f32)
        return sums

    def drain(self):
        for u in range(self.ways.lines):
            for part in (0, 1):
                self.diag(part, u).wait_send()
                self.side_b(part, u).wait_send()
                self.side_a(part, u).wait_send()
            if u > 0:
                self.along(u).wait_send()


def accumulate(dst, others):
    total = dst[...].astype(f32)
    for ref in others:
        total = total + ref[...].astype(f32)
    dst[...] = total.astype(bf16)


def back_kernel(lines, experts, scale, *refs):
    (
        lengths, sums, residual, cot, group, small_t, router_part, attended, q, keys, vals, normed,
        cosine, sine, wall_in,
        layer_out, input_grad, gq, gk, gv, go, small_out,
        wall, part, landed, pq, xr, yr, zr, fin, fin_other,
        s_part, s_landed, s_pq, s_xr, s_yr, s_zr,
        grads, low, datt, dq, dk, dv, dn_part, dn_other, dn_far, bias, rows_t,
        c_send, c_recv, r_send, r_recv, d_send, d_recv, local_sem,
    ) = refs
    ways = Ways(lines)
    z, a, b, c = ways.spot
    ob, oc = 1 - b, 1 - c
    count, width = cot.shape
    half = width // 2
    heads = width // 128
    chip_rows = pq.shape[2]
    d_rows = chip_rows // 2
    load = pltpu.make_async_copy(wall_in, wall, local_sem.at[0])
    load.start()
    ways.greet()

    res = residual[...]
    r2 = lax.rsqrt(jnp.mean(res * res, axis=-1, keepdims=True) + epsilon)
    unit_two = res * r2
    dn2 = sums[:, width : 2 * width]
    gain_two = small_t[experts + 1 : experts + 2, :].astype(f32)
    gain_one = small_t[experts : experts + 1, :].astype(f32)
    rows_t[...] = router_part[...]
    rows_t[experts + 1 : experts + 2, :] = jnp.sum(dn2 * unit_two, axis=0, keepdims=True)
    scaled = dn2 * gain_two
    back = r2 * (scaled - unit_two * jnp.mean(scaled * unit_two, axis=-1, keepdims=True))
    grads[...] = cot[...].astype(f32) + back
    low[...] = grads[...].astype(bf16)
    layer_out[...] = (res + sums[:, 0:width]).astype(bf16)
    make_bias(bias, lengths, b * 2 + c)

    cuts = [half // 256 * 128, (half // 128 - half // 256) * 128] * 2

    def weight_reduce(k):
        def span(p):
            return (0, half) if p is None else ((0, cuts[k]) if p == 0 else (cuts[k], half - cuts[k]))

        def chunk(line, kind, p):
            start, size = span(p)
            rows = pl.multiple_of(ways.chip(line, kind) * chip_rows, 16)
            first = pl.multiple_of((c * 4 + k) * half + start, 128)
            return part.at[pl.ds(rows, chip_rows), pl.ds(first, size)]

        def cut(ref, u, p):
            start, size = span(p)
            return ref.at[k, u, :, pl.ds(start, size)]

        return Reduce(
            ways, chunk, cut, pq, xr, yr, lambda slot: zr.at[k, slot],
            (lambda i: r_send.at[k, i], lambda i: r_recv.at[k, i]),
        )

    def small_span(p):
        first = chip_rows // 32 * 16
        return (0, chip_rows) if p is None else ((0, first) if p == 0 else (first, chip_rows - first))

    def small_chunk(line, kind, p):
        start, size = small_span(p)
        return s_part.at[pl.ds(pl.multiple_of(ways.chip(line, kind) * chip_rows + start, 16), size)]

    def small_cut(ref, u, p):
        start, size = small_span(p)
        return ref.at[u, pl.ds(start, size)]

    small_reduce = Reduce(
        ways, small_chunk, small_cut, s_pq, s_xr, s_yr, lambda slot: s_zr.at[slot],
        (lambda i: r_send.at[4, i], lambda i: r_recv.at[4, i]),
    )
    reduces = [weight_reduce(k) for k in range(4)]

    def across(k):
        cols = pl.ds(pl.multiple_of((oc * 4 + k) * half, 128), half)
        return remote(part.at[:, cols], landed.at[k], c_send.at[k], c_recv.at[k], ways.to_c)

    def own_cols(k):
        return pl.ds(pl.multiple_of((c * 4 + k) * half, 128), half)

    def swapped(k):
        across(k).wait_recv()

        def body(i, carry):
            rows = pl.ds(pl.multiple_of(i * chip_rows, 16), chip_rows)
            accumulate(part.at[rows, own_cols(k)], [landed.at[k, rows]])
            return carry

        lax.fori_loop(0, width // chip_rows, body, 0)

    later = []

    def service(n=1):
        for _ in range(n):
            if later:
                later.pop(0)()

    def weight_grad(k, left, right):
        for h in range(2):
            cols = pl.ds((h * 4 + k) * half, half)
            part[:, cols] = dot_tn(left, right[:, h * half : (h + 1) * half]).astype(bf16)
        across(k).start()
        later.append(lambda: swapped(k))
        later.extend(reduces[k].events())

    weight_grad(3, attended[...], low)
    load.wait()
    datt[...] = (
        dot_nt(low[:, 0:half], wall[:, pl.ds(3 * half, half)])
        + dot_nt(low[:, half:width], wall[:, pl.ds(7 * half, half)])
    ).astype(bf16)
    service()

    own_rows = pl.ds(pl.multiple_of((b * 2 + c) * count, count), count)
    for h in range(heads):
        cols = pl.ds(h * 128, 128)
        probs = softmax_rows(dot_nt(q[:, cols], keys[:, cols]) * scale + bias[...])
        dprobs = dot_nt(datt[:, cols], vals[:, cols])
        dscores = (
            probs * (dprobs - jnp.sum(probs * dprobs, axis=-1, keepdims=True))
        ).astype(bf16)
        dq[:, cols] = turn(
            dense_dot(dscores, keys[:, cols]) * scale, cosine[own_rows, :], -sine[own_rows, :]
        ).astype(bf16)
        dk[:, cols] = turn(dot_tn(dscores, q[:, cols]) * scale, cosine[...], -sine[...]).astype(bf16)
        dv[:, cols] = dot_tn(probs.astype(bf16), datt[:, cols]).astype(bf16)
        service()
    weight_grad(2, normed[...], dv)
    service(2)
    weight_grad(1, normed[...], dk)
    service(2)
    weight_grad(0, normed[own_rows, :], dq)
    service(2)

    for t in range(4):
        rows = slice(t * count, (t + 1) * count)
        total = jnp.zeros((count, width), f32)
        for h in range(2):
            mine = slice(h * half, (h + 1) * half)
            total = total + dot_nt(dk[rows, mine], wall[:, pl.ds((h * 4 + 1) * half, half)])
            total = total + dot_nt(dv[rows, mine], wall[:, pl.ds((h * 4 + 2) * half, half)])
        dn_part[t] = total.astype(bf16)
        x = group[t].astype(f32)
        unit = x * lax.rsqrt(jnp.mean(x * x, axis=-1, keepdims=True) + epsilon)
        gain_row = jnp.sum(total * unit, axis=0, keepdims=True)
        if t == 0:
            rows_t[experts : experts + 1, :] = gain_row
        else:
            rows_t[experts : experts + 1, :] += gain_row
        service()

    def dn_copy(k, src, dst, to):
        return remote(src, dst, d_send.at[k], d_recv.at[k], to)

    dn_copies = [
        dn_copy(0, dn_part.at[b * 2 + oc], dn_other.at[0], ways.to_c),
        dn_copy(1, dn_part.at[ob * 2 + oc], dn_other.at[1], ways.to_c),
    ]
    for copy in dn_copies:
        copy.start()
    own = jnp.zeros((count, width), f32)
    for h in range(2):
        own = own + dot_nt(dq[:, h * half : (h + 1) * half], wall[:, pl.ds(h * 4 * half, half)])
    x = group[b * 2 + c].astype(f32)
    r1 = lax.rsqrt(jnp.mean(x * x, axis=-1, keepdims=True) + epsilon)
    unit_one = x * r1
    rows_t[experts : experts + 1, :] += jnp.sum(own * unit_one, axis=0, keepdims=True)
    s_part[...] = jnp.transpose(rows_t[...]).astype(bf16)
    small_swap = remote(s_part, s_landed, c_send.at[4], c_recv.at[4], ways.to_c)
    small_swap.start()
    service()
    dn_copies[1].wait_recv()
    accumulate(dn_part.at[ob * 2 + c], [dn_other.at[1]])
    dn_copies.append(dn_copy(2, dn_part.at[ob * 2 + c], dn_far, ways.to_b))
    dn_copies[2].start()
    dn_copies[0].wait_recv()
    small_swap.wait()
    accumulate(s_part, [s_landed])
    later.extend(small_reduce.events())
    service(2)
    dn_copies[2].wait_recv()
    total = (
        own
        + dn_part[b * 2 + c].astype(f32)
        + dn_other[0].astype(f32)
        + dn_far[...].astype(f32)
    )
    scaled = total * gain_one
    input_grad[...] = grads[...] + r1 * (
        scaled - unit_one * jnp.mean(scaled * unit_one, axis=-1, keepdims=True)
    )
    service(len(later))

    theirs = pl.ds(pl.multiple_of(oc * d_rows, 8), d_rows)
    mine = pl.ds(pl.multiple_of(c * d_rows, 8), d_rows)
    fin_copies = []
    for k in (3, 2, 1, 0):
        fin[k] = reduces[k].total()
        copy = remote(fin.at[k, theirs], fin_other.at[k], c_send.at[5 + k], c_recv.at[5 + k], ways.to_c)
        copy.start()
        fin_copies.append(copy)
    s_total = small_reduce.total()
    small_out[...] = jnp.where(c == 0, s_total[:d_rows], s_total[d_rows:])
    for k, copy in zip((3, 2, 1, 0), fin_copies):
        copy.wait_recv()
        out = (gq, gk, gv, go)[k]
        out[:, pl.ds(pl.multiple_of(c * half, 128), half)] = fin[k, mine, :]
        out[:, pl.ds(pl.multiple_of(oc * half, 128), half)] = fin_other[k]
    for r in reduces + [small_reduce]:
        r.drain()
    for copy in dn_copies + fin_copies:
        copy.wait_send()
    for k in range(4):
        across(k).wait_send()


def back_call(
    lengths, sums, residual, cot, group, small_t, router_part, attended, q, keys, vals, normed,
    cosine, sine, wall, d_rows, experts, scale, collective_id,
):
    lines = lax.axis_size("ep") // 2
    count, width = cot.shape
    half = width // 2
    chip_rows = 2 * d_rows
    group_len = 4 * count
    anywhere = pl.BlockSpec(memory_space=pl.ANY)
    vmem = pl.BlockSpec(memory_space=pltpu.VMEM)
    smem = pl.BlockSpec(memory_space=pltpu.SMEM)
    shape = jax.ShapeDtypeStruct
    dma = pltpu.SemaphoreType.DMA
    return pl.pallas_call(
        functools.partial(back_kernel, lines, experts, scale),
        out_shape=(
            shape((count, width), bf16),
            shape((count, width), f32),
            shape((d_rows, width), f32),
            shape((d_rows, width), f32),
            shape((d_rows, width), f32),
            shape((d_rows, width), f32),
            shape((d_rows, 128), f32),
        ),
        in_specs=[smem] + [vmem] * 13 + [anywhere],
        out_specs=(vmem,) * 7,
        scratch_shapes=[
            pltpu.VMEM(wall.shape, bf16),
            pltpu.VMEM(wall.shape, bf16),
            pltpu.VMEM((4, width, half), bf16),
            pltpu.VMEM((4, lines, chip_rows, half), bf16),
            pltpu.VMEM((4, lines, chip_rows, half), bf16),
            pltpu.VMEM((4, lines, chip_rows, half), bf16),
            pltpu.VMEM((4, lines - 1, chip_rows, half), bf16),
            pltpu.VMEM((4, chip_rows, half), f32),
            pltpu.VMEM((4, d_rows, half), f32),
            pltpu.VMEM((width, 128), bf16),
            pltpu.VMEM((width, 128), bf16),
            pltpu.VMEM((lines, chip_rows, 128), bf16),
            pltpu.VMEM((lines, chip_rows, 128), bf16),
            pltpu.VMEM((lines, chip_rows, 128), bf16),
            pltpu.VMEM((lines - 1, chip_rows, 128), bf16),
            pltpu.VMEM((count, width), f32),
            pltpu.VMEM((count, width), bf16),
            pltpu.VMEM((count, width), bf16),
            pltpu.VMEM((count, width), bf16),
            pltpu.VMEM((group_len, width), bf16),
            pltpu.VMEM((group_len, width), bf16),
            pltpu.VMEM((4, count, width), bf16),
            pltpu.VMEM((2, count, width), bf16),
            pltpu.VMEM((count, width), bf16),
            pltpu.VMEM((count, group_len), f32),
            pltpu.VMEM((128, width), f32),
            dma((9,)),
            dma((9,)),
            dma((5, 7 * lines)),
            dma((5, 7 * lines)),
            dma((3,)),
            dma((3,)),
            dma((1,)),
        ],
        compiler_params=pltpu.CompilerParams(
            collective_id=collective_id, has_side_effects=True, vmem_limit_bytes=62 * 2**20
        ),
        name="back",
    )(
        lengths, sums, residual, cot, group, small_t, router_part, attended, q, keys, vals, normed,
        cosine, sine, wall,
    )


def documents(positions, lengths):
    seq_ends = jnp.cumsum(lengths)
    doc_index = (positions >= seq_ends[0]).astype(jnp.int32) + (positions >= seq_ends[1]).astype(
        jnp.int32
    )
    seq_starts = jnp.where(doc_index == 0, 0, jnp.where(doc_index == 1, seq_ends[0], seq_ends[1]))
    return (doc_index, positions - seq_starts)


def rotary_tables(offsets, head_dim):
    half_dim = head_dim // 2
    frequency = 10000.0 ** (-2.0 * jnp.arange(half_dim, dtype=f32) / head_dim)
    angles = offsets.astype(f32)[:, None] * frequency[None, :]
    return (jnp.cos(angles)[:, None, :], jnp.sin(angles)[:, None, :])


def rotate(values, cosine, sine_table):
    half_dim = values.shape[-1] // 2
    first_half = values[..., :half_dim]
    second_half = values[..., half_dim:]
    return jnp.concatenate(
        [
            first_half * cosine - second_half * sine_table,
            first_half * sine_table + second_half * cosine,
        ],
        axis=-1,
    )


def norm_back(grad_normed, unit_rows, inverse, gain):
    scaled = grad_normed * gain
    return inverse * (scaled - unit_rows * jnp.mean(scaled * unit_rows, axis=-1, keepdims=True))


def dot(left, right, contract):
    return lax.dot_general(left, right, ((contract[0], contract[1]), ((), ())), preferred_element_type=f32)


def dense_dot(left, right):
    return dot(left, right, ((1,), (0,)))


def dot_nt(left, right):
    return dot(left, right, ((1,), (1,)))


def dot_tn(left, right):
    return dot(left, right, ((0,), (0,)))


def any_slice(
    hidden_in,
    seq_lengths,
    expert_ids,
    attn_gain,
    w_query,
    w_key,
    w_value,
    w_out,
    ffn_gain,
    shared_gate,
    shared_up,
    shared_down,
    router,
    expert_gate,
    expert_up,
    expert_down,
    cotangent,
):
    tok_count, model_width = hidden_in.shape
    eps, tps = lax.axis_size("ep"), lax.axis_size("tp")
    devices = eps * tps
    exp_local, exp_hidden = expert_gate.shape[:2]
    experts = exp_local * eps
    group_len = tps * tok_count
    tokens = devices * tok_count
    d_rows = w_query.shape[0]
    width = w_query.shape[1]
    sh_rows = shared_down.shape[0]
    head_dim = width // HEADS
    attn_scale = head_dim ** (-0.5)

    flat = jnp.concatenate([router.reshape(-1), attn_gain, ffn_gain])
    small_len = -(-flat.shape[0] // model_width) * model_width
    small = jnp.pad(flat, (0, small_len - flat.shape[0])).reshape(-1, model_width)
    small = jnp.pad(small, ((0, -small.shape[0] % 16), (0, 0)))
    weights = jnp.concatenate([w_query, w_key, w_value, w_out], axis=1)

    all_weights, all_small, all_cot = [
        lax.all_gather(v, AXES, axis=0) for v in (weights, small, cotangent)
    ]
    group_hidden = lax.all_gather(hidden_in, "tp", axis=0)
    all_weights = all_weights.reshape(devices * d_rows, 4 * width)
    full_query = all_weights[:, :width]
    full_key = all_weights[:, width : 2 * width]
    full_value = all_weights[:, 2 * width : 3 * width]
    full_out = all_weights[:, 3 * width :]
    all_small = all_small.reshape(devices, -1)
    n_router = d_rows * experts
    full_router = all_small[:, :n_router].reshape(devices * d_rows, experts)
    gain_one = all_small[:, n_router : n_router + d_rows].reshape(-1).astype(f32)
    gain_two = all_small[:, n_router + d_rows : n_router + 2 * d_rows].reshape(-1).astype(f32)
    cot_all = all_cot.reshape(-1, model_width)

    shared_cols = jnp.stack([shared_gate, shared_up], axis=1).reshape(d_rows, 2, devices, sh_rows)
    shared_cols = lax.all_to_all(
        shared_cols.transpose(2, 1, 3, 0), AXES, split_axis=0, concat_axis=0, tiled=True
    )
    shared_t = shared_cols.transpose(1, 2, 0, 3).reshape(2, sh_rows, model_width)

    lengths = seq_lengths[0]
    tp_index = lax.axis_index("tp")
    own_pos = tp_index * tok_count + jnp.arange(tok_count, dtype=jnp.int32)
    all_pos = jnp.arange(group_len, dtype=jnp.int32)
    own_doc, own_offset = documents(own_pos, lengths)
    all_doc, all_offset = documents(all_pos, lengths)
    allowed = (own_doc[:, None] == all_doc[None, :]) & (own_pos[:, None] >= all_pos[None, :])
    cosine, sine_table = rotary_tables(own_offset, head_dim)
    cosine_all, sine_all = rotary_tables(all_offset, head_dim)

    inputs = hidden_in.astype(f32)
    inverse_one = lax.rsqrt(jnp.mean(inputs * inputs, axis=-1, keepdims=True) + epsilon)
    unit_one = inputs * inverse_one
    normed = (unit_one * gain_one).astype(bf16)
    group_in = group_hidden.reshape(group_len, model_width).astype(f32)
    group_unit = group_in * lax.rsqrt(jnp.mean(group_in * group_in, axis=-1, keepdims=True) + epsilon)
    group_normed = (group_unit * gain_one).astype(bf16)

    queries = rotate(
        dense_dot(normed, full_query).reshape(tok_count, HEADS, head_dim), cosine, sine_table
    ).astype(bf16)
    key_rows = rotate(
        dense_dot(group_normed, full_key).reshape(group_len, HEADS, head_dim), cosine_all, sine_all
    ).astype(bf16)
    value_rows = dense_dot(group_normed, full_value).astype(bf16).reshape(group_len, HEADS, head_dim)

    def masked_scores():
        raw_scores = (
            jnp.einsum("qhd,khd->hqk", queries, key_rows, preferred_element_type=f32) * attn_scale
        )
        return jnp.where(allowed[None], raw_scores, -1e30)

    scores = masked_scores()
    row_peak = jnp.max(scores, axis=-1, keepdims=True)
    row_total = jnp.sum(jnp.exp(scores - row_peak), axis=-1, keepdims=True)
    softmaxed = jnp.exp(scores - row_peak) / row_total
    attended = (
        jnp.einsum("hqk,khd->qhd", softmaxed.astype(bf16), value_rows, preferred_element_type=f32)
        .reshape(tok_count, width)
        .astype(bf16)
    )
    residual = inputs + dense_dot(attended, full_out)
    inverse_two = lax.rsqrt(jnp.mean(residual * residual, axis=-1, keepdims=True) + epsilon)
    unit_two = residual * inverse_two
    normed_two = (unit_two * gain_two).astype(bf16)

    affinity = jax.nn.softmax(dense_dot(normed_two, full_router), axis=-1)
    expert_range = jnp.arange(experts, dtype=jnp.int32)
    named = jnp.any(expert_ids[:, :, None] == expert_range[None, None, :], axis=1)
    signed = jnp.where(named, affinity, -affinity)

    first_expert = lax.axis_index("ep") * exp_local
    n_routed = exp_local * exp_hidden
    hidden = n_routed + sh_rows
    gate_w = jnp.concatenate([expert_gate.reshape(n_routed, model_width), shared_t[0]])
    up_w = jnp.concatenate([expert_up.reshape(n_routed, model_width), shared_t[1]])
    down_w = jnp.concatenate([expert_down.reshape(n_routed, model_width), shared_down])

    def mixture(rows, cot_rows, signed):
        count = rows.shape[0]
        mine = lax.dynamic_slice_in_dim(signed, first_expert, exp_local, axis=1)
        mine_named = mine > 0
        gates = jnp.where(mine_named, mine, 0.0)
        scale = jnp.concatenate(
            [jnp.repeat(gates, exp_hidden, axis=1), jnp.ones((count, sh_rows), f32)], axis=1
        )
        gate_pre = dot_nt(rows, gate_w)
        up_pre = dot_nt(rows, up_w)
        sigma = jax.nn.sigmoid(gate_pre)
        silu = gate_pre * sigma
        act = silu * up_pre
        act_scaled = (act * scale).astype(bf16)
        out_part = dense_dot(act_scaled, down_w).astype(bf16)
        grad_hidden = dot_nt(cot_rows, down_w)
        grad_gates = jnp.sum(
            (act * grad_hidden)[:, :n_routed].reshape(count, exp_local, exp_hidden), axis=-1
        )
        grad_gates = jnp.where(mine_named, grad_gates, 0.0)
        grad_hidden = grad_hidden * scale
        grad_gate_pre = (grad_hidden * up_pre * sigma * (1.0 + gate_pre * (1.0 - sigma))).astype(
            bf16
        )
        grad_up_pre = (grad_hidden * silu).astype(bf16)
        affinity_all = jnp.abs(signed)
        grad_aff = lax.dynamic_update_slice_in_dim(
            jnp.zeros((count, experts), f32), grad_gates, first_expert, axis=1
        )
        grad_logits = (
            affinity_all * (grad_aff - jnp.sum(affinity_all * grad_aff, axis=-1, keepdims=True))
        ).astype(bf16)
        dn2_part = (
            dense_dot(grad_gate_pre, gate_w)
            + dense_dot(grad_up_pre, up_w)
            + dot_nt(grad_logits, full_router)
        ).astype(bf16)
        sums = (
            dot_tn(act_scaled, cot_rows),
            dot_tn(grad_gate_pre, rows),
            dot_tn(grad_up_pre, rows),
            dot_tn(rows, grad_logits),
        )
        return out_part, dn2_part, sums

    rows, signed_all = [lax.all_gather(v, AXES, axis=0, tiled=True) for v in (normed_two, signed)]
    blocks = max(1, tokens * hidden * 4 // 2**23)
    while tokens % blocks:
        blocks += 1

    def step(totals, block):
        out_block, dn2_block, sums = mixture(*block)
        return jax.tree.map(jnp.add, totals, sums), (out_block, dn2_block)

    zeros = (jnp.zeros((hidden, model_width), f32),) * 3 + (
        jnp.zeros((model_width, experts), f32),
    )
    sums, (out_part, dn2_part) = lax.scan(
        step,
        zeros,
        jax.tree.map(
            lambda v: v.reshape((blocks, -1) + v.shape[1:]), (rows, cot_all, signed_all)
        ),
    )
    grad_down, grad_gate, grad_up, router_part = sums
    routed_sum, grad_normed_two = [
        lax.psum_scatter(v.reshape(tokens, model_width), AXES, tiled=True).astype(f32)
        for v in (out_part, dn2_part)
    ]
    layer_output = (residual + routed_sum).astype(bf16)

    gain_two_part = jnp.sum(grad_normed_two * unit_two, axis=0)
    grad_resid = cotangent.astype(f32) + norm_back(grad_normed_two, unit_two, inverse_two, gain_two)
    grad_resid_low = grad_resid.astype(bf16)
    wout_part = dot_tn(attended, grad_resid_low)
    grad_att = dot_nt(grad_resid_low, full_out).astype(bf16).reshape(tok_count, HEADS, head_dim)
    softmax_again = jnp.exp(masked_scores() - row_peak) / row_total
    grad_soft = jnp.einsum("qhd,khd->hqk", grad_att, value_rows, preferred_element_type=f32)
    grad_scores = (
        softmax_again * (grad_soft - jnp.sum(softmax_again * grad_soft, axis=-1, keepdims=True))
    ).astype(bf16)
    grad_queries = (
        jnp.einsum("hqk,khd->qhd", grad_scores, key_rows, preferred_element_type=f32) * attn_scale
    )
    grad_key_rows = (
        jnp.einsum("hqk,qhd->khd", grad_scores, queries, preferred_element_type=f32) * attn_scale
    )
    grad_value_rows = jnp.einsum(
        "hqk,qhd->khd", softmax_again.astype(bf16), grad_att, preferred_element_type=f32
    )
    grad_q_pre = rotate(grad_queries, cosine, -sine_table).reshape(tok_count, width).astype(bf16)
    grad_k_pre = rotate(grad_key_rows, cosine_all, -sine_all).reshape(group_len, width).astype(bf16)
    grad_v_pre = grad_value_rows.reshape(group_len, width).astype(bf16)
    wq_part = dot_tn(normed, grad_q_pre)
    wk_part = dot_tn(group_normed, grad_k_pre)
    wv_part = dot_tn(group_normed, grad_v_pre)
    own_normed_grad = dot_nt(grad_q_pre, full_query)
    group_normed_grad = dot_nt(grad_k_pre, full_key) + dot_nt(grad_v_pre, full_value)
    gain_one_part = jnp.sum(own_normed_grad * unit_one, axis=0) + jnp.sum(
        group_normed_grad * group_unit, axis=0
    )

    weight_part = jnp.concatenate([wq_part, wk_part, wv_part, wout_part], axis=1).astype(bf16)
    small_part = jnp.concatenate(
        [
            router_part.reshape(devices, n_router),
            gain_one_part.reshape(devices, d_rows),
            gain_two_part.reshape(devices, d_rows),
        ],
        axis=1,
    )
    small_part = jnp.pad(small_part, ((0, 0), (0, small_len - small_part.shape[1])))
    small_part = small_part.reshape(devices, -1, model_width)
    small_part = jnp.pad(small_part, ((0, 0), (0, -small_part.shape[1] % 16), (0, 0))).astype(bf16)
    weight_part = weight_part.reshape(devices, d_rows, 4 * width)
    group_part = group_normed_grad.astype(bf16).reshape(tps, tok_count, model_width)
    weight_sum, small_sum = [
        lax.psum_scatter(v, AXES).astype(f32) for v in (weight_part, small_part)
    ]
    normed_grad_sum = lax.psum_scatter(group_part, "tp").astype(f32)
    grad_normed = own_normed_grad + normed_grad_sum
    input_grad = grad_resid + norm_back(grad_normed, unit_one, inverse_one, gain_one)
    small_sum = small_sum.reshape(-1)

    shared_back = jnp.stack([grad_gate[n_routed:], grad_up[n_routed:]])
    shared_back = shared_back.reshape(2, sh_rows, devices, d_rows).transpose(2, 0, 1, 3)
    shared_back = lax.all_to_all(shared_back, AXES, split_axis=0, concat_axis=0, tiled=True)
    shared_back = shared_back.transpose(1, 3, 0, 2).reshape(2, d_rows, devices * sh_rows)

    return (
        layer_output,
        input_grad,
        small_sum[n_router : n_router + d_rows],
        weight_sum[:, :width],
        weight_sum[:, width : 2 * width],
        weight_sum[:, 2 * width : 3 * width],
        weight_sum[:, 3 * width :],
        small_sum[n_router + d_rows : n_router + 2 * d_rows],
        shared_back[0],
        shared_back[1],
        grad_down[n_routed:],
        small_sum[:n_router].reshape(d_rows, experts),
        grad_gate[:n_routed].reshape(expert_gate.shape),
        grad_up[:n_routed].reshape(expert_up.shape),
        grad_down[:n_routed].reshape(expert_down.shape),
    )


def small_slice(
    hidden_in,
    seq_lengths,
    expert_ids,
    attn_gain,
    w_query,
    w_key,
    w_value,
    w_out,
    ffn_gain,
    shared_gate,
    shared_up,
    shared_down,
    router,
    expert_gate,
    expert_up,
    expert_down,
    cotangent,
):
    tok_count, model_width = hidden_in.shape
    eps, tps = lax.axis_size("ep"), lax.axis_size("tp")
    devices = eps * tps
    exp_local, exp_hidden = expert_gate.shape[:2]
    experts = exp_local * eps
    group_len = tps * tok_count
    tokens = devices * tok_count
    d_rows = w_query.shape[0]
    width = w_query.shape[1]
    sh_rows = shared_down.shape[0]
    head_dim = width // HEADS
    attn_scale = head_dim ** (-0.5)

    lanes = 128
    vectors = jnp.stack([attn_gain, ffn_gain], axis=1)
    small = jnp.concatenate([router, vectors], axis=1)
    small = jnp.pad(small, ((0, 0), (0, lanes - small.shape[1])))
    (
        w_all, cot_all, normed_two, aux, small_t, residual, attended, queries, key_rows, value_rows,
        group_normed, cos_all, sin_all, group_hidden,
    ) = front_call(
        seq_lengths, expert_ids, hidden_in, small, w_query, w_key, w_value, w_out, cotangent,
        experts, attn_scale, 0,
    )
    shared_cols = jnp.stack([shared_gate, shared_up], axis=1).reshape(d_rows, 2, devices, sh_rows)
    shared_cols = lax.all_to_all(
        shared_cols.transpose(2, 1, 3, 0), AXES, split_axis=0, concat_axis=0, tiled=True
    )
    shared_t = shared_cols.transpose(1, 2, 0, 3).reshape(2, sh_rows, model_width)

    first_expert = lax.axis_index("ep") * exp_local
    n_routed = exp_local * exp_hidden
    hidden = n_routed + sh_rows
    gate_w = jnp.concatenate([expert_gate.reshape(n_routed, model_width), shared_t[0]])
    up_w = jnp.concatenate([expert_up.reshape(n_routed, model_width), shared_t[1]])
    down_w = jnp.concatenate([expert_down.reshape(n_routed, model_width), shared_down])

    h_core = -(-hidden // lanes) * lanes
    pad = ((0, h_core - hidden), (0, 0))
    owner = jnp.arange(h_core, dtype=jnp.int32)
    owner = jnp.where(owner < n_routed, first_expert + owner // exp_hidden, experts)
    owner = jnp.concatenate([owner, owner])
    sel_t = (owner[:, None] == jnp.arange(lanes, dtype=jnp.int32)[None, :]).astype(bf16)
    sel = jnp.concatenate([sel_t[:, :experts].T, jnp.eye(experts, lanes, dtype=bf16)], axis=1)
    sel = jnp.concatenate([sel, sel])
    ones = (jnp.arange(2 * h_core, dtype=jnp.int32) % h_core)[None, :]
    ones = ((ones >= n_routed) & (ones < hidden)).astype(f32)
    token_sums, grads_here, grads_there, router_sum = mixture_call(
        normed_two,
        aux,
        cot_all,
        [jnp.pad(w, pad) for w in (gate_w, up_w, down_w)],
        sel,
        sel_t,
        small_t,
        ones,
        2,
    )
    layer_output, input_grad, grad_q, grad_k, grad_v, grad_o, small_sum = back_call(
        seq_lengths, token_sums, residual, cotangent, group_hidden, small_t, router_sum, attended,
        queries, key_rows, value_rows, group_normed, cos_all, sin_all, w_all, d_rows, experts,
        attn_scale, 3,
    )
    grad_gate, grad_up, grad_down = [(grads_here[k] + grads_there[k])[:hidden] for k in range(3)]

    shared_back = jnp.stack([grad_gate[n_routed:], grad_up[n_routed:]])
    shared_back = shared_back.reshape(2, sh_rows, devices, d_rows).transpose(2, 0, 1, 3)
    shared_back = lax.all_to_all(shared_back, AXES, split_axis=0, concat_axis=0, tiled=True)
    shared_back = shared_back.transpose(1, 3, 0, 2).reshape(2, d_rows, devices * sh_rows)

    return (
        layer_output,
        input_grad,
        small_sum[:, experts],
        grad_q,
        grad_k,
        grad_v,
        grad_o,
        small_sum[:, experts + 1],
        shared_back[0],
        shared_back[1],
        grad_down[n_routed:],
        small_sum[:, :experts],
        grad_gate[:n_routed].reshape(expert_gate.shape),
        grad_up[:n_routed].reshape(expert_up.shape),
        grad_down[:n_routed].reshape(expert_down.shape),
    )


def solution(mesh):
    rows = P(AXES, None)
    vector = P(AXES)
    experts = P("ep", "tp", None)
    small = mesh.shape["ep"] == 8 and mesh.shape["tp"] == 4
    return jax.shard_map(
        small_slice if small else any_slice,
        mesh=mesh,
        in_specs=(
            rows, P("ep", None), rows, vector, rows, rows, rows, rows, vector,
            rows, rows, rows, rows, experts, experts, experts, rows,
        ),
        out_specs=(
            rows, rows, vector, rows, rows, rows, rows, vector,
            rows, rows, rows, rows, experts, experts, experts,
        ),
        check_vma=False,
    )
```

```python
import functools

import jax
import jax.numpy as jnp
from jax import lax
from jax.experimental import pallas as pl
from jax.experimental.pallas import tpu as pltpu
from jax.sharding import PartitionSpec as P

HEADS = 10
AXES = ("ep", "tp")
MESH = pl.DeviceIdType.MESH
VMEM_BUDGET = 56 * 2**20

epsilon = 1e-06

bf16 = jnp.bfloat16
f32 = jnp.float32


def place():
    ep, tp = lax.axis_index("ep"), lax.axis_index("tp")
    return ep // 2, ep % 2, tp // 2, tp % 2


def device(line, a, b, c):
    return (line * 2 + a, b * 2 + c)


def number(line, a, b, c):
    return ((line * 2 + a) * 2 + b) * 2 + c


def greet(partners):
    barrier = pltpu.get_barrier_semaphore()
    for partner in partners:
        pl.semaphore_signal(barrier, inc=1, device_id=partner, device_id_type=MESH)
    pl.semaphore_wait(barrier, len(partners))


O, X, Y, D = 0, 1, 2, 3


def visit_order(lines):
    return [
        sorted(range(lines), key=lambda other: (abs(other - z), other != z ^ 1)) for z in range(lines)
    ]


def lookup(table, index):
    out = jnp.int32(table[0])
    for k in range(1, len(table)):
        out = jnp.where(index == k, jnp.int32(table[k]), out)
    return out


def pick(values, index):
    out = values[0]
    for k in range(1, len(values)):
        out = jnp.where(index == k, values[k], out)
    return out


class Ways:
    def __init__(self, lines):
        self.lines = lines
        z, a, b, c = self.spot = place()
        oa, ob, oc = 1 - a, 1 - b, 1 - c
        self.to_b, self.to_a = device(z, a, ob, c), device(z, oa, b, c)
        self.to_c = device(z, a, b, oc)
        self.up_next = device(lax.rem(z + 1, lines), a, b, c)
        self.down_next = device(lax.rem(z + lines - 1, lines), a, b, c)
        self.peers = [device(lax.rem(z + s, lines), a, b, c) for s in range(1, lines)]
        table = visit_order(lines)
        self.zs = [lookup([table[k][u] for k in range(lines)], z) for u in range(lines)]
        self.column = ((a, b), (a, ob), (oa, b), (oa, ob))
        self.pair = device(z + 1 - 2 * lax.rem(z, 2), a, b, c)
        outer = (z == 0) | (z == lines - 1)
        self.carried = [True, False, outer, jnp.logical_not(outer)]

    def greet(self):
        greet([self.to_b, self.to_a, self.to_c] + self.peers)

    def chip(self, line, kind):
        a, b = self.column[kind]
        return (line * 2 + a) * 2 + b


def when(condition, act):
    if condition is True:
        act()
    elif condition is not False:

        @pl.when(condition)
        def _():
            act()


def other(condition):
    return not condition if isinstance(condition, bool) else jnp.logical_not(condition)


def remote(src, dst, send_sem, recv_sem, to):
    return pltpu.make_async_remote_copy(
        src, dst, send_sem, recv_sem, device_id=to, device_id_type=MESH
    )


class Gather:
    def __init__(self, ways, chunk, sems, own=None, relative=False, across=False):
        self.ways, self.chunk, self.own = ways, chunk, own
        self.send_sem, self.recv_sem = sems
        self.relative, self.across_core = relative, across

    def copy(self, slot, step, src, dst, to):
        k = slot * self.ways.lines + step
        return remote(src, dst, self.send_sem(k), self.recv_sem(k), to)

    def hop(self, slot, step, kind, to_kind, line, to, part=None, own=False):
        src = self.own if own and self.own is not None else self.chunk(line, kind, part, False)
        dst = self.chunk(line, to_kind if self.relative else kind, part, False)
        return self.copy(slot, step, src, dst, to)

    def sends(self, u):
        w, own = self.ways, u == 0
        line, carried = w.zs[u], w.carried[u]
        copies = {
            "X": (True, lambda: self.hop(0, u, O, X, line, w.to_b, own=own)),
            "Y": (True, lambda: self.hop(1, u, O, Y, line, w.to_a, own=own)),
            "p": (carried, lambda: self.hop(2, u, X, D, line, w.to_a, 0)),
            "q": (carried, lambda: self.hop(3, u, Y, D, line, w.to_b, 1)),
            "pair": (carried, lambda: self.hop(11, 1 if own else u, D, D, line, w.pair)),
        }
        if self.across_core:

            def across(slot, kind):
                here = self.chunk(line, kind, None, False)
                src = self.own if kind == O and own and self.own is not None else here
                return self.copy(slot, u, src, here, w.to_c)

            for kind, slot in ((O, 6), (X, 7), (Y, 8), (D, 9)):
                copies[kind] = (True, lambda slot=slot, kind=kind: across(slot, kind))
        return copies

    def send(self, u, *names, condition=True):
        copies = self.sends(u)
        for name in names:
            if name in copies:
                always, make = copies[name]
                when(always if condition is True else condition, lambda: make().start())

    def arrival(self, slot, step, kind, line, part=None, other=False):
        here = self.chunk(line, kind, part, other)
        self.copy(slot, step, here, here, self.ways.to_c).wait_recv()

    def send_own(self, u):
        self.send(u, "X", "Y", O)

    def xy_event(self, u):
        line = self.ways.zs[u]
        self.arrival(0, u, X, line)
        self.send(u, "p")
        self.arrival(1, u, Y, line)
        self.send(u, "q", X, Y)

    def diag_carried(self, u):
        line, carried = self.ways.zs[u], self.ways.carried[u]

        def halves():
            self.arrival(2, u, D, line, 0)
            self.arrival(3, u, D, line, 1)

        when(carried, halves)
        self.send(u, "pair")
        self.send(u, D, condition=carried)

    def diag_handed(self, u):
        handed = other(self.ways.carried[u])
        when(handed, lambda: self.arrival(11, u, D, self.ways.zs[u]))
        self.send(u, D, condition=handed)

    def chain_up(self, k):
        w = self.ways
        return self.hop(4, k, O, O, w.spot[0] - (k - 1), w.up_next, own=k == 1)

    def chain_down(self, k):
        w = self.ways
        return self.hop(5, k, O, O, w.spot[0] + (k - 1), w.down_next, own=k == 1)

    def chain_start(self, k):
        z, lines = self.ways.spot[0], self.ways.lines
        if k >= lines:
            return

        @pl.when((z >= k - 1) & (z + 1 < lines))
        def _():
            self.chain_up(k).start()

        @pl.when((z + k - 1 < lines) & (z > 0))
        def _():
            self.chain_down(k).start()

    def chain_event(self, k):
        z, lines = self.ways.spot[0], self.ways.lines

        @pl.when(z >= k)
        def _():
            self.arrival(4, k, O, z - k)

        @pl.when(z + k < lines)
        def _():
            self.arrival(5, k, O, z + k)

        self.chain_start(k + 1)

    def begin(self):
        self.send_own(0)
        self.chain_start(1)

    def events(self):
        out = [
            lambda: (self.xy_event(0), self.chain_event(1), self.send_own(1)),
            lambda: (self.diag_carried(0), self.chain_event(2), self.send_own(2)),
            lambda: (self.xy_event(1), self.chain_event(3), self.send_own(3)),
            lambda: (self.xy_event(2), self.diag_handed(1)),
            lambda: (self.diag_carried(2), self.xy_event(3)),
            lambda: (self.diag_carried(3), self.diag_handed(2)),
            lambda: self.diag_handed(3),
        ]
        return out

    def other_core(self):
        if self.across_core:
            for u in range(self.ways.lines):
                for slot, kind in ((6, O), (7, X), (8, Y), (9, D)):
                    self.arrival(slot, u, kind, self.ways.zs[u], None, True)

    def drain_unit(self, u):
        for condition, make in self.sends(u).values():
            when(condition, lambda make=make: make().wait_send())

    def drain_chain(self, k):
        z, lines = self.ways.spot[0], self.ways.lines

        @pl.when((z >= k - 1) & (z + 1 < lines))
        def _():
            self.chain_up(k).wait_send()

        @pl.when((z + k - 1 < lines) & (z > 0))
        def _():
            self.chain_down(k).wait_send()

    def drain(self):
        for u in range(self.ways.lines):
            self.drain_unit(u)
        for k in range(1, self.ways.lines):
            self.drain_chain(k)


def softmax_rows(scores):
    weights = jnp.exp(scores - jnp.max(scores, axis=-1, keepdims=True))
    return weights * (1.0 / jnp.sum(weights, axis=-1, keepdims=True))


def turn(values, cosine, signed_sine):
    return values * cosine + pltpu.roll(values, values.shape[-1] // 2, 1) * signed_sine


def document_of(positions, first_end, second_end):
    return (positions >= first_end).astype(jnp.int32) + (positions >= second_end).astype(jnp.int32)


def make_bias(bias, lengths, tp_index):
    rows, cols = bias.shape
    first_end = lengths[0, 0]
    second_end = first_end + lengths[0, 1]
    q_pos = lax.broadcasted_iota(jnp.int32, (rows, cols), 0) + tp_index * rows
    k_pos = lax.broadcasted_iota(jnp.int32, (rows, cols), 1)
    allowed = (
        document_of(q_pos, first_end, second_end) == document_of(k_pos, first_end, second_end)
    ) & (q_pos >= k_pos)
    bias[...] = jnp.where(allowed, 0.0, -1e30)


def front_kernel(lines, experts, scale, *refs):
    (
        lengths, ids, freq, hidden, small, wq, wk, wv, wo, cot,
        w_out, cot_out, tok, aux, small_t, residual, attended, q_out, k_out, v_out, n_out,
        cos_out, sin_out, group,
        wall, stage, small_stage, small_all, bias,
        g_send, g_recv, s_send, s_recv, x_send, x_recv, local_sem,
    ) = refs
    ways = Ways(lines)
    z, a, b, c = ways.spot
    ob, oc = 1 - b, 1 - c
    count, width = hidden.shape
    d_rows = wq.shape[0]
    chip_rows = 2 * d_rows
    half = width // 2
    heads = width // 128
    group_len = 4 * count
    ways.greet()

    def cot_chunk(line, kind, part, other):
        first = (line * 4 + kind) * count
        if part is None:
            return cot_out.at[pl.ds(first, count)]
        return cot_out.at[pl.ds(first + part * (count // 2), count // 2)]

    def sems(i):
        return (lambda k: g_send.at[i, k], lambda k: g_recv.at[i, k])

    g_cot = Gather(ways, cot_chunk, sems(3), own=cot, relative=True)
    g_cot.begin()

    shards = (wq, wk, wv, wo)
    swaps = [
        remote(
            shards[k].at[:, pl.ds(pl.multiple_of(oc * half, 128), half)], stage.at[k],
            s_send.at[k], s_recv.at[k], ways.to_c,
        )
        for k in range(4)
    ] + [remote(small, small_stage, s_send.at[4], s_recv.at[4], ways.to_c)]
    for copy in swaps:
        copy.start()

    def group_copy(k, src, dst, to):
        return remote(src, dst, x_send.at[k], x_recv.at[k], to)

    own_group = group.at[b * 2 + c]
    group_copies = [group_copy(0, hidden, own_group, ways.to_c), group_copy(1, hidden, own_group, ways.to_b)]
    for copy in group_copies:
        copy.start()
    own_group[...] = hidden[...]

    def chip_block(own, other):
        own, other = own.astype(f32), other.astype(f32)
        first = jnp.where(c == 0, own, other)
        second = jnp.where(c == 0, other, own)
        return jnp.concatenate([first, second], axis=0).astype(bf16)

    base = pl.multiple_of(ways.chip(z, O) * chip_rows, 16)
    for copy in swaps:
        copy.wait_recv()
    small_all[pl.ds(base, chip_rows), :] = chip_block(small[...], small_stage[...])
    for k in range(4):
        mine = shards[k][:, pl.ds(pl.multiple_of(c * half, 128), half)]
        wall[pl.ds(base, chip_rows), pl.ds(pl.multiple_of((c * 4 + k) * half, 128), half)] = chip_block(
            mine, stage[k]
        )

    def small_chunk(line, kind, part, other):
        rows = pl.multiple_of(ways.chip(line, kind) * chip_rows, 16)
        if part is None:
            return small_all.at[pl.ds(rows, chip_rows)]
        low = chip_rows // 32 * 16
        return small_all.at[pl.ds(rows, low) if part == 0 else pl.ds(rows + low, chip_rows - low)]

    def weight_chunk(first, cols, cut):
        def chunk(line, kind, part, other):
            rows = pl.multiple_of(ways.chip(line, kind) * chip_rows, 16)
            col = (oc if other else c) * 4 * half + first
            if part is None:
                start, size = col, cols
            elif part == 0:
                start, size = col, cut
            else:
                start, size = col + cut, cols - cut
            return wall.at[pl.ds(rows, chip_rows), pl.ds(pl.multiple_of(start, 128), size)]

        return chunk

    tiles = half // 128
    g_small = Gather(ways, small_chunk, sems(0))
    g_qkv = Gather(ways, weight_chunk(0, 3 * half, (3 * tiles + 1) // 2 * 128), sems(1), across=True)
    g_out = Gather(ways, weight_chunk(3 * half, half, tiles // 2 * 128), sems(2), across=True)
    keep = pltpu.make_async_copy(cot, cot_chunk(z, O, None, False), local_sem.at[0])
    keep.start()
    g_small.begin()
    g_qkv.begin()

    first_end = lengths[0, 0]
    second_end = first_end + lengths[0, 1]
    position = lax.broadcasted_iota(jnp.int32, (group_len, 128), 0)
    doc = document_of(position, first_end, second_end)
    start = jnp.where(doc == 0, 0, jnp.where(doc == 1, first_end, second_end))
    angles = (position - start).astype(f32) * freq[...]
    lane = lax.broadcasted_iota(jnp.int32, (group_len, 128), 1)
    cos_out[...] = jnp.cos(angles)
    sin_out[...] = jnp.where(lane < 64, -1.0, 1.0) * jnp.sin(angles)
    make_bias(bias, lengths, b * 2 + c)
    got = group.at[ob * 2 + c]
    group_copy(1, got, got, ways.to_b).wait_recv()
    group_copies.append(group_copy(2, got, got, ways.to_c))
    group_copies[-1].start()
    for k, t in ((0, b * 2 + oc), (2, ob * 2 + oc)):
        got = group.at[t]
        group_copy(k, got, got, ways.to_c).wait_recv()

    small_events, qkv_events = g_small.events(), g_qkv.events()
    out_events, cot_events = g_out.events(), g_cot.events()
    for k in range(len(qkv_events)):
        if k == 3:
            g_out.begin()
        qkv_events[k]()
        small_events[k]()
        if k >= 4:
            out_events[k - 4]()
    cot_events[0]()
    flat = jnp.transpose(small_all[...].astype(f32))
    small_t[...] = flat.astype(bf16)
    gain_one = flat[experts : experts + 1, :]
    gain_two = flat[experts + 1 : experts + 2, :]
    for t in range(4):
        x = group[t].astype(f32)
        r = lax.rsqrt(jnp.mean(x * x, axis=-1, keepdims=True) + epsilon)
        n_out[t * count : (t + 1) * count, :] = (x * r * gain_one).astype(bf16)
    g_qkv.other_core()

    later = [out_events[3], cot_events[1], out_events[4], cot_events[2], out_events[5]]
    later += [out_events[6], g_out.other_core] + cot_events[3:]

    def service(n=1):
        for _ in range(n):
            if later:
                later.pop(0)()

    own_rows = pl.ds(pl.multiple_of((b * 2 + c) * count, count), count)
    for h in range(2):
        cols = pl.ds((h * 4 + 1) * half, half)
        keys = dense_dot(n_out[...], wall[:, cols])
        for j in range(half // 128):
            k_out[:, h * half + j * 128 : h * half + (j + 1) * 128] = turn(
                keys[:, j * 128 : (j + 1) * 128], cos_out[...], sin_out[...]
            ).astype(bf16)
        service()
        cols = pl.ds((h * 4 + 2) * half, half)
        v_out[:, h * half : (h + 1) * half] = dense_dot(n_out[...], wall[:, cols]).astype(bf16)
        service()
        queries = dense_dot(n_out[own_rows, :], wall[:, pl.ds(h * 4 * half, half)])
        for j in range(half // 128):
            q_out[:, h * half + j * 128 : h * half + (j + 1) * 128] = turn(
                queries[:, j * 128 : (j + 1) * 128], cos_out[own_rows, :], sin_out[own_rows, :]
            ).astype(bf16)
        service()
    for h in range(heads):
        cols = pl.ds(h * 128, 128)
        probs = softmax_rows(dot_nt(q_out[:, cols], k_out[:, cols]) * scale + bias[...])
        attended[:, cols] = dense_dot(probs.astype(bf16), v_out[:, cols]).astype(bf16)
        if h % 2:
            service()
    while len(later) > len(cot_events) - 3:
        service()
    for h in range(2):
        projected = dense_dot(attended[...], wall[:, pl.ds((h * 4 + 3) * half, half)])
        residual[:, h * half : (h + 1) * half] = (
            hidden[:, h * half : (h + 1) * half].astype(f32) + projected
        )
    service()
    res = residual[...]
    r2 = lax.rsqrt(jnp.mean(res * res, axis=-1, keepdims=True) + epsilon)
    normed = (res * r2 * gain_two).astype(bf16)
    tok[...] = normed
    logits = dense_dot(normed, small_all[...])
    lane = lax.broadcasted_iota(jnp.int32, (count, 128), 1)
    affinity = softmax_rows(jnp.where(lane < experts, logits, -1e30))
    named = lane < 0
    for j in range(ids.shape[1]):
        named = named | (ids[:, j : j + 1] == lane)
    signed = jnp.transpose(jnp.where(named, affinity, -affinity))[:experts, :]
    high = signed.astype(bf16)
    aux[0:experts, :] = high
    aux[experts : 2 * experts, :] = (signed - high.astype(f32)).astype(bf16)
    save = pltpu.make_async_copy(wall, w_out, local_sem.at[1])
    save.start()
    service(len(later))
    for g in (g_small, g_qkv, g_out, g_cot):
        g.drain()
    for copy in swaps + group_copies:
        copy.wait_send()
    keep.wait()
    save.wait()


def front_call(lengths, ids, hidden, small, wq, wk, wv, wo, cot, experts, scale, collective_id):
    lines = lax.axis_size("ep") // 2
    count, width = hidden.shape
    d_rows = wq.shape[0]
    group_len = 4 * count
    anywhere = pl.BlockSpec(memory_space=pl.ANY)
    vmem = pl.BlockSpec(memory_space=pltpu.VMEM)
    smem = pl.BlockSpec(memory_space=pltpu.SMEM)
    lane = jnp.arange(128) % 64
    freq = (10000.0 ** (-2.0 * lane.astype(f32) / 128))[None, :]
    shape = jax.ShapeDtypeStruct
    return pl.pallas_call(
        functools.partial(front_kernel, lines, experts, scale),
        out_shape=(
            shape((width, 4 * width), bf16),
            shape((lines * 4 * count, width), bf16),
            shape((count, width), bf16),
            shape((2 * experts, count), bf16),
            shape((128, width), bf16),
            shape((count, width), f32),
            shape((count, width), bf16),
            shape((count, width), bf16),
            shape((group_len, width), bf16),
            shape((group_len, width), bf16),
            shape((group_len, width), bf16),
            shape((group_len, 128), f32),
            shape((group_len, 128), f32),
            shape((4, count, width), bf16),
        ),
        in_specs=[smem] + [vmem] * 8 + [anywhere],
        out_specs=(anywhere, anywhere) + (vmem,) * 12,
        scratch_shapes=[
            pltpu.VMEM((width, 4 * width), bf16),
            pltpu.VMEM((4, d_rows, width // 2), bf16),
            pltpu.VMEM((d_rows, 128), bf16),
            pltpu.VMEM((width, 128), bf16),
            pltpu.VMEM((count, group_len), f32),
            pltpu.SemaphoreType.DMA((4, 12 * lines)),
            pltpu.SemaphoreType.DMA((4, 12 * lines)),
            pltpu.SemaphoreType.DMA((5,)),
            pltpu.SemaphoreType.DMA((5,)),
            pltpu.SemaphoreType.DMA((3,)),
            pltpu.SemaphoreType.DMA((3,)),
            pltpu.SemaphoreType.DMA((2,)),
        ],
        compiler_params=pltpu.CompilerParams(
            collective_id=collective_id, has_side_effects=True, vmem_limit_bytes=60 * 2**20
        ),
        name="front",
    )(lengths, ids, freq, hidden, small, wq, wk, wv, wo, cot)


class Reduce:
    def __init__(self, ways, chunk, cut, pq, xr, yr, dz, zr, sems):
        self.ways, self.chunk, self.cut = ways, chunk, cut
        self.pq, self.xr, self.yr, self.dz, self.zr = pq, xr, yr, dz, zr
        self.send_sem, self.recv_sem = sems

    def copy(self, slot, u, src, dst, to):
        k = slot * self.ways.lines + u
        return remote(src, dst, self.send_sem(k), self.recv_sem(k), to)

    def diag(self, part, u):
        w = self.ways
        return self.copy(
            part, u, self.chunk(w.zs[u], D, part), self.cut(self.pq, u, part),
            w.to_b if part else w.to_a,
        )

    def side_b(self, part, u):
        w = self.ways
        return self.copy(2 + part, u, self.chunk(w.zs[u], X, part), self.cut(self.xr, u, part), w.to_b)

    def side_a(self, part, u):
        w = self.ways
        return self.copy(4 + part, u, self.chunk(w.zs[u], Y, part), self.cut(self.yr, u, part), w.to_a)

    def hand(self, u, at):
        w = self.ways
        return self.copy(
            7, at, self.chunk(w.zs[u], D, None), self.cut(self.dz, min(at, 1), None), w.pair
        )

    def along(self, u):
        w = self.ways
        z, a, b, c = w.spot
        slot = lax.rem(z - w.zs[u] + w.lines, w.lines) - 1
        k = 6 * w.lines
        return remote(
            self.chunk(w.zs[u], O, None), self.zr(slot), self.send_sem(k + u),
            self.recv_sem(k + slot), device(w.zs[u], a, b, c),
        )

    def start(self, u):
        def whole():
            self.hand(u, u if u > 1 else 0).start()
            self.side_b(0, u).start()
            self.side_a(1, u).start()

        self.side_b(1, u).start()
        self.side_a(0, u).start()
        when(other(self.ways.carried[u]), whole)

    def carry(self, u):
        def act():
            self.hand(u, u).wait_recv()
            for part in (0, 1):
                accumulate(
                    self.chunk(self.ways.zs[u], D, part), [self.cut(self.dz, min(u, 1), part)]
                )
                self.diag(part, u).start()

        when(self.ways.carried[u], act)

    def mid(self, u):
        w = self.ways

        def act():
            self.diag(0, u).wait_recv()
            accumulate(self.chunk(w.zs[u], X, 0), [self.cut(self.pq, u, 0)])
            self.side_b(0, u).start()
            self.diag(1, u).wait_recv()
            accumulate(self.chunk(w.zs[u], Y, 1), [self.cut(self.pq, u, 1)])
            self.side_a(1, u).start()

        when(w.carried[u], act)

    def end(self, u):
        w = self.ways
        for part in (0, 1):
            self.side_b(part, u).wait_recv()
            self.side_a(part, u).wait_recv()
            accumulate(
                self.chunk(w.zs[u], O, part), [self.cut(self.xr, u, part), self.cut(self.yr, u, part)]
            )
        if u > 0:
            self.along(u).start()

    def events(self):
        return [
            lambda: (self.start(2), self.start(3)),
            lambda: (self.carry(2), self.carry(3), self.start(1)),
            lambda: (self.mid(2), self.mid(3), self.start(0)),
            lambda: (self.end(2), self.end(3)),
            lambda: (self.carry(0), self.end(1)),
            lambda: self.mid(0),
            lambda: self.end(0),
        ]

    def total(self):
        w = self.ways
        sums = self.chunk(w.spot[0], O, None)[...].astype(f32)
        for slot in range(w.lines - 1):
            k = 6 * w.lines + slot
            here = self.zr(slot)
            remote(here, here, self.send_sem(k), self.recv_sem(k), w.to_c).wait_recv()
            sums = sums + here[...].astype(f32)
        return sums

    def drain(self):
        w = self.ways
        for u in range(w.lines):
            for part in (0, 1):
                when(w.carried[u], lambda part=part, u=u: self.diag(part, u).wait_send())
                self.side_b(part, u).wait_send()
                self.side_a(part, u).wait_send()
            when(other(w.carried[u]), lambda u=u: self.hand(u, u if u > 1 else 0).wait_send())
            if u > 0:
                self.along(u).wait_send()


def accumulate(dst, others):
    total = dst[...].astype(f32)
    for ref in others:
        total = total + ref[...].astype(f32)
    dst[...] = total.astype(bf16)


def mixture_kernel(lines, tok, aux, cot, wg, wu, wd, sel, sel_t, router_t, ones, *refs):
    (
        sums, out_part, dw_own, dw_sib, dr,
        nc, aux_all, vg, vu, vd, dw, acts, dg, du, daff, dlg, pq, xr, yr, dz, zr,
        ag_send, ag_recv, rs_send, rs_recv, w_send, w_recv, local_sem,
    ) = refs
    ways = Ways(lines)
    z, a, b, c = ways.spot
    oc = 1 - c
    zs = ways.zs
    count, width = tok.shape
    half = count // 2
    hc = wg.shape[0]
    hidden = 2 * hc
    n_sel = sel.shape[1]
    block = 256
    unit_rows = 4 * count
    ways.greet()

    def rows_of(line, kind, part):
        first = (line * 4 + kind) * count
        return pl.ds(first, count) if part is None else pl.ds(first + part * half, half)

    def aux_chunk(line, kind, part, _):
        rows = aux.shape[0]
        at = line * 4 + kind
        if part is None:
            return aux_all.at[at]
        return aux_all.at[at, pl.ds(part * (rows // 2), rows // 2)]

    def sems(i):
        return (lambda k: ag_send.at[i, k], lambda k: ag_recv.at[i, k])

    gathers = [
        Gather(
            ways, lambda line, kind, part, _: nc.at[rows_of(line, kind, part), pl.ds(0, width)],
            sems(0), own=tok, relative=True,
        ),
        Gather(ways, aux_chunk, sems(1), own=aux, relative=True),
    ]

    def each(name, *args):
        for g in gathers:
            getattr(g, name)(*args)

    each("begin")
    local = []
    mine = pl.ds(c * hc, hc)
    theirs = pl.ds(oc * hc, hc)
    w_copies = []
    for k, (src, dst) in enumerate(((wg, vg), (wu, vu), (wd, vd))):
        copy = pltpu.make_async_copy(src, dst.at[mine], local_sem.at[k])
        copy.start()
        local.append(copy)
        copy = remote(src, dst.at[mine], w_send.at[k], w_recv.at[k], ways.to_c)
        copy.start()
        w_copies.append(copy)

    copy = pltpu.make_async_copy(tok, nc.at[rows_of(z, O, None), pl.ds(0, width)], local_sem.at[3])
    copy.start()
    local.append(copy)
    copy = pltpu.make_async_copy(aux, aux_chunk(z, O, None, False), local_sem.at[4])
    copy.start()
    local.append(copy)
    copy = pltpu.make_async_copy(cot, nc.at[:, pl.ds(width, width)], local_sem.at[5])
    copy.start()
    local.append(copy)

    def zero(i, carry):
        dw[:, pl.ds(i * 64, 64), :] = jnp.zeros((3, 64, width), f32)
        return carry

    lax.fori_loop(0, hidden // 64, zero, 0)
    dr[...] = jnp.zeros_like(dr)

    def cut(ref, u, part):
        return ref.at[u] if part is None else ref.at[u, pl.ds(part * half, half)]

    back = Reduce(
        ways, lambda line, kind, part: nc.at[rows_of(line, kind, part), pl.ds(width, width)], cut,
        pq, xr, yr, dz, lambda slot: zr.at[slot],
        (lambda k: rs_send.at[k], lambda k: rs_recv.at[k]),
    )

    def save(u):
        rows = pl.ds(pl.multiple_of(zs[u] * unit_rows, unit_rows), unit_rows)
        return pltpu.make_async_copy(
            nc.at[rows, pl.ds(0, width)], out_part.at[rows], local_sem.at[7 + u]
        )

    def expand(line, columns):
        return jnp.concatenate(
            [dot_tn(aux_all[line * 4 + kind], sel[:, columns]) for kind in range(4)], axis=0
        )

    def at_step(s, acts_of):
        for v, act in acts_of.items():
            when(s == v, act)

    order = [1, 2, 3, 0]

    def unit(s, carry):
        line = pick([zs[u] for u in order], s)
        rows = pl.ds(pl.multiple_of(line * unit_rows, unit_rows), unit_rows)
        at_step(
            s,
            {
                1: lambda: (each("diag_handed", 2), each("xy_event", 3)),
                2: lambda: each("diag_handed", 3),
            },
        )
        daff[...] = jnp.zeros_like(daff)

        def hidden_step(i, carry):
            h = pl.ds(pl.multiple_of(i * block, block), block)
            x = nc[rows, 0:width]
            gate_pre = dot_nt(x, vg[h, :])
            up_pre = dot_nt(x, vu[h, :])
            grad = dot_nt(nc[rows, width : 2 * width], vd[h, :])
            scale = jnp.maximum(expand(line, h) + ones[:, h], 0.0)
            sigma = 1.0 / (1.0 + jnp.exp(-gate_pre))
            silu = gate_pre * sigma
            act = silu * up_pre
            acts[:, h] = (act * scale).astype(bf16)
            daff[...] += dense_dot((act * grad).astype(bf16), sel_t[h, :])
            grad = grad * scale
            dg[:, h] = (grad * up_pre * sigma * (1.0 + gate_pre * (1.0 - sigma))).astype(bf16)
            du[:, h] = (grad * silu).astype(bf16)
            return carry

        lax.fori_loop(0, hidden // block, hidden_step, 0, unroll=True)
        signed = expand(line, pl.ds(hidden, n_sel - hidden))
        affinity = jnp.abs(signed)
        grad_aff = jnp.where(signed > 0, daff[...], 0.0)
        total = jnp.sum(affinity * grad_aff, axis=1, keepdims=True)
        dlg[...] = (affinity * (grad_aff - total)).astype(bf16)
        at_step(
            s,
            {
                0: lambda: (each("chain_event", 3), each("xy_event", 2), each("send_own", 3)),
                1: lambda: each("diag_carried", 3),
                2: lambda: (back.carry(2), back.end(1)),
                3: lambda: (back.carry(3), back.end(2)),
            },
        )

        def down_step(i, carry):
            h = pl.ds(pl.multiple_of(i * block, block), block)
            dw[2, h, :] += dot_tn(acts[:, h], nc[rows, width : 2 * width])
            return carry

        lax.fori_loop(0, hidden // block, down_step, 0, unroll=True)

        def back_step(i, carry):
            n = pl.ds(pl.multiple_of(i * block, block), block)
            n2 = pl.ds(pl.multiple_of(width + i * block, block), block)
            nc[rows, n2] = (
                dense_dot(dg[...], vg[:, n])
                + dense_dot(du[...], vu[:, n])
                + dense_dot(dlg[...], router_t[:, n])
            ).astype(bf16)
            return carry

        lax.fori_loop(0, width // block, back_step, 0, unroll=True)
        at_step(
            s,
            {
                0: lambda: (each("diag_carried", 2), back.start(1)),
                1: lambda: back.start(2),
                2: lambda: (back.mid(2), back.start(3)),
                3: lambda: (back.mid(3), back.start(0), back.carry(0)),
            },
        )

        def weight_step(i, carry):
            h = pl.ds(pl.multiple_of(i * block, block), block)
            x = nc[rows, 0:width]
            dw[0, h, :] += dot_tn(dg[:, h], x)
            dw[1, h, :] += dot_tn(du[:, h], x)
            return carry

        lax.fori_loop(0, hidden // block, weight_step, 0, unroll=True)
        dr[...] += dot_tn(dlg[...], nc[rows, 0:width])
        for v, u in enumerate(order):
            when(s == v, lambda u=u: each("drain_unit", u))
        at_step(
            s,
            {
                0: lambda: (each("drain_chain", 1), each("drain_chain", 2)),
                1: lambda: each("drain_chain", 3),
                3: lambda: (back.mid(0), back.end(3)),
            },
        )

        def out_step(i, carry):
            n = pl.ds(pl.multiple_of(i * block, block), block)
            nc[rows, n] = dense_dot(acts[...], vd[:, n]).astype(bf16)
            return carry

        lax.fori_loop(0, width // block, out_step, 0, unroll=True)
        for v, u in enumerate(order):
            when(s == v, lambda u=u: save(u).start())
        return carry

    each("xy_event", 0)
    each("chain_event", 1)
    each("send_own", 1)
    each("diag_carried", 0)
    each("chain_event", 2)
    each("send_own", 2)
    each("xy_event", 1)
    for copy in w_copies:
        copy.wait_recv()
    for copy in local:
        copy.wait()
    each("diag_handed", 1)
    lax.fori_loop(0, lines, unit, 0)

    own_out = pltpu.make_async_copy(dw.at[:, mine], dw_own, local_sem.at[6])
    own_out.start()
    sib_out = pltpu.make_async_copy(dw.at[:, theirs], dw_sib, local_sem.at[7 + lines])
    sib_out.start()
    back.end(0)
    sums[...] = back.total()
    back.drain()
    for u in range(lines):
        save(u).wait()
    for copy in w_copies:
        copy.wait_send()
    sib_out.wait()
    own_out.wait()


def mixture_call(tok, aux, cot, weights, sel, sel_t, router_t, ones, collective_id):
    lines = lax.axis_size("ep") // 2
    count, width = tok.shape
    hc = weights[0].shape[0]
    anywhere = pl.BlockSpec(memory_space=pl.ANY)
    vmem = pl.BlockSpec(memory_space=pltpu.VMEM)
    n_rows = lines * 4 * count
    return pl.pallas_call(
        functools.partial(mixture_kernel, lines),
        out_shape=(
            jax.ShapeDtypeStruct((count, width), f32),
            jax.ShapeDtypeStruct((n_rows, width), bf16),
            jax.ShapeDtypeStruct((3, hc, width), f32),
            jax.ShapeDtypeStruct((3, hc, width), f32),
            jax.ShapeDtypeStruct((128, width), f32),
        ),
        in_specs=[anywhere] * 6 + [vmem] * 4,
        out_specs=(vmem, anywhere, anywhere, anywhere, vmem),
        scratch_shapes=[
            pltpu.VMEM((n_rows, 2 * width), bf16),
            pltpu.VMEM((lines * 4,) + aux.shape, bf16),
            pltpu.VMEM((2 * hc, width), bf16),
            pltpu.VMEM((2 * hc, width), bf16),
            pltpu.VMEM((2 * hc, width), bf16),
            pltpu.VMEM((3, 2 * hc, width), f32),
            pltpu.VMEM((4 * count, 2 * hc), bf16),
            pltpu.VMEM((4 * count, 2 * hc), bf16),
            pltpu.VMEM((4 * count, 2 * hc), bf16),
            pltpu.VMEM((4 * count, 128), f32),
            pltpu.VMEM((4 * count, 128), bf16),
            pltpu.VMEM((lines, count, width), bf16),
            pltpu.VMEM((lines, count, width), bf16),
            pltpu.VMEM((lines, count, width), bf16),
            pltpu.VMEM((2, count, width), bf16),
            pltpu.VMEM((lines - 1, count, width), bf16),
            pltpu.SemaphoreType.DMA((2, 12 * lines)),
            pltpu.SemaphoreType.DMA((2, 12 * lines)),
            pltpu.SemaphoreType.DMA((8 * lines,)),
            pltpu.SemaphoreType.DMA((8 * lines,)),
            pltpu.SemaphoreType.DMA((4,)),
            pltpu.SemaphoreType.DMA((4,)),
            pltpu.SemaphoreType.DMA((8 + lines,)),
        ],
        compiler_params=pltpu.CompilerParams(
            collective_id=collective_id, has_side_effects=True, vmem_limit_bytes=62 * 2**20
        ),
        name="mixture",
    )(tok, aux, cot, *weights, sel, sel_t, router_t, ones)


def back_kernel(lines, experts, scale, *refs):
    (
        lengths, dn2, residual, cot, group, small_t, router_part, attended, q, normed, cosine, sine,
        keys, vals, wall_in, outs_in, dw_sib,
        layer_out, input_grad, gq, gk, gv, go, small_out, dw_got,
        wall, part, staged, landed, pq, xr, yr, dz, zr, fin, fin_other,
        s_part, s_landed, s_pq, s_xr, s_yr, s_dz, s_zr,
        o_part, o_pq, o_xr, o_yr, o_dz, o_zr,
        grads, low, datt, dq, dk, dv, dn_part, dn_other, dn_far, bias, rows_t,
        c_send, c_recv, r_send, r_recv, d_send, d_recv, local_sem,
    ) = refs
    ways = Ways(lines)
    z, a, b, c = ways.spot
    ob, oc = 1 - b, 1 - c
    count, width = cot.shape
    half = width // 2
    heads = width // 128
    chip_rows = pq.shape[1]
    d_rows = chip_rows // 2

    def load(i, src, dst):
        copy = pltpu.make_async_copy(src, dst, local_sem.at[i])
        copy.start()
        return copy

    o_load = load(0, outs_in, o_part)
    wo_loads = [
        load(1 + h, wall_in.at[:, pl.ds((h * 4 + 3) * half, half)], part.at[:, pl.ds(h * half, half)])
        for h in range(2)
    ]
    kv_loads = [load(3, keys, dk), load(4, vals, dv)]
    wall_loads = [
        load(5 + h, wall_in.at[:, pl.ds(h * 4 * half, 3 * half)], wall.at[:, pl.ds(h * 3 * half, 3 * half)])
        for h in range(2)
    ]

    def weight(h, k):
        return wall[:, pl.ds((h * 3 + k) * half, half)]

    ways.greet()

    half_rows = count // 2

    def o_chunk(line, kind, p):
        first = (line * 4 + kind) * count
        return o_part.at[pl.ds(first, count) if p is None else pl.ds(first + p * half_rows, half_rows)]

    def o_cut(ref, u, p):
        return ref.at[u] if p is None else ref.at[u, pl.ds(p * half_rows, half_rows)]

    o_reduce = Reduce(
        ways, o_chunk, o_cut, o_pq, o_xr, o_yr, o_dz, lambda slot: o_zr.at[slot],
        (lambda i: r_send.at[3, i], lambda i: r_recv.at[3, i]),
    )

    def finish_output():
        layer_out[...] = (residual[...] + o_reduce.total()).astype(bf16)

    o_events = o_reduce.events() + [finish_output]
    o_load.wait()
    o_events[0]()
    dw_copy = remote(dw_sib, dw_got, c_send.at[6], c_recv.at[6], ways.to_c)
    dw_copy.start()

    res = residual[...]
    r2 = lax.rsqrt(jnp.mean(res * res, axis=-1, keepdims=True) + epsilon)
    unit_two = res * r2
    gain_two = small_t[experts + 1 : experts + 2, :].astype(f32)
    gain_one = small_t[experts : experts + 1, :].astype(f32)
    rows_t[...] = router_part[...]
    rows_t[experts + 1 : experts + 2, :] = jnp.sum(dn2[...] * unit_two, axis=0, keepdims=True)
    scaled = dn2[...] * gain_two
    back = r2 * (scaled - unit_two * jnp.mean(scaled * unit_two, axis=-1, keepdims=True))
    grads[...] = cot[...].astype(f32) + back
    low[...] = grads[...].astype(bf16)
    make_bias(bias, lengths, b * 2 + c)

    def weight_reduce(k, first, cols):
        low_cols = cols // 256 * 128

        def span(p):
            return (0, cols) if p is None else ((0, low_cols) if p == 0 else (low_cols, cols - low_cols))

        def chunk(line, kind, p):
            start, size = span(p)
            rows = pl.multiple_of(ways.chip(line, kind) * chip_rows, 16)
            return part.at[pl.ds(rows, chip_rows), pl.ds(first + start, size)]

        def cut(ref, u, p):
            start, size = span(p)
            return ref.at[u, :, pl.ds(first + start, size)]

        return Reduce(
            ways, chunk, cut, pq, xr, yr, dz, lambda slot: zr.at[slot, :, pl.ds(first, cols)],
            (lambda i: r_send.at[k, i], lambda i: r_recv.at[k, i]),
        )

    def small_span(p):
        first = chip_rows // 32 * 16
        return (0, chip_rows) if p is None else ((0, first) if p == 0 else (first, chip_rows - first))

    def small_chunk(line, kind, p):
        start, size = small_span(p)
        return s_part.at[pl.ds(pl.multiple_of(ways.chip(line, kind) * chip_rows + start, 16), size)]

    def small_cut(ref, u, p):
        start, size = small_span(p)
        return ref.at[u, pl.ds(start, size)]

    small_reduce = Reduce(
        ways, small_chunk, small_cut, s_pq, s_xr, s_yr, s_dz, lambda slot: s_zr.at[slot],
        (lambda i: r_send.at[2, i], lambda i: r_recv.at[2, i]),
    )
    qkv_reduce = weight_reduce(0, 0, 3 * half)
    wo_reduce = weight_reduce(1, 3 * half, half)

    def across(k):
        return remote(staged.at[k % 2], landed.at[k], c_send.at[k], c_recv.at[k], ways.to_c)

    def swapped(k):
        across(k).wait_recv()

        def body(i, carry):
            rows = pl.ds(pl.multiple_of(i * chip_rows, 16), chip_rows)
            accumulate(part.at[rows, pl.ds(k * half, half)], [landed.at[k, rows]])
            return carry

        lax.fori_loop(0, width // chip_rows, body, 0)

    later = []

    def service(n=1):
        for _ in range(n):
            if later:
                later.pop(0)()

    def columns(core):
        return pl.ds(pl.multiple_of(core * half, 128), half)

    def weight_grad(k, left, right):
        if k < 2:
            across(k + 2).wait_send()
        staged[k % 2] = dot_tn(left, right[:, columns(oc)]).astype(bf16)
        across(k).start()
        part[:, pl.ds(k * half, half)] = dot_tn(left, right[:, columns(c)]).astype(bf16)

    o_events[1]()
    weight_grad(3, attended[...], low)
    for copy in wo_loads:
        copy.wait()
    datt[...] = (
        dot_nt(low[:, 0:half], part[:, 0:half]) + dot_nt(low[:, half:width], part[:, half:width])
    ).astype(bf16)
    wo_events = wo_reduce.events()
    later.append(lambda: swapped(3))
    for k in range(6):
        later.append(o_events[k + 2])
        later.extend(wo_events[:2] if k == 0 else [wo_events[k + 1]])
    for copy in kv_loads:
        copy.wait()

    own_rows = pl.ds(pl.multiple_of((b * 2 + c) * count, count), count)
    for h in range(heads):
        cols = pl.ds(h * 128, 128)
        key, val, query = dk[:, cols], dv[:, cols], q[:, cols]
        probs = softmax_rows(dot_nt(query, key) * scale + bias[...])
        dprobs = dot_nt(datt[:, cols], val)
        dscores = (
            probs * (dprobs - jnp.sum(probs * dprobs, axis=-1, keepdims=True))
        ).astype(bf16)
        dq[:, cols] = turn(
            dense_dot(dscores, key) * scale, cosine[own_rows, :], -sine[own_rows, :]
        ).astype(bf16)
        dk[:, cols] = turn(dot_tn(dscores, query) * scale, cosine[...], -sine[...]).astype(bf16)
        dv[:, cols] = dot_tn(probs.astype(bf16), datt[:, cols]).astype(bf16)
        if h in (1, 3, 4, 6, 8, 9):
            service()
    weight_grad(2, normed[...], dv)
    weight_grad(1, normed[...], dk)
    service()
    weight_grad(0, normed[own_rows, :], dq)
    for k in (2, 1, 0):
        swapped(k)
    qkv_events = qkv_reduce.events()
    qkv_events[0]()
    later = [later[0], later[1], qkv_events[1]] + later[2:]

    for copy in wall_loads:
        copy.wait()
    for t in range(4):
        rows = slice(t * count, (t + 1) * count)
        total = jnp.zeros((count, width), f32)
        for h in range(2):
            mine = slice(h * half, (h + 1) * half)
            total = total + dot_nt(dk[rows, mine], weight(h, 1)) + dot_nt(dv[rows, mine], weight(h, 2))
        dn_part[t] = total.astype(bf16)
        x = group[t].astype(f32)
        unit = x * lax.rsqrt(jnp.mean(x * x, axis=-1, keepdims=True) + epsilon)
        gain_row = jnp.sum(total * unit, axis=0, keepdims=True)
        if t == 0:
            rows_t[experts : experts + 1, :] = gain_row
        else:
            rows_t[experts : experts + 1, :] += gain_row
        service()

    def dn_copy(k, src, dst, to):
        return remote(src, dst, d_send.at[k], d_recv.at[k], to)

    dn_copies = [
        dn_copy(0, dn_part.at[b * 2 + oc], dn_other.at[0], ways.to_c),
        dn_copy(1, dn_part.at[ob * 2 + oc], dn_other.at[1], ways.to_c),
    ]
    for copy in dn_copies:
        copy.start()
    own = jnp.zeros((count, width), f32)
    for h in range(2):
        own = own + dot_nt(dq[:, h * half : (h + 1) * half], weight(h, 0))
    x = group[b * 2 + c].astype(f32)
    r1 = lax.rsqrt(jnp.mean(x * x, axis=-1, keepdims=True) + epsilon)
    unit_one = x * r1
    rows_t[experts : experts + 1, :] += jnp.sum(own * unit_one, axis=0, keepdims=True)
    s_part[...] = jnp.transpose(rows_t[...]).astype(bf16)
    small_swap = remote(s_part, s_landed, c_send.at[4], c_recv.at[4], ways.to_c)
    small_swap.start()
    service()
    dn_copies[1].wait_recv()
    accumulate(dn_part.at[ob * 2 + c], [dn_other.at[1]])
    dn_copies.append(dn_copy(2, dn_part.at[ob * 2 + c], dn_far, ways.to_b))
    dn_copies[2].start()
    dn_copies[0].wait_recv()
    small_swap.wait()
    accumulate(s_part, [s_landed])
    service(len(later))
    small_events = small_reduce.events()
    for k in range(2, len(qkv_events)):
        later.extend([small_events[k - 2], qkv_events[k]])
    later.extend(small_events[-2:])
    service(4)
    dn_copies[2].wait_recv()
    total = (
        own
        + dn_part[b * 2 + c].astype(f32)
        + dn_other[0].astype(f32)
        + dn_far[...].astype(f32)
    )
    scaled = total * gain_one
    input_grad[...] = grads[...] + r1 * (
        scaled - unit_one * jnp.mean(scaled * unit_one, axis=-1, keepdims=True)
    )
    service(len(later))

    theirs = pl.ds(pl.multiple_of(oc * d_rows, 8), d_rows)
    mine = pl.ds(pl.multiple_of(c * d_rows, 8), d_rows)
    fin[:, pl.ds(3 * half, half)] = wo_reduce.total()
    fin[:, pl.ds(0, 3 * half)] = qkv_reduce.total()
    fin_copy = remote(fin.at[theirs], fin_other, c_send.at[5], c_recv.at[5], ways.to_c)
    fin_copy.start()
    s_total = small_reduce.total()
    small_out[...] = jnp.where(c == 0, s_total[:d_rows], s_total[d_rows:])
    for k, out in enumerate((gq, gk, gv, go)):
        out[:, columns(c)] = fin[mine, pl.ds(k * half, half)]
    fin_copy.wait_recv()
    for k, out in enumerate((gq, gk, gv, go)):
        out[:, columns(oc)] = fin_other[:, pl.ds(k * half, half)]
    for r in (qkv_reduce, wo_reduce, small_reduce, o_reduce):
        r.drain()
    for copy in dn_copies + [fin_copy]:
        copy.wait_send()
    dw_copy.wait()
    for k in range(2):
        across(k).wait_send()


def back_call(
    lengths, dn2, residual, cot, group, small_t, router_part, attended, q, normed, cosine, sine,
    keys, vals, wall, outs, dw_sib, d_rows, experts, scale, collective_id,
):
    lines = lax.axis_size("ep") // 2
    count, width = cot.shape
    half = width // 2
    chip_rows = 2 * d_rows
    group_len = 4 * count
    anywhere = pl.BlockSpec(memory_space=pl.ANY)
    vmem = pl.BlockSpec(memory_space=pltpu.VMEM)
    smem = pl.BlockSpec(memory_space=pltpu.SMEM)
    shape = jax.ShapeDtypeStruct
    dma = pltpu.SemaphoreType.DMA

    def landing(rows, cols):
        return [pltpu.VMEM((n, rows, cols), bf16) for n in (lines, lines, lines, 2, lines - 1)]

    return pl.pallas_call(
        functools.partial(back_kernel, lines, experts, scale),
        out_shape=(
            shape((count, width), bf16),
            shape((count, width), f32),
            shape((d_rows, width), f32),
            shape((d_rows, width), f32),
            shape((d_rows, width), f32),
            shape((d_rows, width), f32),
            shape((d_rows, 128), f32),
            shape(dw_sib.shape, f32),
        ),
        in_specs=[smem] + [vmem] * 11 + [anywhere] * 5,
        out_specs=(vmem,) * 7 + (anywhere,),
        scratch_shapes=[
            pltpu.VMEM((width, 6 * half), bf16),
            pltpu.VMEM((width, 4 * half), bf16),
            pltpu.VMEM((2, width, half), bf16),
            pltpu.VMEM((4, width, half), bf16),
            *landing(chip_rows, 4 * half),
            pltpu.VMEM((chip_rows, 4 * half), f32),
            pltpu.VMEM((d_rows, 4 * half), f32),
            pltpu.VMEM((width, 128), bf16),
            pltpu.VMEM((width, 128), bf16),
            *landing(chip_rows, 128),
            pltpu.VMEM(outs.shape, bf16),
            *landing(count, width),
            pltpu.VMEM((count, width), f32),
            pltpu.VMEM((count, width), bf16),
            pltpu.VMEM((count, width), bf16),
            pltpu.VMEM((count, width), bf16),
            pltpu.VMEM((group_len, width), bf16),
            pltpu.VMEM((group_len, width), bf16),
            pltpu.VMEM((4, count, width), bf16),
            pltpu.VMEM((2, count, width), bf16),
            pltpu.VMEM((count, width), bf16),
            pltpu.VMEM((count, group_len), f32),
            pltpu.VMEM((128, width), f32),
            dma((7,)),
            dma((7,)),
            dma((4, 8 * lines)),
            dma((4, 8 * lines)),
            dma((3,)),
            dma((3,)),
            dma((7,)),
        ],
        compiler_params=pltpu.CompilerParams(
            collective_id=collective_id, has_side_effects=True, vmem_limit_bytes=63 * 2**20
        ),
        name="back",
    )(
        lengths, dn2, residual, cot, group, small_t, router_part, attended, q, normed, cosine, sine,
        keys, vals, wall, outs, dw_sib,
    )


def documents(positions, lengths):
    seq_ends = jnp.cumsum(lengths)
    doc_index = (positions >= seq_ends[0]).astype(jnp.int32) + (positions >= seq_ends[1]).astype(
        jnp.int32
    )
    seq_starts = jnp.where(doc_index == 0, 0, jnp.where(doc_index == 1, seq_ends[0], seq_ends[1]))
    return (doc_index, positions - seq_starts)


def rotary_tables(offsets, head_dim):
    half_dim = head_dim // 2
    frequency = 10000.0 ** (-2.0 * jnp.arange(half_dim, dtype=f32) / head_dim)
    angles = offsets.astype(f32)[:, None] * frequency[None, :]
    return (jnp.cos(angles)[:, None, :], jnp.sin(angles)[:, None, :])


def rotate(values, cosine, sine_table):
    half_dim = values.shape[-1] // 2
    first_half = values[..., :half_dim]
    second_half = values[..., half_dim:]
    return jnp.concatenate(
        [
            first_half * cosine - second_half * sine_table,
            first_half * sine_table + second_half * cosine,
        ],
        axis=-1,
    )


def norm_back(grad_normed, unit_rows, inverse, gain):
    scaled = grad_normed * gain
    return inverse * (scaled - unit_rows * jnp.mean(scaled * unit_rows, axis=-1, keepdims=True))


def dot(left, right, contract):
    return lax.dot_general(left, right, ((contract[0], contract[1]), ((), ())), preferred_element_type=f32)


def dense_dot(left, right):
    return dot(left, right, ((1,), (0,)))


def dot_nt(left, right):
    return dot(left, right, ((1,), (1,)))


def dot_tn(left, right):
    return dot(left, right, ((0,), (0,)))


def any_slice(
    hidden_in,
    seq_lengths,
    expert_ids,
    attn_gain,
    w_query,
    w_key,
    w_value,
    w_out,
    ffn_gain,
    shared_gate,
    shared_up,
    shared_down,
    router,
    expert_gate,
    expert_up,
    expert_down,
    cotangent,
):
    tok_count, model_width = hidden_in.shape
    eps, tps = lax.axis_size("ep"), lax.axis_size("tp")
    devices = eps * tps
    exp_local, exp_hidden = expert_gate.shape[:2]
    experts = exp_local * eps
    group_len = tps * tok_count
    tokens = devices * tok_count
    d_rows = w_query.shape[0]
    width = w_query.shape[1]
    sh_rows = shared_down.shape[0]
    head_dim = width // HEADS
    attn_scale = head_dim ** (-0.5)

    flat = jnp.concatenate([router.reshape(-1), attn_gain, ffn_gain])
    small_len = -(-flat.shape[0] // model_width) * model_width
    small = jnp.pad(flat, (0, small_len - flat.shape[0])).reshape(-1, model_width)
    small = jnp.pad(small, ((0, -small.shape[0] % 16), (0, 0)))
    weights = jnp.concatenate([w_query, w_key, w_value, w_out], axis=1)

    all_weights, all_small, all_cot = [
        lax.all_gather(v, AXES, axis=0) for v in (weights, small, cotangent)
    ]
    group_hidden = lax.all_gather(hidden_in, "tp", axis=0)
    all_weights = all_weights.reshape(devices * d_rows, 4 * width)
    full_query = all_weights[:, :width]
    full_key = all_weights[:, width : 2 * width]
    full_value = all_weights[:, 2 * width : 3 * width]
    full_out = all_weights[:, 3 * width :]
    all_small = all_small.reshape(devices, -1)
    n_router = d_rows * experts
    full_router = all_small[:, :n_router].reshape(devices * d_rows, experts)
    gain_one = all_small[:, n_router : n_router + d_rows].reshape(-1).astype(f32)
    gain_two = all_small[:, n_router + d_rows : n_router + 2 * d_rows].reshape(-1).astype(f32)
    cot_all = all_cot.reshape(-1, model_width)

    shared_cols = jnp.stack([shared_gate, shared_up], axis=1).reshape(d_rows, 2, devices, sh_rows)
    shared_cols = lax.all_to_all(
        shared_cols.transpose(2, 1, 3, 0), AXES, split_axis=0, concat_axis=0, tiled=True
    )
    shared_t = shared_cols.transpose(1, 2, 0, 3).reshape(2, sh_rows, model_width)

    lengths = seq_lengths[0]
    tp_index = lax.axis_index("tp")
    own_pos = tp_index * tok_count + jnp.arange(tok_count, dtype=jnp.int32)
    all_pos = jnp.arange(group_len, dtype=jnp.int32)
    own_doc, own_offset = documents(own_pos, lengths)
    all_doc, all_offset = documents(all_pos, lengths)
    allowed = (own_doc[:, None] == all_doc[None, :]) & (own_pos[:, None] >= all_pos[None, :])
    cosine, sine_table = rotary_tables(own_offset, head_dim)
    cosine_all, sine_all = rotary_tables(all_offset, head_dim)

    inputs = hidden_in.astype(f32)
    inverse_one = lax.rsqrt(jnp.mean(inputs * inputs, axis=-1, keepdims=True) + epsilon)
    unit_one = inputs * inverse_one
    normed = (unit_one * gain_one).astype(bf16)
    group_in = group_hidden.reshape(group_len, model_width).astype(f32)
    group_unit = group_in * lax.rsqrt(jnp.mean(group_in * group_in, axis=-1, keepdims=True) + epsilon)
    group_normed = (group_unit * gain_one).astype(bf16)

    queries = rotate(
        dense_dot(normed, full_query).reshape(tok_count, HEADS, head_dim), cosine, sine_table
    ).astype(bf16)
    key_rows = rotate(
        dense_dot(group_normed, full_key).reshape(group_len, HEADS, head_dim), cosine_all, sine_all
    ).astype(bf16)
    value_rows = dense_dot(group_normed, full_value).astype(bf16).reshape(group_len, HEADS, head_dim)

    def masked_scores():
        raw_scores = (
            jnp.einsum("qhd,khd->hqk", queries, key_rows, preferred_element_type=f32) * attn_scale
        )
        return jnp.where(allowed[None], raw_scores, -1e30)

    scores = masked_scores()
    row_peak = jnp.max(scores, axis=-1, keepdims=True)
    row_total = jnp.sum(jnp.exp(scores - row_peak), axis=-1, keepdims=True)
    softmaxed = jnp.exp(scores - row_peak) / row_total
    attended = (
        jnp.einsum("hqk,khd->qhd", softmaxed.astype(bf16), value_rows, preferred_element_type=f32)
        .reshape(tok_count, width)
        .astype(bf16)
    )
    residual = inputs + dense_dot(attended, full_out)
    inverse_two = lax.rsqrt(jnp.mean(residual * residual, axis=-1, keepdims=True) + epsilon)
    unit_two = residual * inverse_two
    normed_two = (unit_two * gain_two).astype(bf16)

    affinity = jax.nn.softmax(dense_dot(normed_two, full_router), axis=-1)
    expert_range = jnp.arange(experts, dtype=jnp.int32)
    named = jnp.any(expert_ids[:, :, None] == expert_range[None, None, :], axis=1)
    signed = jnp.where(named, affinity, -affinity)

    first_expert = lax.axis_index("ep") * exp_local
    n_routed = exp_local * exp_hidden
    hidden = n_routed + sh_rows
    gate_w = jnp.concatenate([expert_gate.reshape(n_routed, model_width), shared_t[0]])
    up_w = jnp.concatenate([expert_up.reshape(n_routed, model_width), shared_t[1]])
    down_w = jnp.concatenate([expert_down.reshape(n_routed, model_width), shared_down])

    def mixture(rows, cot_rows, signed):
        count = rows.shape[0]
        mine = lax.dynamic_slice_in_dim(signed, first_expert, exp_local, axis=1)
        mine_named = mine > 0
        gates = jnp.where(mine_named, mine, 0.0)
        scale = jnp.concatenate(
            [jnp.repeat(gates, exp_hidden, axis=1), jnp.ones((count, sh_rows), f32)], axis=1
        )
        gate_pre = dot_nt(rows, gate_w)
        up_pre = dot_nt(rows, up_w)
        sigma = jax.nn.sigmoid(gate_pre)
        silu = gate_pre * sigma
        act = silu * up_pre
        act_scaled = (act * scale).astype(bf16)
        out_part = dense_dot(act_scaled, down_w).astype(bf16)
        grad_hidden = dot_nt(cot_rows, down_w)
        grad_gates = jnp.sum(
            (act * grad_hidden)[:, :n_routed].reshape(count, exp_local, exp_hidden), axis=-1
        )
        grad_gates = jnp.where(mine_named, grad_gates, 0.0)
        grad_hidden = grad_hidden * scale
        grad_gate_pre = (grad_hidden * up_pre * sigma * (1.0 + gate_pre * (1.0 - sigma))).astype(
            bf16
        )
        grad_up_pre = (grad_hidden * silu).astype(bf16)
        affinity_all = jnp.abs(signed)
        grad_aff = lax.dynamic_update_slice_in_dim(
            jnp.zeros((count, experts), f32), grad_gates, first_expert, axis=1
        )
        grad_logits = (
            affinity_all * (grad_aff - jnp.sum(affinity_all * grad_aff, axis=-1, keepdims=True))
        ).astype(bf16)
        dn2_part = (
            dense_dot(grad_gate_pre, gate_w)
            + dense_dot(grad_up_pre, up_w)
            + dot_nt(grad_logits, full_router)
        ).astype(bf16)
        sums = (
            dot_tn(act_scaled, cot_rows),
            dot_tn(grad_gate_pre, rows),
            dot_tn(grad_up_pre, rows),
            dot_tn(rows, grad_logits),
        )
        return out_part, dn2_part, sums

    rows, signed_all = [lax.all_gather(v, AXES, axis=0, tiled=True) for v in (normed_two, signed)]
    blocks = max(1, tokens * hidden * 4 // 2**23)
    while tokens % blocks:
        blocks += 1

    def step(totals, block):
        out_block, dn2_block, sums = mixture(*block)
        return jax.tree.map(jnp.add, totals, sums), (out_block, dn2_block)

    zeros = (jnp.zeros((hidden, model_width), f32),) * 3 + (
        jnp.zeros((model_width, experts), f32),
    )
    sums, (out_part, dn2_part) = lax.scan(
        step,
        zeros,
        jax.tree.map(
            lambda v: v.reshape((blocks, -1) + v.shape[1:]), (rows, cot_all, signed_all)
        ),
    )
    grad_down, grad_gate, grad_up, router_part = sums
    routed_sum, grad_normed_two = [
        lax.psum_scatter(v.reshape(tokens, model_width), AXES, tiled=True).astype(f32)
        for v in (out_part, dn2_part)
    ]
    layer_output = (residual + routed_sum).astype(bf16)

    gain_two_part = jnp.sum(grad_normed_two * unit_two, axis=0)
    grad_resid = cotangent.astype(f32) + norm_back(grad_normed_two, unit_two, inverse_two, gain_two)
    grad_resid_low = grad_resid.astype(bf16)
    wout_part = dot_tn(attended, grad_resid_low)
    grad_att = dot_nt(grad_resid_low, full_out).astype(bf16).reshape(tok_count, HEADS, head_dim)
    softmax_again = jnp.exp(masked_scores() - row_peak) / row_total
    grad_soft = jnp.einsum("qhd,khd->hqk", grad_att, value_rows, preferred_element_type=f32)
    grad_scores = (
        softmax_again * (grad_soft - jnp.sum(softmax_again * grad_soft, axis=-1, keepdims=True))
    ).astype(bf16)
    grad_queries = (
        jnp.einsum("hqk,khd->qhd", grad_scores, key_rows, preferred_element_type=f32) * attn_scale
    )
    grad_key_rows = (
        jnp.einsum("hqk,qhd->khd", grad_scores, queries, preferred_element_type=f32) * attn_scale
    )
    grad_value_rows = jnp.einsum(
        "hqk,qhd->khd", softmax_again.astype(bf16), grad_att, preferred_element_type=f32
    )
    grad_q_pre = rotate(grad_queries, cosine, -sine_table).reshape(tok_count, width).astype(bf16)
    grad_k_pre = rotate(grad_key_rows, cosine_all, -sine_all).reshape(group_len, width).astype(bf16)
    grad_v_pre = grad_value_rows.reshape(group_len, width).astype(bf16)
    wq_part = dot_tn(normed, grad_q_pre)
    wk_part = dot_tn(group_normed, grad_k_pre)
    wv_part = dot_tn(group_normed, grad_v_pre)
    own_normed_grad = dot_nt(grad_q_pre, full_query)
    group_normed_grad = dot_nt(grad_k_pre, full_key) + dot_nt(grad_v_pre, full_value)
    gain_one_part = jnp.sum(own_normed_grad * unit_one, axis=0) + jnp.sum(
        group_normed_grad * group_unit, axis=0
    )

    weight_part = jnp.concatenate([wq_part, wk_part, wv_part, wout_part], axis=1).astype(bf16)
    small_part = jnp.concatenate(
        [
            router_part.reshape(devices, n_router),
            gain_one_part.reshape(devices, d_rows),
            gain_two_part.reshape(devices, d_rows),
        ],
        axis=1,
    )
    small_part = jnp.pad(small_part, ((0, 0), (0, small_len - small_part.shape[1])))
    small_part = small_part.reshape(devices, -1, model_width)
    small_part = jnp.pad(small_part, ((0, 0), (0, -small_part.shape[1] % 16), (0, 0))).astype(bf16)
    weight_part = weight_part.reshape(devices, d_rows, 4 * width)
    group_part = group_normed_grad.astype(bf16).reshape(tps, tok_count, model_width)
    weight_sum, small_sum = [
        lax.psum_scatter(v, AXES).astype(f32) for v in (weight_part, small_part)
    ]
    normed_grad_sum = lax.psum_scatter(group_part, "tp").astype(f32)
    grad_normed = own_normed_grad + normed_grad_sum
    input_grad = grad_resid + norm_back(grad_normed, unit_one, inverse_one, gain_one)
    small_sum = small_sum.reshape(-1)

    shared_back = jnp.stack([grad_gate[n_routed:], grad_up[n_routed:]])
    shared_back = shared_back.reshape(2, sh_rows, devices, d_rows).transpose(2, 0, 1, 3)
    shared_back = lax.all_to_all(shared_back, AXES, split_axis=0, concat_axis=0, tiled=True)
    shared_back = shared_back.transpose(1, 3, 0, 2).reshape(2, d_rows, devices * sh_rows)

    return (
        layer_output,
        input_grad,
        small_sum[n_router : n_router + d_rows],
        weight_sum[:, :width],
        weight_sum[:, width : 2 * width],
        weight_sum[:, 2 * width : 3 * width],
        weight_sum[:, 3 * width :],
        small_sum[n_router + d_rows : n_router + 2 * d_rows],
        shared_back[0],
        shared_back[1],
        grad_down[n_routed:],
        small_sum[:n_router].reshape(d_rows, experts),
        grad_gate[:n_routed].reshape(expert_gate.shape),
        grad_up[:n_routed].reshape(expert_up.shape),
        grad_down[:n_routed].reshape(expert_down.shape),
    )


def small_slice(
    hidden_in,
    seq_lengths,
    expert_ids,
    attn_gain,
    w_query,
    w_key,
    w_value,
    w_out,
    ffn_gain,
    shared_gate,
    shared_up,
    shared_down,
    router,
    expert_gate,
    expert_up,
    expert_down,
    cotangent,
):
    tok_count, model_width = hidden_in.shape
    eps, tps = lax.axis_size("ep"), lax.axis_size("tp")
    devices = eps * tps
    exp_local, exp_hidden = expert_gate.shape[:2]
    experts = exp_local * eps
    group_len = tps * tok_count
    tokens = devices * tok_count
    d_rows = w_query.shape[0]
    width = w_query.shape[1]
    sh_rows = shared_down.shape[0]
    head_dim = width // HEADS
    attn_scale = head_dim ** (-0.5)

    lanes = 128
    vectors = jnp.stack([attn_gain, ffn_gain], axis=1)
    small = jnp.concatenate([router, vectors], axis=1)
    small = jnp.pad(small, ((0, 0), (0, lanes - small.shape[1])))
    (
        w_all, cot_all, normed_two, aux, small_t, residual, attended, queries, key_rows, value_rows,
        group_normed, cos_all, sin_all, group_hidden,
    ) = front_call(
        seq_lengths, expert_ids, hidden_in, small, w_query, w_key, w_value, w_out, cotangent,
        experts, attn_scale, 0,
    )
    shared_cols = jnp.stack([shared_gate, shared_up], axis=1).reshape(d_rows, 2, devices, sh_rows)
    shared_cols = lax.all_to_all(
        shared_cols.transpose(2, 1, 3, 0), AXES, split_axis=0, concat_axis=0, tiled=True
    )
    shared_t = shared_cols.transpose(1, 2, 0, 3).reshape(2, sh_rows, model_width)

    first_expert = lax.axis_index("ep") * exp_local
    n_routed = exp_local * exp_hidden
    hidden = n_routed + sh_rows
    gate_w = jnp.concatenate([expert_gate.reshape(n_routed, model_width), shared_t[0]])
    up_w = jnp.concatenate([expert_up.reshape(n_routed, model_width), shared_t[1]])
    down_w = jnp.concatenate([expert_down.reshape(n_routed, model_width), shared_down])

    h_core = -(-hidden // lanes) * lanes
    pad = ((0, h_core - hidden), (0, 0))
    owner = jnp.arange(h_core, dtype=jnp.int32)
    owner = jnp.where(owner < n_routed, first_expert + owner // exp_hidden, experts)
    owner = jnp.concatenate([owner, owner])
    sel_t = (owner[:, None] == jnp.arange(lanes, dtype=jnp.int32)[None, :]).astype(bf16)
    sel = jnp.concatenate([sel_t[:, :experts].T, jnp.eye(experts, lanes, dtype=bf16)], axis=1)
    sel = jnp.concatenate([sel, sel])
    ones = (jnp.arange(2 * h_core, dtype=jnp.int32) % h_core)[None, :]
    ones = ((ones >= n_routed) & (ones < hidden)).astype(f32)
    token_grads, out_parts, grads_here, grads_away, router_sum = mixture_call(
        normed_two,
        aux,
        cot_all,
        [jnp.pad(w, pad) for w in (gate_w, up_w, down_w)],
        sel,
        sel_t,
        small_t,
        ones,
        2,
    )
    layer_output, input_grad, grad_q, grad_k, grad_v, grad_o, small_sum, grads_there = back_call(
        seq_lengths, token_grads, residual, cotangent, group_hidden, small_t, router_sum, attended,
        queries, group_normed, cos_all, sin_all, key_rows, value_rows, w_all, out_parts,
        grads_away, d_rows, experts, attn_scale, 3,
    )
    grad_gate, grad_up, grad_down = [(grads_here[k] + grads_there[k])[:hidden] for k in range(3)]

    shared_back = jnp.stack([grad_gate[n_routed:], grad_up[n_routed:]])
    shared_back = shared_back.reshape(2, sh_rows, devices, d_rows).transpose(2, 0, 1, 3)
    shared_back = lax.all_to_all(shared_back, AXES, split_axis=0, concat_axis=0, tiled=True)
    shared_back = shared_back.transpose(1, 3, 0, 2).reshape(2, d_rows, devices * sh_rows)

    return (
        layer_output,
        input_grad,
        small_sum[:, experts],
        grad_q,
        grad_k,
        grad_v,
        grad_o,
        small_sum[:, experts + 1],
        shared_back[0],
        shared_back[1],
        grad_down[n_routed:],
        small_sum[:, :experts],
        grad_gate[:n_routed].reshape(expert_gate.shape),
        grad_up[:n_routed].reshape(expert_up.shape),
        grad_down[:n_routed].reshape(expert_down.shape),
    )


def solution(mesh):
    rows = P(AXES, None)
    vector = P(AXES)
    experts = P("ep", "tp", None)
    small = mesh.shape["ep"] == 8 and mesh.shape["tp"] == 4
    return jax.shard_map(
        small_slice if small else any_slice,
        mesh=mesh,
        in_specs=(
            rows, P("ep", None), rows, vector, rows, rows, rows, rows, vector,
            rows, rows, rows, rows, experts, experts, experts, rows,
        ),
        out_specs=(
            rows, rows, vector, rows, rows, rows, rows, vector,
            rows, rows, rows, rows, experts, experts, experts,
        ),
        check_vma=False,
    )
```

```python
import functools

import jax
import jax.numpy as jnp
from jax import lax
from jax.experimental import pallas as pl
from jax.experimental.pallas import tpu as pltpu
from jax.sharding import PartitionSpec as P

HEADS = 10
AXES = ("ep", "tp")
MESH = pl.DeviceIdType.MESH
VMEM_BUDGET = 56 * 2**20

epsilon = 1e-06

bf16 = jnp.bfloat16
f32 = jnp.float32


def place():
    ep, tp = lax.axis_index("ep"), lax.axis_index("tp")
    return ep // 2, ep % 2, tp // 2, tp % 2


def device(line, a, b, c):
    return (line * 2 + a, b * 2 + c)


def number(line, a, b, c):
    return ((line * 2 + a) * 2 + b) * 2 + c


def greet(partners):
    barrier = pltpu.get_barrier_semaphore()
    for partner in partners:
        pl.semaphore_signal(barrier, inc=1, device_id=partner, device_id_type=MESH)
    pl.semaphore_wait(barrier, len(partners))


O, X, Y, D = 0, 1, 2, 3


def visit_order(lines):
    return [
        sorted(range(lines), key=lambda other: (abs(other - z), other != z ^ 1)) for z in range(lines)
    ]


def lookup(table, index):
    out = jnp.int32(table[0])
    for k in range(1, len(table)):
        out = jnp.where(index == k, jnp.int32(table[k]), out)
    return out


def pick(values, index):
    out = values[0]
    for k in range(1, len(values)):
        out = jnp.where(index == k, values[k], out)
    return out


class Ways:
    def __init__(self, lines):
        self.lines = lines
        z, a, b, c = self.spot = place()
        oa, ob, oc = 1 - a, 1 - b, 1 - c
        self.to_b, self.to_a = device(z, a, ob, c), device(z, oa, b, c)
        self.to_c = device(z, a, b, oc)
        self.up_next = device(lax.rem(z + 1, lines), a, b, c)
        self.down_next = device(lax.rem(z + lines - 1, lines), a, b, c)
        self.peers = [device(lax.rem(z + s, lines), a, b, c) for s in range(1, lines)]
        table = visit_order(lines)
        self.zs = [lookup([table[k][u] for k in range(lines)], z) for u in range(lines)]
        self.column = ((a, b), (a, ob), (oa, b), (oa, ob))
        self.pair = device(z + 1 - 2 * lax.rem(z, 2), a, b, c)
        outer = (z == 0) | (z == lines - 1)
        self.carried = [True, False, outer, jnp.logical_not(outer)]

    def greet(self):
        greet([self.to_b, self.to_a, self.to_c] + self.peers)

    def chip(self, line, kind):
        a, b = self.column[kind]
        return (line * 2 + a) * 2 + b


def when(condition, act):
    if condition is True:
        act()
    elif condition is not False:

        @pl.when(condition)
        def _():
            act()


def other(condition):
    return not condition if isinstance(condition, bool) else jnp.logical_not(condition)


def remote(src, dst, send_sem, recv_sem, to):
    return pltpu.make_async_remote_copy(
        src, dst, send_sem, recv_sem, device_id=to, device_id_type=MESH
    )


class Gather:
    def __init__(self, ways, chunk, sems, own=None, relative=False, across=False):
        self.ways, self.chunk, self.own = ways, chunk, own
        self.send_sem, self.recv_sem = sems
        self.relative, self.across_core = relative, across

    def copy(self, slot, step, src, dst, to):
        k = slot * self.ways.lines + step
        return remote(src, dst, self.send_sem(k), self.recv_sem(k), to)

    def hop(self, slot, step, kind, to_kind, line, to, part=None, own=False):
        src = self.own if own and self.own is not None else self.chunk(line, kind, part, False)
        dst = self.chunk(line, to_kind if self.relative else kind, part, False)
        return self.copy(slot, step, src, dst, to)

    def sends(self, u):
        w, own = self.ways, u == 0
        line, carried = w.zs[u], w.carried[u]
        copies = {
            "X": (True, lambda: self.hop(0, u, O, X, line, w.to_b, own=own)),
            "Y": (True, lambda: self.hop(1, u, O, Y, line, w.to_a, own=own)),
            "p": (carried, lambda: self.hop(2, u, X, D, line, w.to_a, 0)),
            "q": (carried, lambda: self.hop(3, u, Y, D, line, w.to_b, 1)),
            "pair": (carried, lambda: self.hop(11, 1 if own else u, D, D, line, w.pair)),
        }
        if self.across_core:

            def across(slot, kind):
                here = self.chunk(line, kind, None, False)
                src = self.own if kind == O and own and self.own is not None else here
                return self.copy(slot, u, src, here, w.to_c)

            for kind, slot in ((O, 6), (X, 7), (Y, 8), (D, 9)):
                copies[kind] = (True, lambda slot=slot, kind=kind: across(slot, kind))
        return copies

    def send(self, u, *names, condition=True):
        copies = self.sends(u)
        for name in names:
            if name in copies:
                always, make = copies[name]
                when(always if condition is True else condition, lambda: make().start())

    def arrival(self, slot, step, kind, line, part=None, other=False):
        here = self.chunk(line, kind, part, other)
        self.copy(slot, step, here, here, self.ways.to_c).wait_recv()

    def send_own(self, u):
        self.send(u, "X", "Y", O)

    def xy_event(self, u):
        line = self.ways.zs[u]
        self.arrival(0, u, X, line)
        self.send(u, "p")
        self.arrival(1, u, Y, line)
        self.send(u, "q", X, Y)

    def diag_carried(self, u):
        line, carried = self.ways.zs[u], self.ways.carried[u]

        def halves():
            self.arrival(2, u, D, line, 0)
            self.arrival(3, u, D, line, 1)

        when(carried, halves)
        self.send(u, "pair")
        self.send(u, D, condition=carried)

    def diag_handed(self, u):
        handed = other(self.ways.carried[u])
        when(handed, lambda: self.arrival(11, u, D, self.ways.zs[u]))
        self.send(u, D, condition=handed)

    def chain_up(self, k):
        w = self.ways
        return self.hop(4, k, O, O, w.spot[0] - (k - 1), w.up_next, own=k == 1)

    def chain_down(self, k):
        w = self.ways
        return self.hop(5, k, O, O, w.spot[0] + (k - 1), w.down_next, own=k == 1)

    def chain_start(self, k):
        z, lines = self.ways.spot[0], self.ways.lines
        if k >= lines:
            return

        @pl.when((z >= k - 1) & (z + 1 < lines))
        def _():
            self.chain_up(k).start()

        @pl.when((z + k - 1 < lines) & (z > 0))
        def _():
            self.chain_down(k).start()

    def chain_event(self, k):
        z, lines = self.ways.spot[0], self.ways.lines

        @pl.when(z >= k)
        def _():
            self.arrival(4, k, O, z - k)

        @pl.when(z + k < lines)
        def _():
            self.arrival(5, k, O, z + k)

        self.chain_start(k + 1)

    def begin(self):
        self.send_own(0)
        self.chain_start(1)

    def events(self):
        out = [
            lambda: (self.xy_event(0), self.chain_event(1), self.send_own(1)),
            lambda: (self.diag_carried(0), self.chain_event(2), self.send_own(2)),
            lambda: (self.xy_event(1), self.chain_event(3), self.send_own(3)),
            lambda: (self.xy_event(2), self.diag_handed(1)),
            lambda: (self.diag_carried(2), self.xy_event(3)),
            lambda: (self.diag_carried(3), self.diag_handed(2)),
            lambda: self.diag_handed(3),
        ]
        return out

    def other_core(self):
        if self.across_core:
            for u in range(self.ways.lines):
                for slot, kind in ((6, O), (7, X), (8, Y), (9, D)):
                    self.arrival(slot, u, kind, self.ways.zs[u], None, True)

    def drain_unit(self, u):
        for condition, make in self.sends(u).values():
            when(condition, lambda make=make: make().wait_send())

    def drain_chain(self, k):
        z, lines = self.ways.spot[0], self.ways.lines

        @pl.when((z >= k - 1) & (z + 1 < lines))
        def _():
            self.chain_up(k).wait_send()

        @pl.when((z + k - 1 < lines) & (z > 0))
        def _():
            self.chain_down(k).wait_send()

    def drain(self, units=None):
        for u in range(self.ways.lines if units is None else units):
            self.drain_unit(u)
        for k in range(1, self.ways.lines):
            self.drain_chain(k)


class Exchange:
    def __init__(self, ways, blocks, r1, r2, r3, got, sems):
        self.ways, self.blocks, self.r1, self.r2, self.r3, self.got = ways, blocks, r1, r2, r3, got
        self.send_sem, self.recv_sem = sems

    def copy(self, k, src, dst, to):
        return remote(src, dst, self.send_sem(k), self.recv_sem(k), to)

    def over_core(self):
        w = self.ways
        oc = 1 - w.spot[3]
        return [self.copy(0, self.blocks.at[:, :, :, oc], self.r1, w.to_c)]

    def over_b(self):
        w = self.ways
        z, a, b, c = w.spot
        sources = (self.blocks.at[:, :, 1 - b, c], self.r1.at[:, :, 1 - b])
        return [self.copy(1 + k, src, self.r2.at[k], w.to_b) for k, src in enumerate(sources)]

    def over_a(self):
        w = self.ways
        z, a, b, c = w.spot
        oa = 1 - a
        sources = (
            self.blocks.at[:, oa, b, c], self.r1.at[:, oa, b], self.r2.at[0, :, oa], self.r2.at[1, :, oa],
        )
        return [self.copy(3 + k, src, self.r3.at[4 + k], w.to_a) for k, src in enumerate(sources)]

    def over_line(self):
        w = self.ways
        z, a, b, c = w.spot
        out = []
        for step in range(1, w.lines):
            there = lax.rem(z + step, w.lines)
            out.append(
                self.copy(6 + step, self.r3.at[:, there], self.got.at[z], device(there, a, b, c))
            )
        return out

    def line_arrival(self, step):
        w = self.ways
        here = self.got.at[lax.rem(w.spot[0] + w.lines - step, w.lines)]
        self.copy(6 + step, here, here, w.to_c).wait_recv()

    def start(self, copies):
        for copy in copies:
            copy.start()

    def arrive(self, copies):
        for copy in copies:
            copy.wait_recv()

    def collect(self):
        z, a, b, c = self.ways.spot
        for line in range(self.ways.lines):
            self.r3[0, line] = self.blocks[line, a, b, c]
            self.r3[1, line] = self.r1[line, a, b]
            for k in range(2):
                self.r3[2 + k, line] = self.r2[k, line, a]

    def events(self):
        z = self.ways.spot[0]
        return [
            lambda: self.start(self.over_core()),
            lambda: (self.arrive(self.over_core()), self.start(self.over_b())),
            lambda: (self.arrive(self.over_b()), self.start(self.over_a())),
            lambda: (self.arrive(self.over_a()), self.collect(), self.start(self.over_line())),
            lambda: [self.line_arrival(step) for step in range(1, self.ways.lines)],
        ]

    def block(self, line, a, b, c):
        z, ma, mb, mc = self.ways.spot
        i = jnp.abs(a - ma) * 4 + jnp.abs(b - mb) * 2 + jnp.abs(c - mc)
        own = self.r3[i, z]
        return jnp.where(line == z, own, self.got[line, i])

    def drain(self):
        for copies in (self.over_core(), self.over_b(), self.over_a(), self.over_line()):
            for copy in copies:
                copy.wait_send()


def exchange_scratch(lines, rows):
    return [
        pltpu.VMEM((lines, 2, 2, 2, rows, 128), bf16),
        pltpu.VMEM((lines, 2, 2, rows, 128), bf16),
        pltpu.VMEM((2, lines, 2, rows, 128), bf16),
        pltpu.VMEM((8, lines, rows, 128), bf16),
        pltpu.VMEM((lines, 8, rows, 128), bf16),
    ]


def all_places(lines):
    return [(d, d // 8, d // 4 % 2, d // 2 % 2, d % 2) for d in range(8 * lines)]


def padded_rows(value, rows):
    return jnp.concatenate([value, jnp.zeros((rows - value.shape[0],) + value.shape[1:], value.dtype)])


def softmax_rows(scores):
    weights = jnp.exp(scores - jnp.max(scores, axis=-1, keepdims=True))
    return weights * (1.0 / jnp.sum(weights, axis=-1, keepdims=True))


def turn(values, cosine, signed_sine):
    return values * cosine + pltpu.roll(values, values.shape[-1] // 2, 1) * signed_sine


def document_of(positions, first_end, second_end):
    return (positions >= first_end).astype(jnp.int32) + (positions >= second_end).astype(jnp.int32)


def make_bias(bias, lengths, tp_index):
    rows, cols = bias.shape
    first_end = lengths[0, 0]
    second_end = first_end + lengths[0, 1]
    q_pos = lax.broadcasted_iota(jnp.int32, (rows, cols), 0) + tp_index * rows
    k_pos = lax.broadcasted_iota(jnp.int32, (rows, cols), 1)
    allowed = (
        document_of(q_pos, first_end, second_end) == document_of(k_pos, first_end, second_end)
    ) & (q_pos >= k_pos)
    bias[...] = jnp.where(allowed, 0.0, -1e30)


def front_kernel(lines, experts, scale, *refs):
    (
        lengths, ids, freq, hidden, small, wq, wk, wv, wo, s_gate, s_up, s_down, cot,
        w_out, cot_out, tok, aux, small_t, residual, attended, q_out, k_out, v_out, n_out,
        cos_out, sin_out, group, shared,
        wall, stage, small_stage, small_all, bias, e_blocks, e_r1, e_r2, e_r3, e_got,
        g_send, g_recv, s_send, s_recv, x_send, x_recv, e_send, e_recv, local_sem,
    ) = refs
    ways = Ways(lines)
    z, a, b, c = ways.spot
    ob, oc = 1 - b, 1 - c
    count, width = hidden.shape
    d_rows = wq.shape[0]
    chip_rows = 2 * d_rows
    half = width // 2
    heads = width // 128
    group_len = 4 * count
    ways.greet()

    def cot_chunk(line, kind, part, other):
        first = (line * 4 + kind) * count
        if part is None:
            return cot_out.at[pl.ds(first, count)]
        return cot_out.at[pl.ds(first + part * (count // 2), count // 2)]

    def sems(i):
        return (lambda k: g_send.at[i, k], lambda k: g_recv.at[i, k])

    g_cot = Gather(ways, cot_chunk, sems(3), own=cot, relative=True)
    g_cot.begin()

    shards = (wq, wk, wv, wo)
    swaps = [
        remote(
            shards[k].at[:, pl.ds(pl.multiple_of(oc * half, 128), half)], stage.at[k],
            s_send.at[k], s_recv.at[k], ways.to_c,
        )
        for k in range(4)
    ] + [remote(small, small_stage, s_send.at[4], s_recv.at[4], ways.to_c)]
    for copy in swaps:
        copy.start()

    def group_copy(k, src, dst, to):
        return remote(src, dst, x_send.at[k], x_recv.at[k], to)

    own_group = group.at[b * 2 + c]
    group_copies = [group_copy(0, hidden, own_group, ways.to_c), group_copy(1, hidden, own_group, ways.to_b)]
    for copy in group_copies:
        copy.start()
    own_group[...] = hidden[...]

    def chip_block(own, other):
        own, other = own.astype(f32), other.astype(f32)
        first = jnp.where(c == 0, own, other)
        second = jnp.where(c == 0, other, own)
        return jnp.concatenate([first, second], axis=0).astype(bf16)

    sh = s_down.shape[0]
    block_rows = e_blocks.shape[4]
    lane = lax.broadcasted_iota(jnp.int32, (d_rows, 128), 1)

    def columns_at(ref, first, to):
        tile, start = first // 128 * 128, first % 128
        value = pltpu.roll(ref[:, tile : tile + 128].astype(f32), (to - start) % 128, 1)
        if start + sh > 128:
            later = pltpu.roll(ref[:, tile + 128 : tile + 256].astype(f32), (to - start) % 128, 1)
            value = jnp.where(lane < to + 128 - start, value, later)
        return value

    for d, line, da, db, dc in all_places(lines):
        gate, up = columns_at(s_gate, d * sh, 0), columns_at(s_up, d * sh, 64)
        value = jnp.where(lane < sh, gate, jnp.where((lane >= 64) & (lane < 64 + sh), up, 0.0))
        e_blocks[line, da, db, dc] = padded_rows(value, block_rows).astype(bf16)
    exchange = Exchange(
        ways, e_blocks, e_r1, e_r2, e_r3, e_got, (lambda k: e_send.at[k], lambda k: e_recv.at[k])
    )
    e_events = exchange.events()

    base = pl.multiple_of(ways.chip(z, O) * chip_rows, 16)
    for copy in swaps:
        copy.wait_recv()
    small_all[pl.ds(base, chip_rows), :] = chip_block(small[...], small_stage[...])
    for k in range(4):
        mine = shards[k][:, pl.ds(pl.multiple_of(c * half, 128), half)]
        wall[pl.ds(base, chip_rows), pl.ds(pl.multiple_of((c * 4 + k) * half, 128), half)] = chip_block(
            mine, stage[k]
        )

    def small_chunk(line, kind, part, other):
        rows = pl.multiple_of(ways.chip(line, kind) * chip_rows, 16)
        if part is None:
            return small_all.at[pl.ds(rows, chip_rows)]
        low = chip_rows // 32 * 16
        return small_all.at[pl.ds(rows, low) if part == 0 else pl.ds(rows + low, chip_rows - low)]

    def weight_chunk(first, cols, cut):
        def chunk(line, kind, part, other):
            rows = pl.multiple_of(ways.chip(line, kind) * chip_rows, 16)
            col = (oc if other else c) * 4 * half + first
            if part is None:
                start, size = col, cols
            elif part == 0:
                start, size = col, cut
            else:
                start, size = col + cut, cols - cut
            return wall.at[pl.ds(rows, chip_rows), pl.ds(pl.multiple_of(start, 128), size)]

        return chunk

    tiles = half // 128
    g_small = Gather(ways, small_chunk, sems(0))
    g_qkv = Gather(ways, weight_chunk(0, 3 * half, (3 * tiles + 1) // 2 * 128), sems(1), across=True)
    g_out = Gather(ways, weight_chunk(3 * half, half, tiles // 2 * 128), sems(2), across=True)
    keep = pltpu.make_async_copy(cot, cot_chunk(z, O, None, False), local_sem.at[0])
    keep.start()
    g_small.begin()
    g_qkv.begin()
    e_events[0]()

    first_end = lengths[0, 0]
    second_end = first_end + lengths[0, 1]
    position = lax.broadcasted_iota(jnp.int32, (group_len, 128), 0)
    doc = document_of(position, first_end, second_end)
    start = jnp.where(doc == 0, 0, jnp.where(doc == 1, first_end, second_end))
    angles = (position - start).astype(f32) * freq[...]
    lane = lax.broadcasted_iota(jnp.int32, (group_len, 128), 1)
    cos_out[...] = jnp.cos(angles)
    sin_out[...] = jnp.where(lane < 64, -1.0, 1.0) * jnp.sin(angles)
    make_bias(bias, lengths, b * 2 + c)
    got = group.at[ob * 2 + c]
    group_copy(1, got, got, ways.to_b).wait_recv()
    group_copies.append(group_copy(2, got, got, ways.to_c))
    group_copies[-1].start()
    for k, t in ((0, b * 2 + oc), (2, ob * 2 + oc)):
        got = group.at[t]
        group_copy(k, got, got, ways.to_c).wait_recv()

    small_events, qkv_events = g_small.events(), g_qkv.events()
    out_events = g_out.events()
    cot_events = {
        1: lambda: (g_cot.xy_event(0), g_cot.chain_event(1), g_cot.send_own(1)),
        2: lambda: (g_cot.diag_carried(0), g_cot.chain_event(2)),
        4: lambda: (g_cot.xy_event(1), g_cot.chain_event(3)),
        5: lambda: g_cot.diag_handed(1),
    }
    for k in range(len(qkv_events)):
        if k == 3:
            g_out.begin()
        qkv_events[k]()
        small_events[k]()
        if k in cot_events:
            cot_events[k]()
        if 2 <= k < 6:
            e_events[k - 1]()
        if k >= 4:
            out_events[k - 4]()
    flat = jnp.transpose(small_all[...].astype(f32))
    small_t[...] = flat.astype(bf16)
    gain_one = flat[experts : experts + 1, :]
    gain_two = flat[experts + 1 : experts + 2, :]
    for t in range(4):
        x = group[t].astype(f32)
        r = lax.rsqrt(jnp.mean(x * x, axis=-1, keepdims=True) + epsilon)
        n_out[t * count : (t + 1) * count, :] = (x * r * gain_one).astype(bf16)
    g_qkv.other_core()

    later = out_events[3:] + [g_out.other_core]

    def service(n=1):
        for _ in range(n):
            if later:
                later.pop(0)()

    stacked = jnp.concatenate(
        [exchange.block(*there)[:d_rows].astype(f32) for _, *there in all_places(lines)]
    )
    turned = jnp.transpose(stacked)
    shared[0] = turned[:64].astype(bf16)
    shared[1] = turned[64:].astype(bf16)
    shared[2] = padded_rows(s_down[...].astype(f32), 64).astype(bf16)
    own_rows = pl.ds(pl.multiple_of((b * 2 + c) * count, count), count)
    for h in range(2):
        cols = pl.ds((h * 4 + 1) * half, half)
        keys = dense_dot(n_out[...], wall[:, cols])
        for j in range(half // 128):
            k_out[:, h * half + j * 128 : h * half + (j + 1) * 128] = turn(
                keys[:, j * 128 : (j + 1) * 128], cos_out[...], sin_out[...]
            ).astype(bf16)
        service()
        cols = pl.ds((h * 4 + 2) * half, half)
        v_out[:, h * half : (h + 1) * half] = dense_dot(n_out[...], wall[:, cols]).astype(bf16)
        service()
        queries = dense_dot(n_out[own_rows, :], wall[:, pl.ds(h * 4 * half, half)])
        for j in range(half // 128):
            q_out[:, h * half + j * 128 : h * half + (j + 1) * 128] = turn(
                queries[:, j * 128 : (j + 1) * 128], cos_out[own_rows, :], sin_out[own_rows, :]
            ).astype(bf16)
        service()
    for h in range(heads):
        cols = pl.ds(h * 128, 128)
        probs = softmax_rows(dot_nt(q_out[:, cols], k_out[:, cols]) * scale + bias[...])
        attended[:, cols] = dense_dot(probs.astype(bf16), v_out[:, cols]).astype(bf16)
        if h % 2:
            service()
    service(len(later))
    for h in range(2):
        projected = dense_dot(attended[...], wall[:, pl.ds((h * 4 + 3) * half, half)])
        residual[:, h * half : (h + 1) * half] = (
            hidden[:, h * half : (h + 1) * half].astype(f32) + projected
        )
    service()
    res = residual[...]
    r2 = lax.rsqrt(jnp.mean(res * res, axis=-1, keepdims=True) + epsilon)
    normed = (res * r2 * gain_two).astype(bf16)
    tok[...] = normed
    logits = dense_dot(normed, small_all[...])
    lane = lax.broadcasted_iota(jnp.int32, (count, 128), 1)
    affinity = softmax_rows(jnp.where(lane < experts, logits, -1e30))
    named = lane < 0
    for j in range(ids.shape[1]):
        named = named | (ids[:, j : j + 1] == lane)
    signed = jnp.transpose(jnp.where(named, affinity, -affinity))[:experts, :]
    high = signed.astype(bf16)
    aux[0:experts, :] = high
    aux[experts : 2 * experts, :] = (signed - high.astype(f32)).astype(bf16)
    save = pltpu.make_async_copy(wall, w_out, local_sem.at[1])
    save.start()
    service(len(later))
    for g in (g_small, g_qkv, g_out, exchange):
        g.drain()
    g_cot.drain(2)
    for copy in swaps + group_copies:
        copy.wait_send()
    keep.wait()
    save.wait()


def front_call(
    lengths, ids, hidden, small, weights, shared, cot, experts, scale, collective_id
):
    lines = lax.axis_size("ep") // 2
    count, width = hidden.shape
    d_rows = weights[0].shape[0]
    group_len = 4 * count
    block_rows = -(-d_rows // 16) * 16
    anywhere = pl.BlockSpec(memory_space=pl.ANY)
    vmem = pl.BlockSpec(memory_space=pltpu.VMEM)
    smem = pl.BlockSpec(memory_space=pltpu.SMEM)
    lane = jnp.arange(128) % 64
    freq = (10000.0 ** (-2.0 * lane.astype(f32) / 128))[None, :]
    shape = jax.ShapeDtypeStruct
    return pl.pallas_call(
        functools.partial(front_kernel, lines, experts, scale),
        out_shape=(
            shape((width, 4 * width), bf16),
            shape((lines * 4 * count, width), bf16),
            shape((count, width), bf16),
            shape((2 * experts, count), bf16),
            shape((128, width), bf16),
            shape((count, width), f32),
            shape((count, width), bf16),
            shape((count, width), bf16),
            shape((group_len, width), bf16),
            shape((group_len, width), bf16),
            shape((group_len, width), bf16),
            shape((group_len, 128), f32),
            shape((group_len, 128), f32),
            shape((4, count, width), bf16),
            shape((3, 64, width), bf16),
        ),
        in_specs=[smem] + [vmem] * 11 + [anywhere],
        out_specs=(anywhere, anywhere) + (vmem,) * 13,
        scratch_shapes=[
            pltpu.VMEM((width, 4 * width), bf16),
            pltpu.VMEM((4, d_rows, width // 2), bf16),
            pltpu.VMEM((d_rows, 128), bf16),
            pltpu.VMEM((width, 128), bf16),
            pltpu.VMEM((count, group_len), f32),
            *exchange_scratch(lines, block_rows),
            pltpu.SemaphoreType.DMA((4, 12 * lines)),
            pltpu.SemaphoreType.DMA((4, 12 * lines)),
            pltpu.SemaphoreType.DMA((5,)),
            pltpu.SemaphoreType.DMA((5,)),
            pltpu.SemaphoreType.DMA((3,)),
            pltpu.SemaphoreType.DMA((3,)),
            pltpu.SemaphoreType.DMA((7 + lines,)),
            pltpu.SemaphoreType.DMA((7 + lines,)),
            pltpu.SemaphoreType.DMA((2,)),
        ],
        compiler_params=pltpu.CompilerParams(
            collective_id=collective_id, has_side_effects=True, vmem_limit_bytes=60 * 2**20
        ),
        name="front",
    )(lengths, ids, freq, hidden, small, *weights, *shared, cot)


class Reduce:
    def __init__(self, ways, chunk, cut, pq, xr, yr, dz, zr, sems, alone=()):
        self.ways, self.chunk, self.cut = ways, chunk, cut
        self.pq, self.xr, self.yr, self.dz, self.zr = pq, xr, yr, dz, zr
        self.alone = alone
        self.carried = [True if u in alone else ways.carried[u] for u in range(ways.lines)]
        self.send_sem, self.recv_sem = sems

    def copy(self, slot, u, src, dst, to):
        k = slot * self.ways.lines + u
        return remote(src, dst, self.send_sem(k), self.recv_sem(k), to)

    def diag(self, part, u):
        w = self.ways
        return self.copy(
            part, u, self.chunk(w.zs[u], D, part), self.cut(self.pq, self.slot(u), part),
            w.to_b if part else w.to_a,
        )

    def side_b(self, part, u):
        w = self.ways
        return self.copy(2 + part, u, self.chunk(w.zs[u], X, part), self.cut(self.xr, u, part), w.to_b)

    def side_a(self, part, u):
        w = self.ways
        return self.copy(4 + part, u, self.chunk(w.zs[u], Y, part), self.cut(self.yr, u, part), w.to_a)

    def slot(self, u):
        return 2 if u in self.alone else min(u, 1)

    def hand(self, u, at):
        w = self.ways
        return self.copy(
            7, at, self.chunk(w.zs[u], D, None), self.cut(self.dz, min(at, 1), None), w.pair
        )

    def along(self, u):
        w = self.ways
        z, a, b, c = w.spot
        slot = lax.rem(z - w.zs[u] + w.lines, w.lines) - 1
        k = 6 * w.lines
        return remote(
            self.chunk(w.zs[u], O, None), self.zr(slot), self.send_sem(k + u),
            self.recv_sem(k + slot), device(w.zs[u], a, b, c),
        )

    def start(self, u):
        def whole():
            self.hand(u, u if u > 1 else 0).start()
            self.side_b(0, u).start()
            self.side_a(1, u).start()

        self.side_b(1, u).start()
        self.side_a(0, u).start()
        when(other(self.carried[u]), whole)

    def carry(self, u):
        def act():
            if u not in self.alone:
                self.hand(u, u).wait_recv()
            for part in (0, 1):
                if u not in self.alone:
                    accumulate(
                        self.chunk(self.ways.zs[u], D, part), [self.cut(self.dz, min(u, 1), part)]
                    )
                self.diag(part, u).start()

        when(self.carried[u], act)

    def mid(self, u):
        w = self.ways

        def act():
            self.diag(0, u).wait_recv()
            accumulate(self.chunk(w.zs[u], X, 0), [self.cut(self.pq, self.slot(u), 0)])
            self.side_b(0, u).start()
            self.diag(1, u).wait_recv()
            accumulate(self.chunk(w.zs[u], Y, 1), [self.cut(self.pq, self.slot(u), 1)])
            self.side_a(1, u).start()

        when(self.carried[u], act)

    def end(self, u):
        w = self.ways
        for part in (0, 1):
            self.side_b(part, u).wait_recv()
            self.side_a(part, u).wait_recv()
            accumulate(
                self.chunk(w.zs[u], O, part), [self.cut(self.xr, u, part), self.cut(self.yr, u, part)]
            )
        if u > 0:
            self.along(u).start()

    def events(self):
        return [
            lambda: (self.start(2), self.start(3)),
            lambda: (self.carry(2), self.carry(3), self.start(1)),
            lambda: (self.mid(2), self.mid(3), self.start(0)),
            lambda: (self.end(2), self.end(3)),
            lambda: (self.carry(0), self.end(1)),
            lambda: self.mid(0),
            lambda: self.end(0),
        ]

    def total(self):
        w = self.ways
        sums = self.chunk(w.spot[0], O, None)[...].astype(f32)
        for slot in range(w.lines - 1):
            k = 6 * w.lines + slot
            here = self.zr(slot)
            remote(here, here, self.send_sem(k), self.recv_sem(k), w.to_c).wait_recv()
            sums = sums + here[...].astype(f32)
        return sums

    def drain(self):
        w = self.ways
        for u in range(w.lines):
            for part in (0, 1):
                when(self.carried[u], lambda part=part, u=u: self.diag(part, u).wait_send())
                self.side_b(part, u).wait_send()
                self.side_a(part, u).wait_send()
            when(other(self.carried[u]), lambda u=u: self.hand(u, u if u > 1 else 0).wait_send())
            if u > 0:
                self.along(u).wait_send()


def accumulate(dst, others):
    total = dst[...].astype(f32)
    for ref in others:
        total = total + ref[...].astype(f32)
    dst[...] = total.astype(bf16)


def mixture_kernel(lines, tok, aux, cot, wg, wu, wd, shared, sel, sel_t, router_t, ones, *refs):
    (
        sums, out_part, dw_own, dw_sib, dr,
        nc, aux_all, vg, vu, vd, dw, acts, dg, du, daff, dlg, pq, xr, yr, dz, zr,
        ag_send, ag_recv, rs_send, rs_recv, w_send, w_recv, w_local, cot_sem, local_sem,
    ) = refs
    ways = Ways(lines)
    z, a, b, c = ways.spot
    oc = 1 - c
    zs = ways.zs
    count, width = tok.shape
    half = count // 2
    n_routed = wg.shape[0]
    hc = n_routed + shared.shape[1]
    hidden = 2 * hc
    n_sel = sel.shape[1]
    block = 256
    unit_rows = 4 * count
    ways.greet()

    def rows_of(line, kind, part):
        if part is None:
            return pl.ds(pl.multiple_of((line * 4 + kind) * count, count), count)
        return pl.ds(pl.multiple_of((line * 4 + kind) * count + part * half, half), half)

    def aux_chunk(line, kind, part, _):
        rows = aux.shape[0]
        at = line * 4 + kind
        if part is None:
            return aux_all.at[at]
        return aux_all.at[at, pl.ds(part * (rows // 2), rows // 2)]

    def sems(i):
        return (lambda k: ag_send.at[i, k], lambda k: ag_recv.at[i, k])

    gathers = [
        Gather(
            ways, lambda line, kind, part, _: nc.at[rows_of(line, kind, part), pl.ds(0, width)],
            sems(0), own=tok, relative=True,
        ),
        Gather(ways, aux_chunk, sems(1), own=aux, relative=True),
    ]

    cots = Gather(
        ways, lambda line, kind, part, _: nc.at[rows_of(line, kind, part), pl.ds(width, width)],
        sems(2), relative=True,
    )

    def each(name, *args):
        for g in gathers:
            getattr(g, name)(*args)

    def every(name, *args):
        each(name, *args)
        getattr(cots, name)(*args)

    each("begin")
    local = []
    mine = pl.ds(c * hc, hc)
    theirs = pl.ds(oc * hc, hc)
    w_copies = []
    for k, (src, dst) in enumerate(((wg, vg), (wu, vu), (wd, vd))):
        for j, (part, first, size) in enumerate(
            ((src, 0, n_routed), (shared.at[k], n_routed, hc - n_routed))
        ):
            there = dst.at[pl.ds(pl.multiple_of(c * hc + first, 16), size)]
            i = 2 * k + j
            copy = pltpu.make_async_copy(part, there, w_local.at[i])
            copy.start()
            local.append(copy)
            copy = remote(part, there, w_send.at[i], w_recv.at[i], ways.to_c)
            copy.start()
            w_copies.append(copy)

    copy = pltpu.make_async_copy(tok, nc.at[rows_of(z, O, None), pl.ds(0, width)], local_sem.at[3])
    copy.start()
    local.append(copy)
    copy = pltpu.make_async_copy(aux, aux_chunk(z, O, None, False), local_sem.at[4])
    copy.start()
    local.append(copy)
    cot_loads = []
    for u in (2, 3, 0, 1):
        size = unit_rows if u < 2 else count
        there = pl.ds(pl.multiple_of(zs[u] * unit_rows, unit_rows), size)
        cot_loads.append(
            pltpu.make_async_copy(cot.at[there], nc.at[there, pl.ds(width, width)], cot_sem.at[u])
        )
        cot_loads[-1].start()

    def zero(i, carry):
        dw[:, pl.ds(i * 64, 64), :] = jnp.zeros((3, 64, width), f32)
        return carry

    lax.fori_loop(0, hidden // 64, zero, 0)
    dr[...] = jnp.zeros_like(dr)

    def cut(ref, u, part):
        return ref.at[u] if part is None else ref.at[u, pl.ds(part * half, half)]

    back = Reduce(
        ways, lambda line, kind, part: nc.at[rows_of(line, kind, part), pl.ds(width, width)], cut,
        pq, xr, yr, dz, lambda slot: zr.at[slot],
        (lambda k: rs_send.at[k], lambda k: rs_recv.at[k]), alone=(3,),
    )

    def save(u):
        rows = pl.ds(pl.multiple_of(zs[u] * unit_rows, unit_rows), unit_rows)
        return pltpu.make_async_copy(
            nc.at[rows, pl.ds(0, width)], out_part.at[rows], local_sem.at[7 + u]
        )

    def expand(line, columns):
        return jnp.concatenate(
            [dot_tn(aux_all[line * 4 + kind], sel[:, columns]) for kind in range(4)], axis=0
        )

    def at_step(s, acts_of):
        for v, act in acts_of.items():
            when(s == v, act)

    def unit(u, carry):
        line = pick(zs, u)
        rows = pl.ds(pl.multiple_of(line * unit_rows, unit_rows), unit_rows)
        at_step(
            u,
            {
                1: lambda: (each("xy_event", 1), each("diag_handed", 1)),
                2: lambda: (every("diag_handed", 2), every("diag_carried", 3)),
                3: lambda: (every("diag_handed", 3), back.end(1)),
            },
        )
        daff[...] = jnp.zeros_like(daff)

        def hidden_step(i, carry):
            h = pl.ds(pl.multiple_of(i * block, block), block)
            x = nc[rows, 0:width]
            gate_pre = dot_nt(x, vg[h, :])
            up_pre = dot_nt(x, vu[h, :])
            grad = dot_nt(nc[rows, width : 2 * width], vd[h, :])
            scale = jnp.maximum(expand(line, h) + ones[:, h], 0.0)
            sigma = 1.0 / (1.0 + jnp.exp(-gate_pre))
            silu = gate_pre * sigma
            act = silu * up_pre
            acts[:, h] = (act * scale).astype(bf16)
            daff[...] += dense_dot((act * grad).astype(bf16), sel_t[h, :])
            grad = grad * scale
            dg[:, h] = (grad * up_pre * sigma * (1.0 + gate_pre * (1.0 - sigma))).astype(bf16)
            du[:, h] = (grad * silu).astype(bf16)
            return carry

        lax.fori_loop(0, hidden // block, hidden_step, 0, unroll=True)
        signed = expand(line, pl.ds(hidden, n_sel - hidden))
        affinity = jnp.abs(signed)
        grad_aff = jnp.where(signed > 0, daff[...], 0.0)
        total = jnp.sum(affinity * grad_aff, axis=1, keepdims=True)
        dlg[...] = (affinity * (grad_aff - total)).astype(bf16)
        at_step(
            u,
            {
                0: lambda: (each("chain_event", 2), each("send_own", 2)),
                1: lambda: every("diag_carried", 2),
                2: lambda: (back.carry(0), cots.drain_unit(2)),
                3: lambda: (back.carry(2), back.end(0), cots.drain_unit(3)),
            },
        )

        def down_step(i, carry):
            h = pl.ds(pl.multiple_of(i * block, block), block)
            dw[2, h, :] += dot_tn(acts[:, h], nc[rows, width : 2 * width])
            return carry

        lax.fori_loop(0, hidden // block, down_step, 0, unroll=True)

        def back_step(i, carry):
            n = pl.ds(pl.multiple_of(i * block, block), block)
            n2 = pl.ds(pl.multiple_of(width + i * block, block), block)
            nc[rows, n2] = (
                dense_dot(dg[...], vg[:, n])
                + dense_dot(du[...], vu[:, n])
                + dense_dot(dlg[...], router_t[:, n])
            ).astype(bf16)
            return carry

        lax.fori_loop(0, width // block, back_step, 0, unroll=True)
        at_step(
            u,
            {
                0: lambda: (each("chain_event", 3), cots.send_own(3)),
                1: lambda: (every("xy_event", 3), back.start(1), back.start(0)),
                2: lambda: (back.start(2), back.mid(0)),
                3: lambda: (back.carry(3), back.start(3), back.mid(2)),
            },
        )

        def weight_step(i, carry):
            h = pl.ds(pl.multiple_of(i * block, block), block)
            x = nc[rows, 0:width]
            dw[0, h, :] += dot_tn(dg[:, h], x)
            dw[1, h, :] += dot_tn(du[:, h], x)
            return carry

        lax.fori_loop(0, hidden // block, weight_step, 0, unroll=True)
        dr[...] += dot_tn(dlg[...], nc[rows, 0:width])
        at_step(
            u,
            {
                0: lambda: (every("xy_event", 2), each("send_own", 3), each("drain_chain", 1)),
                1: lambda: (each("drain_chain", 2), each("drain_chain", 3)),
                3: lambda: (back.mid(3), back.end(2)),
            },
        )
        for v in range(lines):
            when(u == v, lambda v=v: each("drain_unit", v))

        def out_step(i, carry):
            n = pl.ds(pl.multiple_of(i * block, block), block)
            nc[rows, n] = dense_dot(acts[...], vd[:, n]).astype(bf16)
            return carry

        lax.fori_loop(0, width // block, out_step, 0, unroll=True)
        for v in range(lines):
            when(u == v, lambda v=v: save(v).start())
        return carry

    each("xy_event", 0)
    each("chain_event", 1)
    each("send_own", 1)
    for copy in w_copies:
        copy.wait_recv()
    for copy in local + cot_loads:
        copy.wait()
    cots.send_own(2)
    each("diag_carried", 0)
    lax.fori_loop(0, lines, unit, 0)

    own_out = pltpu.make_async_copy(dw.at[:, mine], dw_own, local_sem.at[6])
    own_out.start()
    sib_out = pltpu.make_async_copy(dw.at[:, theirs], dw_sib, local_sem.at[7 + lines])
    sib_out.start()
    back.end(3)
    sums[...] = back.total()
    back.drain()
    for u in range(lines):
        save(u).wait()
    for copy in w_copies:
        copy.wait_send()
    sib_out.wait()
    own_out.wait()


def mixture_call(tok, aux, cot, weights, shared, sel, sel_t, router_t, ones, collective_id):
    lines = lax.axis_size("ep") // 2
    count, width = tok.shape
    hc = weights[0].shape[0] + shared.shape[1]
    anywhere = pl.BlockSpec(memory_space=pl.ANY)
    vmem = pl.BlockSpec(memory_space=pltpu.VMEM)
    n_rows = lines * 4 * count
    return pl.pallas_call(
        functools.partial(mixture_kernel, lines),
        out_shape=(
            jax.ShapeDtypeStruct((count, width), f32),
            jax.ShapeDtypeStruct((n_rows, width), bf16),
            jax.ShapeDtypeStruct((3, hc, width), f32),
            jax.ShapeDtypeStruct((3, hc, width), f32),
            jax.ShapeDtypeStruct((128, width), f32),
        ),
        in_specs=[anywhere] * 7 + [vmem] * 4,
        out_specs=(vmem, anywhere, anywhere, anywhere, vmem),
        scratch_shapes=[
            pltpu.VMEM((n_rows, 2 * width), bf16),
            pltpu.VMEM((lines * 4,) + aux.shape, bf16),
            pltpu.VMEM((2 * hc, width), bf16),
            pltpu.VMEM((2 * hc, width), bf16),
            pltpu.VMEM((2 * hc, width), bf16),
            pltpu.VMEM((3, 2 * hc, width), f32),
            pltpu.VMEM((4 * count, 2 * hc), bf16),
            pltpu.VMEM((4 * count, 2 * hc), bf16),
            pltpu.VMEM((4 * count, 2 * hc), bf16),
            pltpu.VMEM((4 * count, 128), f32),
            pltpu.VMEM((4 * count, 128), bf16),
            pltpu.VMEM((3, count, width), bf16),
            pltpu.VMEM((lines, count, width), bf16),
            pltpu.VMEM((lines, count, width), bf16),
            pltpu.VMEM((2, count, width), bf16),
            pltpu.VMEM((lines - 1, count, width), bf16),
            pltpu.SemaphoreType.DMA((3, 12 * lines)),
            pltpu.SemaphoreType.DMA((3, 12 * lines)),
            pltpu.SemaphoreType.DMA((8 * lines,)),
            pltpu.SemaphoreType.DMA((8 * lines,)),
            pltpu.SemaphoreType.DMA((6,)),
            pltpu.SemaphoreType.DMA((6,)),
            pltpu.SemaphoreType.DMA((6,)),
            pltpu.SemaphoreType.DMA((lines,)),
            pltpu.SemaphoreType.DMA((8 + lines,)),
        ],
        compiler_params=pltpu.CompilerParams(
            collective_id=collective_id, has_side_effects=True, vmem_limit_bytes=62 * 2**20
        ),
        name="mixture",
    )(tok, aux, cot, *weights, shared, sel, sel_t, router_t, ones)


def back_kernel(lines, experts, scale, sh, *refs):
    (
        lengths, dn2, residual, cot, group, small_t, router_part, attended, q, normed, cosine, sine,
        keys, vals, wall_in, outs_in, dw_own, dw_sib,
        layer_out, input_grad, gq, gk, gv, go, small_out, gsg, gsu, dw_got,
        wall, part, staged, landed, pq, xr, yr, dz, zr, fin, fin_other,
        s_part, s_landed, s_pq, s_xr, s_yr, s_dz, s_zr,
        o_part, o_pq, o_xr, o_yr, o_dz, o_zr,
        grads, low, datt, dq, dk, dv, dn_part, dn_other, dn_far, bias, rows_t,
        e_blocks, e_r1, e_r2, e_r3, e_got,
        c_send, c_recv, r_send, r_recv, d_send, d_recv, e_send, e_recv, local_sem, credit,
    ) = refs
    ways = Ways(lines)
    z, a, b, c = ways.spot
    ob, oc = 1 - b, 1 - c
    count, width = cot.shape
    half = width // 2
    heads = width // 128
    chip_rows = pq.shape[1]
    d_rows = chip_rows // 2

    def load(i, src, dst):
        copy = pltpu.make_async_copy(src, dst, local_sem.at[i])
        copy.start()
        return copy

    o_load = load(0, outs_in, o_part)
    wo_loads = [
        load(1 + h, wall_in.at[:, pl.ds((h * 4 + 3) * half, half)], part.at[:, pl.ds(h * half, half)])
        for h in range(2)
    ]
    kv_loads = [load(3, keys, dk), load(4, vals, dv)]
    wall_loads = [
        load(5 + h, wall_in.at[:, pl.ds(h * 4 * half, 3 * half)], wall.at[:, pl.ds(h * 3 * half, 3 * half)])
        for h in range(2)
    ]

    def weight(h, k):
        return wall[:, pl.ds((h * 3 + k) * half, half)]

    ways.greet()

    half_rows = count // 2

    def o_chunk(line, kind, p):
        size = count if p is None else half_rows
        return o_part.at[pl.ds(pl.multiple_of((line * 4 + kind) * count + (p or 0) * size, size), size)]

    def o_cut(ref, u, p):
        return ref.at[u] if p is None else ref.at[u, pl.ds(p * half_rows, half_rows)]

    o_reduce = Reduce(
        ways, o_chunk, o_cut, o_pq, o_xr, o_yr, o_dz, lambda slot: o_zr.at[slot],
        (lambda i: r_send.at[3, i], lambda i: r_recv.at[3, i]),
    )

    def finish_output():
        layer_out[...] = (residual[...] + o_reduce.total()).astype(bf16)

    o_events = o_reduce.events() + [finish_output]
    o_load.wait()
    o_events[0]()
    dw_copy = remote(dw_sib, dw_got, c_send.at[6], c_recv.at[6], ways.to_c)
    dw_copy.start()
    exchange = Exchange(
        ways, e_blocks, e_r1, e_r2, e_r3, e_got, (lambda k: e_send.at[k], lambda k: e_recv.at[k])
    )
    e_events = exchange.events()
    shared_rows = pl.ds(dw_own.shape[1] - 64, 64)

    def shared_at(j, k):
        return (fin.at[pl.ds(0, 64), pl.ds(k * width, width)], rows_t.at[pl.ds(k * 64, 64)])[j]

    def shared_blocks():
        dw_copy.wait()
        loads = [
            load(7 + 2 * k + j, ref.at[k, shared_rows], shared_at(j, k))
            for k in range(2)
            for j, ref in enumerate((dw_own, dw_got))
        ]
        for copy in loads:
            copy.wait()
        turned = jnp.transpose(
            jnp.concatenate([fin[0:64, 0:width], fin[0:64, width : 2 * width]]) + rows_t[...]
        )
        for d, line, da, db, dc in all_places(lines):
            value = turned[d * d_rows : (d + 1) * d_rows]
            e_blocks[line, da, db, dc] = padded_rows(value, e_blocks.shape[4]).astype(bf16)
        e_events[0]()

    def shared_finish():
        lane = lax.broadcasted_iota(jnp.int32, (d_rows, 128), 1)
        for out, first in ((gsg, 0), (gsu, 64)):
            tiles = [jnp.zeros((d_rows, 128), f32) for _ in range(out.shape[1] // 128)]
            for d, *there in all_places(lines):
                tile, start = d * sh // 128, d * sh % 128
                value = exchange.block(*there)[:d_rows].astype(f32)
                value = pltpu.roll(value, (start - first) % 128, 1)
                if start + sh > 128:
                    tiles[tile] = jnp.where(lane >= start, value, tiles[tile])
                    tiles[tile + 1] = jnp.where(lane < start + sh - 128, value, tiles[tile + 1])
                else:
                    tiles[tile] = jnp.where((lane >= start) & (lane < start + sh), value, tiles[tile])
            for k, tile in enumerate(tiles):
                out[:, k * 128 : (k + 1) * 128] = tile

    res = residual[...]
    r2 = lax.rsqrt(jnp.mean(res * res, axis=-1, keepdims=True) + epsilon)
    unit_two = res * r2
    gain_two = small_t[experts + 1 : experts + 2, :].astype(f32)
    gain_one = small_t[experts : experts + 1, :].astype(f32)
    rows_t[...] = router_part[...]
    rows_t[experts + 1 : experts + 2, :] = jnp.sum(dn2[...] * unit_two, axis=0, keepdims=True)
    scaled = dn2[...] * gain_two
    back = r2 * (scaled - unit_two * jnp.mean(scaled * unit_two, axis=-1, keepdims=True))
    grads[...] = cot[...].astype(f32) + back
    low[...] = grads[...].astype(bf16)
    make_bias(bias, lengths, b * 2 + c)

    def weight_reduce(k, first, cols):
        low_cols = cols // 256 * 128

        def span(p):
            return (0, cols) if p is None else ((0, low_cols) if p == 0 else (low_cols, cols - low_cols))

        def chunk(line, kind, p):
            start, size = span(p)
            rows = pl.multiple_of(ways.chip(line, kind) * chip_rows, 16)
            return part.at[pl.ds(rows, chip_rows), pl.ds(first + start, size)]

        def cut(ref, u, p):
            start, size = span(p)
            return ref.at[u, :, pl.ds(first + start, size)]

        return Reduce(
            ways, chunk, cut, pq, xr, yr, dz, lambda slot: zr.at[slot, :, pl.ds(first, cols)],
            (lambda i: r_send.at[k, i], lambda i: r_recv.at[k, i]),
        )

    def small_span(p):
        first = chip_rows // 32 * 16
        return (0, chip_rows) if p is None else ((0, first) if p == 0 else (first, chip_rows - first))

    def small_chunk(line, kind, p):
        start, size = small_span(p)
        return s_part.at[pl.ds(pl.multiple_of(ways.chip(line, kind) * chip_rows + start, 16), size)]

    def small_cut(ref, u, p):
        start, size = small_span(p)
        return ref.at[u, pl.ds(start, size)]

    small_reduce = Reduce(
        ways, small_chunk, small_cut, s_pq, s_xr, s_yr, s_dz, lambda slot: s_zr.at[slot],
        (lambda i: r_send.at[2, i], lambda i: r_recv.at[2, i]),
    )
    qkv_reduce = weight_reduce(0, 0, 3 * half)
    wo_reduce = weight_reduce(1, 3 * half, half)

    def across(k):
        return remote(staged.at[k % 2], landed.at[k % 3], c_send.at[k], c_recv.at[k], ways.to_c)

    def swapped(k):
        across(k).wait_recv()

        def body(i, carry):
            rows = pl.ds(pl.multiple_of(i * chip_rows, 16), chip_rows)
            accumulate(part.at[rows, pl.ds(k * half, half)], [landed.at[k % 3, rows]])
            return carry

        lax.fori_loop(0, width // chip_rows, body, 0)
        if k == 3:
            pl.semaphore_signal(credit, inc=1, device_id=ways.to_c, device_id_type=MESH)

    later = []

    def service(n=1):
        for _ in range(n):
            if later:
                later.pop(0)()

    def columns(core):
        return pl.ds(pl.multiple_of(core * half, 128), half)

    def weight_grad(k, left, right):
        if k < 2:
            across(k + 2).wait_send()
        staged[k % 2] = dot_tn(left, right[:, columns(oc)]).astype(bf16)
        if k == 0:
            pl.semaphore_wait(credit, 1)
        across(k).start()
        part[:, pl.ds(k * half, half)] = dot_tn(left, right[:, columns(c)]).astype(bf16)

    o_events[1]()
    weight_grad(3, attended[...], low)
    for copy in wo_loads:
        copy.wait()
    datt[...] = (
        dot_nt(low[:, 0:half], part[:, 0:half]) + dot_nt(low[:, half:width], part[:, half:width])
    ).astype(bf16)
    wo_events = wo_reduce.events()
    later.append(lambda: swapped(3))
    for k in range(6):
        later.append(o_events[k + 2])
        later.extend(wo_events[:2] if k == 0 else [wo_events[k + 1]])
    for copy in kv_loads:
        copy.wait()

    own_rows = pl.ds(pl.multiple_of((b * 2 + c) * count, count), count)
    for h in range(heads):
        cols = pl.ds(h * 128, 128)
        key, val, query = dk[:, cols], dv[:, cols], q[:, cols]
        probs = softmax_rows(dot_nt(query, key) * scale + bias[...])
        dprobs = dot_nt(datt[:, cols], val)
        dscores = (
            probs * (dprobs - jnp.sum(probs * dprobs, axis=-1, keepdims=True))
        ).astype(bf16)
        dq[:, cols] = turn(
            dense_dot(dscores, key) * scale, cosine[own_rows, :], -sine[own_rows, :]
        ).astype(bf16)
        dk[:, cols] = turn(dot_tn(dscores, query) * scale, cosine[...], -sine[...]).astype(bf16)
        dv[:, cols] = dot_tn(probs.astype(bf16), datt[:, cols]).astype(bf16)
        if h in (1, 3, 4, 6, 8, 9):
            service()
    weight_grad(2, normed[...], dv)
    weight_grad(1, normed[...], dk)
    service()
    weight_grad(0, normed[own_rows, :], dq)
    for k in (2, 1, 0):
        swapped(k)
    qkv_events = qkv_reduce.events()
    qkv_events[0]()
    later = [later[0], later[1], qkv_events[1]] + later[2:]

    for copy in wall_loads:
        copy.wait()
    for t in range(4):
        rows = slice(t * count, (t + 1) * count)
        total = jnp.zeros((count, width), f32)
        for h in range(2):
            mine = slice(h * half, (h + 1) * half)
            total = total + dot_nt(dk[rows, mine], weight(h, 1)) + dot_nt(dv[rows, mine], weight(h, 2))
        dn_part[t] = total.astype(bf16)
        x = group[t].astype(f32)
        unit = x * lax.rsqrt(jnp.mean(x * x, axis=-1, keepdims=True) + epsilon)
        gain_row = jnp.sum(total * unit, axis=0, keepdims=True)
        if t == 0:
            rows_t[experts : experts + 1, :] = gain_row
        else:
            rows_t[experts : experts + 1, :] += gain_row
        service()

    def dn_copy(k, src, dst, to):
        return remote(src, dst, d_send.at[k], d_recv.at[k], to)

    dn_copies = [
        dn_copy(0, dn_part.at[b * 2 + oc], dn_other.at[0], ways.to_c),
        dn_copy(1, dn_part.at[ob * 2 + oc], dn_other.at[1], ways.to_c),
    ]
    for copy in dn_copies:
        copy.start()
    own = jnp.zeros((count, width), f32)
    for h in range(2):
        own = own + dot_nt(dq[:, h * half : (h + 1) * half], weight(h, 0))
    x = group[b * 2 + c].astype(f32)
    r1 = lax.rsqrt(jnp.mean(x * x, axis=-1, keepdims=True) + epsilon)
    unit_one = x * r1
    rows_t[experts : experts + 1, :] += jnp.sum(own * unit_one, axis=0, keepdims=True)
    s_part[...] = jnp.transpose(rows_t[...]).astype(bf16)
    small_swap = remote(s_part, s_landed, c_send.at[4], c_recv.at[4], ways.to_c)
    small_swap.start()
    service()
    dn_copies[1].wait_recv()
    accumulate(dn_part.at[ob * 2 + c], [dn_other.at[1]])
    dn_copies.append(dn_copy(2, dn_part.at[ob * 2 + c], dn_far, ways.to_b))
    dn_copies[2].start()
    dn_copies[0].wait_recv()
    small_swap.wait()
    accumulate(s_part, [s_landed])
    service(len(later))
    small_events = small_reduce.events()
    shared_events = [shared_blocks] + e_events[1:]
    for k in range(2, len(qkv_events)):
        later.extend([small_events[k - 2], shared_events[k - 2], qkv_events[k]])
    later.extend(small_events[-2:] + [shared_finish])
    service(6)
    dn_copies[2].wait_recv()
    total = (
        own
        + dn_part[b * 2 + c].astype(f32)
        + dn_other[0].astype(f32)
        + dn_far[...].astype(f32)
    )
    scaled = total * gain_one
    input_grad[...] = grads[...] + r1 * (
        scaled - unit_one * jnp.mean(scaled * unit_one, axis=-1, keepdims=True)
    )
    service(len(later))

    theirs = pl.ds(pl.multiple_of(oc * d_rows, 8), d_rows)
    mine = pl.ds(pl.multiple_of(c * d_rows, 8), d_rows)
    fin[:, pl.ds(3 * half, half)] = wo_reduce.total()
    fin[:, pl.ds(0, 3 * half)] = qkv_reduce.total()
    fin_copy = remote(fin.at[theirs], fin_other, c_send.at[5], c_recv.at[5], ways.to_c)
    fin_copy.start()
    s_total = small_reduce.total()
    small_out[...] = jnp.where(c == 0, s_total[:d_rows], s_total[d_rows:])
    for k, out in enumerate((gq, gk, gv, go)):
        out[:, columns(c)] = fin[mine, pl.ds(k * half, half)]
    fin_copy.wait_recv()
    for k, out in enumerate((gq, gk, gv, go)):
        out[:, columns(oc)] = fin_other[:, pl.ds(k * half, half)]
    for r in (qkv_reduce, wo_reduce, small_reduce, o_reduce):
        r.drain()
    for copy in dn_copies + [fin_copy]:
        copy.wait_send()
    exchange.drain()
    for k in range(2):
        across(k).wait_send()


def back_call(
    lengths, dn2, residual, cot, group, small_t, router_part, attended, q, normed, cosine, sine,
    keys, vals, wall, outs, dw_own, dw_sib, d_rows, experts, scale, sh, collective_id,
):
    lines = lax.axis_size("ep") // 2
    count, width = cot.shape
    half = width // 2
    chip_rows = 2 * d_rows
    group_len = 4 * count
    anywhere = pl.BlockSpec(memory_space=pl.ANY)
    vmem = pl.BlockSpec(memory_space=pltpu.VMEM)
    smem = pl.BlockSpec(memory_space=pltpu.SMEM)
    shape = jax.ShapeDtypeStruct
    dma = pltpu.SemaphoreType.DMA

    def landing(rows, cols):
        return [pltpu.VMEM((n, rows, cols), bf16) for n in (2, lines, lines, 2, lines - 1)]

    return pl.pallas_call(
        functools.partial(back_kernel, lines, experts, scale, sh),
        out_shape=(
            shape((count, width), bf16),
            shape((count, width), f32),
            shape((d_rows, width), f32),
            shape((d_rows, width), f32),
            shape((d_rows, width), f32),
            shape((d_rows, width), f32),
            shape((d_rows, 128), f32),
            shape((d_rows, 8 * lines * sh), f32),
            shape((d_rows, 8 * lines * sh), f32),
            shape(dw_sib.shape, f32),
        ),
        in_specs=[smem] + [vmem] * 11 + [anywhere] * 6,
        out_specs=(vmem,) * 9 + (anywhere,),
        scratch_shapes=[
            pltpu.VMEM((width, 6 * half), bf16),
            pltpu.VMEM((width, 4 * half), bf16),
            pltpu.VMEM((2, width, half), bf16),
            pltpu.VMEM((3, width, half), bf16),
            *landing(chip_rows, 4 * half),
            pltpu.VMEM((chip_rows, 4 * half), f32),
            pltpu.VMEM((d_rows, 4 * half), f32),
            pltpu.VMEM((width, 128), bf16),
            pltpu.VMEM((width, 128), bf16),
            *landing(chip_rows, 128),
            pltpu.VMEM(outs.shape, bf16),
            *landing(count, width),
            pltpu.VMEM((count, width), f32),
            pltpu.VMEM((count, width), bf16),
            pltpu.VMEM((count, width), bf16),
            pltpu.VMEM((count, width), bf16),
            pltpu.VMEM((group_len, width), bf16),
            pltpu.VMEM((group_len, width), bf16),
            pltpu.VMEM((4, count, width), bf16),
            pltpu.VMEM((2, count, width), bf16),
            pltpu.VMEM((count, width), bf16),
            pltpu.VMEM((count, group_len), f32),
            pltpu.VMEM((128, width), f32),
            *exchange_scratch(lines, -(-d_rows // 16) * 16),
            dma((7,)),
            dma((7,)),
            dma((4, 8 * lines)),
            dma((4, 8 * lines)),
            dma((3,)),
            dma((3,)),
            dma((7 + lines,)),
            dma((7 + lines,)),
            dma((11,)),
            pltpu.SemaphoreType.REGULAR,
        ],
        compiler_params=pltpu.CompilerParams(
            collective_id=collective_id, has_side_effects=True, vmem_limit_bytes=63 * 2**20
        ),
        name="back",
    )(
        lengths, dn2, residual, cot, group, small_t, router_part, attended, q, normed, cosine, sine,
        keys, vals, wall, outs, dw_own, dw_sib,
    )


def documents(positions, lengths):
    seq_ends = jnp.cumsum(lengths)
    doc_index = (positions >= seq_ends[0]).astype(jnp.int32) + (positions >= seq_ends[1]).astype(
        jnp.int32
    )
    seq_starts = jnp.where(doc_index == 0, 0, jnp.where(doc_index == 1, seq_ends[0], seq_ends[1]))
    return (doc_index, positions - seq_starts)


def rotary_tables(offsets, head_dim):
    half_dim = head_dim // 2
    frequency = 10000.0 ** (-2.0 * jnp.arange(half_dim, dtype=f32) / head_dim)
    angles = offsets.astype(f32)[:, None] * frequency[None, :]
    return (jnp.cos(angles)[:, None, :], jnp.sin(angles)[:, None, :])


def rotate(values, cosine, sine_table):
    half_dim = values.shape[-1] // 2
    first_half = values[..., :half_dim]
    second_half = values[..., half_dim:]
    return jnp.concatenate(
        [
            first_half * cosine - second_half * sine_table,
            first_half * sine_table + second_half * cosine,
        ],
        axis=-1,
    )


def norm_back(grad_normed, unit_rows, inverse, gain):
    scaled = grad_normed * gain
    return inverse * (scaled - unit_rows * jnp.mean(scaled * unit_rows, axis=-1, keepdims=True))


def dot(left, right, contract):
    return lax.dot_general(left, right, ((contract[0], contract[1]), ((), ())), preferred_element_type=f32)


def dense_dot(left, right):
    return dot(left, right, ((1,), (0,)))


def dot_nt(left, right):
    return dot(left, right, ((1,), (1,)))


def dot_tn(left, right):
    return dot(left, right, ((0,), (0,)))


def any_slice(
    hidden_in,
    seq_lengths,
    expert_ids,
    attn_gain,
    w_query,
    w_key,
    w_value,
    w_out,
    ffn_gain,
    shared_gate,
    shared_up,
    shared_down,
    router,
    expert_gate,
    expert_up,
    expert_down,
    cotangent,
):
    tok_count, model_width = hidden_in.shape
    eps, tps = lax.axis_size("ep"), lax.axis_size("tp")
    devices = eps * tps
    exp_local, exp_hidden = expert_gate.shape[:2]
    experts = exp_local * eps
    group_len = tps * tok_count
    tokens = devices * tok_count
    d_rows = w_query.shape[0]
    width = w_query.shape[1]
    sh_rows = shared_down.shape[0]
    head_dim = width // HEADS
    attn_scale = head_dim ** (-0.5)

    flat = jnp.concatenate([router.reshape(-1), attn_gain, ffn_gain])
    small_len = -(-flat.shape[0] // model_width) * model_width
    small = jnp.pad(flat, (0, small_len - flat.shape[0])).reshape(-1, model_width)
    small = jnp.pad(small, ((0, -small.shape[0] % 16), (0, 0)))
    weights = jnp.concatenate([w_query, w_key, w_value, w_out], axis=1)

    all_weights, all_small, all_cot = [
        lax.all_gather(v, AXES, axis=0) for v in (weights, small, cotangent)
    ]
    group_hidden = lax.all_gather(hidden_in, "tp", axis=0)
    all_weights = all_weights.reshape(devices * d_rows, 4 * width)
    full_query = all_weights[:, :width]
    full_key = all_weights[:, width : 2 * width]
    full_value = all_weights[:, 2 * width : 3 * width]
    full_out = all_weights[:, 3 * width :]
    all_small = all_small.reshape(devices, -1)
    n_router = d_rows * experts
    full_router = all_small[:, :n_router].reshape(devices * d_rows, experts)
    gain_one = all_small[:, n_router : n_router + d_rows].reshape(-1).astype(f32)
    gain_two = all_small[:, n_router + d_rows : n_router + 2 * d_rows].reshape(-1).astype(f32)
    cot_all = all_cot.reshape(-1, model_width)

    shared_cols = jnp.stack([shared_gate, shared_up], axis=1).reshape(d_rows, 2, devices, sh_rows)
    shared_cols = lax.all_to_all(
        shared_cols.transpose(2, 1, 3, 0), AXES, split_axis=0, concat_axis=0, tiled=True
    )
    shared_t = shared_cols.transpose(1, 2, 0, 3).reshape(2, sh_rows, model_width)

    lengths = seq_lengths[0]
    tp_index = lax.axis_index("tp")
    own_pos = tp_index * tok_count + jnp.arange(tok_count, dtype=jnp.int32)
    all_pos = jnp.arange(group_len, dtype=jnp.int32)
    own_doc, own_offset = documents(own_pos, lengths)
    all_doc, all_offset = documents(all_pos, lengths)
    allowed = (own_doc[:, None] == all_doc[None, :]) & (own_pos[:, None] >= all_pos[None, :])
    cosine, sine_table = rotary_tables(own_offset, head_dim)
    cosine_all, sine_all = rotary_tables(all_offset, head_dim)

    inputs = hidden_in.astype(f32)
    inverse_one = lax.rsqrt(jnp.mean(inputs * inputs, axis=-1, keepdims=True) + epsilon)
    unit_one = inputs * inverse_one
    normed = (unit_one * gain_one).astype(bf16)
    group_in = group_hidden.reshape(group_len, model_width).astype(f32)
    group_unit = group_in * lax.rsqrt(jnp.mean(group_in * group_in, axis=-1, keepdims=True) + epsilon)
    group_normed = (group_unit * gain_one).astype(bf16)

    queries = rotate(
        dense_dot(normed, full_query).reshape(tok_count, HEADS, head_dim), cosine, sine_table
    ).astype(bf16)
    key_rows = rotate(
        dense_dot(group_normed, full_key).reshape(group_len, HEADS, head_dim), cosine_all, sine_all
    ).astype(bf16)
    value_rows = dense_dot(group_normed, full_value).astype(bf16).reshape(group_len, HEADS, head_dim)

    def masked_scores():
        raw_scores = (
            jnp.einsum("qhd,khd->hqk", queries, key_rows, preferred_element_type=f32) * attn_scale
        )
        return jnp.where(allowed[None], raw_scores, -1e30)

    scores = masked_scores()
    row_peak = jnp.max(scores, axis=-1, keepdims=True)
    row_total = jnp.sum(jnp.exp(scores - row_peak), axis=-1, keepdims=True)
    softmaxed = jnp.exp(scores - row_peak) / row_total
    attended = (
        jnp.einsum("hqk,khd->qhd", softmaxed.astype(bf16), value_rows, preferred_element_type=f32)
        .reshape(tok_count, width)
        .astype(bf16)
    )
    residual = inputs + dense_dot(attended, full_out)
    inverse_two = lax.rsqrt(jnp.mean(residual * residual, axis=-1, keepdims=True) + epsilon)
    unit_two = residual * inverse_two
    normed_two = (unit_two * gain_two).astype(bf16)

    affinity = jax.nn.softmax(dense_dot(normed_two, full_router), axis=-1)
    expert_range = jnp.arange(experts, dtype=jnp.int32)
    named = jnp.any(expert_ids[:, :, None] == expert_range[None, None, :], axis=1)
    signed = jnp.where(named, affinity, -affinity)

    first_expert = lax.axis_index("ep") * exp_local
    n_routed = exp_local * exp_hidden
    hidden = n_routed + sh_rows
    gate_w = jnp.concatenate([expert_gate.reshape(n_routed, model_width), shared_t[0]])
    up_w = jnp.concatenate([expert_up.reshape(n_routed, model_width), shared_t[1]])
    down_w = jnp.concatenate([expert_down.reshape(n_routed, model_width), shared_down])

    def mixture(rows, cot_rows, signed):
        count = rows.shape[0]
        mine = lax.dynamic_slice_in_dim(signed, first_expert, exp_local, axis=1)
        mine_named = mine > 0
        gates = jnp.where(mine_named, mine, 0.0)
        scale = jnp.concatenate(
            [jnp.repeat(gates, exp_hidden, axis=1), jnp.ones((count, sh_rows), f32)], axis=1
        )
        gate_pre = dot_nt(rows, gate_w)
        up_pre = dot_nt(rows, up_w)
        sigma = jax.nn.sigmoid(gate_pre)
        silu = gate_pre * sigma
        act = silu * up_pre
        act_scaled = (act * scale).astype(bf16)
        out_part = dense_dot(act_scaled, down_w).astype(bf16)
        grad_hidden = dot_nt(cot_rows, down_w)
        grad_gates = jnp.sum(
            (act * grad_hidden)[:, :n_routed].reshape(count, exp_local, exp_hidden), axis=-1
        )
        grad_gates = jnp.where(mine_named, grad_gates, 0.0)
        grad_hidden = grad_hidden * scale
        grad_gate_pre = (grad_hidden * up_pre * sigma * (1.0 + gate_pre * (1.0 - sigma))).astype(
            bf16
        )
        grad_up_pre = (grad_hidden * silu).astype(bf16)
        affinity_all = jnp.abs(signed)
        grad_aff = lax.dynamic_update_slice_in_dim(
            jnp.zeros((count, experts), f32), grad_gates, first_expert, axis=1
        )
        grad_logits = (
            affinity_all * (grad_aff - jnp.sum(affinity_all * grad_aff, axis=-1, keepdims=True))
        ).astype(bf16)
        dn2_part = (
            dense_dot(grad_gate_pre, gate_w)
            + dense_dot(grad_up_pre, up_w)
            + dot_nt(grad_logits, full_router)
        ).astype(bf16)
        sums = (
            dot_tn(act_scaled, cot_rows),
            dot_tn(grad_gate_pre, rows),
            dot_tn(grad_up_pre, rows),
            dot_tn(rows, grad_logits),
        )
        return out_part, dn2_part, sums

    rows, signed_all = [lax.all_gather(v, AXES, axis=0, tiled=True) for v in (normed_two, signed)]
    blocks = max(1, tokens * hidden * 4 // 2**23)
    while tokens % blocks:
        blocks += 1

    def step(totals, block):
        out_block, dn2_block, sums = mixture(*block)
        return jax.tree.map(jnp.add, totals, sums), (out_block, dn2_block)

    zeros = (jnp.zeros((hidden, model_width), f32),) * 3 + (
        jnp.zeros((model_width, experts), f32),
    )
    sums, (out_part, dn2_part) = lax.scan(
        step,
        zeros,
        jax.tree.map(
            lambda v: v.reshape((blocks, -1) + v.shape[1:]), (rows, cot_all, signed_all)
        ),
    )
    grad_down, grad_gate, grad_up, router_part = sums
    routed_sum, grad_normed_two = [
        lax.psum_scatter(v.reshape(tokens, model_width), AXES, tiled=True).astype(f32)
        for v in (out_part, dn2_part)
    ]
    layer_output = (residual + routed_sum).astype(bf16)

    gain_two_part = jnp.sum(grad_normed_two * unit_two, axis=0)
    grad_resid = cotangent.astype(f32) + norm_back(grad_normed_two, unit_two, inverse_two, gain_two)
    grad_resid_low = grad_resid.astype(bf16)
    wout_part = dot_tn(attended, grad_resid_low)
    grad_att = dot_nt(grad_resid_low, full_out).astype(bf16).reshape(tok_count, HEADS, head_dim)
    softmax_again = jnp.exp(masked_scores() - row_peak) / row_total
    grad_soft = jnp.einsum("qhd,khd->hqk", grad_att, value_rows, preferred_element_type=f32)
    grad_scores = (
        softmax_again * (grad_soft - jnp.sum(softmax_again * grad_soft, axis=-1, keepdims=True))
    ).astype(bf16)
    grad_queries = (
        jnp.einsum("hqk,khd->qhd", grad_scores, key_rows, preferred_element_type=f32) * attn_scale
    )
    grad_key_rows = (
        jnp.einsum("hqk,qhd->khd", grad_scores, queries, preferred_element_type=f32) * attn_scale
    )
    grad_value_rows = jnp.einsum(
        "hqk,qhd->khd", softmax_again.astype(bf16), grad_att, preferred_element_type=f32
    )
    grad_q_pre = rotate(grad_queries, cosine, -sine_table).reshape(tok_count, width).astype(bf16)
    grad_k_pre = rotate(grad_key_rows, cosine_all, -sine_all).reshape(group_len, width).astype(bf16)
    grad_v_pre = grad_value_rows.reshape(group_len, width).astype(bf16)
    wq_part = dot_tn(normed, grad_q_pre)
    wk_part = dot_tn(group_normed, grad_k_pre)
    wv_part = dot_tn(group_normed, grad_v_pre)
    own_normed_grad = dot_nt(grad_q_pre, full_query)
    group_normed_grad = dot_nt(grad_k_pre, full_key) + dot_nt(grad_v_pre, full_value)
    gain_one_part = jnp.sum(own_normed_grad * unit_one, axis=0) + jnp.sum(
        group_normed_grad * group_unit, axis=0
    )

    weight_part = jnp.concatenate([wq_part, wk_part, wv_part, wout_part], axis=1).astype(bf16)
    small_part = jnp.concatenate(
        [
            router_part.reshape(devices, n_router),
            gain_one_part.reshape(devices, d_rows),
            gain_two_part.reshape(devices, d_rows),
        ],
        axis=1,
    )
    small_part = jnp.pad(small_part, ((0, 0), (0, small_len - small_part.shape[1])))
    small_part = small_part.reshape(devices, -1, model_width)
    small_part = jnp.pad(small_part, ((0, 0), (0, -small_part.shape[1] % 16), (0, 0))).astype(bf16)
    weight_part = weight_part.reshape(devices, d_rows, 4 * width)
    group_part = group_normed_grad.astype(bf16).reshape(tps, tok_count, model_width)
    weight_sum, small_sum = [
        lax.psum_scatter(v, AXES).astype(f32) for v in (weight_part, small_part)
    ]
    normed_grad_sum = lax.psum_scatter(group_part, "tp").astype(f32)
    grad_normed = own_normed_grad + normed_grad_sum
    input_grad = grad_resid + norm_back(grad_normed, unit_one, inverse_one, gain_one)
    small_sum = small_sum.reshape(-1)

    shared_back = jnp.stack([grad_gate[n_routed:], grad_up[n_routed:]])
    shared_back = shared_back.reshape(2, sh_rows, devices, d_rows).transpose(2, 0, 1, 3)
    shared_back = lax.all_to_all(shared_back, AXES, split_axis=0, concat_axis=0, tiled=True)
    shared_back = shared_back.transpose(1, 3, 0, 2).reshape(2, d_rows, devices * sh_rows)

    return (
        layer_output,
        input_grad,
        small_sum[n_router : n_router + d_rows],
        weight_sum[:, :width],
        weight_sum[:, width : 2 * width],
        weight_sum[:, 2 * width : 3 * width],
        weight_sum[:, 3 * width :],
        small_sum[n_router + d_rows : n_router + 2 * d_rows],
        shared_back[0],
        shared_back[1],
        grad_down[n_routed:],
        small_sum[:n_router].reshape(d_rows, experts),
        grad_gate[:n_routed].reshape(expert_gate.shape),
        grad_up[:n_routed].reshape(expert_up.shape),
        grad_down[:n_routed].reshape(expert_down.shape),
    )


def small_slice(
    hidden_in,
    seq_lengths,
    expert_ids,
    attn_gain,
    w_query,
    w_key,
    w_value,
    w_out,
    ffn_gain,
    shared_gate,
    shared_up,
    shared_down,
    router,
    expert_gate,
    expert_up,
    expert_down,
    cotangent,
):
    tok_count, model_width = hidden_in.shape
    eps, tps = lax.axis_size("ep"), lax.axis_size("tp")
    devices = eps * tps
    exp_local, exp_hidden = expert_gate.shape[:2]
    experts = exp_local * eps
    group_len = tps * tok_count
    tokens = devices * tok_count
    d_rows = w_query.shape[0]
    width = w_query.shape[1]
    sh_rows = shared_down.shape[0]
    head_dim = width // HEADS
    attn_scale = head_dim ** (-0.5)

    lanes = 128
    vectors = jnp.stack([attn_gain, ffn_gain], axis=1)
    small = jnp.concatenate([router, vectors], axis=1)
    small = jnp.pad(small, ((0, 0), (0, lanes - small.shape[1])))
    (
        w_all, cot_all, normed_two, aux, small_t, residual, attended, queries, key_rows, value_rows,
        group_normed, cos_all, sin_all, group_hidden, shared,
    ) = front_call(
        seq_lengths, expert_ids, hidden_in, small, (w_query, w_key, w_value, w_out),
        (shared_gate, shared_up, shared_down), cotangent, experts, attn_scale, 0,
    )
    first_expert = lax.axis_index("ep") * exp_local
    n_routed = exp_local * exp_hidden
    hidden = n_routed + sh_rows
    h_core = n_routed + shared.shape[1]
    owner = jnp.arange(h_core, dtype=jnp.int32)
    owner = jnp.where(owner < n_routed, first_expert + owner // exp_hidden, experts)
    owner = jnp.concatenate([owner, owner])
    sel_t = (owner[:, None] == jnp.arange(lanes, dtype=jnp.int32)[None, :]).astype(bf16)
    sel = jnp.concatenate([sel_t[:, :experts].T, jnp.eye(experts, lanes, dtype=bf16)], axis=1)
    sel = jnp.concatenate([sel, sel])
    ones = (jnp.arange(2 * h_core, dtype=jnp.int32) % h_core)[None, :]
    ones = ((ones >= n_routed) & (ones < hidden)).astype(f32)
    token_grads, out_parts, grads_here, grads_away, router_sum = mixture_call(
        normed_two,
        aux,
        cot_all,
        [w.reshape(n_routed, model_width) for w in (expert_gate, expert_up, expert_down)],
        shared,
        sel,
        sel_t,
        small_t,
        ones,
        2,
    )
    (
        layer_output, input_grad, grad_q, grad_k, grad_v, grad_o, small_sum, grad_sg, grad_su, grads_there,
    ) = back_call(
        seq_lengths, token_grads, residual, cotangent, group_hidden, small_t, router_sum, attended,
        queries, group_normed, cos_all, sin_all, key_rows, value_rows, w_all, out_parts,
        grads_here, grads_away, d_rows, experts, attn_scale, sh_rows, 3,
    )
    grad_gate, grad_up, grad_down = [
        (grads_here[k, :n_routed] + grads_there[k, :n_routed]).reshape(expert_gate.shape)
        for k in range(3)
    ]
    grad_sd = grads_here[2, n_routed:hidden] + grads_there[2, n_routed:hidden]

    return (
        layer_output,
        input_grad,
        small_sum[:, experts],
        grad_q,
        grad_k,
        grad_v,
        grad_o,
        small_sum[:, experts + 1],
        grad_sg,
        grad_su,
        grad_sd,
        small_sum[:, :experts],
        grad_gate,
        grad_up,
        grad_down,
    )


def solution(mesh):
    rows = P(AXES, None)
    vector = P(AXES)
    experts = P("ep", "tp", None)
    small = mesh.shape["ep"] == 8 and mesh.shape["tp"] == 4
    return jax.shard_map(
        small_slice if small else any_slice,
        mesh=mesh,
        in_specs=(
            rows, P("ep", None), rows, vector, rows, rows, rows, rows, vector,
            rows, rows, rows, rows, experts, experts, experts, rows,
        ),
        out_specs=(
            rows, rows, vector, rows, rows, rows, rows, vector,
            rows, rows, rows, rows, experts, experts, experts,
        ),
        check_vma=False,
    )
```

```python
import functools

import jax
import jax.numpy as jnp
from jax import lax
from jax.experimental import pallas as pl
from jax.experimental.pallas import tpu as pltpu
from jax.sharding import PartitionSpec as P

HEADS = 10
AXES = ("ep", "tp")
MESH = pl.DeviceIdType.MESH
VMEM_BUDGET = 56 * 2**20

epsilon = 1e-06

bf16 = jnp.bfloat16
f32 = jnp.float32


def place():
    ep, tp = lax.axis_index("ep"), lax.axis_index("tp")
    return ep // 2, ep % 2, tp // 2, tp % 2


def device(line, a, b, c):
    return (line * 2 + a, b * 2 + c)


def number(line, a, b, c):
    return ((line * 2 + a) * 2 + b) * 2 + c


def greet(partners):
    barrier = pltpu.get_barrier_semaphore()
    for partner in partners:
        pl.semaphore_signal(barrier, inc=1, device_id=partner, device_id_type=MESH)
    pl.semaphore_wait(barrier, len(partners))


O, X, Y, D = 0, 1, 2, 3


def visit_order(lines):
    return [
        sorted(range(lines), key=lambda other: (abs(other - z), other != z ^ 1)) for z in range(lines)
    ]


def lookup(table, index):
    out = jnp.int32(table[0])
    for k in range(1, len(table)):
        out = jnp.where(index == k, jnp.int32(table[k]), out)
    return out


def pick(values, index):
    out = values[0]
    for k in range(1, len(values)):
        out = jnp.where(index == k, values[k], out)
    return out


class Ways:
    def __init__(self, lines):
        self.lines = lines
        z, a, b, c = self.spot = place()
        oa, ob, oc = 1 - a, 1 - b, 1 - c
        self.to_b, self.to_a = device(z, a, ob, c), device(z, oa, b, c)
        self.to_c = device(z, a, b, oc)
        self.up_next = device(lax.rem(z + 1, lines), a, b, c)
        self.down_next = device(lax.rem(z + lines - 1, lines), a, b, c)
        self.peers = [device(lax.rem(z + s, lines), a, b, c) for s in range(1, lines)]
        table = visit_order(lines)
        self.zs = [lookup([table[k][u] for k in range(lines)], z) for u in range(lines)]
        self.column = ((a, b), (a, ob), (oa, b), (oa, ob))
        self.pair = device(z + 1 - 2 * lax.rem(z, 2), a, b, c)
        outer = (z == 0) | (z == lines - 1)
        self.carried = [True, False, outer, jnp.logical_not(outer)]

    def greet(self):
        greet([self.to_b, self.to_a, self.to_c] + self.peers)

    def chip(self, line, kind):
        a, b = self.column[kind]
        return (line * 2 + a) * 2 + b


def when(condition, act):
    if condition is True:
        act()
    elif condition is not False:

        @pl.when(condition)
        def _():
            act()


def other(condition):
    return not condition if isinstance(condition, bool) else jnp.logical_not(condition)


def remote(src, dst, send_sem, recv_sem, to):
    return pltpu.make_async_remote_copy(
        src, dst, send_sem, recv_sem, device_id=to, device_id_type=MESH
    )


class Gather:
    def __init__(self, ways, chunk, sems, own=None, relative=False, across=False):
        self.ways, self.chunk, self.own = ways, chunk, own
        self.send_sem, self.recv_sem = sems
        self.relative, self.across_core = relative, across

    def copy(self, slot, step, src, dst, to):
        k = slot * self.ways.lines + step
        return remote(src, dst, self.send_sem(k), self.recv_sem(k), to)

    def hop(self, slot, step, kind, to_kind, line, to, part=None, own=False):
        src = self.own if own and self.own is not None else self.chunk(line, kind, part, False)
        dst = self.chunk(line, to_kind if self.relative else kind, part, False)
        return self.copy(slot, step, src, dst, to)

    def sends(self, u):
        w, own = self.ways, u == 0
        line, carried = w.zs[u], w.carried[u]
        copies = {
            "X": (True, lambda: self.hop(0, u, O, X, line, w.to_b, own=own)),
            "Y": (True, lambda: self.hop(1, u, O, Y, line, w.to_a, own=own)),
            "p": (carried, lambda: self.hop(2, u, X, D, line, w.to_a, 0)),
            "q": (carried, lambda: self.hop(3, u, Y, D, line, w.to_b, 1)),
            "pair": (carried, lambda: self.hop(11, 1 if own else u, D, D, line, w.pair)),
        }
        if self.across_core:

            def across(slot, kind):
                here = self.chunk(line, kind, None, False)
                src = self.own if kind == O and own and self.own is not None else here
                return self.copy(slot, u, src, here, w.to_c)

            for kind, slot in ((O, 6), (X, 7), (Y, 8), (D, 9)):
                copies[kind] = (True, lambda slot=slot, kind=kind: across(slot, kind))
        return copies

    def send(self, u, *names, condition=True):
        copies = self.sends(u)
        for name in names:
            if name in copies:
                always, make = copies[name]
                when(always if condition is True else condition, lambda: make().start())

    def arrival(self, slot, step, kind, line, part=None, other=False):
        here = self.chunk(line, kind, part, other)
        self.copy(slot, step, here, here, self.ways.to_c).wait_recv()

    def send_own(self, u):
        self.send(u, "X", "Y", O)

    def xy_event(self, u):
        line = self.ways.zs[u]
        self.arrival(0, u, X, line)
        self.send(u, "p")
        self.arrival(1, u, Y, line)
        self.send(u, "q", X, Y)

    def diag_carried(self, u):
        line, carried = self.ways.zs[u], self.ways.carried[u]

        def halves():
            self.arrival(2, u, D, line, 0)
            self.arrival(3, u, D, line, 1)

        when(carried, halves)
        self.send(u, "pair")
        self.send(u, D, condition=carried)

    def diag_handed(self, u):
        handed = other(self.ways.carried[u])
        when(handed, lambda: self.arrival(11, u, D, self.ways.zs[u]))
        self.send(u, D, condition=handed)

    def chain_up(self, k):
        w = self.ways
        return self.hop(4, k, O, O, w.spot[0] - (k - 1), w.up_next, own=k == 1)

    def chain_down(self, k):
        w = self.ways
        return self.hop(5, k, O, O, w.spot[0] + (k - 1), w.down_next, own=k == 1)

    def chain_start(self, k):
        z, lines = self.ways.spot[0], self.ways.lines
        if k >= lines:
            return

        @pl.when((z >= k - 1) & (z + 1 < lines))
        def _():
            self.chain_up(k).start()

        @pl.when((z + k - 1 < lines) & (z > 0))
        def _():
            self.chain_down(k).start()

    def chain_event(self, k):
        z, lines = self.ways.spot[0], self.ways.lines

        @pl.when(z >= k)
        def _():
            self.arrival(4, k, O, z - k)

        @pl.when(z + k < lines)
        def _():
            self.arrival(5, k, O, z + k)

        self.chain_start(k + 1)

    def begin(self):
        self.send_own(0)
        self.chain_start(1)

    def events(self):
        out = [
            lambda: (self.xy_event(0), self.chain_event(1), self.send_own(1)),
            lambda: (self.diag_carried(0), self.chain_event(2), self.send_own(2)),
            lambda: (self.xy_event(1), self.chain_event(3), self.send_own(3)),
            lambda: (self.xy_event(2), self.diag_handed(1)),
            lambda: (self.diag_carried(2), self.xy_event(3)),
            lambda: (self.diag_carried(3), self.diag_handed(2)),
            lambda: self.diag_handed(3),
        ]
        return out

    def other_core(self):
        if self.across_core:
            for u in range(self.ways.lines):
                for slot, kind in ((6, O), (7, X), (8, Y), (9, D)):
                    self.arrival(slot, u, kind, self.ways.zs[u], None, True)

    def drain_unit(self, u):
        for condition, make in self.sends(u).values():
            when(condition, lambda make=make: make().wait_send())

    def drain_chain(self, k):
        z, lines = self.ways.spot[0], self.ways.lines

        @pl.when((z >= k - 1) & (z + 1 < lines))
        def _():
            self.chain_up(k).wait_send()

        @pl.when((z + k - 1 < lines) & (z > 0))
        def _():
            self.chain_down(k).wait_send()

    def drain(self, units=None):
        for u in range(self.ways.lines if units is None else units):
            self.drain_unit(u)
        for k in range(1, self.ways.lines):
            self.drain_chain(k)


class Exchange:
    def __init__(self, ways, blocks, r1, r2, r3, got, sems):
        self.ways, self.blocks, self.r1, self.r2, self.r3, self.got = ways, blocks, r1, r2, r3, got
        self.send_sem, self.recv_sem = sems

    def copy(self, k, src, dst, to):
        return remote(src, dst, self.send_sem(k), self.recv_sem(k), to)

    def over_core(self):
        w = self.ways
        oc = 1 - w.spot[3]
        return [self.copy(0, self.blocks.at[:, :, :, oc], self.r1, w.to_c)]

    def over_b(self):
        w = self.ways
        z, a, b, c = w.spot
        sources = (self.blocks.at[:, :, 1 - b, c], self.r1.at[:, :, 1 - b])
        return [self.copy(1 + k, src, self.r2.at[k], w.to_b) for k, src in enumerate(sources)]

    def over_a(self):
        w = self.ways
        z, a, b, c = w.spot
        oa = 1 - a
        sources = (
            self.blocks.at[:, oa, b, c], self.r1.at[:, oa, b], self.r2.at[0, :, oa], self.r2.at[1, :, oa],
        )
        return [self.copy(3 + k, src, self.r3.at[4 + k], w.to_a) for k, src in enumerate(sources)]

    def over_line(self):
        w = self.ways
        z, a, b, c = w.spot
        out = []
        for step in range(1, w.lines):
            there = lax.rem(z + step, w.lines)
            out.append(
                self.copy(6 + step, self.r3.at[:, there], self.got.at[z], device(there, a, b, c))
            )
        return out

    def line_arrival(self, step):
        w = self.ways
        here = self.got.at[lax.rem(w.spot[0] + w.lines - step, w.lines)]
        self.copy(6 + step, here, here, w.to_c).wait_recv()

    def start(self, copies):
        for copy in copies:
            copy.start()

    def arrive(self, copies):
        for copy in copies:
            copy.wait_recv()

    def collect(self):
        z, a, b, c = self.ways.spot
        for line in range(self.ways.lines):
            self.r3[0, line] = self.blocks[line, a, b, c]
            self.r3[1, line] = self.r1[line, a, b]
            for k in range(2):
                self.r3[2 + k, line] = self.r2[k, line, a]

    def events(self):
        z = self.ways.spot[0]
        return [
            lambda: self.start(self.over_core()),
            lambda: (self.arrive(self.over_core()), self.start(self.over_b())),
            lambda: (self.arrive(self.over_b()), self.start(self.over_a())),
            lambda: (self.arrive(self.over_a()), self.collect(), self.start(self.over_line())),
            lambda: [self.line_arrival(step) for step in range(1, self.ways.lines)],
        ]

    def block(self, line, a, b, c):
        z, ma, mb, mc = self.ways.spot
        i = jnp.abs(a - ma) * 4 + jnp.abs(b - mb) * 2 + jnp.abs(c - mc)
        own = self.r3[i, z]
        return jnp.where(line == z, own, self.got[line, i])

    def drain(self):
        for copies in (self.over_core(), self.over_b(), self.over_a(), self.over_line()):
            for copy in copies:
                copy.wait_send()


def exchange_scratch(lines, rows):
    return [
        pltpu.VMEM((lines, 2, 2, 2, rows, 128), bf16),
        pltpu.VMEM((lines, 2, 2, rows, 128), bf16),
        pltpu.VMEM((2, lines, 2, rows, 128), bf16),
        pltpu.VMEM((8, lines, rows, 128), bf16),
        pltpu.VMEM((lines, 8, rows, 128), bf16),
    ]


def all_places(lines):
    return [(d, d // 8, d // 4 % 2, d // 2 % 2, d % 2) for d in range(8 * lines)]


def padded_rows(value, rows):
    return jnp.concatenate([value, jnp.zeros((rows - value.shape[0],) + value.shape[1:], value.dtype)])


def softmax_rows(scores):
    weights = jnp.exp(scores - jnp.max(scores, axis=-1, keepdims=True))
    return weights * (1.0 / jnp.sum(weights, axis=-1, keepdims=True))


def turn(values, cosine, signed_sine):
    return values * cosine + pltpu.roll(values, values.shape[-1] // 2, 1) * signed_sine


def document_of(positions, first_end, second_end):
    return (positions >= first_end).astype(jnp.int32) + (positions >= second_end).astype(jnp.int32)


def make_bias(bias, lengths, tp_index):
    rows, cols = bias.shape
    first_end = lengths[0, 0]
    second_end = first_end + lengths[0, 1]
    q_pos = lax.broadcasted_iota(jnp.int32, (rows, cols), 0) + tp_index * rows
    k_pos = lax.broadcasted_iota(jnp.int32, (rows, cols), 1)
    allowed = (
        document_of(q_pos, first_end, second_end) == document_of(k_pos, first_end, second_end)
    ) & (q_pos >= k_pos)
    bias[...] = jnp.where(allowed, 0.0, -1e30)


def front_kernel(lines, experts, scale, *refs):
    (
        lengths, ids, freq, hidden, small, wq, wk, wv, wo, s_gate, s_up, s_down, cot,
        w_out, cot_out, tok, aux, small_t, residual, attended, q_out, k_out, v_out, n_out,
        cos_out, sin_out, group, shared,
        wall, stage, small_stage, small_all, bias, e_blocks, e_r1, e_r2, e_r3, e_got,
        g_send, g_recv, s_send, s_recv, x_send, x_recv, e_send, e_recv, local_sem,
    ) = refs
    ways = Ways(lines)
    z, a, b, c = ways.spot
    ob, oc = 1 - b, 1 - c
    count, width = hidden.shape
    d_rows = wq.shape[0]
    chip_rows = 2 * d_rows
    half = width // 2
    heads = width // 128
    group_len = 4 * count
    ways.greet()

    def cot_chunk(line, kind, part, other):
        first = (line * 4 + kind) * count
        if part is None:
            return cot_out.at[pl.ds(first, count)]
        return cot_out.at[pl.ds(first + part * (count // 2), count // 2)]

    def sems(i):
        return (lambda k: g_send.at[i, k], lambda k: g_recv.at[i, k])

    g_cot = Gather(ways, cot_chunk, sems(3), own=cot, relative=True)
    g_cot.begin()

    shards = (wq, wk, wv, wo)
    swaps = [
        remote(
            shards[k].at[:, pl.ds(pl.multiple_of(oc * half, 128), half)], stage.at[k],
            s_send.at[k], s_recv.at[k], ways.to_c,
        )
        for k in range(4)
    ] + [remote(small, small_stage, s_send.at[4], s_recv.at[4], ways.to_c)]
    for copy in swaps:
        copy.start()

    def group_copy(k, src, dst, to):
        return remote(src, dst, x_send.at[k], x_recv.at[k], to)

    own_group = group.at[b * 2 + c]
    group_copies = [group_copy(0, hidden, own_group, ways.to_c), group_copy(1, hidden, own_group, ways.to_b)]
    for copy in group_copies:
        copy.start()
    own_group[...] = hidden[...]

    def chip_block(own, other):
        own, other = own.astype(f32), other.astype(f32)
        first = jnp.where(c == 0, own, other)
        second = jnp.where(c == 0, other, own)
        return jnp.concatenate([first, second], axis=0).astype(bf16)

    sh = s_down.shape[0]
    block_rows = e_blocks.shape[4]
    lane = lax.broadcasted_iota(jnp.int32, (d_rows, 128), 1)

    def columns_at(ref, first, to):
        tile, start = first // 128 * 128, first % 128
        value = pltpu.roll(ref[:, tile : tile + 128].astype(f32), (to - start) % 128, 1)
        if start + sh > 128:
            later = pltpu.roll(ref[:, tile + 128 : tile + 256].astype(f32), (to - start) % 128, 1)
            value = jnp.where(lane < to + 128 - start, value, later)
        return value

    for d, line, da, db, dc in all_places(lines):
        gate, up = columns_at(s_gate, d * sh, 0), columns_at(s_up, d * sh, 64)
        value = jnp.where(lane < sh, gate, jnp.where((lane >= 64) & (lane < 64 + sh), up, 0.0))
        e_blocks[line, da, db, dc] = padded_rows(value, block_rows).astype(bf16)
    exchange = Exchange(
        ways, e_blocks, e_r1, e_r2, e_r3, e_got, (lambda k: e_send.at[k], lambda k: e_recv.at[k])
    )
    e_events = exchange.events()

    base = pl.multiple_of(ways.chip(z, O) * chip_rows, 16)
    for copy in swaps:
        copy.wait_recv()
    small_all[pl.ds(base, chip_rows), :] = chip_block(small[...], small_stage[...])
    for k in range(4):
        mine = shards[k][:, pl.ds(pl.multiple_of(c * half, 128), half)]
        wall[pl.ds(base, chip_rows), pl.ds(pl.multiple_of((c * 4 + k) * half, 128), half)] = chip_block(
            mine, stage[k]
        )

    def small_chunk(line, kind, part, other):
        rows = pl.multiple_of(ways.chip(line, kind) * chip_rows, 16)
        if part is None:
            return small_all.at[pl.ds(rows, chip_rows)]
        low = chip_rows // 32 * 16
        return small_all.at[pl.ds(rows, low) if part == 0 else pl.ds(rows + low, chip_rows - low)]

    def weight_chunk(first, cols, cut):
        def chunk(line, kind, part, other):
            rows = pl.multiple_of(ways.chip(line, kind) * chip_rows, 16)
            col = (oc if other else c) * 4 * half + first
            if part is None:
                start, size = col, cols
            elif part == 0:
                start, size = col, cut
            else:
                start, size = col + cut, cols - cut
            return wall.at[pl.ds(rows, chip_rows), pl.ds(pl.multiple_of(start, 128), size)]

        return chunk

    tiles = half // 128
    g_small = Gather(ways, small_chunk, sems(0))
    g_qkv = Gather(ways, weight_chunk(0, 3 * half, (3 * tiles + 1) // 2 * 128), sems(1), across=True)
    g_out = Gather(ways, weight_chunk(3 * half, half, tiles // 2 * 128), sems(2), across=True)
    keep = pltpu.make_async_copy(cot, cot_chunk(z, O, None, False), local_sem.at[0])
    keep.start()
    g_small.begin()
    g_qkv.begin()
    e_events[0]()

    first_end = lengths[0, 0]
    second_end = first_end + lengths[0, 1]
    position = lax.broadcasted_iota(jnp.int32, (group_len, 128), 0)
    doc = document_of(position, first_end, second_end)
    start = jnp.where(doc == 0, 0, jnp.where(doc == 1, first_end, second_end))
    angles = (position - start).astype(f32) * freq[...]
    lane = lax.broadcasted_iota(jnp.int32, (group_len, 128), 1)
    cos_out[...] = jnp.cos(angles)
    sin_out[...] = jnp.where(lane < 64, -1.0, 1.0) * jnp.sin(angles)
    make_bias(bias, lengths, b * 2 + c)
    got = group.at[ob * 2 + c]
    group_copy(1, got, got, ways.to_b).wait_recv()
    group_copies.append(group_copy(2, got, got, ways.to_c))
    group_copies[-1].start()
    for k, t in ((0, b * 2 + oc), (2, ob * 2 + oc)):
        got = group.at[t]
        group_copy(k, got, got, ways.to_c).wait_recv()

    small_events, qkv_events = g_small.events(), g_qkv.events()
    out_events = g_out.events()
    cot_events = {
        1: lambda: (g_cot.xy_event(0), g_cot.chain_event(1), g_cot.send_own(1)),
        2: lambda: (g_cot.diag_carried(0), g_cot.chain_event(2)),
        4: lambda: (g_cot.xy_event(1), g_cot.chain_event(3)),
        5: lambda: g_cot.diag_handed(1),
    }
    for k in range(len(qkv_events)):
        if k == 3:
            g_out.begin()
        qkv_events[k]()
        small_events[k]()
        if k in cot_events:
            cot_events[k]()
        if 2 <= k < 6:
            e_events[k - 1]()
        if k >= 4:
            out_events[k - 4]()
    flat = jnp.transpose(small_all[...].astype(f32))
    small_t[...] = flat.astype(bf16)
    gain_one = flat[experts : experts + 1, :]
    gain_two = flat[experts + 1 : experts + 2, :]
    for t in range(4):
        x = group[t].astype(f32)
        r = lax.rsqrt(jnp.mean(x * x, axis=-1, keepdims=True) + epsilon)
        n_out[t * count : (t + 1) * count, :] = (x * r * gain_one).astype(bf16)
    g_qkv.other_core()

    later = out_events[3:] + [g_out.other_core]

    def service(n=1):
        for _ in range(n):
            if later:
                later.pop(0)()

    stacked = jnp.concatenate(
        [exchange.block(*there)[:d_rows].astype(f32) for _, *there in all_places(lines)]
    )
    turned = jnp.transpose(stacked)
    shared[0] = turned[:64].astype(bf16)
    shared[1] = turned[64:].astype(bf16)
    shared[2] = padded_rows(s_down[...].astype(f32), 64).astype(bf16)
    own_rows = pl.ds(pl.multiple_of((b * 2 + c) * count, count), count)
    for h in range(2):
        cols = pl.ds((h * 4 + 1) * half, half)
        keys = dense_dot(n_out[...], wall[:, cols])
        for j in range(half // 128):
            k_out[:, h * half + j * 128 : h * half + (j + 1) * 128] = turn(
                keys[:, j * 128 : (j + 1) * 128], cos_out[...], sin_out[...]
            ).astype(bf16)
        service()
        cols = pl.ds((h * 4 + 2) * half, half)
        v_out[:, h * half : (h + 1) * half] = dense_dot(n_out[...], wall[:, cols]).astype(bf16)
        service()
        queries = dense_dot(n_out[own_rows, :], wall[:, pl.ds(h * 4 * half, half)])
        for j in range(half // 128):
            q_out[:, h * half + j * 128 : h * half + (j + 1) * 128] = turn(
                queries[:, j * 128 : (j + 1) * 128], cos_out[own_rows, :], sin_out[own_rows, :]
            ).astype(bf16)
        service()
    for h in range(heads):
        cols = pl.ds(h * 128, 128)
        probs = softmax_rows(dot_nt(q_out[:, cols], k_out[:, cols]) * scale + bias[...])
        attended[:, cols] = dense_dot(probs.astype(bf16), v_out[:, cols]).astype(bf16)
        if h % 2:
            service()
    service(len(later))
    save = pltpu.make_async_copy(wall, w_out, local_sem.at[1])
    save.start()
    for h in range(2):
        projected = dense_dot(attended[...], wall[:, pl.ds((h * 4 + 3) * half, half)])
        residual[:, h * half : (h + 1) * half] = (
            hidden[:, h * half : (h + 1) * half].astype(f32) + projected
        )
    service()
    res = residual[...]
    r2 = lax.rsqrt(jnp.mean(res * res, axis=-1, keepdims=True) + epsilon)
    normed = (res * r2 * gain_two).astype(bf16)
    tok[...] = normed
    logits = dense_dot(normed, small_all[...])
    lane = lax.broadcasted_iota(jnp.int32, (count, 128), 1)
    affinity = softmax_rows(jnp.where(lane < experts, logits, -1e30))
    named = lane < 0
    for j in range(ids.shape[1]):
        named = named | (ids[:, j : j + 1] == lane)
    signed = jnp.transpose(jnp.where(named, affinity, -affinity))[:experts, :]
    high = signed.astype(bf16)
    aux[0:experts, :] = high
    aux[experts : 2 * experts, :] = (signed - high.astype(f32)).astype(bf16)
    service(len(later))
    for g in (g_small, g_qkv, g_out, exchange):
        g.drain()
    g_cot.drain(2)
    for copy in swaps + group_copies:
        copy.wait_send()
    keep.wait()
    save.wait()


def front_call(
    lengths, ids, hidden, small, weights, shared, cot, experts, scale, collective_id
):
    lines = lax.axis_size("ep") // 2
    count, width = hidden.shape
    d_rows = weights[0].shape[0]
    group_len = 4 * count
    block_rows = -(-d_rows // 16) * 16
    anywhere = pl.BlockSpec(memory_space=pl.ANY)
    vmem = pl.BlockSpec(memory_space=pltpu.VMEM)
    smem = pl.BlockSpec(memory_space=pltpu.SMEM)
    lane = jnp.arange(128) % 64
    freq = (10000.0 ** (-2.0 * lane.astype(f32) / 128))[None, :]
    shape = jax.ShapeDtypeStruct
    return pl.pallas_call(
        functools.partial(front_kernel, lines, experts, scale),
        out_shape=(
            shape((width, 4 * width), bf16),
            shape((lines * 4 * count, width), bf16),
            shape((count, width), bf16),
            shape((2 * experts, count), bf16),
            shape((128, width), bf16),
            shape((count, width), f32),
            shape((count, width), bf16),
            shape((count, width), bf16),
            shape((group_len, width), bf16),
            shape((group_len, width), bf16),
            shape((group_len, width), bf16),
            shape((group_len, 128), f32),
            shape((group_len, 128), f32),
            shape((4, count, width), bf16),
            shape((3, 64, width), bf16),
        ),
        in_specs=[smem] + [vmem] * 11 + [anywhere],
        out_specs=(anywhere, anywhere) + (vmem,) * 13,
        scratch_shapes=[
            pltpu.VMEM((width, 4 * width), bf16),
            pltpu.VMEM((4, d_rows, width // 2), bf16),
            pltpu.VMEM((d_rows, 128), bf16),
            pltpu.VMEM((width, 128), bf16),
            pltpu.VMEM((count, group_len), f32),
            *exchange_scratch(lines, block_rows),
            pltpu.SemaphoreType.DMA((4, 12 * lines)),
            pltpu.SemaphoreType.DMA((4, 12 * lines)),
            pltpu.SemaphoreType.DMA((5,)),
            pltpu.SemaphoreType.DMA((5,)),
            pltpu.SemaphoreType.DMA((3,)),
            pltpu.SemaphoreType.DMA((3,)),
            pltpu.SemaphoreType.DMA((7 + lines,)),
            pltpu.SemaphoreType.DMA((7 + lines,)),
            pltpu.SemaphoreType.DMA((2,)),
        ],
        compiler_params=pltpu.CompilerParams(
            collective_id=collective_id, has_side_effects=True, vmem_limit_bytes=60 * 2**20
        ),
        name="front",
    )(lengths, ids, freq, hidden, small, *weights, *shared, cot)


class Reduce:
    def __init__(self, ways, chunk, cut, pq, xr, yr, dz, zr, sems, alone=()):
        self.ways, self.chunk, self.cut = ways, chunk, cut
        self.pq, self.xr, self.yr, self.dz, self.zr = pq, xr, yr, dz, zr
        self.alone = alone
        self.carried = [True if u in alone else ways.carried[u] for u in range(ways.lines)]
        self.send_sem, self.recv_sem = sems

    def copy(self, slot, u, src, dst, to):
        k = slot * self.ways.lines + u
        return remote(src, dst, self.send_sem(k), self.recv_sem(k), to)

    def diag(self, part, u):
        w = self.ways
        return self.copy(
            part, u, self.chunk(w.zs[u], D, part), self.cut(self.pq, self.slot(u), part),
            w.to_b if part else w.to_a,
        )

    def side_b(self, part, u):
        w = self.ways
        return self.copy(2 + part, u, self.chunk(w.zs[u], X, part), self.cut(self.xr, u, part), w.to_b)

    def side_a(self, part, u):
        w = self.ways
        return self.copy(4 + part, u, self.chunk(w.zs[u], Y, part), self.cut(self.yr, u, part), w.to_a)

    def slot(self, u):
        return max(u - 1, 0) if self.alone else min(u, 1)

    def hand(self, u, at):
        w = self.ways
        return self.copy(
            7, at, self.chunk(w.zs[u], D, None), self.cut(self.dz, min(at, 1), None), w.pair
        )

    def along(self, u):
        w = self.ways
        z, a, b, c = w.spot
        slot = lax.rem(z - w.zs[u] + w.lines, w.lines) - 1
        k = 6 * w.lines
        return remote(
            self.chunk(w.zs[u], O, None), self.zr(slot), self.send_sem(k + u),
            self.recv_sem(k + slot), device(w.zs[u], a, b, c),
        )

    def start(self, u):
        def whole():
            self.hand(u, u if u > 1 else 0).start()
            self.side_b(0, u).start()
            self.side_a(1, u).start()

        self.side_b(1, u).start()
        self.side_a(0, u).start()
        when(other(self.carried[u]), whole)

    def carry(self, u):
        def act():
            if u not in self.alone:
                self.hand(u, u).wait_recv()
            for part in (0, 1):
                if u not in self.alone:
                    accumulate(
                        self.chunk(self.ways.zs[u], D, part), [self.cut(self.dz, min(u, 1), part)]
                    )
                self.diag(part, u).start()

        when(self.carried[u], act)

    def mid(self, u):
        w = self.ways

        def act():
            self.diag(0, u).wait_recv()
            accumulate(self.chunk(w.zs[u], X, 0), [self.cut(self.pq, self.slot(u), 0)])
            self.side_b(0, u).start()
            self.diag(1, u).wait_recv()
            accumulate(self.chunk(w.zs[u], Y, 1), [self.cut(self.pq, self.slot(u), 1)])
            self.side_a(1, u).start()

        when(self.carried[u], act)

    def end(self, u):
        w = self.ways
        for part in (0, 1):
            self.side_b(part, u).wait_recv()
            self.side_a(part, u).wait_recv()
            accumulate(
                self.chunk(w.zs[u], O, part), [self.cut(self.xr, u, part), self.cut(self.yr, u, part)]
            )
        if u > 0:
            self.along(u).start()

    def events(self):
        return [
            lambda: (self.start(2), self.start(3)),
            lambda: (self.carry(2), self.carry(3), self.start(1)),
            lambda: (self.mid(2), self.mid(3), self.start(0)),
            lambda: (self.end(2), self.end(3)),
            lambda: (self.carry(0), self.end(1)),
            lambda: self.mid(0),
            lambda: self.end(0),
        ]

    def total(self):
        w = self.ways
        sums = self.chunk(w.spot[0], O, None)[...].astype(f32)
        for slot in range(w.lines - 1):
            k = 6 * w.lines + slot
            here = self.zr(slot)
            remote(here, here, self.send_sem(k), self.recv_sem(k), w.to_c).wait_recv()
            sums = sums + here[...].astype(f32)
        return sums

    def drain(self):
        w = self.ways
        for u in range(w.lines):
            for part in (0, 1):
                when(self.carried[u], lambda part=part, u=u: self.diag(part, u).wait_send())
                self.side_b(part, u).wait_send()
                self.side_a(part, u).wait_send()
            when(other(self.carried[u]), lambda u=u: self.hand(u, u if u > 1 else 0).wait_send())
            if u > 0:
                self.along(u).wait_send()


def accumulate(dst, others):
    total = dst[...].astype(f32)
    for ref in others:
        total = total + ref[...].astype(f32)
    dst[...] = total.astype(bf16)


def mixture_kernel(lines, tok, aux, cot, wg, wu, wd, shared, sel, sel_t, router_t, ones, *refs):
    (
        sums, out_part, dw_own, dw_sib, dr,
        nc, aux_all, vg, vu, vd, dw, acts, dg, du, daff, dlg, pq, xr, yr, dz, zr,
        ag_send, ag_recv, rs_send, rs_recv, w_send, w_recv, w_local, cot_sem, local_sem,
    ) = refs
    ways = Ways(lines)
    z, a, b, c = ways.spot
    oc = 1 - c
    zs = ways.zs
    count, width = tok.shape
    half = count // 2
    n_routed = wg.shape[0]
    hc = n_routed + shared.shape[1]
    hidden = 2 * hc
    n_sel = sel.shape[1]
    block = 256
    unit_rows = 4 * count
    ways.greet()

    def rows_of(line, kind, part):
        if part is None:
            return pl.ds(pl.multiple_of((line * 4 + kind) * count, count), count)
        return pl.ds(pl.multiple_of((line * 4 + kind) * count + part * half, half), half)

    def aux_chunk(line, kind, part, _):
        rows = aux.shape[0]
        at = line * 4 + kind
        if part is None:
            return aux_all.at[at]
        return aux_all.at[at, pl.ds(part * (rows // 2), rows // 2)]

    def sems(i):
        return (lambda k: ag_send.at[i, k], lambda k: ag_recv.at[i, k])

    gathers = [
        Gather(
            ways, lambda line, kind, part, _: nc.at[rows_of(line, kind, part), pl.ds(0, width)],
            sems(0), own=tok, relative=True,
        ),
        Gather(ways, aux_chunk, sems(1), own=aux, relative=True),
    ]

    cots = Gather(
        ways, lambda line, kind, part, _: nc.at[rows_of(line, kind, part), pl.ds(width, width)],
        sems(2), relative=True,
    )

    def each(name, *args):
        for g in gathers:
            getattr(g, name)(*args)

    def every(name, *args):
        each(name, *args)
        getattr(cots, name)(*args)

    each("begin")
    local = []
    mine = pl.ds(c * hc, hc)
    theirs = pl.ds(oc * hc, hc)
    w_copies = []
    for k, (src, dst) in enumerate(((wg, vg), (wu, vu), (wd, vd))):
        for j, (part, first, size) in enumerate(
            ((src, 0, n_routed), (shared.at[k], n_routed, hc - n_routed))
        ):
            there = dst.at[pl.ds(pl.multiple_of(c * hc + first, 16), size)]
            i = 2 * k + j
            copy = pltpu.make_async_copy(part, there, w_local.at[i])
            copy.start()
            local.append(copy)
            copy = remote(part, there, w_send.at[i], w_recv.at[i], ways.to_c)
            copy.start()
            w_copies.append(copy)

    copy = pltpu.make_async_copy(tok, nc.at[rows_of(z, O, None), pl.ds(0, width)], local_sem.at[3])
    copy.start()
    local.append(copy)
    copy = pltpu.make_async_copy(aux, aux_chunk(z, O, None, False), local_sem.at[4])
    copy.start()
    local.append(copy)
    cot_loads = []
    for u in (2, 3, 0, 1):
        size = unit_rows if u < 2 else count
        there = pl.ds(pl.multiple_of(zs[u] * unit_rows, unit_rows), size)
        cot_loads.append(
            pltpu.make_async_copy(cot.at[there], nc.at[there, pl.ds(width, width)], cot_sem.at[u])
        )
        cot_loads[-1].start()

    def zero(i, carry):
        dw[:, pl.ds(i * 64, 64), :] = jnp.zeros((3, 64, width), f32)
        return carry

    lax.fori_loop(0, hidden // 64, zero, 0)
    dr[...] = jnp.zeros_like(dr)

    def cut(ref, u, part):
        return ref.at[u] if part is None else ref.at[u, pl.ds(part * half, half)]

    back = Reduce(
        ways, lambda line, kind, part: nc.at[rows_of(line, kind, part), pl.ds(width, width)], cut,
        pq, xr, yr, dz, lambda slot: zr.at[slot],
        (lambda k: rs_send.at[k], lambda k: rs_recv.at[k]), alone=(2, 3),
    )

    def save(u):
        rows = pl.ds(pl.multiple_of(zs[u] * unit_rows, unit_rows), unit_rows)
        return pltpu.make_async_copy(
            nc.at[rows, pl.ds(0, width)], out_part.at[rows], local_sem.at[7 + u]
        )

    def expand(line, columns):
        return jnp.concatenate(
            [dot_tn(aux_all[line * 4 + kind], sel[:, columns]) for kind in range(4)], axis=0
        )

    def at_step(s, acts_of):
        for v, act in acts_of.items():
            when(s == v, act)

    def unit(u, carry):
        line = pick(zs, u)
        rows = pl.ds(pl.multiple_of(line * unit_rows, unit_rows), unit_rows)
        at_step(
            u,
            {
                1: lambda: (each("xy_event", 1), each("diag_handed", 1)),
                2: lambda: (every("diag_handed", 2), every("diag_carried", 3)),
                3: lambda: (every("diag_handed", 3), back.end(1), back.mid(2)),
            },
        )
        daff[...] = jnp.zeros_like(daff)

        def hidden_step(i, carry):
            h = pl.ds(pl.multiple_of(i * block, block), block)
            x = nc[rows, 0:width]
            gate_pre = dot_nt(x, vg[h, :])
            up_pre = dot_nt(x, vu[h, :])
            grad = dot_nt(nc[rows, width : 2 * width], vd[h, :])
            scale = jnp.maximum(expand(line, h) + ones[:, h], 0.0)
            sigma = 1.0 / (1.0 + jnp.exp(-gate_pre))
            silu = gate_pre * sigma
            act = silu * up_pre
            acts[:, h] = (act * scale).astype(bf16)
            daff[...] += dense_dot((act * grad).astype(bf16), sel_t[h, :])
            grad = grad * scale
            dg[:, h] = (grad * up_pre * sigma * (1.0 + gate_pre * (1.0 - sigma))).astype(bf16)
            du[:, h] = (grad * silu).astype(bf16)
            return carry

        lax.fori_loop(0, hidden // block, hidden_step, 0, unroll=True)
        signed = expand(line, pl.ds(hidden, n_sel - hidden))
        affinity = jnp.abs(signed)
        grad_aff = jnp.where(signed > 0, daff[...], 0.0)
        total = jnp.sum(affinity * grad_aff, axis=1, keepdims=True)
        dlg[...] = (affinity * (grad_aff - total)).astype(bf16)
        at_step(
            u,
            {
                0: lambda: (each("chain_event", 2), each("send_own", 2)),
                1: lambda: every("diag_carried", 2),
                2: lambda: (back.carry(0), cots.drain_unit(2)),
                3: lambda: (back.end(2), cots.drain_unit(3)),
            },
        )

        def down_step(i, carry):
            h = pl.ds(pl.multiple_of(i * block, block), block)
            dw[2, h, :] += dot_tn(acts[:, h], nc[rows, width : 2 * width])
            return carry

        lax.fori_loop(0, hidden // block, down_step, 0, unroll=True)

        def back_step(i, carry):
            n = pl.ds(pl.multiple_of(i * block, block), block)
            n2 = pl.ds(pl.multiple_of(width + i * block, block), block)
            nc[rows, n2] = (
                dense_dot(dg[...], vg[:, n])
                + dense_dot(du[...], vu[:, n])
                + dense_dot(dlg[...], router_t[:, n])
            ).astype(bf16)
            return carry

        lax.fori_loop(0, width // block, back_step, 0, unroll=True)
        at_step(
            u,
            {
                0: lambda: (each("chain_event", 3), cots.send_own(3)),
                1: lambda: (every("xy_event", 3), back.start(1), back.start(0)),
                2: lambda: (back.carry(2), back.start(2), back.mid(0)),
                3: lambda: (back.carry(3), back.start(3), back.end(0)),
            },
        )

        def weight_step(i, carry):
            h = pl.ds(pl.multiple_of(i * block, block), block)
            x = nc[rows, 0:width]
            dw[0, h, :] += dot_tn(dg[:, h], x)
            dw[1, h, :] += dot_tn(du[:, h], x)
            return carry

        lax.fori_loop(0, hidden // block, weight_step, 0, unroll=True)
        dr[...] += dot_tn(dlg[...], nc[rows, 0:width])
        at_step(
            u,
            {
                0: lambda: (every("xy_event", 2), each("send_own", 3), each("drain_chain", 1)),
                1: lambda: (each("drain_chain", 2), each("drain_chain", 3)),
                3: lambda: back.mid(3),
            },
        )
        for v in range(lines):
            when(u == v, lambda v=v: each("drain_unit", v))

        def out_step(i, carry):
            n = pl.ds(pl.multiple_of(i * block, block), block)
            nc[rows, n] = dense_dot(acts[...], vd[:, n]).astype(bf16)
            return carry

        lax.fori_loop(0, width // block, out_step, 0, unroll=True)
        for v in range(lines):
            when(u == v, lambda v=v: save(v).start())
        return carry

    each("xy_event", 0)
    each("chain_event", 1)
    each("send_own", 1)
    for copy in w_copies:
        copy.wait_recv()
    for copy in local + cot_loads:
        copy.wait()
    cots.send_own(2)
    each("diag_carried", 0)
    lax.fori_loop(0, lines, unit, 0)

    own_out = pltpu.make_async_copy(dw.at[:, mine], dw_own, local_sem.at[6])
    own_out.start()
    sib_out = pltpu.make_async_copy(dw.at[:, theirs], dw_sib, local_sem.at[7 + lines])
    sib_out.start()
    back.end(3)
    sums[...] = back.total()
    back.drain()
    for u in range(lines):
        save(u).wait()
    for copy in w_copies:
        copy.wait_send()
    sib_out.wait()
    own_out.wait()


def mixture_call(tok, aux, cot, weights, shared, sel, sel_t, router_t, ones, collective_id):
    lines = lax.axis_size("ep") // 2
    count, width = tok.shape
    hc = weights[0].shape[0] + shared.shape[1]
    anywhere = pl.BlockSpec(memory_space=pl.ANY)
    vmem = pl.BlockSpec(memory_space=pltpu.VMEM)
    n_rows = lines * 4 * count
    return pl.pallas_call(
        functools.partial(mixture_kernel, lines),
        out_shape=(
            jax.ShapeDtypeStruct((count, width), f32),
            jax.ShapeDtypeStruct((n_rows, width), bf16),
            jax.ShapeDtypeStruct((3, hc, width), f32),
            jax.ShapeDtypeStruct((3, hc, width), f32),
            jax.ShapeDtypeStruct((128, width), f32),
        ),
        in_specs=[anywhere] * 7 + [vmem] * 4,
        out_specs=(vmem, anywhere, anywhere, anywhere, vmem),
        scratch_shapes=[
            pltpu.VMEM((n_rows, 2 * width), bf16),
            pltpu.VMEM((lines * 4,) + aux.shape, bf16),
            pltpu.VMEM((2 * hc, width), bf16),
            pltpu.VMEM((2 * hc, width), bf16),
            pltpu.VMEM((2 * hc, width), bf16),
            pltpu.VMEM((3, 2 * hc, width), f32),
            pltpu.VMEM((4 * count, 2 * hc), bf16),
            pltpu.VMEM((4 * count, 2 * hc), bf16),
            pltpu.VMEM((4 * count, 2 * hc), bf16),
            pltpu.VMEM((4 * count, 128), f32),
            pltpu.VMEM((4 * count, 128), bf16),
            pltpu.VMEM((3, count, width), bf16),
            pltpu.VMEM((lines, count, width), bf16),
            pltpu.VMEM((lines, count, width), bf16),
            pltpu.VMEM((2, count, width), bf16),
            pltpu.VMEM((lines - 1, count, width), bf16),
            pltpu.SemaphoreType.DMA((3, 12 * lines)),
            pltpu.SemaphoreType.DMA((3, 12 * lines)),
            pltpu.SemaphoreType.DMA((8 * lines,)),
            pltpu.SemaphoreType.DMA((8 * lines,)),
            pltpu.SemaphoreType.DMA((6,)),
            pltpu.SemaphoreType.DMA((6,)),
            pltpu.SemaphoreType.DMA((6,)),
            pltpu.SemaphoreType.DMA((lines,)),
            pltpu.SemaphoreType.DMA((8 + lines,)),
        ],
        compiler_params=pltpu.CompilerParams(
            collective_id=collective_id, has_side_effects=True, vmem_limit_bytes=62 * 2**20
        ),
        name="mixture",
    )(tok, aux, cot, *weights, shared, sel, sel_t, router_t, ones)


def back_kernel(lines, experts, scale, sh, *refs):
    (
        lengths, dn2, residual, cot, group, small_t, router_part, attended, q, normed, cosine, sine,
        keys, vals, wall_in, outs_in, dw_own, dw_sib,
        layer_out, input_grad, gq, gk, gv, go, small_out, gsg, gsu, dw_got,
        wall, part, staged, landed, pq, xr, yr, dz, zr, fin, fin_other,
        s_part, s_landed, s_pq, s_xr, s_yr, s_dz, s_zr,
        o_part, o_pq, o_xr, o_yr, o_dz, o_zr,
        grads, low, datt, dq, dk, dv, dn_part, dn_other, dn_far, bias, rows_t,
        e_blocks, e_r1, e_r2, e_r3, e_got,
        c_send, c_recv, r_send, r_recv, d_send, d_recv, e_send, e_recv, local_sem, credit,
    ) = refs
    ways = Ways(lines)
    z, a, b, c = ways.spot
    ob, oc = 1 - b, 1 - c
    count, width = cot.shape
    half = width // 2
    heads = width // 128
    chip_rows = pq.shape[1]
    d_rows = chip_rows // 2

    def load(i, src, dst):
        copy = pltpu.make_async_copy(src, dst, local_sem.at[i])
        copy.start()
        return copy

    o_load = load(0, outs_in, o_part)
    wo_loads = [
        load(1 + h, wall_in.at[:, pl.ds((h * 4 + 3) * half, half)], part.at[:, pl.ds(h * half, half)])
        for h in range(2)
    ]
    kv_loads = [load(3, keys, dk), load(4, vals, dv)]
    wall_loads = [
        load(5 + h, wall_in.at[:, pl.ds(h * 4 * half, 3 * half)], wall.at[:, pl.ds(h * 3 * half, 3 * half)])
        for h in range(2)
    ]

    def weight(h, k):
        return wall[:, pl.ds((h * 3 + k) * half, half)]

    ways.greet()

    half_rows = count // 2

    def o_chunk(line, kind, p):
        size = count if p is None else half_rows
        return o_part.at[pl.ds(pl.multiple_of((line * 4 + kind) * count + (p or 0) * size, size), size)]

    def o_cut(ref, u, p):
        return ref.at[u] if p is None else ref.at[u, pl.ds(p * half_rows, half_rows)]

    o_reduce = Reduce(
        ways, o_chunk, o_cut, o_pq, o_xr, o_yr, o_dz, lambda slot: o_zr.at[slot],
        (lambda i: r_send.at[3, i], lambda i: r_recv.at[3, i]),
    )

    def finish_output():
        layer_out[...] = (residual[...] + o_reduce.total()).astype(bf16)

    o_events = o_reduce.events() + [finish_output]
    o_load.wait()
    o_events[0]()
    dw_copy = remote(dw_sib, dw_got, c_send.at[6], c_recv.at[6], ways.to_c)
    dw_copy.start()
    exchange = Exchange(
        ways, e_blocks, e_r1, e_r2, e_r3, e_got, (lambda k: e_send.at[k], lambda k: e_recv.at[k])
    )
    e_events = exchange.events()
    shared_rows = pl.ds(dw_own.shape[1] - 64, 64)

    def shared_at(j, k):
        return (fin.at[pl.ds(0, 64), pl.ds(k * width, width)], rows_t.at[pl.ds(k * 64, 64)])[j]

    def shared_blocks():
        dw_copy.wait()
        loads = [
            load(7 + 2 * k + j, ref.at[k, shared_rows], shared_at(j, k))
            for k in range(2)
            for j, ref in enumerate((dw_own, dw_got))
        ]
        for copy in loads:
            copy.wait()
        turned = jnp.transpose(
            jnp.concatenate([fin[0:64, 0:width], fin[0:64, width : 2 * width]]) + rows_t[...]
        )
        for d, line, da, db, dc in all_places(lines):
            value = turned[d * d_rows : (d + 1) * d_rows]
            e_blocks[line, da, db, dc] = padded_rows(value, e_blocks.shape[4]).astype(bf16)
        e_events[0]()

    def shared_finish():
        lane = lax.broadcasted_iota(jnp.int32, (d_rows, 128), 1)
        for out, first in ((gsg, 0), (gsu, 64)):
            tiles = [jnp.zeros((d_rows, 128), f32) for _ in range(out.shape[1] // 128)]
            for d, *there in all_places(lines):
                tile, start = d * sh // 128, d * sh % 128
                value = exchange.block(*there)[:d_rows].astype(f32)
                value = pltpu.roll(value, (start - first) % 128, 1)
                if start + sh > 128:
                    tiles[tile] = jnp.where(lane >= start, value, tiles[tile])
                    tiles[tile + 1] = jnp.where(lane < start + sh - 128, value, tiles[tile + 1])
                else:
                    tiles[tile] = jnp.where((lane >= start) & (lane < start + sh), value, tiles[tile])
            for k, tile in enumerate(tiles):
                out[:, k * 128 : (k + 1) * 128] = tile

    res = residual[...]
    r2 = lax.rsqrt(jnp.mean(res * res, axis=-1, keepdims=True) + epsilon)
    unit_two = res * r2
    gain_two = small_t[experts + 1 : experts + 2, :].astype(f32)
    gain_one = small_t[experts : experts + 1, :].astype(f32)
    gain_two_row = jnp.sum(dn2[...] * unit_two, axis=0, keepdims=True)
    scaled = dn2[...] * gain_two
    back = r2 * (scaled - unit_two * jnp.mean(scaled * unit_two, axis=-1, keepdims=True))
    grads[...] = cot[...].astype(f32) + back
    low[...] = grads[...].astype(bf16)
    make_bias(bias, lengths, b * 2 + c)

    def weight_reduce(k, first, cols):
        low_cols = cols // 256 * 128

        def span(p):
            return (0, cols) if p is None else ((0, low_cols) if p == 0 else (low_cols, cols - low_cols))

        def chunk(line, kind, p):
            start, size = span(p)
            rows = pl.multiple_of(ways.chip(line, kind) * chip_rows, 16)
            return part.at[pl.ds(rows, chip_rows), pl.ds(first + start, size)]

        def cut(ref, u, p):
            start, size = span(p)
            return ref.at[u, :, pl.ds(first + start, size)]

        return Reduce(
            ways, chunk, cut, pq, xr, yr, dz, lambda slot: zr.at[slot, :, pl.ds(first, cols)],
            (lambda i: r_send.at[k, i], lambda i: r_recv.at[k, i]),
        )

    def small_span(p):
        first = chip_rows // 32 * 16
        return (0, chip_rows) if p is None else ((0, first) if p == 0 else (first, chip_rows - first))

    def small_chunk(line, kind, p):
        start, size = small_span(p)
        return s_part.at[pl.ds(pl.multiple_of(ways.chip(line, kind) * chip_rows + start, 16), size)]

    def small_cut(ref, u, p):
        start, size = small_span(p)
        return ref.at[u, pl.ds(start, size)]

    small_reduce = Reduce(
        ways, small_chunk, small_cut, s_pq, s_xr, s_yr, s_dz, lambda slot: s_zr.at[slot],
        (lambda i: r_send.at[2, i], lambda i: r_recv.at[2, i]),
    )
    qkv_reduce = weight_reduce(0, 0, 3 * half)
    wo_reduce = weight_reduce(1, 3 * half, half)

    def across(k):
        return remote(staged.at[k % 2], landed.at[k % 3], c_send.at[k], c_recv.at[k], ways.to_c)

    def swapped(k):
        across(k).wait_recv()

        def body(i, carry):
            rows = pl.ds(pl.multiple_of(i * chip_rows, 16), chip_rows)
            accumulate(part.at[rows, pl.ds(k * half, half)], [landed.at[k % 3, rows]])
            return carry

        lax.fori_loop(0, width // chip_rows, body, 0)
        if k == 3:
            pl.semaphore_signal(credit, inc=1, device_id=ways.to_c, device_id_type=MESH)

    later = []

    def service(n=1):
        for _ in range(n):
            if later:
                later.pop(0)()

    def columns(core):
        return pl.ds(pl.multiple_of(core * half, 128), half)

    def weight_grad(k, left, right):
        if k < 2:
            across(k + 2).wait_send()
        staged[k % 2] = dot_tn(left, right[:, columns(oc)]).astype(bf16)
        if k == 0:
            pl.semaphore_wait(credit, 1)
        across(k).start()
        part[:, pl.ds(k * half, half)] = dot_tn(left, right[:, columns(c)]).astype(bf16)

    o_events[1]()
    weight_grad(3, attended[...], low)
    for copy in wo_loads:
        copy.wait()
    datt[...] = (
        dot_nt(low[:, 0:half], part[:, 0:half]) + dot_nt(low[:, half:width], part[:, half:width])
    ).astype(bf16)
    wo_events = wo_reduce.events()
    later.append(lambda: swapped(3))
    for k in range(6):
        later.append(o_events[k + 2])
        later.extend(wo_events[:2] if k == 0 else [wo_events[k + 1]])
    for copy in kv_loads:
        copy.wait()

    own_rows = pl.ds(pl.multiple_of((b * 2 + c) * count, count), count)
    for h in range(heads):
        cols = pl.ds(h * 128, 128)
        key, val, query = dk[:, cols], dv[:, cols], q[:, cols]
        probs = softmax_rows(dot_nt(query, key) * scale + bias[...])
        dprobs = dot_nt(datt[:, cols], val)
        dscores = (
            probs * (dprobs - jnp.sum(probs * dprobs, axis=-1, keepdims=True))
        ).astype(bf16)
        dq[:, cols] = turn(
            dense_dot(dscores, key) * scale, cosine[own_rows, :], -sine[own_rows, :]
        ).astype(bf16)
        dk[:, cols] = turn(dot_tn(dscores, query) * scale, cosine[...], -sine[...]).astype(bf16)
        dv[:, cols] = dot_tn(probs.astype(bf16), datt[:, cols]).astype(bf16)
        if h in (0, 1, 2, 3, 4, 5, 7, 9):
            service()
    shared_blocks()
    weight_grad(2, normed[...], dv)
    weight_grad(1, normed[...], dk)
    swapped(2)
    service()
    e_events[1]()
    weight_grad(0, normed[own_rows, :], dq)
    swapped(1)
    swapped(0)
    qkv_events = qkv_reduce.events()
    qkv_events[0]()
    later = [later[0], later[1], qkv_events[1]] + later[2:]

    for copy in wall_loads:
        copy.wait()
    e_events[2]()
    rows_t[...] = router_part[...]
    rows_t[experts + 1 : experts + 2, :] = gain_two_row
    for t in range(4):
        rows = slice(t * count, (t + 1) * count)
        total = jnp.zeros((count, width), f32)
        for h in range(2):
            mine = slice(h * half, (h + 1) * half)
            total = total + dot_nt(dk[rows, mine], weight(h, 1)) + dot_nt(dv[rows, mine], weight(h, 2))
        dn_part[t] = total.astype(bf16)
        x = group[t].astype(f32)
        unit = x * lax.rsqrt(jnp.mean(x * x, axis=-1, keepdims=True) + epsilon)
        gain_row = jnp.sum(total * unit, axis=0, keepdims=True)
        if t == 0:
            rows_t[experts : experts + 1, :] = gain_row
        else:
            rows_t[experts : experts + 1, :] += gain_row
        service()

    def dn_copy(k, src, dst, to):
        return remote(src, dst, d_send.at[k], d_recv.at[k], to)

    dn_copies = [
        dn_copy(0, dn_part.at[b * 2 + oc], dn_other.at[0], ways.to_c),
        dn_copy(1, dn_part.at[ob * 2 + oc], dn_other.at[1], ways.to_c),
    ]
    for copy in dn_copies:
        copy.start()
    e_events[3]()
    own = jnp.zeros((count, width), f32)
    for h in range(2):
        own = own + dot_nt(dq[:, h * half : (h + 1) * half], weight(h, 0))
    x = group[b * 2 + c].astype(f32)
    r1 = lax.rsqrt(jnp.mean(x * x, axis=-1, keepdims=True) + epsilon)
    unit_one = x * r1
    rows_t[experts : experts + 1, :] += jnp.sum(own * unit_one, axis=0, keepdims=True)
    s_part[...] = jnp.transpose(rows_t[...]).astype(bf16)
    small_swap = remote(s_part, s_landed, c_send.at[4], c_recv.at[4], ways.to_c)
    small_swap.start()
    service()
    dn_copies[1].wait_recv()
    accumulate(dn_part.at[ob * 2 + c], [dn_other.at[1]])
    dn_copies.append(dn_copy(2, dn_part.at[ob * 2 + c], dn_far, ways.to_b))
    dn_copies[2].start()
    dn_copies[0].wait_recv()
    small_swap.wait()
    accumulate(s_part, [s_landed])
    service(len(later))
    small_events = small_reduce.events()
    for k in range(2, len(qkv_events)):
        later.extend([small_events[k - 2], qkv_events[k]])
    later.insert(2, lambda: (e_events[4](), shared_finish()))
    later.extend(small_events[-2:])
    service(6)
    dn_copies[2].wait_recv()
    total = (
        own
        + dn_part[b * 2 + c].astype(f32)
        + dn_other[0].astype(f32)
        + dn_far[...].astype(f32)
    )
    scaled = total * gain_one
    input_grad[...] = grads[...] + r1 * (
        scaled - unit_one * jnp.mean(scaled * unit_one, axis=-1, keepdims=True)
    )
    service(len(later))

    theirs = pl.ds(pl.multiple_of(oc * d_rows, 8), d_rows)
    mine = pl.ds(pl.multiple_of(c * d_rows, 8), d_rows)
    fin[:, pl.ds(3 * half, half)] = wo_reduce.total()
    fin[:, pl.ds(0, 3 * half)] = qkv_reduce.total()
    fin_copy = remote(fin.at[theirs], fin_other, c_send.at[5], c_recv.at[5], ways.to_c)
    fin_copy.start()
    s_total = small_reduce.total()
    small_out[...] = jnp.where(c == 0, s_total[:d_rows], s_total[d_rows:])
    for k, out in enumerate((gq, gk, gv, go)):
        out[:, columns(c)] = fin[mine, pl.ds(k * half, half)]
    fin_copy.wait_recv()
    for k, out in enumerate((gq, gk, gv, go)):
        out[:, columns(oc)] = fin_other[:, pl.ds(k * half, half)]
    for r in (qkv_reduce, wo_reduce, small_reduce, o_reduce):
        r.drain()
    for copy in dn_copies + [fin_copy]:
        copy.wait_send()
    exchange.drain()
    for k in range(2):
        across(k).wait_send()


def back_call(
    lengths, dn2, residual, cot, group, small_t, router_part, attended, q, normed, cosine, sine,
    keys, vals, wall, outs, dw_own, dw_sib, d_rows, experts, scale, sh, collective_id,
):
    lines = lax.axis_size("ep") // 2
    count, width = cot.shape
    half = width // 2
    chip_rows = 2 * d_rows
    group_len = 4 * count
    anywhere = pl.BlockSpec(memory_space=pl.ANY)
    vmem = pl.BlockSpec(memory_space=pltpu.VMEM)
    smem = pl.BlockSpec(memory_space=pltpu.SMEM)
    shape = jax.ShapeDtypeStruct
    dma = pltpu.SemaphoreType.DMA

    def landing(rows, cols):
        return [pltpu.VMEM((n, rows, cols), bf16) for n in (2, lines, lines, 2, lines - 1)]

    return pl.pallas_call(
        functools.partial(back_kernel, lines, experts, scale, sh),
        out_shape=(
            shape((count, width), bf16),
            shape((count, width), f32),
            shape((d_rows, width), f32),
            shape((d_rows, width), f32),
            shape((d_rows, width), f32),
            shape((d_rows, width), f32),
            shape((d_rows, 128), f32),
            shape((d_rows, 8 * lines * sh), f32),
            shape((d_rows, 8 * lines * sh), f32),
            shape(dw_sib.shape, f32),
        ),
        in_specs=[smem] + [vmem] * 11 + [anywhere] * 6,
        out_specs=(vmem,) * 9 + (anywhere,),
        scratch_shapes=[
            pltpu.VMEM((width, 6 * half), bf16),
            pltpu.VMEM((width, 4 * half), bf16),
            pltpu.VMEM((2, width, half), bf16),
            pltpu.VMEM((3, width, half), bf16),
            *landing(chip_rows, 4 * half),
            pltpu.VMEM((chip_rows, 4 * half), f32),
            pltpu.VMEM((d_rows, 4 * half), f32),
            pltpu.VMEM((width, 128), bf16),
            pltpu.VMEM((width, 128), bf16),
            *landing(chip_rows, 128),
            pltpu.VMEM(outs.shape, bf16),
            *landing(count, width),
            pltpu.VMEM((count, width), f32),
            pltpu.VMEM((count, width), bf16),
            pltpu.VMEM((count, width), bf16),
            pltpu.VMEM((count, width), bf16),
            pltpu.VMEM((group_len, width), bf16),
            pltpu.VMEM((group_len, width), bf16),
            pltpu.VMEM((4, count, width), bf16),
            pltpu.VMEM((2, count, width), bf16),
            pltpu.VMEM((count, width), bf16),
            pltpu.VMEM((count, group_len), f32),
            pltpu.VMEM((128, width), f32),
            *exchange_scratch(lines, -(-d_rows // 16) * 16),
            dma((7,)),
            dma((7,)),
            dma((4, 8 * lines)),
            dma((4, 8 * lines)),
            dma((3,)),
            dma((3,)),
            dma((7 + lines,)),
            dma((7 + lines,)),
            dma((11,)),
            pltpu.SemaphoreType.REGULAR,
        ],
        compiler_params=pltpu.CompilerParams(
            collective_id=collective_id, has_side_effects=True, vmem_limit_bytes=63 * 2**20
        ),
        name="back",
    )(
        lengths, dn2, residual, cot, group, small_t, router_part, attended, q, normed, cosine, sine,
        keys, vals, wall, outs, dw_own, dw_sib,
    )


def documents(positions, lengths):
    seq_ends = jnp.cumsum(lengths)
    doc_index = (positions >= seq_ends[0]).astype(jnp.int32) + (positions >= seq_ends[1]).astype(
        jnp.int32
    )
    seq_starts = jnp.where(doc_index == 0, 0, jnp.where(doc_index == 1, seq_ends[0], seq_ends[1]))
    return (doc_index, positions - seq_starts)


def rotary_tables(offsets, head_dim):
    half_dim = head_dim // 2
    frequency = 10000.0 ** (-2.0 * jnp.arange(half_dim, dtype=f32) / head_dim)
    angles = offsets.astype(f32)[:, None] * frequency[None, :]
    return (jnp.cos(angles)[:, None, :], jnp.sin(angles)[:, None, :])


def rotate(values, cosine, sine_table):
    half_dim = values.shape[-1] // 2
    first_half = values[..., :half_dim]
    second_half = values[..., half_dim:]
    return jnp.concatenate(
        [
            first_half * cosine - second_half * sine_table,
            first_half * sine_table + second_half * cosine,
        ],
        axis=-1,
    )


def norm_back(grad_normed, unit_rows, inverse, gain):
    scaled = grad_normed * gain
    return inverse * (scaled - unit_rows * jnp.mean(scaled * unit_rows, axis=-1, keepdims=True))


def dot(left, right, contract):
    return lax.dot_general(left, right, ((contract[0], contract[1]), ((), ())), preferred_element_type=f32)


def dense_dot(left, right):
    return dot(left, right, ((1,), (0,)))


def dot_nt(left, right):
    return dot(left, right, ((1,), (1,)))


def dot_tn(left, right):
    return dot(left, right, ((0,), (0,)))


def any_slice(
    hidden_in,
    seq_lengths,
    expert_ids,
    attn_gain,
    w_query,
    w_key,
    w_value,
    w_out,
    ffn_gain,
    shared_gate,
    shared_up,
    shared_down,
    router,
    expert_gate,
    expert_up,
    expert_down,
    cotangent,
):
    tok_count, model_width = hidden_in.shape
    eps, tps = lax.axis_size("ep"), lax.axis_size("tp")
    devices = eps * tps
    exp_local, exp_hidden = expert_gate.shape[:2]
    experts = exp_local * eps
    group_len = tps * tok_count
    tokens = devices * tok_count
    d_rows = w_query.shape[0]
    width = w_query.shape[1]
    sh_rows = shared_down.shape[0]
    head_dim = width // HEADS
    attn_scale = head_dim ** (-0.5)

    flat = jnp.concatenate([router.reshape(-1), attn_gain, ffn_gain])
    small_len = -(-flat.shape[0] // model_width) * model_width
    small = jnp.pad(flat, (0, small_len - flat.shape[0])).reshape(-1, model_width)
    small = jnp.pad(small, ((0, -small.shape[0] % 16), (0, 0)))
    weights = jnp.concatenate([w_query, w_key, w_value, w_out], axis=1)

    all_weights, all_small, all_cot = [
        lax.all_gather(v, AXES, axis=0) for v in (weights, small, cotangent)
    ]
    group_hidden = lax.all_gather(hidden_in, "tp", axis=0)
    all_weights = all_weights.reshape(devices * d_rows, 4 * width)
    full_query = all_weights[:, :width]
    full_key = all_weights[:, width : 2 * width]
    full_value = all_weights[:, 2 * width : 3 * width]
    full_out = all_weights[:, 3 * width :]
    all_small = all_small.reshape(devices, -1)
    n_router = d_rows * experts
    full_router = all_small[:, :n_router].reshape(devices * d_rows, experts)
    gain_one = all_small[:, n_router : n_router + d_rows].reshape(-1).astype(f32)
    gain_two = all_small[:, n_router + d_rows : n_router + 2 * d_rows].reshape(-1).astype(f32)
    cot_all = all_cot.reshape(-1, model_width)

    shared_cols = jnp.stack([shared_gate, shared_up], axis=1).reshape(d_rows, 2, devices, sh_rows)
    shared_cols = lax.all_to_all(
        shared_cols.transpose(2, 1, 3, 0), AXES, split_axis=0, concat_axis=0, tiled=True
    )
    shared_t = shared_cols.transpose(1, 2, 0, 3).reshape(2, sh_rows, model_width)

    lengths = seq_lengths[0]
    tp_index = lax.axis_index("tp")
    own_pos = tp_index * tok_count + jnp.arange(tok_count, dtype=jnp.int32)
    all_pos = jnp.arange(group_len, dtype=jnp.int32)
    own_doc, own_offset = documents(own_pos, lengths)
    all_doc, all_offset = documents(all_pos, lengths)
    allowed = (own_doc[:, None] == all_doc[None, :]) & (own_pos[:, None] >= all_pos[None, :])
    cosine, sine_table = rotary_tables(own_offset, head_dim)
    cosine_all, sine_all = rotary_tables(all_offset, head_dim)

    inputs = hidden_in.astype(f32)
    inverse_one = lax.rsqrt(jnp.mean(inputs * inputs, axis=-1, keepdims=True) + epsilon)
    unit_one = inputs * inverse_one
    normed = (unit_one * gain_one).astype(bf16)
    group_in = group_hidden.reshape(group_len, model_width).astype(f32)
    group_unit = group_in * lax.rsqrt(jnp.mean(group_in * group_in, axis=-1, keepdims=True) + epsilon)
    group_normed = (group_unit * gain_one).astype(bf16)

    queries = rotate(
        dense_dot(normed, full_query).reshape(tok_count, HEADS, head_dim), cosine, sine_table
    ).astype(bf16)
    key_rows = rotate(
        dense_dot(group_normed, full_key).reshape(group_len, HEADS, head_dim), cosine_all, sine_all
    ).astype(bf16)
    value_rows = dense_dot(group_normed, full_value).astype(bf16).reshape(group_len, HEADS, head_dim)

    def masked_scores():
        raw_scores = (
            jnp.einsum("qhd,khd->hqk", queries, key_rows, preferred_element_type=f32) * attn_scale
        )
        return jnp.where(allowed[None], raw_scores, -1e30)

    scores = masked_scores()
    row_peak = jnp.max(scores, axis=-1, keepdims=True)
    row_total = jnp.sum(jnp.exp(scores - row_peak), axis=-1, keepdims=True)
    softmaxed = jnp.exp(scores - row_peak) / row_total
    attended = (
        jnp.einsum("hqk,khd->qhd", softmaxed.astype(bf16), value_rows, preferred_element_type=f32)
        .reshape(tok_count, width)
        .astype(bf16)
    )
    residual = inputs + dense_dot(attended, full_out)
    inverse_two = lax.rsqrt(jnp.mean(residual * residual, axis=-1, keepdims=True) + epsilon)
    unit_two = residual * inverse_two
    normed_two = (unit_two * gain_two).astype(bf16)

    affinity = jax.nn.softmax(dense_dot(normed_two, full_router), axis=-1)
    expert_range = jnp.arange(experts, dtype=jnp.int32)
    named = jnp.any(expert_ids[:, :, None] == expert_range[None, None, :], axis=1)
    signed = jnp.where(named, affinity, -affinity)

    first_expert = lax.axis_index("ep") * exp_local
    n_routed = exp_local * exp_hidden
    hidden = n_routed + sh_rows
    gate_w = jnp.concatenate([expert_gate.reshape(n_routed, model_width), shared_t[0]])
    up_w = jnp.concatenate([expert_up.reshape(n_routed, model_width), shared_t[1]])
    down_w = jnp.concatenate([expert_down.reshape(n_routed, model_width), shared_down])

    def mixture(rows, cot_rows, signed):
        count = rows.shape[0]
        mine = lax.dynamic_slice_in_dim(signed, first_expert, exp_local, axis=1)
        mine_named = mine > 0
        gates = jnp.where(mine_named, mine, 0.0)
        scale = jnp.concatenate(
            [jnp.repeat(gates, exp_hidden, axis=1), jnp.ones((count, sh_rows), f32)], axis=1
        )
        gate_pre = dot_nt(rows, gate_w)
        up_pre = dot_nt(rows, up_w)
        sigma = jax.nn.sigmoid(gate_pre)
        silu = gate_pre * sigma
        act = silu * up_pre
        act_scaled = (act * scale).astype(bf16)
        out_part = dense_dot(act_scaled, down_w).astype(bf16)
        grad_hidden = dot_nt(cot_rows, down_w)
        grad_gates = jnp.sum(
            (act * grad_hidden)[:, :n_routed].reshape(count, exp_local, exp_hidden), axis=-1
        )
        grad_gates = jnp.where(mine_named, grad_gates, 0.0)
        grad_hidden = grad_hidden * scale
        grad_gate_pre = (grad_hidden * up_pre * sigma * (1.0 + gate_pre * (1.0 - sigma))).astype(
            bf16
        )
        grad_up_pre = (grad_hidden * silu).astype(bf16)
        affinity_all = jnp.abs(signed)
        grad_aff = lax.dynamic_update_slice_in_dim(
            jnp.zeros((count, experts), f32), grad_gates, first_expert, axis=1
        )
        grad_logits = (
            affinity_all * (grad_aff - jnp.sum(affinity_all * grad_aff, axis=-1, keepdims=True))
        ).astype(bf16)
        dn2_part = (
            dense_dot(grad_gate_pre, gate_w)
            + dense_dot(grad_up_pre, up_w)
            + dot_nt(grad_logits, full_router)
        ).astype(bf16)
        sums = (
            dot_tn(act_scaled, cot_rows),
            dot_tn(grad_gate_pre, rows),
            dot_tn(grad_up_pre, rows),
            dot_tn(rows, grad_logits),
        )
        return out_part, dn2_part, sums

    rows, signed_all = [lax.all_gather(v, AXES, axis=0, tiled=True) for v in (normed_two, signed)]
    blocks = max(1, tokens * hidden * 4 // 2**23)
    while tokens % blocks:
        blocks += 1

    def step(totals, block):
        out_block, dn2_block, sums = mixture(*block)
        return jax.tree.map(jnp.add, totals, sums), (out_block, dn2_block)

    zeros = (jnp.zeros((hidden, model_width), f32),) * 3 + (
        jnp.zeros((model_width, experts), f32),
    )
    sums, (out_part, dn2_part) = lax.scan(
        step,
        zeros,
        jax.tree.map(
            lambda v: v.reshape((blocks, -1) + v.shape[1:]), (rows, cot_all, signed_all)
        ),
    )
    grad_down, grad_gate, grad_up, router_part = sums
    routed_sum, grad_normed_two = [
        lax.psum_scatter(v.reshape(tokens, model_width), AXES, tiled=True).astype(f32)
        for v in (out_part, dn2_part)
    ]
    layer_output = (residual + routed_sum).astype(bf16)

    gain_two_part = jnp.sum(grad_normed_two * unit_two, axis=0)
    grad_resid = cotangent.astype(f32) + norm_back(grad_normed_two, unit_two, inverse_two, gain_two)
    grad_resid_low = grad_resid.astype(bf16)
    wout_part = dot_tn(attended, grad_resid_low)
    grad_att = dot_nt(grad_resid_low, full_out).astype(bf16).reshape(tok_count, HEADS, head_dim)
    softmax_again = jnp.exp(masked_scores() - row_peak) / row_total
    grad_soft = jnp.einsum("qhd,khd->hqk", grad_att, value_rows, preferred_element_type=f32)
    grad_scores = (
        softmax_again * (grad_soft - jnp.sum(softmax_again * grad_soft, axis=-1, keepdims=True))
    ).astype(bf16)
    grad_queries = (
        jnp.einsum("hqk,khd->qhd", grad_scores, key_rows, preferred_element_type=f32) * attn_scale
    )
    grad_key_rows = (
        jnp.einsum("hqk,qhd->khd", grad_scores, queries, preferred_element_type=f32) * attn_scale
    )
    grad_value_rows = jnp.einsum(
        "hqk,qhd->khd", softmax_again.astype(bf16), grad_att, preferred_element_type=f32
    )
    grad_q_pre = rotate(grad_queries, cosine, -sine_table).reshape(tok_count, width).astype(bf16)
    grad_k_pre = rotate(grad_key_rows, cosine_all, -sine_all).reshape(group_len, width).astype(bf16)
    grad_v_pre = grad_value_rows.reshape(group_len, width).astype(bf16)
    wq_part = dot_tn(normed, grad_q_pre)
    wk_part = dot_tn(group_normed, grad_k_pre)
    wv_part = dot_tn(group_normed, grad_v_pre)
    own_normed_grad = dot_nt(grad_q_pre, full_query)
    group_normed_grad = dot_nt(grad_k_pre, full_key) + dot_nt(grad_v_pre, full_value)
    gain_one_part = jnp.sum(own_normed_grad * unit_one, axis=0) + jnp.sum(
        group_normed_grad * group_unit, axis=0
    )

    weight_part = jnp.concatenate([wq_part, wk_part, wv_part, wout_part], axis=1).astype(bf16)
    small_part = jnp.concatenate(
        [
            router_part.reshape(devices, n_router),
            gain_one_part.reshape(devices, d_rows),
            gain_two_part.reshape(devices, d_rows),
        ],
        axis=1,
    )
    small_part = jnp.pad(small_part, ((0, 0), (0, small_len - small_part.shape[1])))
    small_part = small_part.reshape(devices, -1, model_width)
    small_part = jnp.pad(small_part, ((0, 0), (0, -small_part.shape[1] % 16), (0, 0))).astype(bf16)
    weight_part = weight_part.reshape(devices, d_rows, 4 * width)
    group_part = group_normed_grad.astype(bf16).reshape(tps, tok_count, model_width)
    weight_sum, small_sum = [
        lax.psum_scatter(v, AXES).astype(f32) for v in (weight_part, small_part)
    ]
    normed_grad_sum = lax.psum_scatter(group_part, "tp").astype(f32)
    grad_normed = own_normed_grad + normed_grad_sum
    input_grad = grad_resid + norm_back(grad_normed, unit_one, inverse_one, gain_one)
    small_sum = small_sum.reshape(-1)

    shared_back = jnp.stack([grad_gate[n_routed:], grad_up[n_routed:]])
    shared_back = shared_back.reshape(2, sh_rows, devices, d_rows).transpose(2, 0, 1, 3)
    shared_back = lax.all_to_all(shared_back, AXES, split_axis=0, concat_axis=0, tiled=True)
    shared_back = shared_back.transpose(1, 3, 0, 2).reshape(2, d_rows, devices * sh_rows)

    return (
        layer_output,
        input_grad,
        small_sum[n_router : n_router + d_rows],
        weight_sum[:, :width],
        weight_sum[:, width : 2 * width],
        weight_sum[:, 2 * width : 3 * width],
        weight_sum[:, 3 * width :],
        small_sum[n_router + d_rows : n_router + 2 * d_rows],
        shared_back[0],
        shared_back[1],
        grad_down[n_routed:],
        small_sum[:n_router].reshape(d_rows, experts),
        grad_gate[:n_routed].reshape(expert_gate.shape),
        grad_up[:n_routed].reshape(expert_up.shape),
        grad_down[:n_routed].reshape(expert_down.shape),
    )


def small_slice(
    hidden_in,
    seq_lengths,
    expert_ids,
    attn_gain,
    w_query,
    w_key,
    w_value,
    w_out,
    ffn_gain,
    shared_gate,
    shared_up,
    shared_down,
    router,
    expert_gate,
    expert_up,
    expert_down,
    cotangent,
):
    tok_count, model_width = hidden_in.shape
    eps, tps = lax.axis_size("ep"), lax.axis_size("tp")
    devices = eps * tps
    exp_local, exp_hidden = expert_gate.shape[:2]
    experts = exp_local * eps
    group_len = tps * tok_count
    tokens = devices * tok_count
    d_rows = w_query.shape[0]
    width = w_query.shape[1]
    sh_rows = shared_down.shape[0]
    head_dim = width // HEADS
    attn_scale = head_dim ** (-0.5)

    lanes = 128
    vectors = jnp.stack([attn_gain, ffn_gain], axis=1)
    small = jnp.concatenate([router, vectors], axis=1)
    small = jnp.pad(small, ((0, 0), (0, lanes - small.shape[1])))
    (
        w_all, cot_all, normed_two, aux, small_t, residual, attended, queries, key_rows, value_rows,
        group_normed, cos_all, sin_all, group_hidden, shared,
    ) = front_call(
        seq_lengths, expert_ids, hidden_in, small, (w_query, w_key, w_value, w_out),
        (shared_gate, shared_up, shared_down), cotangent, experts, attn_scale, 0,
    )
    first_expert = lax.axis_index("ep") * exp_local
    n_routed = exp_local * exp_hidden
    hidden = n_routed + sh_rows
    h_core = n_routed + shared.shape[1]
    owner = jnp.arange(h_core, dtype=jnp.int32)
    owner = jnp.where(owner < n_routed, first_expert + owner // exp_hidden, experts)
    owner = jnp.concatenate([owner, owner])
    sel_t = (owner[:, None] == jnp.arange(lanes, dtype=jnp.int32)[None, :]).astype(bf16)
    sel = jnp.concatenate([sel_t[:, :experts].T, jnp.eye(experts, lanes, dtype=bf16)], axis=1)
    sel = jnp.concatenate([sel, sel])
    ones = (jnp.arange(2 * h_core, dtype=jnp.int32) % h_core)[None, :]
    ones = ((ones >= n_routed) & (ones < hidden)).astype(f32)
    token_grads, out_parts, grads_here, grads_away, router_sum = mixture_call(
        normed_two,
        aux,
        cot_all,
        [w.reshape(n_routed, model_width) for w in (expert_gate, expert_up, expert_down)],
        shared,
        sel,
        sel_t,
        small_t,
        ones,
        2,
    )
    (
        layer_output, input_grad, grad_q, grad_k, grad_v, grad_o, small_sum, grad_sg, grad_su, grads_there,
    ) = back_call(
        seq_lengths, token_grads, residual, cotangent, group_hidden, small_t, router_sum, attended,
        queries, group_normed, cos_all, sin_all, key_rows, value_rows, w_all, out_parts,
        grads_here, grads_away, d_rows, experts, attn_scale, sh_rows, 3,
    )
    grad_gate, grad_up, grad_down = [
        (grads_here[k, :n_routed] + grads_there[k, :n_routed]).reshape(expert_gate.shape)
        for k in range(3)
    ]
    grad_sd = grads_here[2, n_routed:hidden] + grads_there[2, n_routed:hidden]

    return (
        layer_output,
        input_grad,
        small_sum[:, experts],
        grad_q,
        grad_k,
        grad_v,
        grad_o,
        small_sum[:, experts + 1],
        grad_sg,
        grad_su,
        grad_sd,
        small_sum[:, :experts],
        grad_gate,
        grad_up,
        grad_down,
    )


def solution(mesh):
    rows = P(AXES, None)
    vector = P(AXES)
    experts = P("ep", "tp", None)
    small = mesh.shape["ep"] == 8 and mesh.shape["tp"] == 4
    return jax.shard_map(
        small_slice if small else any_slice,
        mesh=mesh,
        in_specs=(
            rows, P("ep", None), rows, vector, rows, rows, rows, rows, vector,
            rows, rows, rows, rows, experts, experts, experts, rows,
        ),
        out_specs=(
            rows, rows, vector, rows, rows, rows, rows, vector,
            rows, rows, rows, rows, experts, experts, experts,
        ),
        check_vma=False,
    )
```

```python
import functools

import jax
import jax.numpy as jnp
from jax import lax
from jax.experimental import pallas as pl
from jax.experimental.pallas import tpu as pltpu
from jax.sharding import PartitionSpec as P

HEADS = 10
AXES = ("ep", "tp")
MESH = pl.DeviceIdType.MESH
VMEM_BUDGET = 56 * 2**20

epsilon = 1e-06

bf16 = jnp.bfloat16
f32 = jnp.float32


def place():
    ep, tp = lax.axis_index("ep"), lax.axis_index("tp")
    return ep // 2, ep % 2, tp // 2, tp % 2


def device(line, a, b, c):
    return (line * 2 + a, b * 2 + c)


def number(line, a, b, c):
    return ((line * 2 + a) * 2 + b) * 2 + c


def greet(partners):
    barrier = pltpu.get_barrier_semaphore()
    for partner in partners:
        pl.semaphore_signal(barrier, inc=1, device_id=partner, device_id_type=MESH)
    pl.semaphore_wait(barrier, len(partners))


O, X, Y, D = 0, 1, 2, 3


def visit_order(lines):
    return [
        sorted(range(lines), key=lambda other: (abs(other - z), other != z ^ 1)) for z in range(lines)
    ]


def lookup(table, index):
    out = jnp.int32(table[0])
    for k in range(1, len(table)):
        out = jnp.where(index == k, jnp.int32(table[k]), out)
    return out


def pick(values, index):
    out = values[0]
    for k in range(1, len(values)):
        out = jnp.where(index == k, values[k], out)
    return out


class Ways:
    def __init__(self, lines):
        self.lines = lines
        z, a, b, c = self.spot = place()
        oa, ob, oc = 1 - a, 1 - b, 1 - c
        self.to_b, self.to_a = device(z, a, ob, c), device(z, oa, b, c)
        self.to_c = device(z, a, b, oc)
        self.up_next = device(lax.rem(z + 1, lines), a, b, c)
        self.down_next = device(lax.rem(z + lines - 1, lines), a, b, c)
        self.peers = [device(lax.rem(z + s, lines), a, b, c) for s in range(1, lines)]
        table = visit_order(lines)
        self.zs = [lookup([table[k][u] for k in range(lines)], z) for u in range(lines)]
        self.column = ((a, b), (a, ob), (oa, b), (oa, ob))
        self.pair = device(z + 1 - 2 * lax.rem(z, 2), a, b, c)
        outer = (z == 0) | (z == lines - 1)
        self.carried = [True, False, outer, jnp.logical_not(outer)]

    def greet(self):
        greet([self.to_b, self.to_a, self.to_c] + self.peers)

    def chip(self, line, kind):
        a, b = self.column[kind]
        return (line * 2 + a) * 2 + b


def when(condition, act):
    if condition is True:
        act()
    elif condition is not False:

        @pl.when(condition)
        def _():
            act()


def other(condition):
    return not condition if isinstance(condition, bool) else jnp.logical_not(condition)


def remote(src, dst, send_sem, recv_sem, to):
    return pltpu.make_async_remote_copy(
        src, dst, send_sem, recv_sem, device_id=to, device_id_type=MESH
    )


class Gather:
    def __init__(self, ways, chunk, sems, own=None, relative=False, across=False):
        self.ways, self.chunk, self.own = ways, chunk, own
        self.send_sem, self.recv_sem = sems
        self.relative, self.across_core = relative, across

    def copy(self, slot, step, src, dst, to):
        k = slot * self.ways.lines + step
        return remote(src, dst, self.send_sem(k), self.recv_sem(k), to)

    def hop(self, slot, step, kind, to_kind, line, to, part=None, own=False):
        src = self.own if own and self.own is not None else self.chunk(line, kind, part, False)
        dst = self.chunk(line, to_kind if self.relative else kind, part, False)
        return self.copy(slot, step, src, dst, to)

    def sends(self, u):
        w, own = self.ways, u == 0
        line, carried = w.zs[u], w.carried[u]
        copies = {
            "X": (True, lambda: self.hop(0, u, O, X, line, w.to_b, own=own)),
            "Y": (True, lambda: self.hop(1, u, O, Y, line, w.to_a, own=own)),
            "p": (carried, lambda: self.hop(2, u, X, D, line, w.to_a, 0)),
            "q": (carried, lambda: self.hop(3, u, Y, D, line, w.to_b, 1)),
            "pair": (carried, lambda: self.hop(11, 1 if own else u, D, D, line, w.pair)),
        }
        if self.across_core:

            def across(slot, kind):
                here = self.chunk(line, kind, None, False)
                src = self.own if kind == O and own and self.own is not None else here
                return self.copy(slot, u, src, here, w.to_c)

            for kind, slot in ((O, 6), (X, 7), (Y, 8), (D, 9)):
                copies[kind] = (True, lambda slot=slot, kind=kind: across(slot, kind))
        return copies

    def send(self, u, *names, condition=True):
        copies = self.sends(u)
        for name in names:
            if name in copies:
                always, make = copies[name]
                when(always if condition is True else condition, lambda: make().start())

    def arrival(self, slot, step, kind, line, part=None, other=False):
        here = self.chunk(line, kind, part, other)
        self.copy(slot, step, here, here, self.ways.to_c).wait_recv()

    def send_own(self, u):
        self.send(u, "X", "Y", O)

    def xy_event(self, u):
        line = self.ways.zs[u]
        self.arrival(0, u, X, line)
        self.send(u, "p")
        self.arrival(1, u, Y, line)
        self.send(u, "q", X, Y)

    def diag_carried(self, u):
        line, carried = self.ways.zs[u], self.ways.carried[u]

        def halves():
            self.arrival(2, u, D, line, 0)
            self.arrival(3, u, D, line, 1)

        when(carried, halves)
        self.send(u, "pair")
        self.send(u, D, condition=carried)

    def diag_handed(self, u):
        handed = other(self.ways.carried[u])
        when(handed, lambda: self.arrival(11, u, D, self.ways.zs[u]))
        self.send(u, D, condition=handed)

    def chain_up(self, k):
        w = self.ways
        return self.hop(4, k, O, O, w.spot[0] - (k - 1), w.up_next, own=k == 1)

    def chain_down(self, k):
        w = self.ways
        return self.hop(5, k, O, O, w.spot[0] + (k - 1), w.down_next, own=k == 1)

    def chain_start(self, k):
        z, lines = self.ways.spot[0], self.ways.lines
        if k >= lines:
            return

        @pl.when((z >= k - 1) & (z + 1 < lines))
        def _():
            self.chain_up(k).start()

        @pl.when((z + k - 1 < lines) & (z > 0))
        def _():
            self.chain_down(k).start()

    def chain_event(self, k):
        z, lines = self.ways.spot[0], self.ways.lines

        @pl.when(z >= k)
        def _():
            self.arrival(4, k, O, z - k)

        @pl.when(z + k < lines)
        def _():
            self.arrival(5, k, O, z + k)

        self.chain_start(k + 1)

    def begin(self):
        self.send_own(0)
        self.chain_start(1)

    def events(self):
        out = [
            lambda: (self.xy_event(0), self.chain_event(1), self.send_own(1)),
            lambda: (self.diag_carried(0), self.chain_event(2), self.send_own(2)),
            lambda: (self.xy_event(1), self.chain_event(3), self.send_own(3)),
            lambda: (self.xy_event(2), self.diag_handed(1)),
            lambda: (self.diag_carried(2), self.xy_event(3)),
            lambda: (self.diag_carried(3), self.diag_handed(2)),
            lambda: self.diag_handed(3),
        ]
        return out

    def other_core(self):
        if self.across_core:
            for u in range(self.ways.lines):
                for slot, kind in ((6, O), (7, X), (8, Y), (9, D)):
                    self.arrival(slot, u, kind, self.ways.zs[u], None, True)

    def drain_unit(self, u):
        for condition, make in self.sends(u).values():
            when(condition, lambda make=make: make().wait_send())

    def drain_chain(self, k):
        z, lines = self.ways.spot[0], self.ways.lines

        @pl.when((z >= k - 1) & (z + 1 < lines))
        def _():
            self.chain_up(k).wait_send()

        @pl.when((z + k - 1 < lines) & (z > 0))
        def _():
            self.chain_down(k).wait_send()

    def drain(self, units=None):
        for u in range(self.ways.lines if units is None else units):
            self.drain_unit(u)
        for k in range(1, self.ways.lines):
            self.drain_chain(k)


class Exchange:
    def __init__(self, ways, blocks, r1, r2, r3, got, sems):
        self.ways, self.blocks, self.r1, self.r2, self.r3, self.got = ways, blocks, r1, r2, r3, got
        self.send_sem, self.recv_sem = sems

    def copy(self, k, src, dst, to):
        return remote(src, dst, self.send_sem(k), self.recv_sem(k), to)

    def over_core(self):
        w = self.ways
        oc = 1 - w.spot[3]
        return [self.copy(0, self.blocks.at[:, :, :, oc], self.r1, w.to_c)]

    def over_b(self):
        w = self.ways
        z, a, b, c = w.spot
        sources = (self.blocks.at[:, :, 1 - b, c], self.r1.at[:, :, 1 - b])
        return [self.copy(1 + k, src, self.r2.at[k], w.to_b) for k, src in enumerate(sources)]

    def over_a(self):
        w = self.ways
        z, a, b, c = w.spot
        oa = 1 - a
        sources = (
            self.blocks.at[:, oa, b, c], self.r1.at[:, oa, b], self.r2.at[0, :, oa], self.r2.at[1, :, oa],
        )
        return [self.copy(3 + k, src, self.r3.at[4 + k], w.to_a) for k, src in enumerate(sources)]

    def over_line(self):
        w = self.ways
        z, a, b, c = w.spot
        out = []
        for step in range(1, w.lines):
            there = lax.rem(z + step, w.lines)
            out.append(
                self.copy(6 + step, self.r3.at[:, there], self.got.at[z], device(there, a, b, c))
            )
        return out

    def line_arrival(self, step):
        w = self.ways
        here = self.got.at[lax.rem(w.spot[0] + w.lines - step, w.lines)]
        self.copy(6 + step, here, here, w.to_c).wait_recv()

    def start(self, copies):
        for copy in copies:
            copy.start()

    def arrive(self, copies):
        for copy in copies:
            copy.wait_recv()

    def collect(self):
        z, a, b, c = self.ways.spot
        for line in range(self.ways.lines):
            self.r3[0, line] = self.blocks[line, a, b, c]
            self.r3[1, line] = self.r1[line, a, b]
            for k in range(2):
                self.r3[2 + k, line] = self.r2[k, line, a]

    def events(self):
        z = self.ways.spot[0]
        return [
            lambda: self.start(self.over_core()),
            lambda: (self.arrive(self.over_core()), self.start(self.over_b())),
            lambda: (self.arrive(self.over_b()), self.start(self.over_a())),
            lambda: (self.arrive(self.over_a()), self.collect(), self.start(self.over_line())),
            lambda: [self.line_arrival(step) for step in range(1, self.ways.lines)],
        ]

    def block(self, line, a, b, c):
        z, ma, mb, mc = self.ways.spot
        i = jnp.abs(a - ma) * 4 + jnp.abs(b - mb) * 2 + jnp.abs(c - mc)
        own = self.r3[i, z]
        return jnp.where(line == z, own, self.got[line, i])

    def drain(self):
        for copies in (self.over_core(), self.over_b(), self.over_a(), self.over_line()):
            for copy in copies:
                copy.wait_send()


def exchange_scratch(lines, rows):
    return [
        pltpu.VMEM((lines, 2, 2, 2, rows, 128), bf16),
        pltpu.VMEM((lines, 2, 2, rows, 128), bf16),
        pltpu.VMEM((2, lines, 2, rows, 128), bf16),
        pltpu.VMEM((8, lines, rows, 128), bf16),
        pltpu.VMEM((lines, 8, rows, 128), bf16),
    ]


def all_places(lines):
    return [(d, d // 8, d // 4 % 2, d // 2 % 2, d % 2) for d in range(8 * lines)]


def padded_rows(value, rows):
    return jnp.concatenate([value, jnp.zeros((rows - value.shape[0],) + value.shape[1:], value.dtype)])


def softmax_rows(scores):
    weights = jnp.exp(scores - jnp.max(scores, axis=-1, keepdims=True))
    return weights * (1.0 / jnp.sum(weights, axis=-1, keepdims=True))


def turn(values, cosine, signed_sine):
    return values * cosine + pltpu.roll(values, values.shape[-1] // 2, 1) * signed_sine


def document_of(positions, first_end, second_end):
    return (positions >= first_end).astype(jnp.int32) + (positions >= second_end).astype(jnp.int32)


def make_bias(bias, lengths, tp_index):
    rows, cols = bias.shape
    first_end = lengths[0, 0]
    second_end = first_end + lengths[0, 1]
    q_pos = lax.broadcasted_iota(jnp.int32, (rows, cols), 0) + tp_index * rows
    k_pos = lax.broadcasted_iota(jnp.int32, (rows, cols), 1)
    allowed = (
        document_of(q_pos, first_end, second_end) == document_of(k_pos, first_end, second_end)
    ) & (q_pos >= k_pos)
    bias[...] = jnp.where(allowed, 0.0, -1e30)


def front_kernel(lines, experts, scale, *refs):
    (
        lengths, ids, freq, hidden, small, wq, wk, wv, wo, s_gate, s_up, s_down, cot,
        w_out, cot_out, tok, aux, small_t, residual, attended, q_out, k_far, v_far, n_far,
        cos_out, sin_out, group_far, shared,
        k_out, v_out, n_out, group, wall, stage, small_stage, small_all, bias, e_blocks, e_r1, e_r2, e_r3, e_got,
        g_send, g_recv, s_send, s_recv, x_send, x_recv, e_send, e_recv, local_sem,
    ) = refs
    ways = Ways(lines)
    z, a, b, c = ways.spot
    ob, oc = 1 - b, 1 - c
    count, width = hidden.shape
    d_rows = wq.shape[0]
    chip_rows = 2 * d_rows
    half = width // 2
    heads = width // 128
    group_len = 4 * count
    ways.greet()

    def cot_chunk(line, kind, part, other):
        first = (line * 4 + kind) * count
        if part is None:
            return cot_out.at[pl.ds(first, count)]
        return cot_out.at[pl.ds(first + part * (count // 2), count // 2)]

    def sems(i):
        return (lambda k: g_send.at[i, k], lambda k: g_recv.at[i, k])

    g_cot = Gather(ways, cot_chunk, sems(3), own=cot, relative=True)
    g_cot.begin()

    shards = (wq, wk, wv, wo)
    swaps = [
        remote(
            shards[k].at[:, pl.ds(pl.multiple_of(oc * half, 128), half)], stage.at[k],
            s_send.at[k], s_recv.at[k], ways.to_c,
        )
        for k in range(4)
    ] + [remote(small, small_stage, s_send.at[4], s_recv.at[4], ways.to_c)]
    for copy in swaps:
        copy.start()

    def group_copy(k, src, dst, to):
        return remote(src, dst, x_send.at[k], x_recv.at[k], to)

    own_group = group.at[b * 2 + c]
    group_copies = [group_copy(0, hidden, own_group, ways.to_c), group_copy(1, hidden, own_group, ways.to_b)]
    for copy in group_copies:
        copy.start()
    own_group[...] = hidden[...]

    def chip_block(own, other):
        own, other = own.astype(f32), other.astype(f32)
        first = jnp.where(c == 0, own, other)
        second = jnp.where(c == 0, other, own)
        return jnp.concatenate([first, second], axis=0).astype(bf16)

    sh = s_down.shape[0]
    block_rows = e_blocks.shape[4]
    lane = lax.broadcasted_iota(jnp.int32, (d_rows, 128), 1)

    def columns_at(ref, first, to):
        tile, start = first // 128 * 128, first % 128
        value = pltpu.roll(ref[:, tile : tile + 128].astype(f32), (to - start) % 128, 1)
        if start + sh > 128:
            later = pltpu.roll(ref[:, tile + 128 : tile + 256].astype(f32), (to - start) % 128, 1)
            value = jnp.where(lane < to + 128 - start, value, later)
        return value

    for d, line, da, db, dc in all_places(lines):
        gate, up = columns_at(s_gate, d * sh, 0), columns_at(s_up, d * sh, 64)
        value = jnp.where(lane < sh, gate, jnp.where((lane >= 64) & (lane < 64 + sh), up, 0.0))
        e_blocks[line, da, db, dc] = padded_rows(value, block_rows).astype(bf16)
    exchange = Exchange(
        ways, e_blocks, e_r1, e_r2, e_r3, e_got, (lambda k: e_send.at[k], lambda k: e_recv.at[k])
    )
    e_events = exchange.events()

    base = pl.multiple_of(ways.chip(z, O) * chip_rows, 16)
    for copy in swaps:
        copy.wait_recv()
    small_all[pl.ds(base, chip_rows), :] = chip_block(small[...], small_stage[...])
    for k in range(4):
        mine = shards[k][:, pl.ds(pl.multiple_of(c * half, 128), half)]
        wall[pl.ds(base, chip_rows), pl.ds(pl.multiple_of((c * 4 + k) * half, 128), half)] = chip_block(
            mine, stage[k]
        )

    def small_chunk(line, kind, part, other):
        rows = pl.multiple_of(ways.chip(line, kind) * chip_rows, 16)
        if part is None:
            return small_all.at[pl.ds(rows, chip_rows)]
        low = chip_rows // 32 * 16
        return small_all.at[pl.ds(rows, low) if part == 0 else pl.ds(rows + low, chip_rows - low)]

    def weight_chunk(first, cols, cut):
        def chunk(line, kind, part, other):
            rows = pl.multiple_of(ways.chip(line, kind) * chip_rows, 16)
            col = (oc if other else c) * 4 * half + first
            if part is None:
                start, size = col, cols
            elif part == 0:
                start, size = col, cut
            else:
                start, size = col + cut, cols - cut
            return wall.at[pl.ds(rows, chip_rows), pl.ds(pl.multiple_of(start, 128), size)]

        return chunk

    tiles = half // 128
    g_small = Gather(ways, small_chunk, sems(0))
    g_qkv = Gather(ways, weight_chunk(0, 3 * half, (3 * tiles + 1) // 2 * 128), sems(1), across=True)
    g_out = Gather(ways, weight_chunk(3 * half, half, tiles // 2 * 128), sems(2), across=True)
    keep = pltpu.make_async_copy(cot, cot_chunk(z, O, None, False), local_sem.at[0])
    keep.start()
    g_small.begin()
    g_qkv.begin()
    e_events[0]()

    first_end = lengths[0, 0]
    second_end = first_end + lengths[0, 1]
    position = lax.broadcasted_iota(jnp.int32, (group_len, 128), 0)
    doc = document_of(position, first_end, second_end)
    start = jnp.where(doc == 0, 0, jnp.where(doc == 1, first_end, second_end))
    angles = (position - start).astype(f32) * freq[...]
    lane = lax.broadcasted_iota(jnp.int32, (group_len, 128), 1)
    cos_out[...] = jnp.cos(angles)
    sin_out[...] = jnp.where(lane < 64, -1.0, 1.0) * jnp.sin(angles)
    make_bias(bias, lengths, b * 2 + c)
    got = group.at[ob * 2 + c]
    group_copy(1, got, got, ways.to_b).wait_recv()
    group_copies.append(group_copy(2, got, got, ways.to_c))
    group_copies[-1].start()
    for k, t in ((0, b * 2 + oc), (2, ob * 2 + oc)):
        got = group.at[t]
        group_copy(k, got, got, ways.to_c).wait_recv()

    small_events, qkv_events = g_small.events(), g_qkv.events()
    out_events = g_out.events()
    cot_events = {
        1: lambda: (g_cot.xy_event(0), g_cot.chain_event(1), g_cot.send_own(1)),
        2: lambda: (g_cot.diag_carried(0), g_cot.chain_event(2)),
        4: lambda: (g_cot.xy_event(1), g_cot.chain_event(3)),
        5: lambda: g_cot.diag_handed(1),
    }
    for k in range(len(qkv_events)):
        if k == 3:
            g_out.begin()
        qkv_events[k]()
        small_events[k]()
        if k in cot_events:
            cot_events[k]()
        if 2 <= k < 6:
            e_events[k - 1]()
        if k >= 4:
            out_events[k - 4]()
    flat = jnp.transpose(small_all[...].astype(f32))
    small_t[...] = flat.astype(bf16)
    gain_one = flat[experts : experts + 1, :]
    gain_two = flat[experts + 1 : experts + 2, :]
    for t in range(4):
        x = group[t].astype(f32)
        r = lax.rsqrt(jnp.mean(x * x, axis=-1, keepdims=True) + epsilon)
        n_out[t * count : (t + 1) * count, :] = (x * r * gain_one).astype(bf16)
    g_qkv.other_core()

    later = out_events[3:] + [g_out.other_core]

    def service(n=1):
        for _ in range(n):
            if later:
                later.pop(0)()

    stacked = jnp.concatenate(
        [exchange.block(*there)[:d_rows].astype(f32) for _, *there in all_places(lines)]
    )
    turned = jnp.transpose(stacked)
    shared[0] = turned[:64].astype(bf16)
    shared[1] = turned[64:].astype(bf16)
    shared[2] = padded_rows(s_down[...].astype(f32), 64).astype(bf16)
    own_rows = pl.ds(pl.multiple_of((b * 2 + c) * count, count), count)
    for h in range(2):
        cols = pl.ds((h * 4 + 1) * half, half)
        keys = dense_dot(n_out[...], wall[:, cols])
        for j in range(half // 128):
            k_out[:, h * half + j * 128 : h * half + (j + 1) * 128] = turn(
                keys[:, j * 128 : (j + 1) * 128], cos_out[...], sin_out[...]
            ).astype(bf16)
        service()
        cols = pl.ds((h * 4 + 2) * half, half)
        v_out[:, h * half : (h + 1) * half] = dense_dot(n_out[...], wall[:, cols]).astype(bf16)
        service()
        queries = dense_dot(n_out[own_rows, :], wall[:, pl.ds(h * 4 * half, half)])
        for j in range(half // 128):
            q_out[:, h * half + j * 128 : h * half + (j + 1) * 128] = turn(
                queries[:, j * 128 : (j + 1) * 128], cos_out[own_rows, :], sin_out[own_rows, :]
            ).astype(bf16)
        service()
    for h in range(heads):
        cols = pl.ds(h * 128, 128)
        probs = softmax_rows(dot_nt(q_out[:, cols], k_out[:, cols]) * scale + bias[...])
        attended[:, cols] = dense_dot(probs.astype(bf16), v_out[:, cols]).astype(bf16)
        if h % 2:
            service()
    service(len(later))
    saves = [
        pltpu.make_async_copy(src, dst, local_sem.at[1 + k])
        for k, (src, dst) in enumerate(
            ((wall, w_out), (k_out, k_far), (v_out, v_far), (n_out, n_far), (group, group_far))
        )
    ]
    for save in saves:
        save.start()
    for h in range(2):
        projected = dense_dot(attended[...], wall[:, pl.ds((h * 4 + 3) * half, half)])
        residual[:, h * half : (h + 1) * half] = (
            hidden[:, h * half : (h + 1) * half].astype(f32) + projected
        )
    service()
    res = residual[...]
    r2 = lax.rsqrt(jnp.mean(res * res, axis=-1, keepdims=True) + epsilon)
    normed = (res * r2 * gain_two).astype(bf16)
    tok[...] = normed
    logits = dense_dot(normed, small_all[...])
    lane = lax.broadcasted_iota(jnp.int32, (count, 128), 1)
    affinity = softmax_rows(jnp.where(lane < experts, logits, -1e30))
    named = lane < 0
    for j in range(ids.shape[1]):
        named = named | (ids[:, j : j + 1] == lane)
    signed = jnp.transpose(jnp.where(named, affinity, -affinity))[:experts, :]
    high = signed.astype(bf16)
    aux[0:experts, :] = high
    aux[experts : 2 * experts, :] = (signed - high.astype(f32)).astype(bf16)
    service(len(later))
    for g in (g_small, g_qkv, g_out, exchange):
        g.drain()
    g_cot.drain(2)
    for copy in swaps + group_copies:
        copy.wait_send()
    keep.wait()
    for save in saves:
        save.wait()


def front_call(
    lengths, ids, hidden, small, weights, shared, cot, experts, scale, collective_id
):
    lines = lax.axis_size("ep") // 2
    count, width = hidden.shape
    d_rows = weights[0].shape[0]
    group_len = 4 * count
    block_rows = -(-d_rows // 16) * 16
    anywhere = pl.BlockSpec(memory_space=pl.ANY)
    vmem = pl.BlockSpec(memory_space=pltpu.VMEM)
    smem = pl.BlockSpec(memory_space=pltpu.SMEM)
    lane = jnp.arange(128) % 64
    freq = (10000.0 ** (-2.0 * lane.astype(f32) / 128))[None, :]
    shape = jax.ShapeDtypeStruct
    return pl.pallas_call(
        functools.partial(front_kernel, lines, experts, scale),
        out_shape=(
            shape((width, 4 * width), bf16),
            shape((lines * 4 * count, width), bf16),
            shape((count, width), bf16),
            shape((2 * experts, count), bf16),
            shape((128, width), bf16),
            shape((count, width), f32),
            shape((count, width), bf16),
            shape((count, width), bf16),
            shape((group_len, width), bf16),
            shape((group_len, width), bf16),
            shape((group_len, width), bf16),
            shape((group_len, 128), f32),
            shape((group_len, 128), f32),
            shape((4, count, width), bf16),
            shape((3, 64, width), bf16),
        ),
        in_specs=[smem] + [vmem] * 11 + [anywhere],
        out_specs=(
            (anywhere,) * 2 + (vmem,) * 6 + (anywhere,) * 3 + (vmem,) * 2 + (anywhere, vmem)
        ),
        scratch_shapes=[
            pltpu.VMEM((group_len, width), bf16),
            pltpu.VMEM((group_len, width), bf16),
            pltpu.VMEM((group_len, width), bf16),
            pltpu.VMEM((4, count, width), bf16),
            pltpu.VMEM((width, 4 * width), bf16),
            pltpu.VMEM((4, d_rows, width // 2), bf16),
            pltpu.VMEM((d_rows, 128), bf16),
            pltpu.VMEM((width, 128), bf16),
            pltpu.VMEM((count, group_len), f32),
            *exchange_scratch(lines, block_rows),
            pltpu.SemaphoreType.DMA((4, 12 * lines)),
            pltpu.SemaphoreType.DMA((4, 12 * lines)),
            pltpu.SemaphoreType.DMA((5,)),
            pltpu.SemaphoreType.DMA((5,)),
            pltpu.SemaphoreType.DMA((3,)),
            pltpu.SemaphoreType.DMA((3,)),
            pltpu.SemaphoreType.DMA((7 + lines,)),
            pltpu.SemaphoreType.DMA((7 + lines,)),
            pltpu.SemaphoreType.DMA((6,)),
        ],
        compiler_params=pltpu.CompilerParams(
            collective_id=collective_id, has_side_effects=True, vmem_limit_bytes=60 * 2**20
        ),
        name="front",
    )(lengths, ids, freq, hidden, small, *weights, *shared, cot)


class Reduce:
    def __init__(self, ways, chunk, cut, pq, xr, yr, dz, zr, sems, alone=()):
        self.ways, self.chunk, self.cut = ways, chunk, cut
        self.pq, self.xr, self.yr, self.dz, self.zr = pq, xr, yr, dz, zr
        self.alone = alone
        self.carried = [True if u in alone else ways.carried[u] for u in range(ways.lines)]
        self.send_sem, self.recv_sem = sems

    def copy(self, slot, u, src, dst, to):
        k = slot * self.ways.lines + u
        return remote(src, dst, self.send_sem(k), self.recv_sem(k), to)

    def diag(self, part, u):
        w = self.ways
        return self.copy(
            part, u, self.chunk(w.zs[u], D, part), self.cut(self.pq, self.slot(u), part),
            w.to_b if part else w.to_a,
        )

    def side_b(self, part, u):
        w = self.ways
        return self.copy(2 + part, u, self.chunk(w.zs[u], X, part), self.cut(self.xr, u, part), w.to_b)

    def side_a(self, part, u):
        w = self.ways
        return self.copy(4 + part, u, self.chunk(w.zs[u], Y, part), self.cut(self.yr, u, part), w.to_a)

    def slot(self, u):
        return max(u - 1, 0) if self.alone else min(u, 1)

    def hand(self, u, at):
        w = self.ways
        return self.copy(
            7, at, self.chunk(w.zs[u], D, None), self.cut(self.dz, min(at, 1), None), w.pair
        )

    def along(self, u):
        w = self.ways
        z, a, b, c = w.spot
        slot = lax.rem(z - w.zs[u] + w.lines, w.lines) - 1
        k = 6 * w.lines
        return remote(
            self.chunk(w.zs[u], O, None), self.zr(slot), self.send_sem(k + u),
            self.recv_sem(k + slot), device(w.zs[u], a, b, c),
        )

    def start(self, u):
        def whole():
            self.hand(u, u if u > 1 else 0).start()
            self.side_b(0, u).start()
            self.side_a(1, u).start()

        self.side_b(1, u).start()
        self.side_a(0, u).start()
        when(other(self.carried[u]), whole)

    def carry(self, u):
        def act():
            if u not in self.alone:
                self.hand(u, u).wait_recv()
            for part in (0, 1):
                if u not in self.alone:
                    accumulate(
                        self.chunk(self.ways.zs[u], D, part), [self.cut(self.dz, min(u, 1), part)]
                    )
                self.diag(part, u).start()

        when(self.carried[u], act)

    def mid(self, u):
        w = self.ways

        def act():
            self.diag(0, u).wait_recv()
            accumulate(self.chunk(w.zs[u], X, 0), [self.cut(self.pq, self.slot(u), 0)])
            self.side_b(0, u).start()
            self.diag(1, u).wait_recv()
            accumulate(self.chunk(w.zs[u], Y, 1), [self.cut(self.pq, self.slot(u), 1)])
            self.side_a(1, u).start()

        when(self.carried[u], act)

    def end(self, u):
        w = self.ways
        for part in (0, 1):
            self.side_b(part, u).wait_recv()
            self.side_a(part, u).wait_recv()
            accumulate(
                self.chunk(w.zs[u], O, part), [self.cut(self.xr, u, part), self.cut(self.yr, u, part)]
            )
        if u > 0:
            self.along(u).start()

    def events(self):
        return [
            lambda: (self.start(2), self.start(3)),
            lambda: (self.carry(2), self.carry(3), self.start(1)),
            lambda: (self.mid(2), self.mid(3), self.start(0)),
            lambda: (self.end(2), self.end(3)),
            lambda: (self.carry(0), self.end(1)),
            lambda: self.mid(0),
            lambda: self.end(0),
        ]

    def total(self):
        w = self.ways
        sums = self.chunk(w.spot[0], O, None)[...].astype(f32)
        for slot in range(w.lines - 1):
            k = 6 * w.lines + slot
            here = self.zr(slot)
            remote(here, here, self.send_sem(k), self.recv_sem(k), w.to_c).wait_recv()
            sums = sums + here[...].astype(f32)
        return sums

    def drain(self):
        w = self.ways
        for u in range(w.lines):
            for part in (0, 1):
                when(self.carried[u], lambda part=part, u=u: self.diag(part, u).wait_send())
                self.side_b(part, u).wait_send()
                self.side_a(part, u).wait_send()
            when(other(self.carried[u]), lambda u=u: self.hand(u, u if u > 1 else 0).wait_send())
            if u > 0:
                self.along(u).wait_send()


def accumulate(dst, others):
    total = dst[...].astype(f32)
    for ref in others:
        total = total + ref[...].astype(f32)
    dst[...] = total.astype(bf16)


def mixture_kernel(lines, tok, aux, cot, wg, wu, wd, shared, sel, sel_t, router_t, ones, *refs):
    (
        sums, out_part, dw_own, dw_sib, dr,
        nc, aux_all, vg, vu, vd, dw, acts, dg, du, daff, dlg, pq, xr, yr, dz, zr,
        ag_send, ag_recv, rs_send, rs_recv, w_send, w_recv, w_local, cot_sem, local_sem,
    ) = refs
    ways = Ways(lines)
    z, a, b, c = ways.spot
    oc = 1 - c
    zs = ways.zs
    count, width = tok.shape
    half = count // 2
    n_routed = wg.shape[0]
    hc = n_routed + shared.shape[1]
    hidden = 2 * hc
    n_sel = sel.shape[1]
    block = 256
    unit_rows = 4 * count
    ways.greet()

    def rows_of(line, kind, part):
        if part is None:
            return pl.ds(pl.multiple_of((line * 4 + kind) * count, count), count)
        return pl.ds(pl.multiple_of((line * 4 + kind) * count + part * half, half), half)

    def aux_chunk(line, kind, part, _):
        rows = aux.shape[0]
        at = line * 4 + kind
        if part is None:
            return aux_all.at[at]
        return aux_all.at[at, pl.ds(part * (rows // 2), rows // 2)]

    def sems(i):
        return (lambda k: ag_send.at[i, k], lambda k: ag_recv.at[i, k])

    gathers = [
        Gather(
            ways, lambda line, kind, part, _: nc.at[rows_of(line, kind, part), pl.ds(0, width)],
            sems(0), own=tok, relative=True,
        ),
        Gather(ways, aux_chunk, sems(1), own=aux, relative=True),
    ]

    cots = Gather(
        ways, lambda line, kind, part, _: nc.at[rows_of(line, kind, part), pl.ds(width, width)],
        sems(2), relative=True,
    )

    def each(name, *args):
        for g in gathers:
            getattr(g, name)(*args)

    def every(name, *args):
        each(name, *args)
        getattr(cots, name)(*args)

    each("begin")
    local = []
    mine = pl.ds(c * hc, hc)
    theirs = pl.ds(oc * hc, hc)
    w_copies = []
    for k, (src, dst) in enumerate(((wg, vg), (wu, vu), (wd, vd))):
        for j, (part, first, size) in enumerate(
            ((src, 0, n_routed), (shared.at[k], n_routed, hc - n_routed))
        ):
            there = dst.at[pl.ds(pl.multiple_of(c * hc + first, 16), size)]
            i = 2 * k + j
            copy = pltpu.make_async_copy(part, there, w_local.at[i])
            copy.start()
            local.append(copy)
            copy = remote(part, there, w_send.at[i], w_recv.at[i], ways.to_c)
            copy.start()
            w_copies.append(copy)

    copy = pltpu.make_async_copy(tok, nc.at[rows_of(z, O, None), pl.ds(0, width)], local_sem.at[3])
    copy.start()
    local.append(copy)
    copy = pltpu.make_async_copy(aux, aux_chunk(z, O, None, False), local_sem.at[4])
    copy.start()
    local.append(copy)
    cot_loads = []
    for u in (2, 3, 0, 1):
        size = unit_rows if u < 2 else count
        there = pl.ds(pl.multiple_of(zs[u] * unit_rows, unit_rows), size)
        cot_loads.append(
            pltpu.make_async_copy(cot.at[there], nc.at[there, pl.ds(width, width)], cot_sem.at[u])
        )
        cot_loads[-1].start()

    def zero(i, carry):
        dw[:, pl.ds(i * 64, 64), :] = jnp.zeros((3, 64, width), f32)
        return carry

    lax.fori_loop(0, hidden // 64, zero, 0)
    dr[...] = jnp.zeros_like(dr)

    def cut(ref, u, part):
        return ref.at[u] if part is None else ref.at[u, pl.ds(part * half, half)]

    back = Reduce(
        ways, lambda line, kind, part: nc.at[rows_of(line, kind, part), pl.ds(width, width)], cut,
        pq, xr, yr, dz, lambda slot: zr.at[slot],
        (lambda k: rs_send.at[k], lambda k: rs_recv.at[k]), alone=(2, 3),
    )

    def save(u):
        rows = pl.ds(pl.multiple_of(zs[u] * unit_rows, unit_rows), unit_rows)
        return pltpu.make_async_copy(
            nc.at[rows, pl.ds(0, width)], out_part.at[rows], local_sem.at[7 + u]
        )

    def expand(line, columns):
        return jnp.concatenate(
            [dot_tn(aux_all[line * 4 + kind], sel[:, columns]) for kind in range(4)], axis=0
        )

    def at_step(s, acts_of):
        for v, act in acts_of.items():
            when(s == v, act)

    def unit(u, carry):
        line = pick(zs, u)
        rows = pl.ds(pl.multiple_of(line * unit_rows, unit_rows), unit_rows)
        at_step(
            u,
            {
                1: lambda: (each("xy_event", 1), each("diag_handed", 1)),
                2: lambda: (every("diag_handed", 2), every("diag_carried", 3)),
                3: lambda: (every("diag_handed", 3), back.end(1), back.mid(2)),
            },
        )
        daff[...] = jnp.zeros_like(daff)

        def hidden_step(i, carry):
            h = pl.ds(pl.multiple_of(i * block, block), block)
            x = nc[rows, 0:width]
            gate_pre = dot_nt(x, vg[h, :])
            up_pre = dot_nt(x, vu[h, :])
            grad = dot_nt(nc[rows, width : 2 * width], vd[h, :])
            scale = jnp.maximum(expand(line, h) + ones[:, h], 0.0)
            sigma = 1.0 / (1.0 + jnp.exp(-gate_pre))
            silu = gate_pre * sigma
            act = silu * up_pre
            acts[:, h] = (act * scale).astype(bf16)
            daff[...] += dense_dot((act * grad).astype(bf16), sel_t[h, :])
            grad = grad * scale
            dg[:, h] = (grad * up_pre * sigma * (1.0 + gate_pre * (1.0 - sigma))).astype(bf16)
            du[:, h] = (grad * silu).astype(bf16)
            return carry

        lax.fori_loop(0, hidden // block, hidden_step, 0, unroll=True)
        signed = expand(line, pl.ds(hidden, n_sel - hidden))
        affinity = jnp.abs(signed)
        grad_aff = jnp.where(signed > 0, daff[...], 0.0)
        total = jnp.sum(affinity * grad_aff, axis=1, keepdims=True)
        dlg[...] = (affinity * (grad_aff - total)).astype(bf16)
        at_step(
            u,
            {
                0: lambda: (each("chain_event", 2), each("send_own", 2)),
                1: lambda: every("diag_carried", 2),
                2: lambda: (back.carry(0), cots.drain_unit(2)),
                3: lambda: (back.end(2), cots.drain_unit(3)),
            },
        )

        def down_step(i, carry):
            h = pl.ds(pl.multiple_of(i * block, block), block)
            dw[2, h, :] += dot_tn(acts[:, h], nc[rows, width : 2 * width])
            return carry

        lax.fori_loop(0, hidden // block, down_step, 0, unroll=True)

        def back_step(i, carry):
            n = pl.ds(pl.multiple_of(i * block, block), block)
            n2 = pl.ds(pl.multiple_of(width + i * block, block), block)
            nc[rows, n2] = (
                dense_dot(dg[...], vg[:, n])
                + dense_dot(du[...], vu[:, n])
                + dense_dot(dlg[...], router_t[:, n])
            ).astype(bf16)
            return carry

        lax.fori_loop(0, width // block, back_step, 0, unroll=True)
        at_step(
            u,
            {
                0: lambda: (each("chain_event", 3), cots.send_own(3)),
                1: lambda: (every("xy_event", 3), back.start(1), back.start(0)),
                2: lambda: (back.carry(2), back.start(2), back.mid(0)),
                3: lambda: (back.carry(3), back.start(3), back.end(0)),
            },
        )

        def weight_step(i, carry):
            h = pl.ds(pl.multiple_of(i * block, block), block)
            x = nc[rows, 0:width]
            dw[0, h, :] += dot_tn(dg[:, h], x)
            dw[1, h, :] += dot_tn(du[:, h], x)
            return carry

        lax.fori_loop(0, hidden // block, weight_step, 0, unroll=True)
        dr[...] += dot_tn(dlg[...], nc[rows, 0:width])
        at_step(
            u,
            {
                0: lambda: (every("xy_event", 2), each("send_own", 3), each("drain_chain", 1)),
                1: lambda: (each("drain_chain", 2), each("drain_chain", 3)),
                3: lambda: back.mid(3),
            },
        )
        for v in range(lines):
            when(u == v, lambda v=v: each("drain_unit", v))

        def out_step(i, carry):
            n = pl.ds(pl.multiple_of(i * block, block), block)
            nc[rows, n] = dense_dot(acts[...], vd[:, n]).astype(bf16)
            return carry

        lax.fori_loop(0, width // block, out_step, 0, unroll=True)
        for v in range(lines):
            when(u == v, lambda v=v: save(v).start())
        return carry

    each("xy_event", 0)
    each("chain_event", 1)
    each("send_own", 1)
    for copy in w_copies:
        copy.wait_recv()
    for copy in local + cot_loads:
        copy.wait()
    cots.send_own(2)
    each("diag_carried", 0)
    lax.fori_loop(0, lines, unit, 0)

    own_out = pltpu.make_async_copy(dw.at[:, mine], dw_own, local_sem.at[6])
    own_out.start()
    sib_out = pltpu.make_async_copy(dw.at[:, theirs], dw_sib, local_sem.at[7 + lines])
    sib_out.start()
    back.end(3)
    sums[...] = back.total()
    back.drain()
    for u in range(lines):
        save(u).wait()
    for copy in w_copies:
        copy.wait_send()
    sib_out.wait()
    own_out.wait()


def mixture_call(tok, aux, cot, weights, shared, sel, sel_t, router_t, ones, collective_id):
    lines = lax.axis_size("ep") // 2
    count, width = tok.shape
    hc = weights[0].shape[0] + shared.shape[1]
    anywhere = pl.BlockSpec(memory_space=pl.ANY)
    vmem = pl.BlockSpec(memory_space=pltpu.VMEM)
    n_rows = lines * 4 * count
    return pl.pallas_call(
        functools.partial(mixture_kernel, lines),
        out_shape=(
            jax.ShapeDtypeStruct((count, width), f32),
            jax.ShapeDtypeStruct((n_rows, width), bf16),
            jax.ShapeDtypeStruct((3, hc, width), f32),
            jax.ShapeDtypeStruct((3, hc, width), f32),
            jax.ShapeDtypeStruct((128, width), f32),
        ),
        in_specs=[anywhere] * 7 + [vmem] * 4,
        out_specs=(vmem, anywhere, anywhere, anywhere, vmem),
        scratch_shapes=[
            pltpu.VMEM((n_rows, 2 * width), bf16),
            pltpu.VMEM((lines * 4,) + aux.shape, bf16),
            pltpu.VMEM((2 * hc, width), bf16),
            pltpu.VMEM((2 * hc, width), bf16),
            pltpu.VMEM((2 * hc, width), bf16),
            pltpu.VMEM((3, 2 * hc, width), f32),
            pltpu.VMEM((4 * count, 2 * hc), bf16),
            pltpu.VMEM((4 * count, 2 * hc), bf16),
            pltpu.VMEM((4 * count, 2 * hc), bf16),
            pltpu.VMEM((4 * count, 128), f32),
            pltpu.VMEM((4 * count, 128), bf16),
            pltpu.VMEM((3, count, width), bf16),
            pltpu.VMEM((lines, count, width), bf16),
            pltpu.VMEM((lines, count, width), bf16),
            pltpu.VMEM((2, count, width), bf16),
            pltpu.VMEM((lines - 1, count, width), bf16),
            pltpu.SemaphoreType.DMA((3, 12 * lines)),
            pltpu.SemaphoreType.DMA((3, 12 * lines)),
            pltpu.SemaphoreType.DMA((8 * lines,)),
            pltpu.SemaphoreType.DMA((8 * lines,)),
            pltpu.SemaphoreType.DMA((6,)),
            pltpu.SemaphoreType.DMA((6,)),
            pltpu.SemaphoreType.DMA((6,)),
            pltpu.SemaphoreType.DMA((lines,)),
            pltpu.SemaphoreType.DMA((8 + lines,)),
        ],
        compiler_params=pltpu.CompilerParams(
            collective_id=collective_id, has_side_effects=True, vmem_limit_bytes=62 * 2**20
        ),
        name="mixture",
    )(tok, aux, cot, *weights, shared, sel, sel_t, router_t, ones)


def back_kernel(lines, experts, scale, sh, *refs):
    (
        lengths, dn2, residual, cot, group_in, small_t, router_part, attended, q, normed_in, cosine, sine,
        keys, vals, wall_in, outs_in, dw_own, dw_sib,
        layer_out, input_grad, gq, gk, gv, go, small_out, gsg, gsu, dw_got,
        normed, group, wall, part, staged, landed, pq, xr, yr, dz, zr, fin, fin_other,
        s_part, s_landed, s_pq, s_xr, s_yr, s_dz, s_zr,
        o_part, o_pq, o_xr, o_yr, o_dz, o_zr,
        grads, low, datt, dq, dk, dv, dn_part, dn_other, dn_far, bias, rows_t,
        e_blocks, e_r1, e_r2, e_r3, e_got,
        c_send, c_recv, r_send, r_recv, d_send, d_recv, e_send, e_recv, local_sem, credit,
    ) = refs
    ways = Ways(lines)
    z, a, b, c = ways.spot
    ob, oc = 1 - b, 1 - c
    count, width = cot.shape
    half = width // 2
    heads = width // 128
    chip_rows = pq.shape[1]
    d_rows = chip_rows // 2

    def load(i, src, dst):
        copy = pltpu.make_async_copy(src, dst, local_sem.at[i])
        copy.start()
        return copy

    o_load = load(0, outs_in, o_part)
    wo_loads = [
        load(1 + h, wall_in.at[:, pl.ds((h * 4 + 3) * half, half)], part.at[:, pl.ds(h * half, half)])
        for h in range(2)
    ]
    kv_loads = [load(3, keys, dk), load(4, vals, dv), load(11, normed_in, normed)]
    wall_loads = [
        load(5 + h, wall_in.at[:, pl.ds(h * 4 * half, 3 * half)], wall.at[:, pl.ds(h * 3 * half, 3 * half)])
        for h in range(2)
    ]

    wall_loads.append(load(12, group_in, group))

    def weight(h, k):
        return wall[:, pl.ds((h * 3 + k) * half, half)]

    ways.greet()

    half_rows = count // 2

    def o_chunk(line, kind, p):
        size = count if p is None else half_rows
        return o_part.at[pl.ds(pl.multiple_of((line * 4 + kind) * count + (p or 0) * size, size), size)]

    def o_cut(ref, u, p):
        return ref.at[u] if p is None else ref.at[u, pl.ds(p * half_rows, half_rows)]

    o_reduce = Reduce(
        ways, o_chunk, o_cut, o_pq, o_xr, o_yr, o_dz, lambda slot: o_zr.at[slot],
        (lambda i: r_send.at[3, i], lambda i: r_recv.at[3, i]),
    )

    def finish_output():
        layer_out[...] = (residual[...] + o_reduce.total()).astype(bf16)

    o_events = o_reduce.events() + [finish_output]
    o_load.wait()
    o_events[0]()
    dw_copy = remote(dw_sib, dw_got, c_send.at[6], c_recv.at[6], ways.to_c)
    dw_copy.start()
    exchange = Exchange(
        ways, e_blocks, e_r1, e_r2, e_r3, e_got, (lambda k: e_send.at[k], lambda k: e_recv.at[k])
    )
    e_events = exchange.events()
    shared_rows = pl.ds(dw_own.shape[1] - 64, 64)

    def shared_at(j, k):
        return (fin.at[pl.ds(0, 64), pl.ds(k * width, width)], rows_t.at[pl.ds(k * 64, 64)])[j]

    def shared_blocks():
        dw_copy.wait()
        loads = [
            load(7 + 2 * k + j, ref.at[k, shared_rows], shared_at(j, k))
            for k in range(2)
            for j, ref in enumerate((dw_own, dw_got))
        ]
        for copy in loads:
            copy.wait()
        turned = jnp.transpose(
            jnp.concatenate([fin[0:64, 0:width], fin[0:64, width : 2 * width]]) + rows_t[...]
        )
        for d, line, da, db, dc in all_places(lines):
            value = turned[d * d_rows : (d + 1) * d_rows]
            e_blocks[line, da, db, dc] = padded_rows(value, e_blocks.shape[4]).astype(bf16)
        e_events[0]()

    def shared_finish():
        lane = lax.broadcasted_iota(jnp.int32, (d_rows, 128), 1)
        for out, first in ((gsg, 0), (gsu, 64)):
            tiles = [jnp.zeros((d_rows, 128), f32) for _ in range(out.shape[1] // 128)]
            for d, *there in all_places(lines):
                tile, start = d * sh // 128, d * sh % 128
                value = exchange.block(*there)[:d_rows].astype(f32)
                value = pltpu.roll(value, (start - first) % 128, 1)
                if start + sh > 128:
                    tiles[tile] = jnp.where(lane >= start, value, tiles[tile])
                    tiles[tile + 1] = jnp.where(lane < start + sh - 128, value, tiles[tile + 1])
                else:
                    tiles[tile] = jnp.where((lane >= start) & (lane < start + sh), value, tiles[tile])
            for k, tile in enumerate(tiles):
                out[:, k * 128 : (k + 1) * 128] = tile

    res = residual[...]
    r2 = lax.rsqrt(jnp.mean(res * res, axis=-1, keepdims=True) + epsilon)
    unit_two = res * r2
    gain_two = small_t[experts + 1 : experts + 2, :].astype(f32)
    gain_one = small_t[experts : experts + 1, :].astype(f32)
    gain_two_row = jnp.sum(dn2[...] * unit_two, axis=0, keepdims=True)
    scaled = dn2[...] * gain_two
    back = r2 * (scaled - unit_two * jnp.mean(scaled * unit_two, axis=-1, keepdims=True))
    grads[...] = cot[...].astype(f32) + back
    low[...] = grads[...].astype(bf16)
    make_bias(bias, lengths, b * 2 + c)

    def weight_reduce(k, first, cols):
        low_cols = cols // 256 * 128

        def span(p):
            return (0, cols) if p is None else ((0, low_cols) if p == 0 else (low_cols, cols - low_cols))

        def chunk(line, kind, p):
            start, size = span(p)
            rows = pl.multiple_of(ways.chip(line, kind) * chip_rows, 16)
            return part.at[pl.ds(rows, chip_rows), pl.ds(first + start, size)]

        def cut(ref, u, p):
            start, size = span(p)
            return ref.at[u, :, pl.ds(first + start, size)]

        return Reduce(
            ways, chunk, cut, pq, xr, yr, dz, lambda slot: zr.at[slot, :, pl.ds(first, cols)],
            (lambda i: r_send.at[k, i], lambda i: r_recv.at[k, i]),
        )

    def small_span(p):
        first = chip_rows // 32 * 16
        return (0, chip_rows) if p is None else ((0, first) if p == 0 else (first, chip_rows - first))

    def small_chunk(line, kind, p):
        start, size = small_span(p)
        return s_part.at[pl.ds(pl.multiple_of(ways.chip(line, kind) * chip_rows + start, 16), size)]

    def small_cut(ref, u, p):
        start, size = small_span(p)
        return ref.at[u, pl.ds(start, size)]

    small_reduce = Reduce(
        ways, small_chunk, small_cut, s_pq, s_xr, s_yr, s_dz, lambda slot: s_zr.at[slot],
        (lambda i: r_send.at[2, i], lambda i: r_recv.at[2, i]),
    )
    qkv_reduce = weight_reduce(0, 0, 3 * half)
    wo_reduce = weight_reduce(1, 3 * half, half)

    def across(k):
        return remote(staged.at[k % 2], landed.at[k % 3], c_send.at[k], c_recv.at[k], ways.to_c)

    def swapped(k):
        across(k).wait_recv()

        def body(i, carry):
            rows = pl.ds(pl.multiple_of(i * chip_rows, 16), chip_rows)
            accumulate(part.at[rows, pl.ds(k * half, half)], [landed.at[k % 3, rows]])
            return carry

        lax.fori_loop(0, width // chip_rows, body, 0)
        if k == 3:
            pl.semaphore_signal(credit, inc=1, device_id=ways.to_c, device_id_type=MESH)

    later = []

    def service(n=1):
        for _ in range(n):
            if later:
                later.pop(0)()

    def columns(core):
        return pl.ds(pl.multiple_of(core * half, 128), half)

    def weight_grad(k, left, right):
        if k < 2:
            across(k + 2).wait_send()
        staged[k % 2] = dot_tn(left, right[:, columns(oc)]).astype(bf16)
        if k == 0:
            pl.semaphore_wait(credit, 1)
        across(k).start()
        part[:, pl.ds(k * half, half)] = dot_tn(left, right[:, columns(c)]).astype(bf16)

    o_events[1]()
    weight_grad(3, attended[...], low)
    for copy in wo_loads:
        copy.wait()
    datt[...] = (
        dot_nt(low[:, 0:half], part[:, 0:half]) + dot_nt(low[:, half:width], part[:, half:width])
    ).astype(bf16)
    wo_events = wo_reduce.events()
    later.append(lambda: swapped(3))
    for k in range(6):
        later.append(o_events[k + 2])
        later.extend(wo_events[:2] if k == 0 else [wo_events[k + 1]])
    for copy in kv_loads:
        copy.wait()

    own_rows = pl.ds(pl.multiple_of((b * 2 + c) * count, count), count)
    for h in range(heads):
        cols = pl.ds(h * 128, 128)
        key, val, query = dk[:, cols], dv[:, cols], q[:, cols]
        probs = softmax_rows(dot_nt(query, key) * scale + bias[...])
        dprobs = dot_nt(datt[:, cols], val)
        dscores = (
            probs * (dprobs - jnp.sum(probs * dprobs, axis=-1, keepdims=True))
        ).astype(bf16)
        dq[:, cols] = turn(
            dense_dot(dscores, key) * scale, cosine[own_rows, :], -sine[own_rows, :]
        ).astype(bf16)
        dk[:, cols] = turn(dot_tn(dscores, query) * scale, cosine[...], -sine[...]).astype(bf16)
        dv[:, cols] = dot_tn(probs.astype(bf16), datt[:, cols]).astype(bf16)
        if h in (0, 1, 2, 3, 4, 5, 7, 9):
            service()
    shared_blocks()
    weight_grad(2, normed[...], dv)
    weight_grad(1, normed[...], dk)
    swapped(2)
    service()
    e_events[1]()
    weight_grad(0, normed[own_rows, :], dq)
    swapped(1)
    swapped(0)
    qkv_events = qkv_reduce.events()
    qkv_events[0]()
    later = [later[0], later[1], qkv_events[1]] + later[2:]

    for copy in wall_loads:
        copy.wait()
    e_events[2]()
    rows_t[...] = router_part[...]
    rows_t[experts + 1 : experts + 2, :] = gain_two_row
    for t in range(4):
        rows = slice(t * count, (t + 1) * count)
        total = jnp.zeros((count, width), f32)
        for h in range(2):
            mine = slice(h * half, (h + 1) * half)
            total = total + dot_nt(dk[rows, mine], weight(h, 1)) + dot_nt(dv[rows, mine], weight(h, 2))
        dn_part[t] = total.astype(bf16)
        x = group[t].astype(f32)
        unit = x * lax.rsqrt(jnp.mean(x * x, axis=-1, keepdims=True) + epsilon)
        gain_row = jnp.sum(total * unit, axis=0, keepdims=True)
        if t == 0:
            rows_t[experts : experts + 1, :] = gain_row
        else:
            rows_t[experts : experts + 1, :] += gain_row
        service()

    def dn_copy(k, src, dst, to):
        return remote(src, dst, d_send.at[k], d_recv.at[k], to)

    dn_copies = [
        dn_copy(0, dn_part.at[b * 2 + oc], dn_other.at[0], ways.to_c),
        dn_copy(1, dn_part.at[ob * 2 + oc], dn_other.at[1], ways.to_c),
    ]
    for copy in dn_copies:
        copy.start()
    e_events[3]()
    own = jnp.zeros((count, width), f32)
    for h in range(2):
        own = own + dot_nt(dq[:, h * half : (h + 1) * half], weight(h, 0))
    x = group[b * 2 + c].astype(f32)
    r1 = lax.rsqrt(jnp.mean(x * x, axis=-1, keepdims=True) + epsilon)
    unit_one = x * r1
    rows_t[experts : experts + 1, :] += jnp.sum(own * unit_one, axis=0, keepdims=True)
    s_part[...] = jnp.transpose(rows_t[...]).astype(bf16)
    small_swap = remote(s_part, s_landed, c_send.at[4], c_recv.at[4], ways.to_c)
    small_swap.start()
    service()
    dn_copies[1].wait_recv()
    accumulate(dn_part.at[ob * 2 + c], [dn_other.at[1]])
    dn_copies.append(dn_copy(2, dn_part.at[ob * 2 + c], dn_far, ways.to_b))
    dn_copies[2].start()
    dn_copies[0].wait_recv()
    small_swap.wait()
    accumulate(s_part, [s_landed])
    service(len(later))
    small_events = small_reduce.events()
    for k in range(2, len(qkv_events)):
        later.extend([small_events[k - 2], qkv_events[k]])
    later.insert(2, lambda: (e_events[4](), shared_finish()))
    later.extend(small_events[-2:])
    service(6)
    dn_copies[2].wait_recv()
    total = (
        own
        + dn_part[b * 2 + c].astype(f32)
        + dn_other[0].astype(f32)
        + dn_far[...].astype(f32)
    )
    scaled = total * gain_one
    input_grad[...] = grads[...] + r1 * (
        scaled - unit_one * jnp.mean(scaled * unit_one, axis=-1, keepdims=True)
    )
    service(len(later))

    theirs = pl.ds(pl.multiple_of(oc * d_rows, 8), d_rows)
    mine = pl.ds(pl.multiple_of(c * d_rows, 8), d_rows)
    fin[:, pl.ds(3 * half, half)] = wo_reduce.total()
    fin[:, pl.ds(0, 3 * half)] = qkv_reduce.total()
    fin_copy = remote(fin.at[theirs], fin_other, c_send.at[5], c_recv.at[5], ways.to_c)
    fin_copy.start()
    s_total = small_reduce.total()
    small_out[...] = jnp.where(c == 0, s_total[:d_rows], s_total[d_rows:])
    for k, out in enumerate((gq, gk, gv, go)):
        out[:, columns(c)] = fin[mine, pl.ds(k * half, half)]
    fin_copy.wait_recv()
    for k, out in enumerate((gq, gk, gv, go)):
        out[:, columns(oc)] = fin_other[:, pl.ds(k * half, half)]
    for r in (qkv_reduce, wo_reduce, small_reduce, o_reduce):
        r.drain()
    for copy in dn_copies + [fin_copy]:
        copy.wait_send()
    exchange.drain()
    for k in range(2):
        across(k).wait_send()


def back_call(
    lengths, dn2, residual, cot, group, small_t, router_part, attended, q, normed, cosine, sine,
    keys, vals, wall, outs, dw_own, dw_sib, d_rows, experts, scale, sh, collective_id,
):
    lines = lax.axis_size("ep") // 2
    count, width = cot.shape
    half = width // 2
    chip_rows = 2 * d_rows
    group_len = 4 * count
    anywhere = pl.BlockSpec(memory_space=pl.ANY)
    vmem = pl.BlockSpec(memory_space=pltpu.VMEM)
    smem = pl.BlockSpec(memory_space=pltpu.SMEM)
    shape = jax.ShapeDtypeStruct
    dma = pltpu.SemaphoreType.DMA

    def landing(rows, cols):
        return [pltpu.VMEM((n, rows, cols), bf16) for n in (2, lines, lines, 2, lines - 1)]

    return pl.pallas_call(
        functools.partial(back_kernel, lines, experts, scale, sh),
        out_shape=(
            shape((count, width), bf16),
            shape((count, width), f32),
            shape((d_rows, width), f32),
            shape((d_rows, width), f32),
            shape((d_rows, width), f32),
            shape((d_rows, width), f32),
            shape((d_rows, 128), f32),
            shape((d_rows, 8 * lines * sh), f32),
            shape((d_rows, 8 * lines * sh), f32),
            shape(dw_sib.shape, f32),
        ),
        in_specs=(
            [smem] + [vmem] * 3 + [anywhere] + [vmem] * 4 + [anywhere] + [vmem] * 2 + [anywhere] * 6
        ),
        out_specs=(vmem,) * 9 + (anywhere,),
        scratch_shapes=[
            pltpu.VMEM((group_len, width), bf16),
            pltpu.VMEM((4, count, width), bf16),
            pltpu.VMEM((width, 6 * half), bf16),
            pltpu.VMEM((width, 4 * half), bf16),
            pltpu.VMEM((2, width, half), bf16),
            pltpu.VMEM((3, width, half), bf16),
            *landing(chip_rows, 4 * half),
            pltpu.VMEM((chip_rows, 4 * half), f32),
            pltpu.VMEM((d_rows, 4 * half), f32),
            pltpu.VMEM((width, 128), bf16),
            pltpu.VMEM((width, 128), bf16),
            *landing(chip_rows, 128),
            pltpu.VMEM(outs.shape, bf16),
            *landing(count, width),
            pltpu.VMEM((count, width), f32),
            pltpu.VMEM((count, width), bf16),
            pltpu.VMEM((count, width), bf16),
            pltpu.VMEM((count, width), bf16),
            pltpu.VMEM((group_len, width), bf16),
            pltpu.VMEM((group_len, width), bf16),
            pltpu.VMEM((4, count, width), bf16),
            pltpu.VMEM((2, count, width), bf16),
            pltpu.VMEM((count, width), bf16),
            pltpu.VMEM((count, group_len), f32),
            pltpu.VMEM((128, width), f32),
            *exchange_scratch(lines, -(-d_rows // 16) * 16),
            dma((7,)),
            dma((7,)),
            dma((4, 8 * lines)),
            dma((4, 8 * lines)),
            dma((3,)),
            dma((3,)),
            dma((7 + lines,)),
            dma((7 + lines,)),
            dma((13,)),
            pltpu.SemaphoreType.REGULAR,
        ],
        compiler_params=pltpu.CompilerParams(
            collective_id=collective_id, has_side_effects=True, vmem_limit_bytes=63 * 2**20
        ),
        name="back",
    )(
        lengths, dn2, residual, cot, group, small_t, router_part, attended, q, normed, cosine, sine,
        keys, vals, wall, outs, dw_own, dw_sib,
    )


def documents(positions, lengths):
    seq_ends = jnp.cumsum(lengths)
    doc_index = (positions >= seq_ends[0]).astype(jnp.int32) + (positions >= seq_ends[1]).astype(
        jnp.int32
    )
    seq_starts = jnp.where(doc_index == 0, 0, jnp.where(doc_index == 1, seq_ends[0], seq_ends[1]))
    return (doc_index, positions - seq_starts)


def rotary_tables(offsets, head_dim):
    half_dim = head_dim // 2
    frequency = 10000.0 ** (-2.0 * jnp.arange(half_dim, dtype=f32) / head_dim)
    angles = offsets.astype(f32)[:, None] * frequency[None, :]
    return (jnp.cos(angles)[:, None, :], jnp.sin(angles)[:, None, :])


def rotate(values, cosine, sine_table):
    half_dim = values.shape[-1] // 2
    first_half = values[..., :half_dim]
    second_half = values[..., half_dim:]
    return jnp.concatenate(
        [
            first_half * cosine - second_half * sine_table,
            first_half * sine_table + second_half * cosine,
        ],
        axis=-1,
    )


def norm_back(grad_normed, unit_rows, inverse, gain):
    scaled = grad_normed * gain
    return inverse * (scaled - unit_rows * jnp.mean(scaled * unit_rows, axis=-1, keepdims=True))


def dot(left, right, contract):
    return lax.dot_general(left, right, ((contract[0], contract[1]), ((), ())), preferred_element_type=f32)


def dense_dot(left, right):
    return dot(left, right, ((1,), (0,)))


def dot_nt(left, right):
    return dot(left, right, ((1,), (1,)))


def dot_tn(left, right):
    return dot(left, right, ((0,), (0,)))


def any_slice(
    hidden_in,
    seq_lengths,
    expert_ids,
    attn_gain,
    w_query,
    w_key,
    w_value,
    w_out,
    ffn_gain,
    shared_gate,
    shared_up,
    shared_down,
    router,
    expert_gate,
    expert_up,
    expert_down,
    cotangent,
):
    tok_count, model_width = hidden_in.shape
    eps, tps = lax.axis_size("ep"), lax.axis_size("tp")
    devices = eps * tps
    exp_local, exp_hidden = expert_gate.shape[:2]
    experts = exp_local * eps
    group_len = tps * tok_count
    tokens = devices * tok_count
    d_rows = w_query.shape[0]
    width = w_query.shape[1]
    sh_rows = shared_down.shape[0]
    head_dim = width // HEADS
    attn_scale = head_dim ** (-0.5)

    flat = jnp.concatenate([router.reshape(-1), attn_gain, ffn_gain])
    small_len = -(-flat.shape[0] // model_width) * model_width
    small = jnp.pad(flat, (0, small_len - flat.shape[0])).reshape(-1, model_width)
    small = jnp.pad(small, ((0, -small.shape[0] % 16), (0, 0)))
    weights = jnp.concatenate([w_query, w_key, w_value, w_out], axis=1)

    all_weights, all_small, all_cot = [
        lax.all_gather(v, AXES, axis=0) for v in (weights, small, cotangent)
    ]
    group_hidden = lax.all_gather(hidden_in, "tp", axis=0)
    all_weights = all_weights.reshape(devices * d_rows, 4 * width)
    full_query = all_weights[:, :width]
    full_key = all_weights[:, width : 2 * width]
    full_value = all_weights[:, 2 * width : 3 * width]
    full_out = all_weights[:, 3 * width :]
    all_small = all_small.reshape(devices, -1)
    n_router = d_rows * experts
    full_router = all_small[:, :n_router].reshape(devices * d_rows, experts)
    gain_one = all_small[:, n_router : n_router + d_rows].reshape(-1).astype(f32)
    gain_two = all_small[:, n_router + d_rows : n_router + 2 * d_rows].reshape(-1).astype(f32)
    cot_all = all_cot.reshape(-1, model_width)

    shared_cols = jnp.stack([shared_gate, shared_up], axis=1).reshape(d_rows, 2, devices, sh_rows)
    shared_cols = lax.all_to_all(
        shared_cols.transpose(2, 1, 3, 0), AXES, split_axis=0, concat_axis=0, tiled=True
    )
    shared_t = shared_cols.transpose(1, 2, 0, 3).reshape(2, sh_rows, model_width)

    lengths = seq_lengths[0]
    tp_index = lax.axis_index("tp")
    own_pos = tp_index * tok_count + jnp.arange(tok_count, dtype=jnp.int32)
    all_pos = jnp.arange(group_len, dtype=jnp.int32)
    own_doc, own_offset = documents(own_pos, lengths)
    all_doc, all_offset = documents(all_pos, lengths)
    allowed = (own_doc[:, None] == all_doc[None, :]) & (own_pos[:, None] >= all_pos[None, :])
    cosine, sine_table = rotary_tables(own_offset, head_dim)
    cosine_all, sine_all = rotary_tables(all_offset, head_dim)

    inputs = hidden_in.astype(f32)
    inverse_one = lax.rsqrt(jnp.mean(inputs * inputs, axis=-1, keepdims=True) + epsilon)
    unit_one = inputs * inverse_one
    normed = (unit_one * gain_one).astype(bf16)
    group_in = group_hidden.reshape(group_len, model_width).astype(f32)
    group_unit = group_in * lax.rsqrt(jnp.mean(group_in * group_in, axis=-1, keepdims=True) + epsilon)
    group_normed = (group_unit * gain_one).astype(bf16)

    queries = rotate(
        dense_dot(normed, full_query).reshape(tok_count, HEADS, head_dim), cosine, sine_table
    ).astype(bf16)
    key_rows = rotate(
        dense_dot(group_normed, full_key).reshape(group_len, HEADS, head_dim), cosine_all, sine_all
    ).astype(bf16)
    value_rows = dense_dot(group_normed, full_value).astype(bf16).reshape(group_len, HEADS, head_dim)

    def masked_scores():
        raw_scores = (
            jnp.einsum("qhd,khd->hqk", queries, key_rows, preferred_element_type=f32) * attn_scale
        )
        return jnp.where(allowed[None], raw_scores, -1e30)

    scores = masked_scores()
    row_peak = jnp.max(scores, axis=-1, keepdims=True)
    row_total = jnp.sum(jnp.exp(scores - row_peak), axis=-1, keepdims=True)
    softmaxed = jnp.exp(scores - row_peak) / row_total
    attended = (
        jnp.einsum("hqk,khd->qhd", softmaxed.astype(bf16), value_rows, preferred_element_type=f32)
        .reshape(tok_count, width)
        .astype(bf16)
    )
    residual = inputs + dense_dot(attended, full_out)
    inverse_two = lax.rsqrt(jnp.mean(residual * residual, axis=-1, keepdims=True) + epsilon)
    unit_two = residual * inverse_two
    normed_two = (unit_two * gain_two).astype(bf16)

    affinity = jax.nn.softmax(dense_dot(normed_two, full_router), axis=-1)
    expert_range = jnp.arange(experts, dtype=jnp.int32)
    named = jnp.any(expert_ids[:, :, None] == expert_range[None, None, :], axis=1)
    signed = jnp.where(named, affinity, -affinity)

    first_expert = lax.axis_index("ep") * exp_local
    n_routed = exp_local * exp_hidden
    hidden = n_routed + sh_rows
    gate_w = jnp.concatenate([expert_gate.reshape(n_routed, model_width), shared_t[0]])
    up_w = jnp.concatenate([expert_up.reshape(n_routed, model_width), shared_t[1]])
    down_w = jnp.concatenate([expert_down.reshape(n_routed, model_width), shared_down])

    def mixture(rows, cot_rows, signed):
        count = rows.shape[0]
        mine = lax.dynamic_slice_in_dim(signed, first_expert, exp_local, axis=1)
        mine_named = mine > 0
        gates = jnp.where(mine_named, mine, 0.0)
        scale = jnp.concatenate(
            [jnp.repeat(gates, exp_hidden, axis=1), jnp.ones((count, sh_rows), f32)], axis=1
        )
        gate_pre = dot_nt(rows, gate_w)
        up_pre = dot_nt(rows, up_w)
        sigma = jax.nn.sigmoid(gate_pre)
        silu = gate_pre * sigma
        act = silu * up_pre
        act_scaled = (act * scale).astype(bf16)
        out_part = dense_dot(act_scaled, down_w).astype(bf16)
        grad_hidden = dot_nt(cot_rows, down_w)
        grad_gates = jnp.sum(
            (act * grad_hidden)[:, :n_routed].reshape(count, exp_local, exp_hidden), axis=-1
        )
        grad_gates = jnp.where(mine_named, grad_gates, 0.0)
        grad_hidden = grad_hidden * scale
        grad_gate_pre = (grad_hidden * up_pre * sigma * (1.0 + gate_pre * (1.0 - sigma))).astype(
            bf16
        )
        grad_up_pre = (grad_hidden * silu).astype(bf16)
        affinity_all = jnp.abs(signed)
        grad_aff = lax.dynamic_update_slice_in_dim(
            jnp.zeros((count, experts), f32), grad_gates, first_expert, axis=1
        )
        grad_logits = (
            affinity_all * (grad_aff - jnp.sum(affinity_all * grad_aff, axis=-1, keepdims=True))
        ).astype(bf16)
        dn2_part = (
            dense_dot(grad_gate_pre, gate_w)
            + dense_dot(grad_up_pre, up_w)
            + dot_nt(grad_logits, full_router)
        ).astype(bf16)
        sums = (
            dot_tn(act_scaled, cot_rows),
            dot_tn(grad_gate_pre, rows),
            dot_tn(grad_up_pre, rows),
            dot_tn(rows, grad_logits),
        )
        return out_part, dn2_part, sums

    rows, signed_all = [lax.all_gather(v, AXES, axis=0, tiled=True) for v in (normed_two, signed)]
    blocks = max(1, tokens * hidden * 4 // 2**23)
    while tokens % blocks:
        blocks += 1

    def step(totals, block):
        out_block, dn2_block, sums = mixture(*block)
        return jax.tree.map(jnp.add, totals, sums), (out_block, dn2_block)

    zeros = (jnp.zeros((hidden, model_width), f32),) * 3 + (
        jnp.zeros((model_width, experts), f32),
    )
    sums, (out_part, dn2_part) = lax.scan(
        step,
        zeros,
        jax.tree.map(
            lambda v: v.reshape((blocks, -1) + v.shape[1:]), (rows, cot_all, signed_all)
        ),
    )
    grad_down, grad_gate, grad_up, router_part = sums
    routed_sum, grad_normed_two = [
        lax.psum_scatter(v.reshape(tokens, model_width), AXES, tiled=True).astype(f32)
        for v in (out_part, dn2_part)
    ]
    layer_output = (residual + routed_sum).astype(bf16)

    gain_two_part = jnp.sum(grad_normed_two * unit_two, axis=0)
    grad_resid = cotangent.astype(f32) + norm_back(grad_normed_two, unit_two, inverse_two, gain_two)
    grad_resid_low = grad_resid.astype(bf16)
    wout_part = dot_tn(attended, grad_resid_low)
    grad_att = dot_nt(grad_resid_low, full_out).astype(bf16).reshape(tok_count, HEADS, head_dim)
    softmax_again = jnp.exp(masked_scores() - row_peak) / row_total
    grad_soft = jnp.einsum("qhd,khd->hqk", grad_att, value_rows, preferred_element_type=f32)
    grad_scores = (
        softmax_again * (grad_soft - jnp.sum(softmax_again * grad_soft, axis=-1, keepdims=True))
    ).astype(bf16)
    grad_queries = (
        jnp.einsum("hqk,khd->qhd", grad_scores, key_rows, preferred_element_type=f32) * attn_scale
    )
    grad_key_rows = (
        jnp.einsum("hqk,qhd->khd", grad_scores, queries, preferred_element_type=f32) * attn_scale
    )
    grad_value_rows = jnp.einsum(
        "hqk,qhd->khd", softmax_again.astype(bf16), grad_att, preferred_element_type=f32
    )
    grad_q_pre = rotate(grad_queries, cosine, -sine_table).reshape(tok_count, width).astype(bf16)
    grad_k_pre = rotate(grad_key_rows, cosine_all, -sine_all).reshape(group_len, width).astype(bf16)
    grad_v_pre = grad_value_rows.reshape(group_len, width).astype(bf16)
    wq_part = dot_tn(normed, grad_q_pre)
    wk_part = dot_tn(group_normed, grad_k_pre)
    wv_part = dot_tn(group_normed, grad_v_pre)
    own_normed_grad = dot_nt(grad_q_pre, full_query)
    group_normed_grad = dot_nt(grad_k_pre, full_key) + dot_nt(grad_v_pre, full_value)
    gain_one_part = jnp.sum(own_normed_grad * unit_one, axis=0) + jnp.sum(
        group_normed_grad * group_unit, axis=0
    )

    weight_part = jnp.concatenate([wq_part, wk_part, wv_part, wout_part], axis=1).astype(bf16)
    small_part = jnp.concatenate(
        [
            router_part.reshape(devices, n_router),
            gain_one_part.reshape(devices, d_rows),
            gain_two_part.reshape(devices, d_rows),
        ],
        axis=1,
    )
    small_part = jnp.pad(small_part, ((0, 0), (0, small_len - small_part.shape[1])))
    small_part = small_part.reshape(devices, -1, model_width)
    small_part = jnp.pad(small_part, ((0, 0), (0, -small_part.shape[1] % 16), (0, 0))).astype(bf16)
    weight_part = weight_part.reshape(devices, d_rows, 4 * width)
    group_part = group_normed_grad.astype(bf16).reshape(tps, tok_count, model_width)
    weight_sum, small_sum = [
        lax.psum_scatter(v, AXES).astype(f32) for v in (weight_part, small_part)
    ]
    normed_grad_sum = lax.psum_scatter(group_part, "tp").astype(f32)
    grad_normed = own_normed_grad + normed_grad_sum
    input_grad = grad_resid + norm_back(grad_normed, unit_one, inverse_one, gain_one)
    small_sum = small_sum.reshape(-1)

    shared_back = jnp.stack([grad_gate[n_routed:], grad_up[n_routed:]])
    shared_back = shared_back.reshape(2, sh_rows, devices, d_rows).transpose(2, 0, 1, 3)
    shared_back = lax.all_to_all(shared_back, AXES, split_axis=0, concat_axis=0, tiled=True)
    shared_back = shared_back.transpose(1, 3, 0, 2).reshape(2, d_rows, devices * sh_rows)

    return (
        layer_output,
        input_grad,
        small_sum[n_router : n_router + d_rows],
        weight_sum[:, :width],
        weight_sum[:, width : 2 * width],
        weight_sum[:, 2 * width : 3 * width],
        weight_sum[:, 3 * width :],
        small_sum[n_router + d_rows : n_router + 2 * d_rows],
        shared_back[0],
        shared_back[1],
        grad_down[n_routed:],
        small_sum[:n_router].reshape(d_rows, experts),
        grad_gate[:n_routed].reshape(expert_gate.shape),
        grad_up[:n_routed].reshape(expert_up.shape),
        grad_down[:n_routed].reshape(expert_down.shape),
    )


def small_slice(
    hidden_in,
    seq_lengths,
    expert_ids,
    attn_gain,
    w_query,
    w_key,
    w_value,
    w_out,
    ffn_gain,
    shared_gate,
    shared_up,
    shared_down,
    router,
    expert_gate,
    expert_up,
    expert_down,
    cotangent,
):
    tok_count, model_width = hidden_in.shape
    eps, tps = lax.axis_size("ep"), lax.axis_size("tp")
    devices = eps * tps
    exp_local, exp_hidden = expert_gate.shape[:2]
    experts = exp_local * eps
    group_len = tps * tok_count
    tokens = devices * tok_count
    d_rows = w_query.shape[0]
    width = w_query.shape[1]
    sh_rows = shared_down.shape[0]
    head_dim = width // HEADS
    attn_scale = head_dim ** (-0.5)

    lanes = 128
    vectors = jnp.stack([attn_gain, ffn_gain], axis=1)
    small = jnp.concatenate([router, vectors], axis=1)
    small = jnp.pad(small, ((0, 0), (0, lanes - small.shape[1])))
    (
        w_all, cot_all, normed_two, aux, small_t, residual, attended, queries, key_rows, value_rows,
        group_normed, cos_all, sin_all, group_hidden, shared,
    ) = front_call(
        seq_lengths, expert_ids, hidden_in, small, (w_query, w_key, w_value, w_out),
        (shared_gate, shared_up, shared_down), cotangent, experts, attn_scale, 0,
    )
    first_expert = lax.axis_index("ep") * exp_local
    n_routed = exp_local * exp_hidden
    hidden = n_routed + sh_rows
    h_core = n_routed + shared.shape[1]
    owner = jnp.arange(h_core, dtype=jnp.int32)
    owner = jnp.where(owner < n_routed, first_expert + owner // exp_hidden, experts)
    owner = jnp.concatenate([owner, owner])
    sel_t = (owner[:, None] == jnp.arange(lanes, dtype=jnp.int32)[None, :]).astype(bf16)
    sel = jnp.concatenate([sel_t[:, :experts].T, jnp.eye(experts, lanes, dtype=bf16)], axis=1)
    sel = jnp.concatenate([sel, sel])
    ones = (jnp.arange(2 * h_core, dtype=jnp.int32) % h_core)[None, :]
    ones = ((ones >= n_routed) & (ones < hidden)).astype(f32)
    token_grads, out_parts, grads_here, grads_away, router_sum = mixture_call(
        normed_two,
        aux,
        cot_all,
        [w.reshape(n_routed, model_width) for w in (expert_gate, expert_up, expert_down)],
        shared,
        sel,
        sel_t,
        small_t,
        ones,
        2,
    )
    (
        layer_output, input_grad, grad_q, grad_k, grad_v, grad_o, small_sum, grad_sg, grad_su, grads_there,
    ) = back_call(
        seq_lengths, token_grads, residual, cotangent, group_hidden, small_t, router_sum, attended,
        queries, group_normed, cos_all, sin_all, key_rows, value_rows, w_all, out_parts,
        grads_here, grads_away, d_rows, experts, attn_scale, sh_rows, 3,
    )
    grad_gate, grad_up, grad_down = [
        (grads_here[k, :n_routed] + grads_there[k, :n_routed]).reshape(expert_gate.shape)
        for k in range(3)
    ]
    grad_sd = grads_here[2, n_routed:hidden] + grads_there[2, n_routed:hidden]

    return (
        layer_output,
        input_grad,
        small_sum[:, experts],
        grad_q,
        grad_k,
        grad_v,
        grad_o,
        small_sum[:, experts + 1],
        grad_sg,
        grad_su,
        grad_sd,
        small_sum[:, :experts],
        grad_gate,
        grad_up,
        grad_down,
    )


def solution(mesh):
    rows = P(AXES, None)
    vector = P(AXES)
    experts = P("ep", "tp", None)
    small = mesh.shape["ep"] == 8 and mesh.shape["tp"] == 4
    return jax.shard_map(
        small_slice if small else any_slice,
        mesh=mesh,
        in_specs=(
            rows, P("ep", None), rows, vector, rows, rows, rows, rows, vector,
            rows, rows, rows, rows, experts, experts, experts, rows,
        ),
        out_specs=(
            rows, rows, vector, rows, rows, rows, rows, vector,
            rows, rows, rows, rows, experts, experts, experts,
        ),
        check_vma=False,
    )
```
